32 devices in a mesh: videos: 2 (over x), rows: 16 (over z, y, core).
Axes of the slice: x: 2, y: 2, z: 4, core: 2. Of those that a mesh axis runs over, the one named last changes fastest.
Arguments:
- latents: bfloat16 [4, 32, 64, 384], P('videos', 'rows'), parts along dimension 0, may hold values from -6 to 6
- conv_cache: bfloat16 [4, 32, 64, 384], P('videos', 'rows'), parts along dimension 0, may hold values from -4 to 4
- norm_gain: float32 [384], replicated, may hold values from 0.1 to 1.9
- conv_weight: bfloat16 [3, 3, 3, 384, 384], replicated, may hold values from -0.0625 to 0.0625
- attn_gain: float32 [384], replicated, may hold values from 0.1 to 1.9
- query_weight: bfloat16 [384, 384], replicated, may hold values from -3 to 3
- key_weight: bfloat16 [384, 384], replicated, may hold values from -3 to 3
- value_weight: bfloat16 [384, 384], replicated, may hold values from -0.3125 to 0.3125
- out_weight: bfloat16 [384, 384], replicated, may hold values from -0.3125 to 0.3125
- up_weight: bfloat16 [3, 3, 384, 192], replicated, may hold values from -0.109375 to 0.109375
Outputs:
- decoded: bfloat16 [4, 64, 128, 192], P('videos', 'rows'), parts along dimension 0
- next_cache: bfloat16 [4, 32, 64, 384], P('videos', 'rows'), parts along dimension 0
The draws below stay inside these ranges and needn't reach their ends.
There are 2 independent parts, one for each index of `videos`. The reference program is written for one: setup_inputs(seed, part) draws one part's arguments, and reference() takes and returns one part's arrays. A program takes and returns all parts, laid end to end along the dimension named above; an argument that names none is the same for every part. Nothing has to cross between parts.
All inputs are finite; a program needn't handle non-finite values.
Results may differ from the reference program's by a relative error of at most 0.0058.
Values may be sent and summed in bfloat16 or wider, within the bound.
No kernel may reach another device: no remote copies, remote signals or barrier semaphores. Data moves between devices by JAX's collectives and lax.ppermute only.
A program may use at most 128 MiB of HBM per device.

```python
import math
import jax
import jax.numpy as jnp
from jax import lax

C = 384
C_HALF = 192
FRAMES = 2
CACHE = 2
WIDTH = 64
HEIGHT = 32


def own_noise(key, label, factor):
    noise = jnp.clip(jax.random.normal(jax.random.fold_in(key, label), (C, C), jnp.float32), -4.0, 4.0)
    return factor * noise / math.sqrt(C)


def draw_query_weight(key, part):
    mixed = own_noise(key, 201, 1.25)
    return jnp.clip(mixed, -3.0, 3.0).astype(jnp.bfloat16)


def draw_key_weight(key, part):
    mixed = own_noise(key, 202, 1.25)
    return jnp.clip(mixed, -3.0, 3.0).astype(jnp.bfloat16)


def levels(stream_key, shape, pieces, smallest, high):
    loudness = 1.0
    for dim, blocks in pieces:
        steps = jax.random.uniform(jax.random.fold_in(jax.random.fold_in(stream_key, 6), dim), (blocks,), jnp.float32, smallest / len(pieces), high / len(pieces))
        loudness = loudness * jnp.repeat(jnp.exp(steps), shape[dim] // blocks).reshape((-1,) + (1,) * (len(shape) - 1 - dim))
    return loudness


def normal_values(stream_key, shape, spread, most, split=(), dtype=jnp.bfloat16):
    loudness = levels(stream_key, shape, split, -0.22, 0.18) if split else 1.0
    drawn = jax.random.normal(stream_key, shape, jnp.float32) * spread * loudness
    return jnp.minimum(jnp.maximum(drawn, -most), most).astype(dtype)


def setup_inputs(seed: int = 0, part: int = 0) -> dict:
    splits = jax.random.split(jax.random.key(seed), 11)
    own_keys = jax.random.split(jax.random.fold_in(splits[10], part), 11)
    return {
        "latents": normal_values(own_keys[0], (FRAMES, HEIGHT, WIDTH, C), 1.0, 6.0, ((1, 16),)),
        "conv_cache": normal_values(own_keys[1], (CACHE, HEIGHT, WIDTH, C), 0.6, 4.0, ((1, 16),)),
        "norm_gain": jnp.clip(1.0 + 0.18 * jax.random.normal(splits[2], (C,), jnp.float32), 0.1, 1.9),
        "conv_weight": normal_values(splits[3], (3, 3, 3, C, C), (27 * C) ** -0.5, 0.0625),
        "attn_gain": jnp.clip(1.0 + 0.18 * jax.random.normal(splits[4], (C,), jnp.float32), 0.1, 1.9),
        "query_weight": draw_query_weight(jax.random.fold_in(splits[10], 71), part),
        "key_weight": draw_key_weight(jax.random.fold_in(splits[10], 71), part),
        "value_weight": normal_values(splits[7], (C, C), C ** -0.5, 0.3125),
        "out_weight": normal_values(splits[8], (C, C), C ** -0.5, 0.3125),
        "up_weight": normal_values(splits[9], (3, 3, C, C_HALF), (9 * C) ** -0.5, 0.109375),
    }


def normalize(values, gain):
    return values * lax.rsqrt(lax.optimization_barrier(jnp.mean(values * values, axis=-1, keepdims=True)) + 1e-06) * gain

def frame_attention(operands):
    query_rows, key_rows, value_rows = operands
    scores = jnp.dot(query_rows, key_rows.T, preferred_element_type=jnp.float32) * C ** (-0.5)
    largest = lax.optimization_barrier(jnp.max(scores, axis=-1, keepdims=True))
    weights = jnp.exp(scores - largest)
    totals = lax.optimization_barrier(jnp.sum(weights, axis=-1, keepdims=True))
    summed = jnp.dot(weights.astype(jnp.bfloat16), value_rows, preferred_element_type=jnp.float32)
    return (summed / totals).astype(jnp.bfloat16)

def reference(latents, conv_cache, norm_gain, conv_weight, attn_gain, query_weight, key_weight, value_weight, out_weight, up_weight):
    frames, height, width, channels = latents.shape
    values_in = latents.astype(jnp.float32)
    conv_input = jax.nn.silu(normalize(values_in, norm_gain)).astype(jnp.bfloat16)
    stacked = jnp.concatenate([conv_cache, conv_input], axis=0)
    padded = jnp.pad(stacked, ((0, 0), (1, 1), (1, 1), (0, 0)))
    total = jnp.zeros((frames * height * width, channels), jnp.float32)
    for tap_time in range(3):
        for tap_row in range(3):
            for tap_col in range(3):
                window = padded[tap_time:tap_time + frames, tap_row:tap_row + height, tap_col:tap_col + width]
                total = total + jnp.dot(window.reshape(-1, channels), conv_weight[tap_time, tap_row, tap_col], preferred_element_type=jnp.float32)
    resid = values_in + total.reshape(frames, height, width, channels)
    normed = normalize(resid, attn_gain).astype(jnp.bfloat16).reshape(-1, channels)
    queries = jnp.dot(normed, query_weight, preferred_element_type=jnp.float32).astype(jnp.bfloat16).reshape(frames, height * width, channels)
    keys = jnp.dot(normed, key_weight, preferred_element_type=jnp.float32).astype(jnp.bfloat16).reshape(frames, height * width, channels)
    values = jnp.dot(normed, value_weight, preferred_element_type=jnp.float32).astype(jnp.bfloat16).reshape(frames, height * width, channels)
    attended = lax.map(frame_attention, (queries, keys, values))
    projected = jnp.dot(attended.reshape(-1, channels), out_weight, preferred_element_type=jnp.float32)
    mid = (resid + projected.reshape(frames, height, width, channels)).astype(jnp.bfloat16)
    upsampled = jnp.repeat(jnp.repeat(mid, 2, axis=1), 2, axis=2)
    fine_pad = jnp.pad(upsampled, ((0, 0), (1, 1), (1, 1), (0, 0)))
    outputs = up_weight.shape[3]
    result = jnp.zeros((frames * 2 * height * 2 * width, outputs), jnp.float32)
    for tap_row in range(3):
        for tap_col in range(3):
            window = fine_pad[:, tap_row:tap_row + 2 * height, tap_col:tap_col + 2 * width]
            result = result + jnp.dot(window.reshape(-1, channels), up_weight[tap_row, tap_col], preferred_element_type=jnp.float32)
    decoded = result.reshape(frames, 2 * height, 2 * width, outputs).astype(jnp.bfloat16)
    next_cache = conv_input[frames - CACHE:]
    return (decoded, next_cache)
```

```python
import functools

import jax
import jax.numpy as jnp
from jax import lax
from jax.experimental import pallas as pl
from jax.experimental.pallas import tpu as pltpu
from jax.sharding import PartitionSpec as P

BF16 = jnp.bfloat16
F32 = jnp.float32
EPS = 1e-06
MIB = 1024 * 1024


def normalize(values, gain):
    return values * lax.rsqrt(jnp.mean(values * values, axis=-1, keepdims=True) + EPS) * gain


def activate(values, gain):
    normed = normalize(values.astype(F32), gain)
    return (normed / (1.0 + jnp.exp(-normed))).astype(BF16)


def vmem():
    return pl.BlockSpec(memory_space=pltpu.VMEM)


def params(mib):
    return pltpu.CompilerParams(vmem_limit_bytes=mib * MIB)


def cost(flops, size, exps=0):
    return pl.CostEstimate(flops=flops, bytes_accessed=size, transcendentals=exps)


def activate_kernel(latents_ref, gain_ref, out_ref):
    out_ref[...] = activate(latents_ref[...], gain_ref[...])


def conv_kernel(
    width,
    latents_ref,
    cache_ref,
    act_ref,
    swap_ref,
    first_ref,
    second_ref,
    norm_gain_ref,
    attn_gain_ref,
    weight_ref,
    normed_ref,
    resid_ref,
    held,
    weights,
    base,
    total,
    sems,
):
    channels = latents_ref.shape[-1]
    core = lax.axis_index("rows") % 2
    copies = []
    for time in range(3):
        for col in range(3):
            copy = pltpu.make_async_copy(
                weight_ref.at[time, :, col],
                weights.at[time, :, :, pl.ds(col * channels, channels)],
                sems.at[time, col],
            )
            copy.start()
            copies.append(copy)
    own = 2 * width
    mine = pl.multiple_of((1 + 2 * core) * width, width)
    other = pl.multiple_of((3 - 2 * core) * width, width)
    edge_first = pl.multiple_of(5 * core * width, width)
    edge_second = pl.multiple_of(5 * (1 - core) * width, width)
    gain = norm_gain_ref[...]

    def place(time, value_own, convert):
        held[time, pl.ds(mine, own), :] = value_own
        held[time, pl.ds(other, own), :] = convert(swap_ref[time])
        held[time, pl.ds(edge_first, width), :] = convert(first_ref[time])
        held[time, pl.ds(edge_second, width), :] = convert(second_ref[time])

    place(0, cache_ref[core], lambda v: v)

    @pl.when(core == 0)
    def _():
        place(1, cache_ref[1], lambda v: v)

    @pl.when(core == 1)
    def _():
        place(1, act_ref[0], lambda v: activate(v, gain))

    place(2, act_ref[core], lambda v: activate(v, gain))
    base[pl.ds(pl.multiple_of(2 * core * width, width), own), :] = latents_ref[core].astype(F32)
    base[pl.ds(pl.multiple_of(2 * (1 - core) * width, width), own), :] = swap_ref[2].astype(F32)

    span = 4 * width
    for time in range(3):
        for col in range(3):
            copies[3 * time + col].wait()
        lhs = jnp.concatenate(
            [held[time, row * width : row * width + span, :] for row in range(3)], axis=1
        )
        rhs = weights[time].reshape(3 * channels, 3 * channels)
        part = jnp.dot(lhs, rhs, preferred_element_type=F32)
        if time == 0:
            total[...] = part
        else:
            total[...] += part
    column = lax.broadcasted_iota(jnp.int32, (span, 1), 0) % width
    left = pltpu.roll(total[:, :channels], 1, axis=0)
    right = pltpu.roll(total[:, 2 * channels :], span - 1, axis=0)
    conv_out = total[:, channels : 2 * channels]
    conv_out = conv_out + jnp.where(column == 0, 0.0, left)
    conv_out = conv_out + jnp.where(column == width - 1, 0.0, right)
    resid = base[...] + conv_out
    resid_ref[...] = resid
    normed_ref[...] = normalize(resid, attn_gain_ref[...]).astype(BF16)


def nt_dot(a, b):
    return lax.dot_general(a, b, (((1,), (1,)), ((), ())), preferred_element_type=F32)


def query_kernel(scale, normed_ref, query_ref, key_ref, out_ref):
    queries = jnp.dot(normed_ref[...], query_ref[...], preferred_element_type=F32).astype(BF16)
    out_ref[...] = (nt_dot(queries, key_ref[...]) * scale).astype(BF16)


def attention_kernel(width, count, query_ref, resid_ref, value_ref, out_weight_ref, *refs):
    blocks = refs[:count]
    mid_ref, swap_ref, first_ref, second_ref, scores = refs[count:]
    core = lax.axis_index("rows") % 2
    span = query_ref.shape[0]
    queries = query_ref[...]
    peak = None
    for i, block in enumerate(blocks):
        part = nt_dot(queries, block[...])
        scores[i] = part
        for lane in range(0, span, 128):
            piece = part[:, lane : lane + 128]
            peak = piece if peak is None else jnp.maximum(peak, piece)
    peak = jnp.max(peak, axis=-1, keepdims=True)
    sums = jnp.zeros((span, 128), F32)
    added = jnp.zeros((span, query_ref.shape[1]), F32)
    for i, block in enumerate(blocks):
        weights = jnp.exp2(scores[i] - peak)
        for lane in range(0, span, 128):
            sums = sums + weights[:, lane : lane + 128]
        added = added + jnp.dot(weights.astype(BF16), block[...], preferred_element_type=F32)
    mixed = (added / jnp.sum(sums, axis=-1, keepdims=True)).astype(BF16)
    attended = jnp.dot(mixed, value_ref[...], preferred_element_type=F32).astype(BF16)
    projected = jnp.dot(attended, out_weight_ref[...], preferred_element_type=F32)
    mid_ref[...] = (resid_ref[...] + projected).astype(BF16)
    low = pl.multiple_of((1 - core) * width, width)
    swap_ref[...] = mid_ref[pl.ds(low, 3 * width), :]
    first_ref[...] = mid_ref[pl.ds(pl.multiple_of(3 * (1 - core) * width, width), width), :]
    second_ref[...] = mid_ref[pl.ds(pl.multiple_of(3 * core * width, width), width), :]


def up_kernel(
    width, mid_ref, swap_ref, first_ref, second_ref, weight_ref, out_ref, rows, fine, total
):
    core = lax.axis_index("rows") % 2
    channels = mid_ref.shape[1]
    outputs = weight_ref.shape[2]
    full = pl.multiple_of((1 - core) * width, width)
    edge = pl.multiple_of(3 * core * width, width)
    rows[0, pl.ds(full, 3 * width), :] = mid_ref[
        pl.ds(pl.multiple_of(core * width, width), 3 * width), :
    ].astype(F32)
    rows[1, pl.ds(full, 3 * width), :] = swap_ref[...].astype(F32)
    rows[0, pl.ds(edge, width), :] = first_ref[...].astype(F32)
    rows[1, pl.ds(edge, width), :] = second_ref[...].astype(F32)
    wide = 2 * width
    lane = lax.broadcasted_iota(jnp.int32, (1, wide), 1)
    lhs = weight_ref[...].reshape(9 * outputs, channels)
    for slot in range(2):
        frame = core if slot == 0 else 1 - core
        values = rows[slot]
        pieces = []
        for i in range(channels // 128):
            piece = values[:, 128 * i : 128 * (i + 1)]
            fine[i, pl.ds(0, 4 * width, stride=2), :] = piece
            fine[i, pl.ds(1, 4 * width, stride=2), :] = piece
            pieces.append(fine[i].astype(BF16))
        total[...] = nt_dot(lhs, jnp.concatenate(pieces, axis=1))
        for row in range(4):
            low = row // 2 + 1
            picks = (low - 1, low, low) if row % 2 == 0 else (low, low, low + 1)
            taps = []
            for col in range(3):
                tap = None
                for j, pick in enumerate(picks):
                    piece = total[
                        (3 * j + col) * outputs : (3 * j + col + 1) * outputs,
                        pick * wide : (pick + 1) * wide,
                    ]
                    tap = piece if tap is None else tap + piece
                taps.append(tap)
            result = taps[1]
            result = result + jnp.where(lane == 0, 0.0, pltpu.roll(taps[0], 1, axis=1))
            result = result + jnp.where(
                lane == wide - 1, 0.0, pltpu.roll(taps[2], wide - 1, axis=1)
            )
            out_ref[frame, row] = result.astype(BF16)


def gather_blocks(block, count):
    chips = count // 2
    depth = 2 if chips % 2 == 0 else 1
    length = chips // depth

    def index(a, b, core):
        return (a * depth + b) * 2 + core

    def shift(values, steps):
        pairs = [
            (index(a, b, core), index((a + steps) % length, b, core))
            for a in range(length)
            for b in range(depth)
            for core in range(2)
        ]
        return lax.ppermute(values, "rows", pairs)

    def cross(values):
        pairs = [
            (index(a, b, core), index(a, 1 - b, core))
            for a in range(length)
            for b in range(2)
            for core in range(2)
        ]
        return lax.ppermute(values, "rows", pairs)

    order = []
    for steps in range(1, length // 2 + 1):
        order.append(steps)
        if length - steps != steps:
            order.append(length - steps)
    arrived = [block] + [shift(block, steps) for steps in order]
    if depth == 2:
        arrived = arrived + [cross(values) for values in arrived]
    return arrived


def shards(
    latents,
    conv_cache,
    norm_gain,
    conv_weight,
    attn_gain,
    query_weight,
    key_weight,
    value_weight,
    out_weight,
    up_weight,
):
    frames, rows_here, width, channels = latents.shape
    outputs = up_weight.shape[3]
    count = lax.axis_size("rows")
    core = lax.axis_index("rows") % 2
    span = 2 * rows_here * width
    own = rows_here * width
    gain = norm_gain.reshape(1, channels)

    chips = count // 2
    swap = [(2 * k + c, 2 * k + 1 - c) for k in range(chips) for c in range(2)]
    ahead_low = [(2 * k + 1, 2 * k + 2) for k in range(chips - 1)]
    back_high = [(2 * k + 2, 2 * k + 1) for k in range(chips - 1)]
    ahead_high = [(2 * k + 1, 2 * k + 3) for k in range(chips - 1)]
    back_low = [(2 * k + 2, 2 * k) for k in range(chips - 1)]
    ahead_lows = [(2 * k, 2 * k + 2) for k in range(chips - 1)]
    back_highs = [(2 * k + 3, 2 * k + 1) for k in range(chips - 1)]

    stacked = jnp.concatenate([conv_cache, latents], axis=0)
    even = core == 0
    first = jnp.where(even, stacked[1:4, 0], stacked[0:3, rows_here - 1])
    second = jnp.where(even, stacked[0:3, 0], stacked[1:4, rows_here - 1])
    both = jnp.where(even, stacked[1:4], stacked[0:3]).reshape(3, own, channels)
    first = lax.ppermute(first, "rows", ahead_low + back_high)
    second = lax.ppermute(second, "rows", ahead_high + back_low)
    both = lax.ppermute(both, "rows", swap)

    latents_flat = latents.reshape(frames, own, channels)
    act = pl.pallas_call(
        activate_kernel,
        out_shape=jax.ShapeDtypeStruct((frames, own, channels), BF16),
        in_specs=[vmem()] * 2,
        out_specs=vmem(),
        cost_estimate=cost(10 * frames * own * channels, 4 * frames * own * channels),
        compiler_params=params(16),
    )(latents_flat, gain)

    normed, resid = pl.pallas_call(
        functools.partial(conv_kernel, width),
        out_shape=(
            jax.ShapeDtypeStruct((span, channels), BF16),
            jax.ShapeDtypeStruct((span, channels), F32),
        ),
        in_specs=[vmem()] * 8 + [pl.BlockSpec(memory_space=pl.ANY)],
        out_specs=(vmem(), vmem()),
        scratch_shapes=[
            pltpu.VMEM((3, 6 * width, channels), BF16),
            pltpu.VMEM((3, 3, channels, 3 * channels), BF16),
            pltpu.VMEM((span, channels), F32),
            pltpu.VMEM((span, 3 * channels), F32),
            pltpu.SemaphoreType.DMA((3, 3)),
        ],
        cost_estimate=cost(2 * 27 * span * channels * channels, 2 * 27 * channels * channels),
        compiler_params=params(32),
    )(
        latents_flat,
        conv_cache.reshape(frames, own, channels),
        act,
        both,
        first,
        second,
        gain,
        attn_gain.reshape(1, channels),
        conv_weight,
    )

    scale = channels ** (-0.5) * 1.4426950408889634
    queries = pl.pallas_call(
        functools.partial(query_kernel, scale),
        out_shape=jax.ShapeDtypeStruct((span, channels), BF16),
        in_specs=[vmem()] * 3,
        out_specs=vmem(),
        cost_estimate=cost(4 * span * channels * channels, 8 * span * channels),
        compiler_params=params(16),
    )(normed, query_weight, key_weight)

    blocks = gather_blocks(normed, count)
    row = jax.ShapeDtypeStruct((width, channels), BF16)
    mid, swap_rows, first_row, second_row = pl.pallas_call(
        functools.partial(attention_kernel, width, len(blocks)),
        out_shape=(
            jax.ShapeDtypeStruct((span, channels), BF16),
            jax.ShapeDtypeStruct((3 * width, channels), BF16),
            row,
            row,
        ),
        in_specs=[vmem()] * (4 + len(blocks)),
        out_specs=(vmem(),) * 4,
        scratch_shapes=[pltpu.VMEM((len(blocks), span, span), F32)],
        cost_estimate=cost(
            4 * span * span * len(blocks) * channels,
            2 * span * channels * len(blocks),
            span * span * len(blocks),
        ),
        compiler_params=params(32),
    )(queries, resid, value_weight, out_weight, *blocks)

    swap_rows = lax.ppermute(swap_rows, "rows", swap)
    first_row = lax.ppermute(first_row, "rows", ahead_lows + back_highs)
    second_row = lax.ppermute(second_row, "rows", ahead_low + back_high)

    decoded = pl.pallas_call(
        functools.partial(up_kernel, width),
        out_shape=jax.ShapeDtypeStruct((frames, 2 * rows_here, outputs, 2 * width), BF16),
        in_specs=[vmem()] * 5,
        out_specs=vmem(),
        scratch_shapes=[
            pltpu.VMEM((2, 4 * width, channels), F32),
            pltpu.VMEM((channels // 128, 8 * width, 128), F32),
            pltpu.VMEM((9 * outputs, 8 * width), F32),
        ],
        cost_estimate=cost(
            2 * 9 * outputs * channels * 16 * width, 2 * 9 * outputs * channels
        ),
        compiler_params=params(32),
    )(mid, swap_rows, first_row, second_row, jnp.transpose(up_weight, (0, 1, 3, 2)))
    decoded = jnp.transpose(decoded, (0, 1, 3, 2))
    return (decoded, act.reshape(frames, rows_here, width, channels))


def solution(mesh):
    return jax.shard_map(
        shards,
        mesh=mesh,
        in_specs=(
            P("videos", "rows", None, None),
            P("videos", "rows", None, None),
            P(),
            P(),
            P(),
            P(),
            P(),
            P(),
            P(),
            P(),
        ),
        out_specs=(P("videos", "rows", None, None), P("videos", "rows", None, None)),
        check_vma=False,
    )
```

```python
import functools

import jax
import jax.numpy as jnp
from jax import lax
from jax.experimental import pallas as pl
from jax.experimental.pallas import tpu as pltpu
from jax.sharding import PartitionSpec as P

BF16 = jnp.bfloat16
F32 = jnp.float32
EPS = 1e-06
MIB = 1024 * 1024


def normalize(values, gain):
    return values * lax.rsqrt(jnp.mean(values * values, axis=-1, keepdims=True) + EPS) * gain


def activate(values, gain):
    normed = normalize(values.astype(F32), gain)
    return (normed / (1.0 + jnp.exp(-normed))).astype(BF16)


def vmem():
    return pl.BlockSpec(memory_space=pltpu.VMEM)


def params(mib):
    return pltpu.CompilerParams(vmem_limit_bytes=mib * MIB)


def cost(flops, size, exps=0):
    return pl.CostEstimate(flops=flops, bytes_accessed=size, transcendentals=exps)


def edges_kernel(latents_ref, cache_ref, first_ref, second_ref, both_ref, sems):
    core = lax.axis_index("rows") % 2
    last = latents_ref.shape[1] - 1

    def move(pairs):
        copies = [
            pltpu.make_async_copy(source, target, sems.at[i])
            for i, (source, target) in enumerate(pairs)
        ]
        for copy in copies:
            copy.start()
        for copy in copies:
            copy.wait()

    @pl.when(core == 0)
    def _():
        move(
            [
                (cache_ref.at[pl.ds(0, 2), 0], second_ref.at[pl.ds(0, 2)]),
                (latents_ref.at[0, 0], second_ref.at[2]),
                (cache_ref.at[1, 0], first_ref.at[0]),
                (latents_ref.at[pl.ds(0, 2), 0], first_ref.at[pl.ds(1, 2)]),
                (cache_ref.at[1], both_ref.at[0]),
                (latents_ref.at[pl.ds(0, 2)], both_ref.at[pl.ds(1, 2)]),
            ]
        )

    @pl.when(core == 1)
    def _():
        move(
            [
                (cache_ref.at[pl.ds(0, 2), last], first_ref.at[pl.ds(0, 2)]),
                (latents_ref.at[0, last], first_ref.at[2]),
                (cache_ref.at[1, last], second_ref.at[0]),
                (latents_ref.at[pl.ds(0, 2), last], second_ref.at[pl.ds(1, 2)]),
                (cache_ref.at[pl.ds(0, 2)], both_ref.at[pl.ds(0, 2)]),
                (latents_ref.at[0], both_ref.at[2]),
            ]
        )


def prepare_kernel(
    latents_ref,
    cache_ref,
    weight_ref,
    gain_ref,
    act_ref,
    own_ref,
    base_ref,
    staged_ref,
    latents,
    cache,
    sems,
    weight_sems,
):
    channels = latents_ref.shape[-1]
    core = lax.axis_index("rows") % 2
    loads = [
        pltpu.make_async_copy(latents_ref, latents, sems.at[0]),
        pltpu.make_async_copy(cache_ref, cache, sems.at[1]),
    ]
    copies = []
    for time in range(3):
        for col in range(3):
            copies.append(
                pltpu.make_async_copy(
                    weight_ref.at[time, :, col],
                    staged_ref.at[time, :, :, pl.ds(col * channels, channels)],
                    weight_sems.at[time, col],
                )
            )
    for copy in loads + copies:
        copy.start()
    loads[0].wait()
    act_ref[...] = activate(latents[...], gain_ref[...].reshape(1, channels))
    loads[1].wait()
    base_ref[...] = latents[core]
    own_ref[0] = cache[core]
    own_ref[2] = act_ref[core]

    @pl.when(core == 0)
    def _():
        own_ref[1] = cache[1]

    @pl.when(core == 1)
    def _():
        own_ref[1] = act_ref[0]

    for copy in copies:
        copy.wait()


def conv_kernel(
    width,
    own_ref,
    base_ref,
    swap_ref,
    first_ref,
    second_ref,
    norm_gain_ref,
    attn_gain_ref,
    weights,
    front_ref,
    back_ref,
    resid_ref,
    top_ref,
    bottom_ref,
    held,
    base,
    total,
):
    channels = own_ref.shape[-1]
    core = lax.axis_index("rows") % 2
    own = 2 * width
    mine = pl.multiple_of((1 + 2 * core) * width, width)
    other = pl.multiple_of((3 - 2 * core) * width, width)
    edge_first = pl.multiple_of(5 * core * width, width)
    edge_second = pl.multiple_of(5 * (1 - core) * width, width)
    gain = norm_gain_ref[...].reshape(1, channels)

    def place(time, convert):
        held[time, pl.ds(mine, own), :] = own_ref[time]
        held[time, pl.ds(other, own), :] = convert(swap_ref[time])
        held[time, pl.ds(edge_first, width), :] = convert(first_ref[time])
        held[time, pl.ds(edge_second, width), :] = convert(second_ref[time])

    place(0, lambda v: v)

    @pl.when(core == 0)
    def _():
        place(1, lambda v: v)

    @pl.when(core == 1)
    def _():
        place(1, lambda v: activate(v, gain))

    place(2, lambda v: activate(v, gain))
    base[pl.ds(pl.multiple_of(2 * core * width, width), own), :] = base_ref[...].astype(F32)
    base[pl.ds(pl.multiple_of(2 * (1 - core) * width, width), own), :] = swap_ref[2].astype(F32)

    span = 4 * width
    for time in range(3):
        lhs = jnp.concatenate(
            [held[time, row * width : row * width + span, :] for row in range(3)], axis=1
        )
        rhs = weights[time].reshape(3 * channels, 3 * channels)
        part = jnp.dot(lhs, rhs, preferred_element_type=F32)
        if time == 0:
            total[...] = part
        else:
            total[...] += part
    column = lax.broadcasted_iota(jnp.int32, (span, 1), 0) % width
    left = pltpu.roll(total[:, :channels], 1, axis=0)
    right = pltpu.roll(total[:, 2 * channels :], span - 1, axis=0)
    conv_out = total[:, channels : 2 * channels]
    conv_out = conv_out + jnp.where(column == 0, 0.0, left)
    conv_out = conv_out + jnp.where(column == width - 1, 0.0, right)
    resid = base[...] + conv_out
    resid_ref[...] = resid
    top_ref[...] = resid[:width].astype(BF16)
    bottom_ref[...] = resid[span - width :].astype(BF16)
    normed = normalize(resid, attn_gain_ref[...].reshape(1, channels)).astype(BF16)
    front_ref[...] = normed[: span // 2]
    back_ref[...] = normed[span // 2 :]


def nt_dot(a, b):
    return lax.dot_general(a, b, (((1,), (1,)), ((), ())), preferred_element_type=F32)


def query_kernel(
    scale, front_ref, back_ref, above_ref, below_ref, gain_ref, query_ref, key_ref, out_ref
):
    gain = gain_ref[...].reshape(1, front_ref.shape[1])
    above = normalize(above_ref[...].astype(F32), gain).astype(BF16)
    below = normalize(below_ref[...].astype(F32), gain).astype(BF16)
    normed = jnp.concatenate([above, front_ref[...], back_ref[...], below], axis=0)
    queries = jnp.dot(normed, query_ref[...], preferred_element_type=F32).astype(BF16)
    out_ref[...] = (nt_dot(queries, key_ref[...]) * scale).astype(BF16)


def attention_kernel(
    width,
    devices,
    count,
    query_ref,
    resid_ref,
    above_ref,
    below_ref,
    value_ref,
    out_weight_ref,
    *refs,
):
    blocks = refs[:count]
    mid_ref, swap_ref, scores, mid = refs[count:]
    place = lax.axis_index("rows")
    core = place % 2
    span, channels = query_ref.shape
    queries = query_ref[...]
    keys = [
        jnp.concatenate([blocks[i][...], blocks[i + 1][...]], axis=0) for i in range(0, count, 2)
    ]
    peak = None
    for i, key in enumerate(keys):
        part = nt_dot(queries, key)
        scores[i] = part
        for lane in range(0, part.shape[1], 128):
            piece = part[:, lane : lane + 128]
            peak = piece if peak is None else jnp.maximum(peak, piece)
    peak = jnp.max(peak, axis=-1, keepdims=True)
    sums = jnp.zeros((span, 128), F32)
    added = jnp.zeros((span, channels), F32)
    for i, key in enumerate(keys):
        weights = jnp.exp2(scores[i] - peak)
        for lane in range(0, weights.shape[1], 128):
            sums = sums + weights[:, lane : lane + 128]
        added = added + jnp.dot(weights.astype(BF16), key, preferred_element_type=F32)
    mixed = (added / jnp.sum(sums, axis=-1, keepdims=True)).astype(BF16)
    attended = jnp.dot(mixed, value_ref[...], preferred_element_type=F32).astype(BF16)
    projected = jnp.dot(attended, out_weight_ref[...], preferred_element_type=F32)
    inner = span - width
    mid[width:inner] = (resid_ref[...] + projected[width:inner]).astype(BF16)
    above = above_ref[...].astype(F32) + projected[:width]
    below = below_ref[...].astype(F32) + projected[inner:]
    mid[:width] = jnp.where(place < 2, 0.0, above).astype(BF16)
    mid[inner:] = jnp.where(place >= devices - 2, 0.0, below).astype(BF16)
    mid_ref[...] = mid[pl.ds(pl.multiple_of(2 * core * width, width), 4 * width), :]
    swap_ref[...] = mid[pl.ds(pl.multiple_of(2 * (1 - core) * width, width), 4 * width), :]


def up_kernel(width, mid_ref, swap_ref, weight_ref, out_ref, fine, total):
    core = lax.axis_index("rows") % 2
    channels = mid_ref.shape[1]
    outputs = weight_ref.shape[2]
    wide = 2 * width
    lane = lax.broadcasted_iota(jnp.int32, (1, wide), 1)
    lhs = weight_ref[...].reshape(9 * outputs, channels)
    for slot in range(2):
        frame = core if slot == 0 else 1 - core
        values = (mid_ref if slot == 0 else swap_ref)[...].astype(F32)
        pieces = []
        for i in range(channels // 128):
            piece = values[:, 128 * i : 128 * (i + 1)]
            fine[i, pl.ds(0, 4 * width, stride=2), :] = piece
            fine[i, pl.ds(1, 4 * width, stride=2), :] = piece
            pieces.append(fine[i].astype(BF16))
        total[...] = nt_dot(lhs, jnp.concatenate(pieces, axis=1))
        for row in range(4):
            low = row // 2 + 1
            picks = (low - 1, low, low) if row % 2 == 0 else (low, low, low + 1)
            taps = []
            for col in range(3):
                tap = None
                for j, pick in enumerate(picks):
                    piece = total[
                        (3 * j + col) * outputs : (3 * j + col + 1) * outputs,
                        pick * wide : (pick + 1) * wide,
                    ]
                    tap = piece if tap is None else tap + piece
                taps.append(tap)
            result = taps[1]
            result = result + jnp.where(lane == 0, 0.0, pltpu.roll(taps[0], 1, axis=1))
            result = result + jnp.where(
                lane == wide - 1, 0.0, pltpu.roll(taps[2], wide - 1, axis=1)
            )
            out_ref[frame, row] = result.astype(BF16)


def gather_blocks(halves, count):
    chips = count // 2
    depth = 2 if chips % 2 == 0 else 1
    length = chips // depth

    def index(a, b, core):
        return (a * depth + b) * 2 + core

    ring = [0] + list(range(1, length, 2)) + list(range(2, length, 2))[::-1]
    follow = {a: ring[(i + 1) % length] for i, a in enumerate(ring)}
    around = [
        (index(a, b, core), index(follow[a], b, core))
        for a in range(length)
        for b in range(depth)
        for core in range(2)
    ]
    across = [
        (index(a, b, core), index(a, 1 - b, core))
        for a in range(length)
        for b in range(depth)
        for core in range(2)
    ]
    held = list(halves)
    arrived = list(halves)
    for step in range(length):
        later = []
        if step < length - 1:
            later = [lax.ppermute(values, "rows", around) for values in held]
        if depth == 2:
            arrived = arrived + [lax.ppermute(values, "rows", across) for values in held]
        arrived = arrived + later
        held = later
    return arrived


def shards(
    latents,
    conv_cache,
    norm_gain,
    conv_weight,
    attn_gain,
    query_weight,
    key_weight,
    value_weight,
    out_weight,
    up_weight,
):
    frames, rows_here, width, channels = latents.shape
    outputs = up_weight.shape[3]
    count = lax.axis_size("rows")
    span = 2 * rows_here * width
    own = rows_here * width
    edge = jax.ShapeDtypeStruct((width, channels), BF16)
    anywhere = pl.BlockSpec(memory_space=pl.ANY)
    hbm = pl.BlockSpec(memory_space=pltpu.HBM)

    chips = count // 2
    swap = [(2 * k + c, 2 * k + 1 - c) for k in range(chips) for c in range(2)]
    ahead_low = [(2 * k + 1, 2 * k + 2) for k in range(chips - 1)]
    back_high = [(2 * k + 2, 2 * k + 1) for k in range(chips - 1)]
    ahead_high = [(2 * k + 1, 2 * k + 3) for k in range(chips - 1)]
    back_low = [(2 * k + 2, 2 * k) for k in range(chips - 1)]
    ahead = [(2 * k + c, 2 * k + 2 + c) for k in range(chips - 1) for c in range(2)]
    back = [(target, source) for source, target in ahead]

    first, second, both = pl.pallas_call(
        edges_kernel,
        out_shape=(
            jax.ShapeDtypeStruct((3, width, channels), BF16),
            jax.ShapeDtypeStruct((3, width, channels), BF16),
            jax.ShapeDtypeStruct((3, rows_here, width, channels), BF16),
        ),
        in_specs=[hbm] * 2,
        out_specs=(anywhere,) * 3,
        scratch_shapes=[pltpu.SemaphoreType.DMA((6,))],
        cost_estimate=cost(0, 24 * width * channels),
        compiler_params=params(4),
    )(latents, conv_cache)
    first = lax.ppermute(first, "rows", ahead_low + back_high)
    second = lax.ppermute(second, "rows", ahead_high + back_low)
    both = lax.ppermute(both, "rows", swap)

    act, own_rows, base, staged = pl.pallas_call(
        prepare_kernel,
        out_shape=(
            jax.ShapeDtypeStruct((frames, own, channels), BF16),
            jax.ShapeDtypeStruct((3, own, channels), BF16),
            jax.ShapeDtypeStruct((own, channels), BF16),
            jax.ShapeDtypeStruct((3, 3, channels, 3 * channels), BF16),
        ),
        in_specs=[hbm, hbm, hbm, vmem()],
        out_specs=(vmem(), vmem(), vmem(), anywhere),
        scratch_shapes=[
            pltpu.VMEM((frames, own, channels), BF16),
            pltpu.VMEM((frames, own, channels), BF16),
            pltpu.SemaphoreType.DMA((2,)),
            pltpu.SemaphoreType.DMA((3, 3)),
        ],
        cost_estimate=cost(10 * frames * own * channels, 2 * 27 * channels * channels),
        compiler_params=params(8),
    )(
        latents.reshape(frames, own, channels),
        conv_cache.reshape(frames, own, channels),
        conv_weight,
        norm_gain,
    )

    front, back_half, resid, top, bottom = pl.pallas_call(
        functools.partial(conv_kernel, width),
        out_shape=(
            jax.ShapeDtypeStruct((span // 2, channels), BF16),
            jax.ShapeDtypeStruct((span // 2, channels), BF16),
            jax.ShapeDtypeStruct((span, channels), F32),
            edge,
            edge,
        ),
        in_specs=[vmem()] * 8,
        out_specs=(vmem(),) * 5,
        scratch_shapes=[
            pltpu.VMEM((3, 6 * width, channels), BF16),
            pltpu.VMEM((span, channels), F32),
            pltpu.VMEM((span, 3 * channels), F32),
        ],
        cost_estimate=cost(2 * 27 * span * channels * channels, 2 * 27 * channels * channels),
        compiler_params=params(16),
    )(
        own_rows,
        base,
        both.reshape(3, own, channels),
        first,
        second,
        norm_gain,
        attn_gain,
        staged,
    )

    blocks = gather_blocks((front, back_half), count)
    above = lax.ppermute(bottom, "rows", ahead)
    below = lax.ppermute(top, "rows", back)

    scale = channels ** (-0.5) * 1.4426950408889634
    wide = span + 2 * width
    queries = pl.pallas_call(
        functools.partial(query_kernel, scale),
        out_shape=jax.ShapeDtypeStruct((wide, channels), BF16),
        in_specs=[vmem()] * 7,
        out_specs=vmem(),
        cost_estimate=cost(4 * wide * channels * channels, 8 * wide * channels),
        compiler_params=params(16),
    )(front, back_half, above, below, attn_gain, query_weight, key_weight)

    mid, swap_rows = pl.pallas_call(
        functools.partial(attention_kernel, width, count, len(blocks)),
        out_shape=(jax.ShapeDtypeStruct((4 * width, channels), BF16),) * 2,
        in_specs=[vmem()] * (6 + len(blocks)),
        out_specs=(vmem(),) * 2,
        scratch_shapes=[
            pltpu.VMEM((len(blocks) // 2, wide, span), F32),
            pltpu.VMEM((wide, channels), BF16),
        ],
        cost_estimate=cost(
            2 * wide * span * len(blocks) * channels,
            span * channels * len(blocks),
            wide * span * len(blocks) // 2,
        ),
        compiler_params=params(32),
    )(queries, resid, above, below, value_weight, out_weight, *blocks)

    swap_rows = lax.ppermute(swap_rows, "rows", swap)

    decoded = pl.pallas_call(
        functools.partial(up_kernel, width),
        out_shape=jax.ShapeDtypeStruct((frames, 2 * rows_here, outputs, 2 * width), BF16),
        in_specs=[vmem()] * 3,
        out_specs=vmem(),
        scratch_shapes=[
            pltpu.VMEM((channels // 128, 8 * width, 128), F32),
            pltpu.VMEM((9 * outputs, 8 * width), F32),
        ],
        cost_estimate=cost(
            2 * 9 * outputs * channels * 16 * width, 2 * 9 * outputs * channels
        ),
        compiler_params=params(32),
    )(mid, swap_rows, jnp.transpose(up_weight, (0, 1, 3, 2)))
    decoded = jnp.transpose(decoded, (0, 1, 3, 2))
    return (decoded, act.reshape(frames, rows_here, width, channels))


def solution(mesh):
    return jax.shard_map(
        shards,
        mesh=mesh,
        in_specs=(
            P("videos", "rows", None, None),
            P("videos", "rows", None, None),
            P(),
            P(),
            P(),
            P(),
            P(),
            P(),
            P(),
            P(),
        ),
        out_specs=(P("videos", "rows", None, None), P("videos", "rows", None, None)),
        check_vma=False,
    )
```

```python
import functools

import jax
import jax.numpy as jnp
from jax import lax
from jax.experimental import pallas as pl
from jax.experimental.pallas import tpu as pltpu
from jax.sharding import PartitionSpec as P

BF16 = jnp.bfloat16
F32 = jnp.float32
EPS = 1e-06
MIB = 1024 * 1024
EXTRA = 16


def normalize(values, gain):
    return values * lax.rsqrt(jnp.mean(values * values, axis=-1, keepdims=True) + EPS) * gain


def activate(values, gain):
    normed = normalize(values.astype(F32), gain)
    return (normed / (1.0 + jnp.exp(-normed))).astype(BF16)


def vmem():
    return pl.BlockSpec(memory_space=pltpu.VMEM)


def params(mib):
    return pltpu.CompilerParams(vmem_limit_bytes=mib * MIB)


def cost(flops, size, exps=0):
    return pl.CostEstimate(flops=flops, bytes_accessed=size, transcendentals=exps)


def edges_kernel(latents_ref, cache_ref, edge_ref, both_ref, sems):
    core = lax.axis_index("rows") % 2
    row = core * (latents_ref.shape[1] - 1)
    copies = [
        pltpu.make_async_copy(cache_ref.at[:, row], edge_ref.at[pl.ds(0, 2)], sems.at[0]),
        pltpu.make_async_copy(latents_ref.at[:, row], edge_ref.at[pl.ds(2, 2)], sems.at[1]),
        pltpu.make_async_copy(cache_ref.at[1], both_ref.at[core], sems.at[2]),
        pltpu.make_async_copy(latents_ref.at[0], both_ref.at[1 + core], sems.at[3]),
    ]
    for copy in copies:
        copy.start()

    @pl.when(core == 0)
    def _():
        last = pltpu.make_async_copy(latents_ref.at[1], both_ref.at[2], sems.at[4])
        last.start()
        last.wait()

    @pl.when(core == 1)
    def _():
        last = pltpu.make_async_copy(cache_ref.at[0], both_ref.at[0], sems.at[4])
        last.start()
        last.wait()

    for copy in copies:
        copy.wait()


def prepare_kernel(
    latents_ref,
    cache_ref,
    weight_ref,
    gain_ref,
    act_ref,
    own_ref,
    base_ref,
    staged_ref,
    latents,
    cache,
    gain,
    sems,
    weight_sems,
):
    channels = latents_ref.shape[-1]
    core = lax.axis_index("rows") % 2
    loads = [
        pltpu.make_async_copy(latents_ref, latents, sems.at[0]),
        pltpu.make_async_copy(cache_ref, cache, sems.at[1]),
        pltpu.make_async_copy(gain_ref, gain, sems.at[2]),
    ]
    copies = []
    for time in range(3):
        for col in range(3):
            copies.append(
                pltpu.make_async_copy(
                    weight_ref.at[time, :, col],
                    staged_ref.at[time, :, :, pl.ds(col * channels, channels)],
                    weight_sems.at[time, col],
                )
            )
    for copy in loads + copies:
        copy.start()
    for copy in loads:
        copy.wait()
    act_ref[...] = activate(latents[...], gain[...].reshape(1, channels))
    base_ref[...] = latents[core]
    own_ref[0] = cache[core]
    own_ref[2] = act_ref[core]

    @pl.when(core == 0)
    def _():
        own_ref[1] = cache[1]

    @pl.when(core == 1)
    def _():
        own_ref[1] = act_ref[0]

    for copy in copies:
        copy.wait()


def conv_kernel(
    width,
    own_ref,
    base_ref,
    swap_ref,
    edge_ref,
    far_ref,
    norm_gain_ref,
    attn_gain_ref,
    weights,
    sent_ref,
    resid_ref,
    held,
    base,
    total,
):
    channels = own_ref.shape[-1]
    core = lax.axis_index("rows") % 2
    own = 2 * width
    mine = pl.multiple_of((1 + 2 * core) * width, width)
    other = pl.multiple_of((3 - 2 * core) * width, width)
    near = pl.multiple_of(5 * core * width, width)
    far = pl.multiple_of(5 * (1 - core) * width, width)
    gain = norm_gain_ref[...].reshape(1, channels)

    def place(time, convert):
        held[time, pl.ds(mine, own), :] = own_ref[time]
        held[time, pl.ds(other, own), :] = convert(swap_ref[time])
        held[time, pl.ds(near, width), :] = convert(edge_ref[time + core])
        held[time, pl.ds(far, width), :] = convert(far_ref[time + core])

    place(0, lambda v: v)

    @pl.when(core == 0)
    def _():
        place(1, lambda v: v)

    @pl.when(core == 1)
    def _():
        place(1, lambda v: activate(v, gain))

    place(2, lambda v: activate(v, gain))
    base[pl.ds(pl.multiple_of(2 * core * width, width), own), :] = base_ref[...].astype(F32)
    base[pl.ds(pl.multiple_of(2 * (1 - core) * width, width), own), :] = swap_ref[2].astype(F32)

    span = 4 * width
    for time in range(3):
        lhs = jnp.concatenate(
            [held[time, row * width : row * width + span, :] for row in range(3)], axis=1
        )
        rhs = weights[time].reshape(3 * channels, 3 * channels)
        part = jnp.dot(lhs, rhs, preferred_element_type=F32)
        if time == 0:
            total[...] = part
        else:
            total[...] += part
    column = lax.broadcasted_iota(jnp.int32, (span, 1), 0) % width
    left = pltpu.roll(total[:, :channels], 1, axis=0)
    right = pltpu.roll(total[:, 2 * channels :], span - 1, axis=0)
    conv_out = total[:, channels : 2 * channels]
    conv_out = conv_out + jnp.where(column == 0, 0.0, left)
    conv_out = conv_out + jnp.where(column == width - 1, 0.0, right)
    resid = base[...] + conv_out
    resid_ref[...] = resid
    size = jnp.mean(resid * resid, axis=-1, keepdims=True) + EPS
    sent_ref[:span] = (resid * lax.rsqrt(size) * attn_gain_ref[...].reshape(1, channels)).astype(
        BF16
    )
    edges = jnp.sqrt(jnp.concatenate([size[:width], size[span - width :]], axis=0))
    across = jnp.transpose(jnp.broadcast_to(edges, (2 * width, 128)))[:EXTRA]
    high = across.astype(BF16).astype(F32)
    line = lax.broadcasted_iota(jnp.int32, (EXTRA, 1), 0)
    extra = jnp.where(line == 0, high, jnp.where(line == 1, across - high, 0.0))
    sent_ref[span:] = jnp.zeros((EXTRA, channels), BF16)
    sent_ref[span:, : 2 * width] = extra.astype(BF16)


def nt_dot(a, b):
    return lax.dot_general(a, b, (((1,), (1,)), ((), ())), preferred_element_type=F32)


def lead(scale, normed, query_ref, key_ref):
    queries = jnp.dot(normed, query_ref[...], preferred_element_type=F32).astype(BF16)
    return (nt_dot(queries, key_ref[...]) * scale).astype(BF16)


def query_kernel(scale, sent_ref, query_ref, key_ref, out_ref):
    out_ref[...] = lead(scale, sent_ref[: out_ref.shape[0]], query_ref, key_ref)


def attention_kernel(
    width,
    scale,
    sources,
    own_query_ref,
    resid_ref,
    gain_ref,
    query_ref,
    key_ref,
    value_ref,
    out_weight_ref,
    *refs,
):
    count = len(sources)
    blocks = refs[:count]
    mid_ref, swap_ref, scores, mid, halo, sizes = refs[count:]
    place = lax.axis_index("rows")
    core = place % 2
    chip = place // 2
    own, channels = own_query_ref.shape
    chips = len(sources[0])

    for block, origin in zip(blocks, sources):
        for step, first, low in ((-1, own - width, 0), (1, 0, width)):
            takers = [k for k in range(chips) if origin[k] == k + step]
            if not takers:
                continue
            wanted = chip == takers[0]
            for k in takers[1:]:
                wanted = jnp.logical_or(wanted, chip == k)

            @pl.when(wanted)
            def _(block=block, first=first, low=low):
                halo[low : low + width] = block[first : first + width, :]
                sizes[low // width] = block[own : own + EXTRA, : 2 * width]

    no_above = chip == 0
    no_below = chip == chips - 1

    @pl.when(no_above)
    def _():
        halo[:width] = jnp.zeros((width, channels), BF16)
        sizes[0] = jnp.zeros((EXTRA, 2 * width), BF16)

    @pl.when(no_below)
    def _():
        halo[width:] = jnp.zeros((width, channels), BF16)
        sizes[1] = jnp.zeros((EXTRA, 2 * width), BF16)

    def column(index):
        parts = sizes[index].astype(F32)
        line = parts[0:1] + parts[1:2]
        return jnp.transpose(jnp.broadcast_to(line, (128, 2 * width)))[:, :1]

    edge_rows = halo[...]
    edge_size = jnp.concatenate([column(0)[width:], column(1)[:width]], axis=0)
    edge_resid = edge_rows.astype(F32) * edge_size / gain_ref[...].reshape(1, channels)
    edge_query = lead(scale, edge_rows, query_ref, key_ref)
    queries = jnp.concatenate([edge_query[:width], own_query_ref[...], edge_query[width:]], axis=0)
    span = queries.shape[0]
    keys = [block[:own] for block in blocks]
    peak = None
    for i, key in enumerate(keys):
        part = nt_dot(queries, key)
        scores[i] = part
        for lane in range(0, part.shape[1], 128):
            piece = part[:, lane : lane + 128]
            peak = piece if peak is None else jnp.maximum(peak, piece)
    peak = jnp.max(peak, axis=-1, keepdims=True)
    sums = jnp.zeros((span, 128), F32)
    added = jnp.zeros((span, channels), F32)
    for i, key in enumerate(keys):
        weights = jnp.exp2(scores[i] - peak)
        for lane in range(0, weights.shape[1], 128):
            sums = sums + weights[:, lane : lane + 128]
        added = added + jnp.dot(weights.astype(BF16), key, preferred_element_type=F32)
    mixed = (added / jnp.sum(sums, axis=-1, keepdims=True)).astype(BF16)
    attended = jnp.dot(mixed, value_ref[...], preferred_element_type=F32).astype(BF16)
    projected = jnp.dot(attended, out_weight_ref[...], preferred_element_type=F32)
    inner = span - width
    mid[width:inner] = (resid_ref[...] + projected[width:inner]).astype(BF16)
    above = edge_resid[:width] + projected[:width]
    below = edge_resid[width:] + projected[inner:]
    mid[:width] = jnp.where(no_above, 0.0, above).astype(BF16)
    mid[inner:] = jnp.where(no_below, 0.0, below).astype(BF16)
    mid_ref[...] = mid[pl.ds(pl.multiple_of(2 * core * width, width), 4 * width), :]
    swap_ref[...] = mid[pl.ds(pl.multiple_of(2 * (1 - core) * width, width), 4 * width), :]


def up_kernel(width, mid_ref, swap_ref, weight_ref, out_ref, fine, total):
    core = lax.axis_index("rows") % 2
    channels = mid_ref.shape[1]
    outputs = weight_ref.shape[2]
    wide = 2 * width
    lane = lax.broadcasted_iota(jnp.int32, (1, wide), 1)
    lhs = weight_ref[...].reshape(9 * outputs, channels)
    for slot in range(2):
        frame = core if slot == 0 else 1 - core
        values = (mid_ref if slot == 0 else swap_ref)[...].astype(F32)
        pieces = []
        for i in range(channels // 128):
            piece = values[:, 128 * i : 128 * (i + 1)]
            fine[i, pl.ds(0, 4 * width, stride=2), :] = piece
            fine[i, pl.ds(1, 4 * width, stride=2), :] = piece
            pieces.append(fine[i].astype(BF16))
        total[...] = nt_dot(lhs, jnp.concatenate(pieces, axis=1))
        for row in range(4):
            low = row // 2 + 1
            picks = (low - 1, low, low) if row % 2 == 0 else (low, low, low + 1)
            taps = []
            for col in range(3):
                tap = None
                for j, pick in enumerate(picks):
                    piece = total[
                        (3 * j + col) * outputs : (3 * j + col + 1) * outputs,
                        pick * wide : (pick + 1) * wide,
                    ]
                    tap = piece if tap is None else tap + piece
                taps.append(tap)
            result = taps[1]
            result = result + jnp.where(lane == 0, 0.0, pltpu.roll(taps[0], 1, axis=1))
            result = result + jnp.where(
                lane == wide - 1, 0.0, pltpu.roll(taps[2], wide - 1, axis=1)
            )
            out_ref[frame, row] = result.astype(BF16)


def gather_blocks(block, count):
    chips = count // 2
    depth = 2 if chips % 2 == 0 else 1
    length = chips // depth

    ring = [0] + list(range(1, length, 2)) + list(range(2, length, 2))[::-1]
    follow = {a: ring[(i + 1) % length] for i, a in enumerate(ring)}
    onward = {a * depth + b: follow[a] * depth + b for a in range(length) for b in range(depth)}
    backward = {target: source for source, target in onward.items()}
    across = {k: k ^ 1 for k in range(chips)}

    def send(values, origin, targets):
        pairs = [(2 * k + c, 2 * targets[k] + c) for k in range(chips) for c in range(2)]
        came = {targets[k]: origin[k] for k in range(chips)}
        return lax.ppermute(values, "rows", pairs), came

    here = (block, {k: k for k in range(chips)})
    arrived = [here]
    held = here
    first = None
    for step in range(1, length):
        later = send(*held, onward)
        if depth == 2:
            crossed = send(*held, across)
            first = crossed if first is None else first
            values, crossed_values = lax.optimization_barrier((later[0], crossed[0]))
            later = (values, later[1])
            arrived.append((crossed_values, crossed[1]))
        arrived.append(later)
        held = later
    if depth == 2:
        if length > 1:
            arrived.append(send(*arrived[1], backward))
        else:
            arrived.append(send(*here, across))
    return arrived


def shards(
    latents,
    conv_cache,
    norm_gain,
    conv_weight,
    attn_gain,
    query_weight,
    key_weight,
    value_weight,
    out_weight,
    up_weight,
):
    frames, rows_here, width, channels = latents.shape
    outputs = up_weight.shape[3]
    count = lax.axis_size("rows")
    span = 2 * rows_here * width
    own = rows_here * width
    edge = jax.ShapeDtypeStruct((width, channels), BF16)
    anywhere = pl.BlockSpec(memory_space=pl.ANY)
    hbm = pl.BlockSpec(memory_space=pltpu.HBM)

    chips = count // 2
    swap = [(2 * k + c, 2 * k + 1 - c) for k in range(chips) for c in range(2)]
    neighbour = [(2 * k + 1, 2 * k + 2) for k in range(chips - 1)]
    neighbour = neighbour + [(target, source) for source, target in neighbour]

    latents_in = pltpu.with_memory_space_constraint(latents, pltpu.HBM)
    cache_in = pltpu.with_memory_space_constraint(conv_cache, pltpu.HBM)
    edge_rows, both = pl.pallas_call(
        edges_kernel,
        out_shape=(
            jax.ShapeDtypeStruct((2 * frames, width, channels), BF16),
            jax.ShapeDtypeStruct((3, rows_here, width, channels), BF16),
        ),
        in_specs=[hbm] * 2,
        out_specs=(anywhere,) * 2,
        scratch_shapes=[pltpu.SemaphoreType.DMA((5,))],
        cost_estimate=cost(0, 20 * width * channels),
        compiler_params=params(4),
    )(latents_in, cache_in)
    edge_rows = lax.ppermute(edge_rows, "rows", neighbour)
    both = lax.ppermute(both, "rows", swap)
    act, own_rows, base, staged = pl.pallas_call(
        prepare_kernel,
        out_shape=(
            jax.ShapeDtypeStruct((frames, own, channels), BF16),
            jax.ShapeDtypeStruct((3, own, channels), BF16),
            jax.ShapeDtypeStruct((own, channels), BF16),
            jax.ShapeDtypeStruct((3, 3, channels, 3 * channels), BF16),
        ),
        in_specs=[hbm] * 4,
        out_specs=(vmem(), vmem(), vmem(), anywhere),
        scratch_shapes=[
            pltpu.VMEM((frames, own, channels), BF16),
            pltpu.VMEM((frames, own, channels), BF16),
            pltpu.VMEM((channels,), F32),
            pltpu.SemaphoreType.DMA((3,)),
            pltpu.SemaphoreType.DMA((3, 3)),
        ],
        cost_estimate=cost(10 * frames * own * channels, 2 * 27 * channels * channels),
        compiler_params=params(8),
    )(
        pltpu.with_memory_space_constraint(latents.reshape(frames, own, channels), pltpu.HBM),
        pltpu.with_memory_space_constraint(conv_cache.reshape(frames, own, channels), pltpu.HBM),
        pltpu.with_memory_space_constraint(conv_weight, pltpu.HBM),
        pltpu.with_memory_space_constraint(norm_gain, pltpu.HBM),
    )

    edge_rows, base = lax.optimization_barrier((edge_rows, base))
    far_rows = lax.ppermute(edge_rows, "rows", swap)
    sent, resid = pl.pallas_call(
        functools.partial(conv_kernel, width),
        out_shape=(
            jax.ShapeDtypeStruct((span + EXTRA, channels), BF16),
            jax.ShapeDtypeStruct((span, channels), F32),
        ),
        in_specs=[vmem()] * 8,
        out_specs=(vmem(),) * 2,
        scratch_shapes=[
            pltpu.VMEM((3, 6 * width, channels), BF16),
            pltpu.VMEM((span, channels), F32),
            pltpu.VMEM((span, 3 * channels), F32),
        ],
        cost_estimate=cost(2 * 27 * span * channels * channels, 2 * 27 * channels * channels),
        compiler_params=params(16),
    )(
        own_rows,
        base,
        both.reshape(3, own, channels),
        edge_rows,
        far_rows,
        norm_gain,
        attn_gain,
        staged,
    )

    gathered = gather_blocks(sent, count)
    blocks = [block for block, _ in gathered]
    sources = [[origin[k] for k in range(chips)] for _, origin in gathered]

    scale = channels ** (-0.5) * 1.4426950408889634
    wide = span + 2 * width
    queries = pl.pallas_call(
        functools.partial(query_kernel, scale),
        out_shape=jax.ShapeDtypeStruct((span, channels), BF16),
        in_specs=[vmem()] * 3,
        out_specs=vmem(),
        cost_estimate=cost(4 * span * channels * channels, 8 * span * channels),
        compiler_params=params(16),
    )(sent, query_weight, key_weight)

    mid, swap_rows = pl.pallas_call(
        functools.partial(attention_kernel, width, scale, sources),
        out_shape=(jax.ShapeDtypeStruct((4 * width, channels), BF16),) * 2,
        in_specs=[vmem()] * (7 + len(blocks)),
        out_specs=(vmem(),) * 2,
        scratch_shapes=[
            pltpu.VMEM((len(blocks), wide, span), F32),
            pltpu.VMEM((wide, channels), BF16),
            pltpu.VMEM((2 * width, channels), BF16),
            pltpu.VMEM((2, EXTRA, 2 * width), BF16),
        ],
        cost_estimate=cost(
            4 * wide * span * len(blocks) * channels,
            2 * span * channels * len(blocks),
            wide * span * len(blocks),
        ),
        compiler_params=params(32),
    )(
        queries,
        resid,
        attn_gain,
        query_weight,
        key_weight,
        value_weight,
        out_weight,
        *blocks,
    )

    swap_rows = lax.ppermute(swap_rows, "rows", swap)

    decoded = pl.pallas_call(
        functools.partial(up_kernel, width),
        out_shape=jax.ShapeDtypeStruct((frames, 2 * rows_here, outputs, 2 * width), BF16),
        in_specs=[vmem()] * 3,
        out_specs=vmem(),
        scratch_shapes=[
            pltpu.VMEM((channels // 128, 8 * width, 128), F32),
            pltpu.VMEM((9 * outputs, 8 * width), F32),
        ],
        cost_estimate=cost(
            2 * 9 * outputs * channels * 16 * width, 2 * 9 * outputs * channels
        ),
        compiler_params=params(32),
    )(mid, swap_rows, jnp.transpose(up_weight, (0, 1, 3, 2)))
    decoded = jnp.transpose(decoded, (0, 1, 3, 2))
    return (decoded, act.reshape(frames, rows_here, width, channels))


def solution(mesh):
    return jax.shard_map(
        shards,
        mesh=mesh,
        in_specs=(
            P("videos", "rows", None, None),
            P("videos", "rows", None, None),
            P(),
            P(),
            P(),
            P(),
            P(),
            P(),
            P(),
            P(),
        ),
        out_specs=(P("videos", "rows", None, None), P("videos", "rows", None, None)),
        check_vma=False,
    )
```

```python
import functools

import jax
import jax.numpy as jnp
from jax import lax
from jax.experimental import pallas as pl
from jax.experimental.pallas import tpu as pltpu
from jax.sharding import PartitionSpec as P

BF16 = jnp.bfloat16
F32 = jnp.float32
EPS = 1e-06
MIB = 1024 * 1024
EXTRA = 16


def normalize(values, gain):
    return values * lax.rsqrt(jnp.mean(values * values, axis=-1, keepdims=True) + EPS) * gain


def activate(values, gain):
    normed = normalize(values.astype(F32), gain)
    return (normed / (1.0 + jnp.exp(-normed))).astype(BF16)


def vmem():
    return pl.BlockSpec(memory_space=pltpu.VMEM)


def params(mib):
    return pltpu.CompilerParams(vmem_limit_bytes=mib * MIB)


def cost(flops, size, exps=0):
    return pl.CostEstimate(flops=flops, bytes_accessed=size, transcendentals=exps)


def edges_kernel(latents_ref, cache_ref, edge_ref, both_ref, sems):
    core = lax.axis_index("rows") % 2
    row = core * (latents_ref.shape[1] - 1)
    copies = [
        pltpu.make_async_copy(cache_ref.at[:, row], edge_ref.at[pl.ds(0, 2)], sems.at[0]),
        pltpu.make_async_copy(latents_ref.at[:, row], edge_ref.at[pl.ds(2, 2)], sems.at[1]),
        pltpu.make_async_copy(cache_ref.at[1], both_ref.at[core], sems.at[2]),
        pltpu.make_async_copy(latents_ref.at[0], both_ref.at[1 + core], sems.at[3]),
    ]
    for copy in copies:
        copy.start()

    @pl.when(core == 0)
    def _():
        last = pltpu.make_async_copy(latents_ref.at[1], both_ref.at[2], sems.at[4])
        last.start()
        last.wait()

    @pl.when(core == 1)
    def _():
        last = pltpu.make_async_copy(cache_ref.at[0], both_ref.at[0], sems.at[4])
        last.start()
        last.wait()

    for copy in copies:
        copy.wait()


def stage(weight_ref, target, sems, time):
    channels = weight_ref.shape[-1]
    return [
        pltpu.make_async_copy(
            weight_ref.at[time, :, col],
            target.at[:, :, pl.ds(col * channels, channels)],
            sems.at[col],
        )
        for col in range(3)
    ]


def prepare_kernel(
    latents_ref,
    cache_ref,
    weight_ref,
    gain_ref,
    act_ref,
    own_ref,
    base_ref,
    staged_ref,
    latents,
    cache,
    gain,
    sems,
    weight_sems,
):
    channels = latents_ref.shape[-1]
    core = lax.axis_index("rows") % 2
    loads = [
        pltpu.make_async_copy(latents_ref, latents, sems.at[0]),
        pltpu.make_async_copy(cache_ref, cache, sems.at[1]),
        pltpu.make_async_copy(gain_ref, gain, sems.at[2]),
    ]
    copies = [
        copy
        for time in range(2)
        for copy in stage(weight_ref, staged_ref.at[time], weight_sems.at[time], time)
    ]
    for copy in loads + copies:
        copy.start()
    for copy in loads:
        copy.wait()
    act_ref[...] = activate(latents[...], gain[...].reshape(1, channels))
    base_ref[...] = latents[core]
    own_ref[0] = cache[core]
    own_ref[2] = act_ref[core]

    @pl.when(core == 0)
    def _():
        own_ref[1] = cache[1]

    @pl.when(core == 1)
    def _():
        own_ref[1] = act_ref[0]

    for copy in copies:
        copy.wait()


def conv_kernel(
    width,
    own_ref,
    base_ref,
    swap_ref,
    edge_ref,
    far_ref,
    norm_gain_ref,
    attn_gain_ref,
    staged_ref,
    weight_ref,
    front_ref,
    back_ref,
    resid_ref,
    held,
    base,
    total,
    last_weights,
    sems,
):
    channels = own_ref.shape[-1]
    core = lax.axis_index("rows") % 2
    copies = stage(weight_ref, last_weights, sems, 2)
    for copy in copies:
        copy.start()
    own = 2 * width
    mine = pl.multiple_of((1 + 2 * core) * width, width)
    other = pl.multiple_of((3 - 2 * core) * width, width)
    near = pl.multiple_of(5 * core * width, width)
    far = pl.multiple_of(5 * (1 - core) * width, width)
    gain = norm_gain_ref[...].reshape(1, channels)

    def place(time, convert):
        held[time, pl.ds(mine, own), :] = own_ref[time]
        held[time, pl.ds(other, own), :] = convert(swap_ref[time])
        held[time, pl.ds(near, width), :] = convert(edge_ref[time + core])
        held[time, pl.ds(far, width), :] = convert(far_ref[time + core])

    place(0, lambda v: v)

    @pl.when(core == 0)
    def _():
        place(1, lambda v: v)

    @pl.when(core == 1)
    def _():
        place(1, lambda v: activate(v, gain))

    place(2, lambda v: activate(v, gain))
    base[pl.ds(pl.multiple_of(2 * core * width, width), own), :] = base_ref[...].astype(F32)
    base[pl.ds(pl.multiple_of(2 * (1 - core) * width, width), own), :] = swap_ref[2].astype(F32)

    span = 4 * width
    for time in range(3):
        lhs = jnp.concatenate(
            [held[time, row * width : row * width + span, :] for row in range(3)], axis=1
        )
        if time == 2:
            for copy in copies:
                copy.wait()
        rhs = staged_ref[time] if time < 2 else last_weights[...]
        rhs = rhs.reshape(3 * channels, 3 * channels)
        part = jnp.dot(lhs, rhs, preferred_element_type=F32)
        if time == 0:
            total[...] = part
        else:
            total[...] += part
    column = lax.broadcasted_iota(jnp.int32, (span, 1), 0) % width
    left = pltpu.roll(total[:, :channels], 1, axis=0)
    right = pltpu.roll(total[:, 2 * channels :], span - 1, axis=0)
    conv_out = total[:, channels : 2 * channels]
    conv_out = conv_out + jnp.where(column == 0, 0.0, left)
    conv_out = conv_out + jnp.where(column == width - 1, 0.0, right)
    resid = base[...] + conv_out
    resid_ref[...] = resid
    size = jnp.mean(resid * resid, axis=-1, keepdims=True) + EPS
    normed = resid * lax.rsqrt(size) * attn_gain_ref[...].reshape(1, channels)
    edges = jnp.sqrt(jnp.concatenate([size[:width], size[span - width :]], axis=0))
    across = jnp.transpose(jnp.broadcast_to(edges, (2 * width, 128)))[:EXTRA]
    high = across.astype(BF16).astype(F32)
    line = lax.broadcasted_iota(jnp.int32, (EXTRA, 1), 0)
    extra = jnp.where(line == 0, high, jnp.where(line == 1, across - high, 0.0)).astype(BF16)
    half = span // 2
    for ref, low in ((front_ref, 0), (back_ref, half)):
        ref[:half] = normed[low : low + half].astype(BF16)
        ref[half:] = jnp.zeros((EXTRA, channels), BF16)
        ref[half:, : 2 * width] = extra


def nt_dot(a, b):
    return lax.dot_general(a, b, (((1,), (1,)), ((), ())), preferred_element_type=F32)


def lead(scale, normed, query_ref, key_ref):
    queries = jnp.dot(normed, query_ref[...], preferred_element_type=F32).astype(BF16)
    return (nt_dot(queries, key_ref[...]) * scale).astype(BF16)


def whole(pair):
    return jnp.concatenate([half[: half.shape[0] - EXTRA] for half in pair], axis=0)


def pairs_of(refs):
    return [(refs[i], refs[i + 1]) for i in range(0, len(refs), 2)]


def fold(values, combine, total):
    for lane in range(0, values.shape[1], 128):
        piece = values[:, lane : lane + 128]
        total = piece if total is None else combine(total, piece)
    return total


def attend(queries, keys, scores, start, peak, sums, added):
    height = queries.shape[0]
    top = None
    for i, key in enumerate(keys):
        part = nt_dot(queries, key)
        scores[i, start : start + height] = part
        top = fold(part, jnp.maximum, top)
    top = jnp.max(top, axis=-1, keepdims=True)
    if peak is not None:
        top = jnp.maximum(top, peak)
        shrink = jnp.exp2(peak - top)
        sums = sums * shrink
        added = added * shrink
    for i, key in enumerate(keys):
        weights = jnp.exp2(scores[i, start : start + height] - top)
        sums = fold(weights, jnp.add, sums)
        part = jnp.dot(weights.astype(BF16), key, preferred_element_type=F32)
        added = part if added is None else added + part
    return top, sums, added


def early_kernel(scale, query_ref, key_ref, *refs):
    blocks = pairs_of(refs[:-5])
    own_query_ref, peak_ref, sums_ref, added_ref, scores = refs[-5:]
    keys = [whole(pair) for pair in blocks]
    queries = lead(scale, keys[0], query_ref, key_ref)
    own_query_ref[...] = queries
    peak, sums, added = attend(queries, keys, scores, 0, None, None, None)
    peak_ref[...] = jnp.broadcast_to(peak, peak_ref.shape)
    sums_ref[...] = sums
    added_ref[...] = added


def late_kernel(
    width,
    scale,
    sources,
    early,
    own_query_ref,
    peak_ref,
    sums_ref,
    added_ref,
    resid_ref,
    gain_ref,
    query_ref,
    key_ref,
    value_ref,
    out_weight_ref,
    *refs,
):
    count = len(sources)
    blocks = pairs_of(refs[: 2 * count])
    mid_ref, swap_ref, scores, mid, halo, sizes = refs[2 * count :]
    place = lax.axis_index("rows")
    core = place % 2
    chip = place // 2
    own, channels = own_query_ref.shape
    half = own // 2
    chips = len(sources[0])

    for block, origin in zip(blocks, sources):
        for step, part, first, low in (
            (-1, block[1], half - width, 0),
            (1, block[0], 0, width),
        ):
            takers = [k for k in range(chips) if origin[k] == k + step]
            if not takers:
                continue
            wanted = chip == takers[0]
            for k in takers[1:]:
                wanted = jnp.logical_or(wanted, chip == k)

            @pl.when(wanted)
            def _(part=part, first=first, low=low):
                halo[low : low + width] = part[first : first + width, :]
                sizes[low // width] = part[half : half + EXTRA, : 2 * width]

    no_above = chip == 0
    no_below = chip == chips - 1

    @pl.when(no_above)
    def _():
        halo[:width] = jnp.zeros((width, channels), BF16)
        sizes[0] = jnp.zeros((EXTRA, 2 * width), BF16)

    @pl.when(no_below)
    def _():
        halo[width:] = jnp.zeros((width, channels), BF16)
        sizes[1] = jnp.zeros((EXTRA, 2 * width), BF16)

    def column(index):
        parts = sizes[index].astype(F32)
        line = parts[0:1] + parts[1:2]
        return jnp.transpose(jnp.broadcast_to(line, (128, 2 * width)))[:, :1]

    edge_rows = halo[...]
    edge_size = jnp.concatenate([column(0)[width:], column(1)[:width]], axis=0)
    edge_resid = edge_rows.astype(F32) * edge_size / gain_ref[...].reshape(1, channels)
    edge_query = lead(scale, edge_rows, query_ref, key_ref)
    keys = [whole(pair) for pair in blocks]
    _, edge_sums, edge_added = attend(edge_query, keys, scores, own, None, None, None)
    _, own_sums, own_added = attend(
        own_query_ref[...],
        keys[early:],
        scores,
        0,
        peak_ref[:, :1],
        sums_ref[...],
        added_ref[...],
    )

    def finish(added, sums):
        return (added / jnp.sum(sums, axis=-1, keepdims=True)).astype(BF16)

    mixed = jnp.concatenate([finish(own_added, own_sums), finish(edge_added, edge_sums)], axis=0)
    attended = jnp.dot(mixed, value_ref[...], preferred_element_type=F32).astype(BF16)
    projected = jnp.dot(attended, out_weight_ref[...], preferred_element_type=F32)
    inner = own + width
    mid[width:inner] = (resid_ref[...] + projected[:own]).astype(BF16)
    edges = edge_resid + projected[own:]
    mid[:width] = jnp.where(no_above, 0.0, edges[:width]).astype(BF16)
    mid[inner:] = jnp.where(no_below, 0.0, edges[width:]).astype(BF16)
    mid_ref[...] = mid[pl.ds(pl.multiple_of(2 * core * width, width), 4 * width), :]
    swap_ref[...] = mid[pl.ds(pl.multiple_of(2 * (1 - core) * width, width), 4 * width), :]


def up_kernel(width, own, rows_ref, weight_ref, *refs):
    out_ref, fine, total, result_ref, sem = refs[-5:]
    core = lax.axis_index("rows") % 2
    frame = core if own else 1 - core
    channels = rows_ref.shape[1]
    outputs = weight_ref.shape[2]
    wide = 2 * width
    lane = lax.broadcasted_iota(jnp.int32, (1, wide), 1)
    lhs = weight_ref[...].reshape(9 * outputs, channels)
    values = rows_ref[...].astype(F32)
    pieces = []
    for i in range(channels // 128):
        piece = values[:, 128 * i : 128 * (i + 1)]
        fine[i, pl.ds(0, 4 * width, stride=2), :] = piece
        fine[i, pl.ds(1, 4 * width, stride=2), :] = piece
        pieces.append(fine[i].astype(BF16))
    total[...] = nt_dot(lhs, jnp.concatenate(pieces, axis=1))
    for row in range(4):
        low = row // 2 + 1
        picks = (low - 1, low, low) if row % 2 == 0 else (low, low, low + 1)
        taps = []
        for col in range(3):
            tap = None
            for j, pick in enumerate(picks):
                piece = total[
                    (3 * j + col) * outputs : (3 * j + col + 1) * outputs,
                    pick * wide : (pick + 1) * wide,
                ]
                tap = piece if tap is None else tap + piece
            taps.append(tap)
        result = taps[1]
        result = result + jnp.where(lane == 0, 0.0, pltpu.roll(taps[0], 1, axis=1))
        result = result + jnp.where(lane == wide - 1, 0.0, pltpu.roll(taps[2], wide - 1, axis=1))
        result_ref[row] = result.astype(BF16)
    copy = pltpu.make_async_copy(result_ref, out_ref.at[frame], sem)
    copy.start()
    copy.wait()


def gather_blocks(halves, count):
    chips = count // 2
    depth = 2 if chips % 2 == 0 else 1
    length = chips // depth

    ring = [0] + list(range(1, length, 2)) + list(range(2, length, 2))[::-1]
    follow = {a: ring[(i + 1) % length] for i, a in enumerate(ring)}
    onward = {a * depth + b: follow[a] * depth + b for a in range(length) for b in range(depth)}
    backward = {target: source for source, target in onward.items()}
    across = {k: k ^ 1 for k in range(chips)}

    def send(values, targets):
        pairs = [(2 * k + c, 2 * targets[k] + c) for k in range(chips) for c in range(2)]
        return lax.ppermute(values, "rows", pairs)

    def moved(origin, targets):
        return {targets[k]: origin[k] for k in range(chips)}

    here = {k: k for k in range(chips)}
    blocks = [list(halves)]
    origins = [here]
    crossed, crossed_origins = [], []
    back = []
    if length > 1:
        back = [send(values, backward) for values in halves]
    if depth == 2:
        crossed.append([send(values, across) for values in halves])
        crossed_origins.append(moved(here, across))
    waits = {(1, 1): [(back, 0)], (2, 0): [(back, 1)]}
    far = []
    for step in range(1, length - 1):
        blocks.append([send(values, onward) for values in blocks[-1]])
        origins.append(moved(origins[-1], onward))
        if depth == 2 and step == 1:
            far = [send(values, backward) for values in crossed[0]]
            waits[(2, 1)] = [(far, 0)]
        for h in range(2):
            tied = [(blocks[-1], h)]
            if depth == 2:
                tied.append((crossed[-1], h))
            tied = tied + waits.get((step, h), [])
            fixed = lax.optimization_barrier(tuple(where[i] for where, i in tied))
            for (where, i), value in zip(tied, fixed):
                where[i] = value
        if depth == 2:
            crossed.append([send(values, across) for values in blocks[-1]])
            crossed_origins.append(moved(origins[-1], across))
    if depth == 2 and length > 1 and not far:
        far = [send(values, backward) for values in crossed[0]]
    if back:
        blocks.append(back)
        origins.append(moved(here, backward))
    late, late_origins = [], []
    if crossed:
        late, late_origins = [crossed.pop()], [crossed_origins.pop()]
    if far:
        late.append(far)
        late_origins.append(moved(moved(here, across), backward))
    return blocks + crossed, origins + crossed_origins, late, late_origins


def shards(
    latents,
    conv_cache,
    norm_gain,
    conv_weight,
    attn_gain,
    query_weight,
    key_weight,
    value_weight,
    out_weight,
    up_weight,
):
    frames, rows_here, width, channels = latents.shape
    outputs = up_weight.shape[3]
    count = lax.axis_size("rows")
    span = 2 * rows_here * width
    own = rows_here * width
    edge = jax.ShapeDtypeStruct((width, channels), BF16)
    anywhere = pl.BlockSpec(memory_space=pl.ANY)
    hbm = pl.BlockSpec(memory_space=pltpu.HBM)

    chips = count // 2
    swap = [(2 * k + c, 2 * k + 1 - c) for k in range(chips) for c in range(2)]
    neighbour = [(2 * k + 1, 2 * k + 2) for k in range(chips - 1)]
    neighbour = neighbour + [(target, source) for source, target in neighbour]

    latents_in = pltpu.with_memory_space_constraint(latents, pltpu.HBM)
    cache_in = pltpu.with_memory_space_constraint(conv_cache, pltpu.HBM)
    edge_rows, both = pl.pallas_call(
        edges_kernel,
        out_shape=(
            jax.ShapeDtypeStruct((2 * frames, width, channels), BF16),
            jax.ShapeDtypeStruct((3, rows_here, width, channels), BF16),
        ),
        in_specs=[hbm] * 2,
        out_specs=(anywhere,) * 2,
        scratch_shapes=[pltpu.SemaphoreType.DMA((5,))],
        cost_estimate=cost(0, 20 * width * channels),
        compiler_params=params(4),
    )(latents_in, cache_in)
    edge_rows = lax.ppermute(edge_rows, "rows", neighbour)
    both = lax.ppermute(both, "rows", swap)
    act, own_rows, base, staged = pl.pallas_call(
        prepare_kernel,
        out_shape=(
            jax.ShapeDtypeStruct((frames, own, channels), BF16),
            jax.ShapeDtypeStruct((3, own, channels), BF16),
            jax.ShapeDtypeStruct((own, channels), BF16),
            jax.ShapeDtypeStruct((2, 3, channels, 3 * channels), BF16),
        ),
        in_specs=[hbm] * 4,
        out_specs=(vmem(), vmem(), vmem(), anywhere),
        scratch_shapes=[
            pltpu.VMEM((frames, own, channels), BF16),
            pltpu.VMEM((frames, own, channels), BF16),
            pltpu.VMEM((channels,), F32),
            pltpu.SemaphoreType.DMA((3,)),
            pltpu.SemaphoreType.DMA((2, 3)),
        ],
        cost_estimate=cost(10 * frames * own * channels, 2 * 27 * channels * channels),
        compiler_params=params(8),
    )(
        pltpu.with_memory_space_constraint(latents.reshape(frames, own, channels), pltpu.HBM),
        pltpu.with_memory_space_constraint(conv_cache.reshape(frames, own, channels), pltpu.HBM),
        pltpu.with_memory_space_constraint(conv_weight, pltpu.HBM),
        pltpu.with_memory_space_constraint(norm_gain, pltpu.HBM),
    )

    edge_rows, base = lax.optimization_barrier((edge_rows, base))
    far_rows = lax.ppermute(edge_rows, "rows", swap)
    half = jax.ShapeDtypeStruct((span // 2 + EXTRA, channels), BF16)
    front, back, resid = pl.pallas_call(
        functools.partial(conv_kernel, width),
        out_shape=(half, half, jax.ShapeDtypeStruct((span, channels), F32)),
        in_specs=[vmem()] * 8 + [hbm],
        out_specs=(vmem(),) * 3,
        scratch_shapes=[
            pltpu.VMEM((3, 6 * width, channels), BF16),
            pltpu.VMEM((span, channels), F32),
            pltpu.VMEM((span, 3 * channels), F32),
            pltpu.VMEM((3, channels, 3 * channels), BF16),
            pltpu.SemaphoreType.DMA((3,)),
        ],
        cost_estimate=cost(2 * 27 * span * channels * channels, 2 * 27 * channels * channels),
        compiler_params=params(20),
    )(
        own_rows,
        base,
        both.reshape(3, own, channels),
        edge_rows,
        far_rows,
        norm_gain,
        attn_gain,
        staged,
        pltpu.with_memory_space_constraint(conv_weight, pltpu.HBM),
    )

    early, early_origins, late, late_origins = gather_blocks((front, back), count)
    sources = [[origin[k] for k in range(chips)] for origin in early_origins + late_origins]
    early_parts = [part for block in early for part in block]
    late_parts = [part for block in late for part in block]

    scale = channels ** (-0.5) * 1.4426950408889634
    wide = span + 2 * width
    lanes = jax.ShapeDtypeStruct((span, 128), F32)
    own_query, peak, sums, added = pl.pallas_call(
        functools.partial(early_kernel, scale),
        out_shape=(
            jax.ShapeDtypeStruct((span, channels), BF16),
            lanes,
            lanes,
            jax.ShapeDtypeStruct((span, channels), F32),
        ),
        in_specs=[vmem()] * (2 + len(early_parts)),
        out_specs=(vmem(),) * 4,
        scratch_shapes=[pltpu.VMEM((len(early), span, span), F32)],
        cost_estimate=cost(
            4 * span * span * len(early) * channels,
            2 * span * channels * len(early),
            span * span * len(early),
        ),
        compiler_params=params(24),
    )(query_weight, key_weight, *early_parts)

    mid, swap_rows = pl.pallas_call(
        functools.partial(late_kernel, width, scale, sources, len(early)),
        out_shape=(jax.ShapeDtypeStruct((4 * width, channels), BF16),) * 2,
        in_specs=[vmem()] * (10 + len(early_parts) + len(late_parts)),
        out_specs=(vmem(),) * 2,
        scratch_shapes=[
            pltpu.VMEM((len(sources), wide, span), F32),
            pltpu.VMEM((wide, channels), BF16),
            pltpu.VMEM((2 * width, channels), BF16),
            pltpu.VMEM((2, EXTRA, 2 * width), BF16),
        ],
        cost_estimate=cost(
            2 * wide * span * len(sources) * channels,
            2 * span * channels * len(sources),
            wide * span * len(sources) // 2,
        ),
        compiler_params=params(28),
    )(
        own_query,
        peak,
        sums,
        added,
        resid,
        attn_gain,
        query_weight,
        key_weight,
        value_weight,
        out_weight,
        *early_parts,
        *late_parts,
    )

    swap_rows = lax.ppermute(swap_rows, "rows", swap)

    fine_shape = (2 * rows_here, outputs, 2 * width)
    taps = jnp.transpose(up_weight, (0, 1, 3, 2))

    def up(is_own, *operands):
        return pl.pallas_call(
            functools.partial(up_kernel, width, is_own),
            out_shape=jax.ShapeDtypeStruct((frames, *fine_shape), BF16),
            in_specs=[vmem()] * 2 + [anywhere] * (len(operands) - 2),
            out_specs=anywhere,
            input_output_aliases={} if is_own else {2: 0},
            scratch_shapes=[
                pltpu.VMEM((channels // 128, 8 * width, 128), F32),
                pltpu.VMEM((9 * outputs, 8 * width), F32),
                pltpu.VMEM(fine_shape, BF16),
                pltpu.SemaphoreType.DMA(()),
            ],
            cost_estimate=cost(
                2 * 9 * outputs * channels * 8 * width, 2 * 9 * outputs * channels
            ),
            compiler_params=params(16),
        )(*operands)

    decoded = up(False, swap_rows, taps, up(True, mid, taps))
    decoded = jnp.transpose(decoded, (0, 1, 3, 2))
    return (decoded, act.reshape(frames, rows_here, width, channels))


def solution(mesh):
    return jax.shard_map(
        shards,
        mesh=mesh,
        in_specs=(
            P("videos", "rows", None, None),
            P("videos", "rows", None, None),
            P(),
            P(),
            P(),
            P(),
            P(),
            P(),
            P(),
            P(),
        ),
        out_specs=(P("videos", "rows", None, None), P("videos", "rows", None, None)),
        check_vma=False,
    )
```

```python
import functools

import jax
import jax.numpy as jnp
from jax import lax
from jax.experimental import pallas as pl
from jax.experimental.pallas import tpu as pltpu
from jax.sharding import PartitionSpec as P

BF16 = jnp.bfloat16
F32 = jnp.float32
EPS = 1e-06
MIB = 1024 * 1024
EXTRA = 16
STAGED = 2


def normalize(values, gain):
    return values * lax.rsqrt(jnp.mean(values * values, axis=-1, keepdims=True) + EPS) * gain


def activate(values, gain):
    normed = normalize(values.astype(F32), gain)
    return (normed / (1.0 + jnp.exp(-normed))).astype(BF16)


def params(mib):
    return pltpu.CompilerParams(vmem_limit_bytes=mib * MIB)


def cost(flops, size, exps=0):
    return pl.CostEstimate(flops=flops, bytes_accessed=size, transcendentals=exps)


def edges_kernel(latents_ref, cache_ref, edge_ref, both_ref, sems):
    core = lax.axis_index("rows") % 2
    row = core * (latents_ref.shape[1] - 1)
    copies = [
        pltpu.make_async_copy(cache_ref.at[:, row], edge_ref.at[pl.ds(0, 2)], sems.at[0]),
        pltpu.make_async_copy(latents_ref.at[:, row], edge_ref.at[pl.ds(2, 2)], sems.at[1]),
        pltpu.make_async_copy(cache_ref.at[1], both_ref.at[core], sems.at[2]),
        pltpu.make_async_copy(latents_ref.at[0], both_ref.at[1 + core], sems.at[3]),
    ]
    for copy in copies:
        copy.start()

    @pl.when(core == 0)
    def _():
        last = pltpu.make_async_copy(latents_ref.at[1], both_ref.at[2], sems.at[4])
        last.start()
        last.wait()

    @pl.when(core == 1)
    def _():
        last = pltpu.make_async_copy(cache_ref.at[0], both_ref.at[0], sems.at[4])
        last.start()
        last.wait()

    for copy in copies:
        copy.wait()


def start_all(pairs, sems, first=0):
    copies = [
        pltpu.make_async_copy(source, target, sems.at[first + i])
        for i, (source, target) in enumerate(pairs)
    ]
    for copy in copies:
        copy.start()
    return copies


def wait_all(copies):
    for copy in copies:
        copy.wait()


def laid_out(weight_ref, target, time):
    channels = weight_ref.shape[-1]
    return [
        (weight_ref.at[time, :, col], target.at[:, :, pl.ds(col * channels, channels)])
        for col in range(3)
    ]


def activate_kernel(latents_ref, gain_ref, act_ref, latents, gain, act, sems):
    wait_all(start_all([(latents_ref, latents), (gain_ref, gain)], sems))
    act[...] = activate(latents[...], gain[...].reshape(1, latents.shape[-1]))
    wait_all(start_all([(act, act_ref)], sems))


def stage_kernel(latents_ref, cache_ref, weight_ref, own_ref, staged_ref, sems):
    core = lax.axis_index("rows") % 2
    pairs = [(cache_ref.at[core], own_ref.at[0]), (latents_ref.at[core], own_ref.at[2])]
    for time in range(staged_ref.shape[0]):
        pairs = pairs + laid_out(weight_ref, staged_ref.at[time], time)
    copies = start_all(pairs, sems, 1)

    @pl.when(core == 0)
    def _():
        wait_all(start_all([(cache_ref.at[1], own_ref.at[1])], sems))

    @pl.when(core == 1)
    def _():
        wait_all(start_all([(latents_ref.at[0], own_ref.at[1])], sems))

    wait_all(copies)


def conv_kernel(
    width,
    own_ref,
    swap_ref,
    edge_ref,
    far_ref,
    norm_gain_ref,
    attn_gain_ref,
    staged_ref,
    weight_ref,
    front_ref,
    back_ref,
    resid_ref,
    raw,
    second,
    third,
    weights,
    total,
    front,
    back,
    resid,
    norm_gain,
    attn_gain,
    sems,
):
    channels = own_ref.shape[-1]
    core = lax.axis_index("rows") % 2
    own = 2 * width
    span = 4 * width
    staged = staged_ref.shape[0]

    def rows_at(index, count):
        return raw.at[:, pl.ds(pl.multiple_of(index * width, width), count)]

    frames = pl.ds(core, 3)
    small = start_all(
        [
            (own_ref, rows_at(1 + 2 * core, own)),
            (swap_ref, rows_at(3 - 2 * core, own)),
            (edge_ref.at[frames], rows_at(5 * core, width)),
            (far_ref.at[frames], rows_at(5 * (1 - core), width)),
            (norm_gain_ref, norm_gain),
            (attn_gain_ref, attn_gain),
        ],
        sems,
    )
    large = []
    for time in range(3):
        if time < staged:
            pairs = [(staged_ref.at[time], weights.at[time])]
        else:
            pairs = laid_out(weight_ref, weights.at[time], time)
        large.append(start_all(pairs, sems, 6 + 3 * time))
    wait_all(small)
    gain = norm_gain[...].reshape(1, channels)

    def taps(ref, time):
        lhs = jnp.concatenate([ref[row * width : row * width + span] for row in range(3)], axis=1)
        rhs = weights[time].reshape(3 * channels, 3 * channels)
        return jnp.dot(lhs, rhs, preferred_element_type=F32)

    wait_all(large[0])
    total[...] = taps(raw.at[0], 0)
    second[...] = jnp.where(core == 1, activate(raw[1], gain), raw[1])
    third[...] = activate(raw[2], gain)
    wait_all(large[1])
    total[...] += taps(second, 1)
    wait_all(large[2])
    total[...] += taps(third, 2)

    column = lax.broadcasted_iota(jnp.int32, (span, 1), 0) % width
    left = pltpu.roll(total[:, :channels], 1, axis=0)
    right = pltpu.roll(total[:, 2 * channels :], span - 1, axis=0)
    conv_out = total[:, channels : 2 * channels]
    conv_out = conv_out + jnp.where(column == 0, 0.0, left)
    conv_out = conv_out + jnp.where(column == width - 1, 0.0, right)
    value = raw[2, width : width + span].astype(F32) + conv_out
    resid[...] = value
    size = jnp.mean(value * value, axis=-1, keepdims=True) + EPS
    normed = value * lax.rsqrt(size) * attn_gain[...].reshape(1, channels)
    edges = jnp.sqrt(jnp.concatenate([size[:width], size[span - width :]], axis=0))
    across = jnp.transpose(jnp.broadcast_to(edges, (2 * width, 128)))[:EXTRA]
    high = across.astype(BF16).astype(F32)
    line = lax.broadcasted_iota(jnp.int32, (EXTRA, 1), 0)
    extra = jnp.where(line == 0, high, jnp.where(line == 1, across - high, 0.0)).astype(BF16)
    half = span // 2
    for ref, low in ((front, 0), (back, half)):
        ref[:half] = normed[low : low + half].astype(BF16)
        ref[half:] = jnp.zeros((EXTRA, channels), BF16)
        ref[half:, : 2 * width] = extra
    wait_all(start_all([(front, front_ref), (back, back_ref), (resid, resid_ref)], sems))


def nt_dot(a, b):
    return lax.dot_general(a, b, (((1,), (1,)), ((), ())), preferred_element_type=F32)


def lead(scale, normed, query_ref, key_ref):
    queries = jnp.dot(normed, query_ref[...], preferred_element_type=F32).astype(BF16)
    return (nt_dot(queries, key_ref[...]) * scale).astype(BF16)


def pairs_of(refs):
    return [(refs[i], refs[i + 1]) for i in range(0, len(refs), 2)]


def load_keys(blocks, keys, sems, first):
    half = keys.shape[1] // 2
    copies = []
    for i, pair in enumerate(blocks):
        halves = [
            (ref.at[pl.ds(0, half)], keys.at[i, pl.ds(part * half, half)])
            for part, ref in enumerate(pair)
        ]
        copies.append(start_all(halves, sems, first + 2 * i))
    return copies


def fold(values, combine, total):
    for lane in range(0, values.shape[1], 128):
        piece = values[:, lane : lane + 128]
        total = piece if total is None else combine(total, piece)
    return total


def attend(queries, keys, indices, scores, start, peak, sums, added):
    height = queries.shape[0]
    top = None
    for i in indices:
        part = nt_dot(queries, keys[i])
        scores[i, start : start + height] = part
        top = fold(part, jnp.maximum, top)
    top = jnp.max(top, axis=-1, keepdims=True)
    if peak is not None:
        top = jnp.maximum(top, peak)
        shrink = jnp.exp2(peak - top)
        sums = sums * shrink
        added = added * shrink
    for i in indices:
        weights = jnp.exp2(scores[i, start : start + height] - top)
        sums = fold(weights, jnp.add, sums)
        part = jnp.dot(weights.astype(BF16), keys[i], preferred_element_type=F32)
        added = part if added is None else added + part
    return top, sums, added


def early_kernel(scale, count, query_ref, key_ref, *refs):
    blocks = pairs_of(refs[: 2 * count])
    outs, held = refs[2 * count : 2 * count + 4], refs[2 * count + 4 : 2 * count + 8]
    keys, scores, query_weight, key_weight, sems = refs[2 * count + 8 :]
    own_query, peak_out, sums_out, added_out = held
    small = start_all([(query_ref, query_weight), (key_ref, key_weight)], sems)
    loads = load_keys(blocks, keys, sems, 2)
    wait_all(small)
    for copies in loads:
        wait_all(copies)
    queries = lead(scale, keys[0], query_weight, key_weight)
    own_query[...] = queries
    peak, sums, added = attend(queries, keys, range(count), scores, 0, None, None, None)
    peak_out[...] = jnp.broadcast_to(peak, peak_out.shape)
    sums_out[...] = sums
    added_out[...] = added
    wait_all(start_all(list(zip(held, outs)), sems))


def late_kernel(width, scale, above, below, early, count, *refs):
    inputs, refs = refs[:10], refs[10:]
    blocks, refs = pairs_of(refs[: 2 * count]), refs[2 * count :]
    mid_ref, swap_ref = refs[:2]
    held, refs = refs[2:12], refs[12:]
    keys, extras, scores, mid, sems = refs
    own_query, peak, sums, added, resid, gain, query_weight, key_weight, value_weight, out = held
    place = lax.axis_index("rows")
    core = place % 2
    chip = place // 2
    own, channels = own_query.shape
    chips = len(above)

    base = len(held)
    loads = load_keys(blocks, keys, sems, base)
    base = base + 2 * count
    notes = start_all(
        [
            (pair[0].at[pl.ds(own // 2, EXTRA), pl.ds(0, 2 * width)], extras.at[i])
            for i, pair in enumerate(blocks)
        ],
        sems,
        base,
    )
    small = start_all(list(zip(inputs, held)), sems)
    for copies in loads:
        wait_all(copies)
    wait_all(notes)
    wait_all(small)

    def pick(table):
        index = 0
        for k, entry in enumerate(table):
            if entry:
                index = jnp.where(chip == k, entry, index)
        return index

    before, after = pick(above), pick(below)
    no_above = chip == 0
    no_below = chip == chips - 1

    def column(index):
        parts = extras[index].astype(F32)
        line = parts[0:1] + parts[1:2]
        return jnp.transpose(jnp.broadcast_to(line, (128, 2 * width)))[:, :1]

    edge_rows = jnp.concatenate([keys[before][own - width :], keys[after][:width]], axis=0)
    edge_size = jnp.concatenate([column(before)[width:], column(after)[:width]], axis=0)
    edge_resid = edge_rows.astype(F32) * edge_size / gain[...].reshape(1, channels)
    edge_query = lead(scale, edge_rows, query_weight, key_weight)
    _, edge_sums, edge_added = attend(
        edge_query, keys, range(count), scores, own, None, None, None
    )
    _, own_sums, own_added = attend(
        own_query[...],
        keys,
        range(early, count),
        scores,
        0,
        peak[:, :1],
        sums[...],
        added[...],
    )

    def finish(values, parts):
        return (values / jnp.sum(parts, axis=-1, keepdims=True)).astype(BF16)

    mixed = jnp.concatenate([finish(own_added, own_sums), finish(edge_added, edge_sums)], axis=0)
    attended = jnp.dot(mixed, value_weight[...], preferred_element_type=F32).astype(BF16)
    projected = jnp.dot(attended, out[...], preferred_element_type=F32)
    inner = own + width
    mid[width:inner] = (resid[...] + projected[:own]).astype(BF16)
    edges = edge_resid + projected[own:]
    mid[:width] = jnp.where(no_above, 0.0, edges[:width]).astype(BF16)
    mid[inner:] = jnp.where(no_below, 0.0, edges[width:]).astype(BF16)

    def part(index):
        return mid.at[pl.ds(pl.multiple_of(2 * index * width, width), 4 * width)]

    wait_all(start_all([(part(1 - core), swap_ref), (part(core), mid_ref)], sems))


def up_kernel(
    width, mid_ref, swap_ref, weight_ref, out_ref, rows, weights, fine, total, results, sems
):
    core = lax.axis_index("rows") % 2
    channels = mid_ref.shape[1]
    outputs = weight_ref.shape[2]
    wide = 2 * width
    loads = start_all(
        [(mid_ref, rows.at[0]), (weight_ref, weights), (swap_ref, rows.at[1])], sems
    )
    lane = lax.broadcasted_iota(jnp.int32, (1, wide), 1)

    def spread(slot):
        values = rows[slot].astype(F32)
        pieces = []
        for i in range(channels // 128):
            piece = values[:, 128 * i : 128 * (i + 1)]
            fine[slot, i, pl.ds(0, 4 * width, stride=2), :] = piece
            fine[slot, i, pl.ds(1, 4 * width, stride=2), :] = piece
            pieces.append(fine[slot, i].astype(BF16))
        return jnp.concatenate(pieces, axis=1)

    def combine(slot):
        for row in range(4):
            low = row // 2 + 1
            picks = (low - 1, low, low) if row % 2 == 0 else (low, low, low + 1)
            taps = []
            for col in range(3):
                tap = None
                for j, pick in enumerate(picks):
                    piece = total[
                        slot,
                        (3 * j + col) * outputs : (3 * j + col + 1) * outputs,
                        pick * wide : (pick + 1) * wide,
                    ]
                    tap = piece if tap is None else tap + piece
                taps.append(tap)
            result = taps[1]
            result = result + jnp.where(lane == 0, 0.0, pltpu.roll(taps[0], 1, axis=1))
            result = result + jnp.where(
                lane == wide - 1, 0.0, pltpu.roll(taps[2], wide - 1, axis=1)
            )
            results[slot, row] = result.astype(BF16)

    loads[0].wait()
    first = spread(0)
    loads[2].wait()
    second = spread(1)
    loads[1].wait()
    lhs = weights[...].reshape(9 * outputs, channels)
    total[0] = nt_dot(lhs, first)
    total[1] = nt_dot(lhs, second)
    combine(0)
    stores = start_all([(results.at[0], out_ref.at[core])], sems, 3)
    combine(1)
    stores = stores + start_all([(results.at[1], out_ref.at[1 - core])], sems, 4)
    wait_all(stores)


def gather_blocks(halves, count):
    chips = count // 2
    depth = 2 if chips % 2 == 0 else 1
    length = chips // depth

    ring = [0] + list(range(1, length, 2)) + list(range(2, length, 2))[::-1]
    follow = {a: ring[(i + 1) % length] for i, a in enumerate(ring)}
    onward = {a * depth + b: follow[a] * depth + b for a in range(length) for b in range(depth)}
    backward = {target: source for source, target in onward.items()}
    across = {k: k ^ 1 for k in range(chips)}

    def send(values, targets):
        pairs = [(2 * k + c, 2 * targets[k] + c) for k in range(chips) for c in range(2)]
        return lax.ppermute(values, "rows", pairs)

    def moved(origin, targets):
        return {targets[k]: origin[k] for k in range(chips)}

    here = {k: k for k in range(chips)}
    blocks = [list(halves)]
    origins = [here]
    crossed, crossed_origins = [], []
    back = []
    if length > 1:
        back = [send(values, backward) for values in halves]
    if depth == 2:
        crossed.append([send(values, across) for values in halves])
        crossed_origins.append(moved(here, across))
    waits = {(1, 1): [(back, 0)], (2, 0): [(back, 1)]}
    far = []
    for step in range(1, length - 1):
        blocks.append([send(values, onward) for values in blocks[-1]])
        origins.append(moved(origins[-1], onward))
        if depth == 2 and step == 1:
            far = [send(values, backward) for values in crossed[0]]
            waits[(2, 1)] = [(far, 0)]
        for h in range(2):
            tied = [(blocks[-1], h)]
            if depth == 2:
                tied.append((crossed[-1], h))
            tied = tied + waits.get((step, h), [])
            fixed = lax.optimization_barrier(tuple(where[i] for where, i in tied))
            for (where, i), value in zip(tied, fixed):
                where[i] = value
        if depth == 2:
            crossed.append([send(values, across) for values in blocks[-1]])
            crossed_origins.append(moved(origins[-1], across))
    if depth == 2 and length > 1 and not far:
        far = [send(values, backward) for values in crossed[0]]
    if back:
        blocks.append(back)
        origins.append(moved(here, backward))
    late, late_origins = [], []
    if crossed:
        late, late_origins = [crossed.pop()], [crossed_origins.pop()]
    if far:
        late.append(far)
        late_origins.append(moved(moved(here, across), backward))
    return blocks + crossed, origins + crossed_origins, late, late_origins


def shards(
    latents,
    conv_cache,
    norm_gain,
    conv_weight,
    attn_gain,
    query_weight,
    key_weight,
    value_weight,
    out_weight,
    up_weight,
):
    frames, rows_here, width, channels = latents.shape
    outputs = up_weight.shape[3]
    count = lax.axis_size("rows")
    span = 2 * rows_here * width
    own = rows_here * width
    edge = jax.ShapeDtypeStruct((width, channels), BF16)
    anywhere = pl.BlockSpec(memory_space=pl.ANY)
    hbm = pl.BlockSpec(memory_space=pltpu.HBM)

    chips = count // 2
    swap = [(2 * k + c, 2 * k + 1 - c) for k in range(chips) for c in range(2)]
    neighbour = [(2 * k + 1, 2 * k + 2) for k in range(chips - 1)]
    neighbour = neighbour + [(target, source) for source, target in neighbour]

    latents_in = pltpu.with_memory_space_constraint(latents, pltpu.HBM)
    cache_in = pltpu.with_memory_space_constraint(conv_cache, pltpu.HBM)
    edge_rows, both = pl.pallas_call(
        edges_kernel,
        out_shape=(
            jax.ShapeDtypeStruct((2 * frames, width, channels), BF16),
            jax.ShapeDtypeStruct((3, rows_here, width, channels), BF16),
        ),
        in_specs=[hbm] * 2,
        out_specs=(anywhere,) * 2,
        scratch_shapes=[pltpu.SemaphoreType.DMA((5,))],
        cost_estimate=cost(0, 20 * width * channels),
        compiler_params=params(4),
    )(latents_in, cache_in)
    edge_rows = lax.ppermute(edge_rows, "rows", neighbour)
    both = lax.ppermute(both, "rows", swap)
    flat_in = pltpu.with_memory_space_constraint(latents.reshape(frames, own, channels), pltpu.HBM)
    flat_cache = pltpu.with_memory_space_constraint(
        conv_cache.reshape(frames, own, channels), pltpu.HBM
    )
    weight_in = pltpu.with_memory_space_constraint(conv_weight, pltpu.HBM)
    taps_shape = (3, channels, 3 * channels)
    own_rows, staged = pl.pallas_call(
        stage_kernel,
        out_shape=(
            jax.ShapeDtypeStruct((3, own, channels), BF16),
            jax.ShapeDtypeStruct((STAGED, *taps_shape), BF16),
        ),
        in_specs=[hbm] * 3,
        out_specs=(anywhere,) * 2,
        scratch_shapes=[pltpu.SemaphoreType.DMA((3 + 3 * STAGED,))],
        cost_estimate=cost(0, 4 * 9 * STAGED * channels * channels),
        compiler_params=params(4),
    )(flat_in, flat_cache, weight_in)

    edge_rows, own_rows = lax.optimization_barrier((edge_rows, own_rows))
    far_rows = lax.ppermute(edge_rows, "rows", swap)
    half = (span // 2 + EXTRA, channels)
    halo_rows = (6 * width, channels)
    front, back, resid = pl.pallas_call(
        functools.partial(conv_kernel, width),
        out_shape=(
            jax.ShapeDtypeStruct(half, BF16),
            jax.ShapeDtypeStruct(half, BF16),
            jax.ShapeDtypeStruct((span, channels), F32),
        ),
        in_specs=[anywhere] * 7 + [hbm],
        out_specs=(anywhere,) * 3,
        scratch_shapes=[
            pltpu.VMEM((3, *halo_rows), BF16),
            pltpu.VMEM(halo_rows, BF16),
            pltpu.VMEM(halo_rows, BF16),
            pltpu.VMEM((3, *taps_shape), BF16),
            pltpu.VMEM((span, 3 * channels), F32),
            pltpu.VMEM(half, BF16),
            pltpu.VMEM(half, BF16),
            pltpu.VMEM((span, channels), F32),
            pltpu.VMEM((channels,), F32),
            pltpu.VMEM((channels,), F32),
            pltpu.SemaphoreType.DMA((15,)),
        ],
        cost_estimate=cost(2 * 27 * span * channels * channels, 2 * 27 * channels * channels),
        compiler_params=params(24),
    )(
        own_rows,
        both.reshape(3, own, channels),
        edge_rows,
        far_rows,
        norm_gain,
        attn_gain,
        staged,
        weight_in,
    )

    early, early_origins, late, late_origins = gather_blocks((front, back), count)
    sources = early_origins + late_origins
    above, below = (
        [next((i for i, o in enumerate(sources) if o[k] == k + step), 0) for k in range(chips)]
        for step in (-1, 1)
    )
    early_parts = [part for block in early for part in block]
    late_parts = [part for block in late for part in block]

    act = pl.pallas_call(
        activate_kernel,
        out_shape=jax.ShapeDtypeStruct((frames, own, channels), BF16),
        in_specs=[hbm] * 2,
        out_specs=anywhere,
        scratch_shapes=[
            pltpu.VMEM((frames, own, channels), BF16),
            pltpu.VMEM((channels,), F32),
            pltpu.VMEM((frames, own, channels), BF16),
            pltpu.SemaphoreType.DMA((2,)),
        ],
        cost_estimate=cost(20 * frames * own * channels, 4 * frames * own * channels),
        compiler_params=params(8),
    )(flat_in, pltpu.with_memory_space_constraint(norm_gain, pltpu.HBM))

    scale = channels ** (-0.5) * 1.4426950408889634
    wide = span + 2 * width
    square = pltpu.VMEM((channels, channels), BF16)
    state = [((span, channels), BF16), ((span, 128), F32), ((span, 128), F32)]
    state = state + [((span, channels), F32)]
    own_query, peak, sums, added = pl.pallas_call(
        functools.partial(early_kernel, scale, len(early)),
        out_shape=tuple(jax.ShapeDtypeStruct(*item) for item in state),
        in_specs=[anywhere] * (2 + len(early_parts)),
        out_specs=(anywhere,) * 4,
        scratch_shapes=[pltpu.VMEM(*item) for item in state]
        + [
            pltpu.VMEM((len(early), span, channels), BF16),
            pltpu.VMEM((len(early), span, span), F32),
            square,
            square,
            pltpu.SemaphoreType.DMA((max(4, 2 + len(early_parts)),)),
        ],
        cost_estimate=cost(
            4 * span * span * len(early) * channels,
            2 * span * channels * len(early),
            span * span * len(early),
        ),
        compiler_params=params(24),
    )(query_weight, key_weight, *early_parts)

    blocks = len(sources)
    mid, swap_rows = pl.pallas_call(
        functools.partial(late_kernel, width, scale, above, below, len(early), blocks),
        out_shape=(jax.ShapeDtypeStruct((4 * width, channels), BF16),) * 2,
        in_specs=[anywhere] * (10 + 2 * blocks),
        out_specs=(anywhere,) * 2,
        scratch_shapes=[pltpu.VMEM(*item) for item in state]
        + [
            pltpu.VMEM((span, channels), F32),
            pltpu.VMEM((channels,), F32),
            square,
            square,
            square,
            square,
            pltpu.VMEM((blocks, span, channels), BF16),
            pltpu.VMEM((blocks, EXTRA, 2 * width), BF16),
            pltpu.VMEM((blocks, wide, span), F32),
            pltpu.VMEM((wide, channels), BF16),
            pltpu.SemaphoreType.DMA((10 + 3 * blocks,)),
        ],
        cost_estimate=cost(
            2 * wide * span * blocks * channels,
            2 * span * channels * blocks,
            wide * span * blocks // 2,
        ),
        compiler_params=params(36),
    )(
        own_query,
        peak,
        sums,
        added,
        resid,
        attn_gain,
        query_weight,
        key_weight,
        value_weight,
        out_weight,
        *early_parts,
        *late_parts,
    )

    swap_rows = lax.ppermute(swap_rows, "rows", swap)

    fine_shape = (2 * rows_here, outputs, 2 * width)
    decoded = pl.pallas_call(
        functools.partial(up_kernel, width),
        out_shape=jax.ShapeDtypeStruct((frames, *fine_shape), BF16),
        in_specs=[anywhere] * 3,
        out_specs=anywhere,
        scratch_shapes=[
            pltpu.VMEM((2, 4 * width, channels), BF16),
            pltpu.VMEM((3, 3, outputs, channels), BF16),
            pltpu.VMEM((2, channels // 128, 8 * width, 128), F32),
            pltpu.VMEM((2, 9 * outputs, 8 * width), F32),
            pltpu.VMEM((2, *fine_shape), BF16),
            pltpu.SemaphoreType.DMA((5,)),
        ],
        cost_estimate=cost(
            2 * 9 * outputs * channels * 16 * width, 2 * 9 * outputs * channels
        ),
        compiler_params=params(24),
    )(mid, swap_rows, jnp.transpose(up_weight, (0, 1, 3, 2)))
    decoded = jnp.transpose(decoded, (0, 1, 3, 2))
    return (decoded, act.reshape(frames, rows_here, width, channels))


def solution(mesh):
    return jax.shard_map(
        shards,
        mesh=mesh,
        in_specs=(
            P("videos", "rows", None, None),
            P("videos", "rows", None, None),
            P(),
            P(),
            P(),
            P(),
            P(),
            P(),
            P(),
            P(),
        ),
        out_specs=(P("videos", "rows", None, None), P("videos", "rows", None, None)),
        check_vma=False,
    )
```

```python
import functools

import jax
import jax.numpy as jnp
from jax import lax
from jax.experimental import pallas as pl
from jax.experimental.pallas import tpu as pltpu
from jax.sharding import PartitionSpec as P

BF16 = jnp.bfloat16
F32 = jnp.float32
EPS = 1e-06
MIB = 1024 * 1024
EXTRA = 16


def normalize(values, gain):
    return values * lax.rsqrt(jnp.mean(values * values, axis=-1, keepdims=True) + EPS) * gain


def activate(values, gain):
    normed = normalize(values.astype(F32), gain)
    return (normed / (1.0 + jnp.exp(-normed))).astype(BF16)


def vmem():
    return pl.BlockSpec(memory_space=pltpu.VMEM)


def params(mib):
    return pltpu.CompilerParams(vmem_limit_bytes=mib * MIB)


def cost(flops, size, exps=0):
    return pl.CostEstimate(flops=flops, bytes_accessed=size, transcendentals=exps)


def edges_kernel(latents_ref, cache_ref, edge_ref, both_ref, sems):
    core = lax.axis_index("rows") % 2
    row = core * (latents_ref.shape[1] - 1)
    copies = [
        pltpu.make_async_copy(cache_ref.at[:, row], edge_ref.at[pl.ds(0, 2)], sems.at[0]),
        pltpu.make_async_copy(latents_ref.at[:, row], edge_ref.at[pl.ds(2, 2)], sems.at[1]),
        pltpu.make_async_copy(cache_ref.at[1], both_ref.at[core], sems.at[2]),
        pltpu.make_async_copy(latents_ref.at[0], both_ref.at[1 + core], sems.at[3]),
    ]
    for copy in copies:
        copy.start()

    @pl.when(core == 0)
    def _():
        last = pltpu.make_async_copy(latents_ref.at[1], both_ref.at[2], sems.at[4])
        last.start()
        last.wait()

    @pl.when(core == 1)
    def _():
        last = pltpu.make_async_copy(cache_ref.at[0], both_ref.at[0], sems.at[4])
        last.start()
        last.wait()

    for copy in copies:
        copy.wait()


def start_all(pairs, sems, first=0):
    copies = [
        pltpu.make_async_copy(source, target, sems.at[first + i])
        for i, (source, target) in enumerate(pairs)
    ]
    for copy in copies:
        copy.start()
    return copies


def wait_all(copies):
    for copy in copies:
        copy.wait()


def prepare_kernel(
    latents_ref,
    cache_ref,
    weight_ref,
    gain_ref,
    act_ref,
    own_ref,
    staged_ref,
    latents,
    cache,
    gain,
    act,
    sems,
):
    channels = latents_ref.shape[-1]
    core = lax.axis_index("rows") % 2
    loads = start_all([(latents_ref, latents), (cache_ref, cache), (gain_ref, gain)], sems)
    stages = start_all(
        [
            (
                weight_ref.at[time, :, col],
                staged_ref.at[time, :, :, pl.ds(col * channels, channels)],
            )
            for time in range(3)
            for col in range(3)
        ],
        sems,
        4,
    )
    wait_all(loads)
    act[...] = activate(latents[...], gain[...].reshape(1, channels))
    store = start_all([(act, act_ref)], sems, 3)
    own_ref[0] = cache[core]
    own_ref[1] = jnp.where(core == 0, cache[1], latents[0])
    own_ref[2] = latents[core]
    wait_all(store + stages)


def conv_kernel(
    width,
    own_ref,
    swap_ref,
    edge_ref,
    far_ref,
    norm_gain_ref,
    attn_gain_ref,
    weights,
    sent_ref,
    front_ref,
    back_ref,
    resid_ref,
    raw,
    second,
    third,
    total,
):
    channels = own_ref.shape[-1]
    core = lax.axis_index("rows") % 2
    own = 2 * width
    span = 4 * width
    gain = norm_gain_ref[...].reshape(1, channels)

    def put(index, values):
        rows = pl.ds(pl.multiple_of(index * width, width), values.shape[1])
        raw[:, rows, :] = values

    put(1 + 2 * core, own_ref[...])
    put(3 - 2 * core, swap_ref[...])
    put(5 * core, edge_ref[pl.ds(core, 3)])
    put(5 * (1 - core), far_ref[pl.ds(core, 3)])

    def taps(ref, time):
        lhs = jnp.concatenate([ref[row * width : row * width + span] for row in range(3)], axis=1)
        rhs = weights[time].reshape(3 * channels, 3 * channels)
        return jnp.dot(lhs, rhs, preferred_element_type=F32)

    total[...] = taps(raw.at[0], 0)
    second[...] = jnp.where(core == 1, activate(raw[1], gain), raw[1])
    third[...] = activate(raw[2], gain)
    total[...] += taps(second, 1)
    total[...] += taps(third, 2)

    column = lax.broadcasted_iota(jnp.int32, (span, 1), 0) % width
    left = pltpu.roll(total[:, :channels], 1, axis=0)
    right = pltpu.roll(total[:, 2 * channels :], span - 1, axis=0)
    conv_out = total[:, channels : 2 * channels]
    conv_out = conv_out + jnp.where(column == 0, 0.0, left)
    conv_out = conv_out + jnp.where(column == width - 1, 0.0, right)
    resid = raw[2, width : width + span].astype(F32) + conv_out
    resid_ref[...] = resid
    size = jnp.mean(resid * resid, axis=-1, keepdims=True) + EPS
    normed = resid * lax.rsqrt(size) * attn_gain_ref[...].reshape(1, channels)
    edges = jnp.sqrt(jnp.concatenate([size[:width], size[span - width :]], axis=0))
    across = jnp.transpose(jnp.broadcast_to(edges, (2 * width, 128)))[:EXTRA]
    high = across.astype(BF16).astype(F32)
    line = lax.broadcasted_iota(jnp.int32, (EXTRA, 1), 0)
    extra = jnp.where(line == 0, high, jnp.where(line == 1, across - high, 0.0)).astype(BF16)
    half = span // 2
    for ref, low, count in ((sent_ref, 0, span), (front_ref, 0, half), (back_ref, half, half)):
        ref[:count] = normed[low : low + count].astype(BF16)
        ref[count:] = jnp.zeros((EXTRA, channels), BF16)
        ref[count:, : 2 * width] = extra


def nt_dot(a, b):
    return lax.dot_general(a, b, (((1,), (1,)), ((), ())), preferred_element_type=F32)


def whole(parts):
    rows = [part[: part.shape[0] - EXTRA] for part in parts]
    return rows[0] if len(rows) == 1 else jnp.concatenate(rows, axis=0)


def grouped(refs, counts):
    blocks, first = [], 0
    for count in counts:
        blocks.append(refs[first : first + count])
        first += count
    return blocks


def fold(values, combine, total):
    for lane in range(0, values.shape[1], 128):
        piece = values[:, lane : lane + 128]
        total = piece if total is None else combine(total, piece)
    return total


def attend(queries, keys, scores, start, peak, sums, added):
    height = queries.shape[0]
    top = None
    for i, key in enumerate(keys):
        part = nt_dot(queries, key)
        scores[i, start : start + height] = part
        top = fold(part, jnp.maximum, top)
    top = jnp.max(top, axis=-1, keepdims=True)
    if peak is not None:
        top = jnp.maximum(top, peak)
        shrink = jnp.exp2(peak - top)
        sums = sums * shrink
        added = added * shrink
    for i, key in enumerate(keys):
        weights = jnp.exp2(scores[i, start : start + height] - top)
        sums = fold(weights, jnp.add, sums)
        part = jnp.dot(weights.astype(BF16), key, preferred_element_type=F32)
        added = part if added is None else added + part
    return top, sums, added


def fuse_kernel(scale, query_ref, key_ref, value_ref, out_ref, score_ref, mix_ref):
    score_ref[...] = (nt_dot(query_ref[...], key_ref[...]) * scale).astype(BF16)
    mix_ref[...] = jnp.dot(
        value_ref[...], out_ref[...], preferred_element_type=F32
    ).astype(BF16)


def lead(rows, score_weight):
    return jnp.dot(rows, score_weight[...], preferred_element_type=F32).astype(BF16)


def early_kernel(counts, score_ref, *refs):
    blocks = grouped(refs, counts)
    own_query_ref, peak_ref, sums_ref, added_ref, scores = refs[-5:]
    keys = [whole(parts) for parts in blocks]
    queries = lead(keys[0], score_ref)
    own_query_ref[...] = queries
    peak, sums, added = attend(queries, keys, scores, 0, None, None, None)
    peak_ref[...] = jnp.broadcast_to(peak, peak_ref.shape)
    sums_ref[...] = sums
    added_ref[...] = added


def late_kernel(
    width,
    sources,
    counts,
    early,
    own_query_ref,
    peak_ref,
    sums_ref,
    added_ref,
    resid_ref,
    gain_ref,
    score_ref,
    mix_weight_ref,
    *refs,
):
    blocks = grouped(refs, counts)
    mid_ref, swap_ref, scores, mid, halo, sizes = refs[sum(counts) :]
    place = lax.axis_index("rows")
    core = place % 2
    chip = place // 2
    own, channels = own_query_ref.shape
    chips = len(sources[0])

    for block, origin in zip(blocks, sources):
        for step, part, low in ((-1, block[-1], 0), (1, block[0], width)):
            rows = part.shape[0] - EXTRA
            first = rows - width if step < 0 else 0
            takers = [k for k in range(chips) if origin[k] == k + step]
            if not takers:
                continue
            wanted = chip == takers[0]
            for k in takers[1:]:
                wanted = jnp.logical_or(wanted, chip == k)

            @pl.when(wanted)
            def _(part=part, rows=rows, first=first, low=low):
                halo[low : low + width] = part[first : first + width, :]
                sizes[low // width] = part[rows : rows + EXTRA, : 2 * width]

    no_above = chip == 0
    no_below = chip == chips - 1

    @pl.when(no_above)
    def _():
        halo[:width] = jnp.zeros((width, channels), BF16)
        sizes[0] = jnp.zeros((EXTRA, 2 * width), BF16)

    @pl.when(no_below)
    def _():
        halo[width:] = jnp.zeros((width, channels), BF16)
        sizes[1] = jnp.zeros((EXTRA, 2 * width), BF16)

    def column(index):
        parts = sizes[index].astype(F32)
        line = parts[0:1] + parts[1:2]
        return jnp.transpose(jnp.broadcast_to(line, (128, 2 * width)))[:, :1]

    edge_rows = halo[...]
    edge_size = jnp.concatenate([column(0)[width:], column(1)[:width]], axis=0)
    edge_resid = edge_rows.astype(F32) * edge_size / gain_ref[...].reshape(1, channels)
    edge_query = lead(edge_rows, score_ref)
    keys = [whole(parts) for parts in blocks]
    _, edge_sums, edge_added = attend(edge_query, keys, scores, own, None, None, None)
    _, own_sums, own_added = attend(
        own_query_ref[...],
        keys[early:],
        scores,
        0,
        peak_ref[:, :1],
        sums_ref[...],
        added_ref[...],
    )

    def finish(added, sums):
        return (added / jnp.sum(sums, axis=-1, keepdims=True)).astype(BF16)

    mixed = jnp.concatenate([finish(own_added, own_sums), finish(edge_added, edge_sums)], axis=0)
    projected = jnp.dot(mixed, mix_weight_ref[...], preferred_element_type=F32)
    inner = own + width
    mid[width:inner] = (resid_ref[...] + projected[:own]).astype(BF16)
    edges = edge_resid + projected[own:]
    mid[:width] = jnp.where(no_above, 0.0, edges[:width]).astype(BF16)
    mid[inner:] = jnp.where(no_below, 0.0, edges[width:]).astype(BF16)
    mid_ref[...] = mid[pl.ds(pl.multiple_of(2 * core * width, width), 4 * width), :]
    swap_ref[...] = mid[pl.ds(pl.multiple_of(2 * (1 - core) * width, width), 4 * width), :]


def up_kernel(width, mid_ref, swap_ref, weight_ref, out_ref, fine, total, results, sems):
    core = lax.axis_index("rows") % 2
    channels = mid_ref.shape[1]
    outputs = weight_ref.shape[2]
    wide = 2 * width
    lane = lax.broadcasted_iota(jnp.int32, (1, wide), 1)
    lhs = weight_ref[...].reshape(9 * outputs, channels)
    stores = []
    for slot, ref, frame in ((0, mid_ref, core), (1, swap_ref, 1 - core)):
        values = ref[...].astype(F32)
        pieces = []
        for i in range(channels // 128):
            piece = values[:, 128 * i : 128 * (i + 1)]
            fine[slot, i, pl.ds(0, 4 * width, stride=2), :] = piece
            fine[slot, i, pl.ds(1, 4 * width, stride=2), :] = piece
            pieces.append(fine[slot, i].astype(BF16))
        total[slot] = nt_dot(lhs, jnp.concatenate(pieces, axis=1))
        for row in range(4):
            low = row // 2 + 1
            picks = (low - 1, low, low) if row % 2 == 0 else (low, low, low + 1)
            taps = []
            for col in range(3):
                tap = None
                for j, pick in enumerate(picks):
                    piece = total[
                        slot,
                        (3 * j + col) * outputs : (3 * j + col + 1) * outputs,
                        pick * wide : (pick + 1) * wide,
                    ]
                    tap = piece if tap is None else tap + piece
                taps.append(tap)
            result = taps[1]
            result = result + jnp.where(lane == 0, 0.0, pltpu.roll(taps[0], 1, axis=1))
            result = result + jnp.where(
                lane == wide - 1, 0.0, pltpu.roll(taps[2], wide - 1, axis=1)
            )
            results[slot, row] = result.astype(BF16)
        stores = stores + start_all([(results.at[slot], out_ref.at[frame])], sems, slot)
    wait_all(stores)


def gather_blocks(block, halves, count):
    chips = count // 2
    depth = 2 if chips % 2 == 0 else 1
    length = chips // depth

    ring = [0] + list(range(1, length, 2)) + list(range(2, length, 2))[::-1]
    follow = {a: ring[(i + 1) % length] for i, a in enumerate(ring)}
    onward = {a * depth + b: follow[a] * depth + b for a in range(length) for b in range(depth)}
    backward = {target: source for source, target in onward.items()}
    across = {k: k ^ 1 for k in range(chips)}

    def send(parts, targets):
        pairs = [(2 * k + c, 2 * targets[k] + c) for k in range(chips) for c in range(2)]
        return [lax.ppermute(part, "rows", pairs) for part in parts]

    def moved(origin, targets):
        return {targets[k]: origin[k] for k in range(chips)}

    here = {k: k for k in range(chips)}
    early, late = [([block], here)], []
    back = crossed = far = None
    if length > 1:
        back = send([block], backward)
        early.append((back, moved(here, backward)))
    if depth == 2:
        crossed = send([block], across)
        (early if length > 1 else late).append((crossed, moved(here, across)))
    ties = {}
    if depth == 2:
        ties[(1, 1)] = [(crossed, 0)]
    if length > 1:
        ties[(2, 0)] = [(back, 0)]
    parts, origin, last = list(halves), here, None
    for step in range(1, length - 1):
        parts, origin = send(parts, onward), moved(origin, onward)
        for h in range(2):
            tied = [(parts, h)] + ([(last, h)] if last else []) + ties.get((step, h), [])
            fixed = lax.optimization_barrier(tuple(where[i] for where, i in tied))
            for (where, i), value in zip(tied, fixed):
                where[i] = value
        early.append((parts, origin))
        if depth == 2:
            last = send(parts, across)
            (late if step == length - 2 else early).append((last, moved(origin, across)))
    if depth == 2 and length > 1:
        far = send(crossed, backward)
        late.append((far, moved(moved(here, across), backward)))
    return early, late


def shards(
    latents,
    conv_cache,
    norm_gain,
    conv_weight,
    attn_gain,
    query_weight,
    key_weight,
    value_weight,
    out_weight,
    up_weight,
):
    frames, rows_here, width, channels = latents.shape
    outputs = up_weight.shape[3]
    count = lax.axis_size("rows")
    span = 2 * rows_here * width
    own = rows_here * width
    edge = jax.ShapeDtypeStruct((width, channels), BF16)
    anywhere = pl.BlockSpec(memory_space=pl.ANY)
    hbm = pl.BlockSpec(memory_space=pltpu.HBM)

    chips = count // 2
    swap = [(2 * k + c, 2 * k + 1 - c) for k in range(chips) for c in range(2)]
    neighbour = [(2 * k + 1, 2 * k + 2) for k in range(chips - 1)]
    neighbour = neighbour + [(target, source) for source, target in neighbour]

    latents_in = pltpu.with_memory_space_constraint(latents, pltpu.HBM)
    cache_in = pltpu.with_memory_space_constraint(conv_cache, pltpu.HBM)
    edge_rows, both = pl.pallas_call(
        edges_kernel,
        out_shape=(
            jax.ShapeDtypeStruct((2 * frames, width, channels), BF16),
            jax.ShapeDtypeStruct((3, rows_here, width, channels), BF16),
        ),
        in_specs=[hbm] * 2,
        out_specs=(anywhere,) * 2,
        scratch_shapes=[pltpu.SemaphoreType.DMA((5,))],
        cost_estimate=cost(0, 20 * width * channels),
        compiler_params=params(4),
    )(latents_in, cache_in)
    edge_rows = lax.ppermute(edge_rows, "rows", neighbour)
    both = lax.ppermute(both, "rows", swap)
    act, own_rows, staged = pl.pallas_call(
        prepare_kernel,
        out_shape=(
            jax.ShapeDtypeStruct((frames, own, channels), BF16),
            jax.ShapeDtypeStruct((3, own, channels), BF16),
            jax.ShapeDtypeStruct((3, 3, channels, 3 * channels), BF16),
        ),
        in_specs=[hbm] * 4,
        out_specs=(anywhere, vmem(), anywhere),
        scratch_shapes=[
            pltpu.VMEM((frames, own, channels), BF16),
            pltpu.VMEM((frames, own, channels), BF16),
            pltpu.VMEM((channels,), F32),
            pltpu.VMEM((frames, own, channels), BF16),
            pltpu.SemaphoreType.DMA((13,)),
        ],
        cost_estimate=cost(10 * frames * own * channels, 2 * 27 * channels * channels),
        compiler_params=params(8),
    )(
        pltpu.with_memory_space_constraint(latents.reshape(frames, own, channels), pltpu.HBM),
        pltpu.with_memory_space_constraint(conv_cache.reshape(frames, own, channels), pltpu.HBM),
        pltpu.with_memory_space_constraint(conv_weight, pltpu.HBM),
        pltpu.with_memory_space_constraint(norm_gain, pltpu.HBM),
    )

    edge_rows, own_rows = lax.optimization_barrier((edge_rows, own_rows))
    far_rows = lax.ppermute(edge_rows, "rows", swap)
    block = jax.ShapeDtypeStruct((span + EXTRA, channels), BF16)
    half = jax.ShapeDtypeStruct((span // 2 + EXTRA, channels), BF16)
    sent, front, back, resid = pl.pallas_call(
        functools.partial(conv_kernel, width),
        out_shape=(block, half, half, jax.ShapeDtypeStruct((span, channels), F32)),
        in_specs=[vmem()] * 7,
        out_specs=(vmem(),) * 4,
        scratch_shapes=[
            pltpu.VMEM((3, 6 * width, channels), BF16),
            pltpu.VMEM((6 * width, channels), BF16),
            pltpu.VMEM((6 * width, channels), BF16),
            pltpu.VMEM((span, 3 * channels), F32),
        ],
        cost_estimate=cost(2 * 27 * span * channels * channels, 2 * 27 * channels * channels),
        compiler_params=params(20),
    )(
        own_rows,
        both.reshape(3, own, channels),
        edge_rows,
        far_rows,
        norm_gain,
        attn_gain,
        staged,
    )

    early, late = gather_blocks(sent, (front, back), count)
    blocks = early + late
    sources = [[origin[k] for k in range(chips)] for _, origin in blocks]
    counts = [len(parts) for parts, _ in blocks]
    early_parts = [part for parts, _ in early for part in parts]
    all_parts = [part for parts, _ in blocks for part in parts]

    scale = channels ** (-0.5) * 1.4426950408889634
    square = jax.ShapeDtypeStruct((channels, channels), BF16)
    score_weight, mix_weight = pl.pallas_call(
        functools.partial(fuse_kernel, scale),
        out_shape=(square, square),
        in_specs=[vmem()] * 4,
        out_specs=(vmem(),) * 2,
        cost_estimate=cost(4 * channels**3, 12 * channels * channels),
        compiler_params=params(8),
    )(query_weight, key_weight, value_weight, out_weight)

    wide = span + 2 * width
    lanes = jax.ShapeDtypeStruct((span, 128), F32)
    own_query, peak, sums, added = pl.pallas_call(
        functools.partial(early_kernel, counts[: len(early)]),
        out_shape=(
            jax.ShapeDtypeStruct((span, channels), BF16),
            lanes,
            lanes,
            jax.ShapeDtypeStruct((span, channels), F32),
        ),
        in_specs=[vmem()] * (1 + len(early_parts)),
        out_specs=(vmem(),) * 4,
        scratch_shapes=[pltpu.VMEM((len(early), span, span), F32)],
        cost_estimate=cost(
            4 * span * span * len(early) * channels,
            2 * span * channels * len(early),
            span * span * len(early),
        ),
        compiler_params=params(24),
    )(score_weight, *early_parts)

    mid, swap_rows = pl.pallas_call(
        functools.partial(late_kernel, width, sources, counts, len(early)),
        out_shape=(jax.ShapeDtypeStruct((4 * width, channels), BF16),) * 2,
        in_specs=[vmem()] * (8 + len(all_parts)),
        out_specs=(vmem(),) * 2,
        scratch_shapes=[
            pltpu.VMEM((len(blocks), wide, span), F32),
            pltpu.VMEM((wide, channels), BF16),
            pltpu.VMEM((2 * width, channels), BF16),
            pltpu.VMEM((2, EXTRA, 2 * width), BF16),
        ],
        cost_estimate=cost(
            2 * wide * span * len(blocks) * channels,
            2 * span * channels * len(blocks),
            wide * span * len(blocks) // 2,
        ),
        compiler_params=params(28),
    )(
        own_query,
        peak,
        sums,
        added,
        resid,
        attn_gain,
        score_weight,
        mix_weight,
        *all_parts,
    )

    swap_rows = lax.ppermute(swap_rows, "rows", swap)

    fine_shape = (2 * rows_here, outputs, 2 * width)
    decoded = pl.pallas_call(
        functools.partial(up_kernel, width),
        out_shape=jax.ShapeDtypeStruct((frames, *fine_shape), BF16),
        in_specs=[vmem()] * 3,
        out_specs=anywhere,
        scratch_shapes=[
            pltpu.VMEM((2, channels // 128, 8 * width, 128), F32),
            pltpu.VMEM((2, 9 * outputs, 8 * width), F32),
            pltpu.VMEM((2, *fine_shape), BF16),
            pltpu.SemaphoreType.DMA((2,)),
        ],
        cost_estimate=cost(
            2 * 9 * outputs * channels * 16 * width, 2 * 9 * outputs * channels
        ),
        compiler_params=params(24),
    )(mid, swap_rows, jnp.transpose(up_weight, (0, 1, 3, 2)))
    decoded = jnp.transpose(decoded, (0, 1, 3, 2))
    return (decoded, act.reshape(frames, rows_here, width, channels))


def solution(mesh):
    return jax.shard_map(
        shards,
        mesh=mesh,
        in_specs=(
            P("videos", "rows", None, None),
            P("videos", "rows", None, None),
            P(),
            P(),
            P(),
            P(),
            P(),
            P(),
            P(),
            P(),
        ),
        out_specs=(P("videos", "rows", None, None), P("videos", "rows", None, None)),
        check_vma=False,
    )
```

```python
import functools

import jax
import jax.numpy as jnp
from jax import lax
from jax.experimental import pallas as pl
from jax.experimental.pallas import tpu as pltpu
from jax.sharding import PartitionSpec as P

BF16 = jnp.bfloat16
F32 = jnp.float32
EPS = 1e-06
MIB = 1024 * 1024
EXTRA = 16


def normalize(values, gain):
    return values * lax.rsqrt(jnp.mean(values * values, axis=-1, keepdims=True) + EPS) * gain


def activate(values, gain):
    normed = normalize(values.astype(F32), gain)
    return (normed / (1.0 + jnp.exp(-normed))).astype(BF16)


def vmem():
    return pl.BlockSpec(memory_space=pltpu.VMEM)


def params(mib):
    return pltpu.CompilerParams(vmem_limit_bytes=mib * MIB)


def cost(flops, size, exps=0):
    return pl.CostEstimate(flops=flops, bytes_accessed=size, transcendentals=exps)


def edges_kernel(latents_ref, cache_ref, edge_ref, both_ref, sems):
    core = lax.axis_index("rows") % 2
    row = core * (latents_ref.shape[1] - 1)
    copies = [
        pltpu.make_async_copy(cache_ref.at[:, row], edge_ref.at[pl.ds(0, 2)], sems.at[0]),
        pltpu.make_async_copy(latents_ref.at[:, row], edge_ref.at[pl.ds(2, 2)], sems.at[1]),
        pltpu.make_async_copy(cache_ref.at[1], both_ref.at[core], sems.at[2]),
        pltpu.make_async_copy(latents_ref.at[0], both_ref.at[1 + core], sems.at[3]),
    ]
    for copy in copies:
        copy.start()

    @pl.when(core == 0)
    def _():
        last = pltpu.make_async_copy(latents_ref.at[1], both_ref.at[2], sems.at[4])
        last.start()
        last.wait()

    @pl.when(core == 1)
    def _():
        last = pltpu.make_async_copy(cache_ref.at[0], both_ref.at[0], sems.at[4])
        last.start()
        last.wait()

    for copy in copies:
        copy.wait()


def start_all(pairs, sems, first=0):
    copies = [
        pltpu.make_async_copy(source, target, sems.at[first + i])
        for i, (source, target) in enumerate(pairs)
    ]
    for copy in copies:
        copy.start()
    return copies


def wait_all(copies):
    for copy in copies:
        copy.wait()


def prepare_kernel(
    latents_ref,
    cache_ref,
    weight_ref,
    gain_ref,
    act_ref,
    own_ref,
    staged_ref,
    latents,
    cache,
    gain,
    act,
    sems,
):
    channels = latents_ref.shape[-1]
    core = lax.axis_index("rows") % 2
    loads = start_all([(latents_ref, latents), (cache_ref, cache), (gain_ref, gain)], sems)
    stages = start_all(
        [
            (
                weight_ref.at[time, :, col],
                staged_ref.at[time, :, :, pl.ds(col * channels, channels)],
            )
            for time in range(3)
            for col in range(3)
        ],
        sems,
        4,
    )
    wait_all(loads)
    act[...] = activate(latents[...], gain[...].reshape(1, channels))
    store = start_all([(act, act_ref)], sems, 3)
    own_ref[0] = cache[core]
    own_ref[1] = jnp.where(core == 0, cache[1], latents[0])
    own_ref[2] = latents[core]
    wait_all(store + stages)


def conv_kernel(
    width,
    own_ref,
    swap_ref,
    edge_ref,
    far_ref,
    norm_gain_ref,
    attn_gain_ref,
    weights,
    sent_ref,
    front_ref,
    back_ref,
    resid_ref,
    raw,
    second,
    third,
    total,
):
    channels = own_ref.shape[-1]
    core = lax.axis_index("rows") % 2
    own = 2 * width
    span = 4 * width
    gain = norm_gain_ref[...].reshape(1, channels)

    def put(index, values):
        rows = pl.ds(pl.multiple_of(index * width, width), values.shape[1])
        raw[:, rows, :] = values

    put(1 + 2 * core, own_ref[...])
    put(3 - 2 * core, swap_ref[...])
    put(5 * core, edge_ref[pl.ds(core, 3)])
    put(5 * (1 - core), far_ref[pl.ds(core, 3)])

    def taps(ref, time):
        lhs = jnp.concatenate([ref[row * width : row * width + span] for row in range(3)], axis=1)
        rhs = weights[time].reshape(3 * channels, 3 * channels)
        return jnp.dot(lhs, rhs, preferred_element_type=F32)

    total[...] = taps(raw.at[0], 0)
    second[...] = jnp.where(core == 1, activate(raw[1], gain), raw[1])
    third[...] = activate(raw[2], gain)
    total[...] += taps(second, 1)
    total[...] += taps(third, 2)

    column = lax.broadcasted_iota(jnp.int32, (span, 1), 0) % width
    left = pltpu.roll(total[:, :channels], 1, axis=0)
    right = pltpu.roll(total[:, 2 * channels :], span - 1, axis=0)
    conv_out = total[:, channels : 2 * channels]
    conv_out = conv_out + jnp.where(column == 0, 0.0, left)
    conv_out = conv_out + jnp.where(column == width - 1, 0.0, right)
    resid = raw[2, width : width + span].astype(F32) + conv_out
    resid_ref[...] = resid
    size = jnp.mean(resid * resid, axis=-1, keepdims=True) + EPS
    normed = resid * lax.rsqrt(size) * attn_gain_ref[...].reshape(1, channels)
    edges = jnp.sqrt(jnp.concatenate([size[:width], size[span - width :]], axis=0))
    across = jnp.transpose(jnp.broadcast_to(edges, (2 * width, 128)))[:EXTRA]
    high = across.astype(BF16).astype(F32)
    line = lax.broadcasted_iota(jnp.int32, (EXTRA, 1), 0)
    extra = jnp.where(line == 0, high, jnp.where(line == 1, across - high, 0.0)).astype(BF16)
    half = span // 2
    for ref, low, count in ((sent_ref, 0, span), (front_ref, 0, half), (back_ref, half, half)):
        ref[:count] = normed[low : low + count].astype(BF16)
        ref[count:] = jnp.zeros((EXTRA, channels), BF16)
        ref[count:, : 2 * width] = extra


def nt_dot(a, b):
    return lax.dot_general(a, b, (((1,), (1,)), ((), ())), preferred_element_type=F32)


def whole(parts):
    rows = [part[: part.shape[0] - EXTRA] for part in parts]
    return rows[0] if len(rows) == 1 else jnp.concatenate(rows, axis=0)


def grouped(refs, counts):
    blocks, first = [], 0
    for count in counts:
        blocks.append(refs[first : first + count])
        first += count
    return blocks


def fold(values, combine, total):
    for lane in range(0, values.shape[1], 128):
        piece = values[:, lane : lane + 128]
        total = piece if total is None else combine(total, piece)
    return total


def attend(queries, keys, scores, start, peak, sums, added):
    height = queries.shape[0]
    top = None
    for i, key in enumerate(keys):
        part = nt_dot(queries, key)
        scores[i, start : start + height] = part
        top = fold(part, jnp.maximum, top)
    top = jnp.max(top, axis=-1, keepdims=True)
    if peak is not None:
        top = jnp.maximum(top, peak)
        shrink = jnp.exp2(peak - top)
        sums = sums * shrink
        added = added * shrink
    for i, key in enumerate(keys):
        weights = jnp.exp2(scores[i, start : start + height] - top)
        sums = fold(weights, jnp.add, sums)
        part = jnp.dot(weights.astype(BF16), key, preferred_element_type=F32)
        added = part if added is None else added + part
    return top, sums, added


def fuse_kernel(scale, query_ref, key_ref, value_ref, out_ref, score_ref, mix_ref):
    score_ref[...] = (nt_dot(query_ref[...], key_ref[...]) * scale).astype(BF16)
    mix_ref[...] = jnp.dot(
        value_ref[...], out_ref[...], preferred_element_type=F32
    ).astype(BF16)


def lead(rows, score_weight):
    return jnp.dot(rows, score_weight[...], preferred_element_type=F32).astype(BF16)


def early_kernel(counts, score_ref, *refs):
    blocks = grouped(refs, counts)
    own_query_ref, peak_ref, sums_ref, added_ref, scores = refs[-5:]
    keys = [whole(parts) for parts in blocks]
    queries = lead(keys[0], score_ref)
    own_query_ref[...] = queries
    peak, sums, added = attend(queries, keys, scores, 0, None, None, None)
    peak_ref[...] = jnp.broadcast_to(peak, peak_ref.shape)
    sums_ref[...] = sums
    added_ref[...] = added


def late_kernel(
    width,
    sources,
    counts,
    early,
    own_query_ref,
    peak_ref,
    sums_ref,
    added_ref,
    resid_ref,
    gain_ref,
    score_ref,
    mix_weight_ref,
    *refs,
):
    blocks = grouped(refs, counts)
    mid_ref, swap_ref, scores, mid, halo, sizes = refs[sum(counts) :]
    place = lax.axis_index("rows")
    core = place % 2
    chip = place // 2
    own, channels = own_query_ref.shape
    chips = len(sources[0])

    for block, origin in zip(blocks, sources):
        for step, part, low in ((-1, block[-1], 0), (1, block[0], width)):
            rows = part.shape[0] - EXTRA
            first = rows - width if step < 0 else 0
            takers = [k for k in range(chips) if origin[k] == k + step]
            if not takers:
                continue
            wanted = chip == takers[0]
            for k in takers[1:]:
                wanted = jnp.logical_or(wanted, chip == k)

            @pl.when(wanted)
            def _(part=part, rows=rows, first=first, low=low):
                halo[low : low + width] = part[first : first + width, :]
                sizes[low // width] = part[rows : rows + EXTRA, : 2 * width]

    no_above = chip == 0
    no_below = chip == chips - 1

    @pl.when(no_above)
    def _():
        halo[:width] = jnp.zeros((width, channels), BF16)
        sizes[0] = jnp.zeros((EXTRA, 2 * width), BF16)

    @pl.when(no_below)
    def _():
        halo[width:] = jnp.zeros((width, channels), BF16)
        sizes[1] = jnp.zeros((EXTRA, 2 * width), BF16)

    def column(index):
        parts = sizes[index].astype(F32)
        line = parts[0:1] + parts[1:2]
        return jnp.transpose(jnp.broadcast_to(line, (128, 2 * width)))[:, :1]

    edge_rows = halo[...]
    edge_size = jnp.concatenate([column(0)[width:], column(1)[:width]], axis=0)
    edge_resid = edge_rows.astype(F32) * edge_size / gain_ref[...].reshape(1, channels)
    edge_query = lead(edge_rows, score_ref)
    keys = [whole(parts) for parts in blocks]
    _, edge_sums, edge_added = attend(edge_query, keys, scores, own, None, None, None)
    _, own_sums, own_added = attend(
        own_query_ref[...],
        keys[early:],
        scores,
        0,
        peak_ref[:, :1],
        sums_ref[...],
        added_ref[...],
    )

    def finish(added, sums):
        return (added / jnp.sum(sums, axis=-1, keepdims=True)).astype(BF16)

    mixed = jnp.concatenate([finish(own_added, own_sums), finish(edge_added, edge_sums)], axis=0)
    projected = jnp.dot(mixed, mix_weight_ref[...], preferred_element_type=F32)
    inner = own + width
    mid[width:inner] = (resid_ref[...] + projected[:own]).astype(BF16)
    edges = edge_resid + projected[own:]
    mid[:width] = jnp.where(no_above, 0.0, edges[:width]).astype(BF16)
    mid[inner:] = jnp.where(no_below, 0.0, edges[width:]).astype(BF16)
    mid_ref[...] = mid[pl.ds(pl.multiple_of(2 * core * width, width), 4 * width), :]
    swap_ref[...] = mid[pl.ds(pl.multiple_of(2 * (1 - core) * width, width), 4 * width), :]


def up_kernel(width, mid_ref, swap_ref, weight_ref, out_ref, fine, total, results, sems):
    core = lax.axis_index("rows") % 2
    channels = mid_ref.shape[1]
    outputs = weight_ref.shape[2]
    wide = 2 * width
    lane = lax.broadcasted_iota(jnp.int32, (1, wide), 1)
    lhs = weight_ref[...].reshape(9 * outputs, channels)
    stores = []
    for slot, ref, frame in ((0, mid_ref, core), (1, swap_ref, 1 - core)):
        values = ref[...].astype(F32)
        pieces = []
        for i in range(channels // 128):
            piece = values[:, 128 * i : 128 * (i + 1)]
            fine[slot, i, pl.ds(0, 4 * width, stride=2), :] = piece
            fine[slot, i, pl.ds(1, 4 * width, stride=2), :] = piece
            pieces.append(fine[slot, i].astype(BF16))
        total[slot] = nt_dot(lhs, jnp.concatenate(pieces, axis=1))
        for row in range(4):
            low = row // 2 + 1
            picks = (low - 1, low, low) if row % 2 == 0 else (low, low, low + 1)
            taps = []
            for col in range(3):
                tap = None
                for j, pick in enumerate(picks):
                    piece = total[
                        slot,
                        (3 * j + col) * outputs : (3 * j + col + 1) * outputs,
                        pick * wide : (pick + 1) * wide,
                    ]
                    tap = piece if tap is None else tap + piece
                taps.append(tap)
            result = taps[1]
            result = result + jnp.where(lane == 0, 0.0, pltpu.roll(taps[0], 1, axis=1))
            result = result + jnp.where(
                lane == wide - 1, 0.0, pltpu.roll(taps[2], wide - 1, axis=1)
            )
            results[slot, row] = result.astype(BF16)
        stores = stores + start_all([(results.at[slot], out_ref.at[frame])], sems, slot)
    wait_all(stores)


def gather_blocks(block, halves, count):
    chips = count // 2
    depth = 2 if chips % 2 == 0 else 1
    length = chips // depth

    ring = [0] + list(range(1, length, 2)) + list(range(2, length, 2))[::-1]
    follow = {a: ring[(i + 1) % length] for i, a in enumerate(ring)}
    onward = {a * depth + b: follow[a] * depth + b for a in range(length) for b in range(depth)}
    backward = {target: source for source, target in onward.items()}
    across = {k: k ^ 1 for k in range(chips)}

    def send(parts, targets):
        pairs = [(2 * k + c, 2 * targets[k] + c) for k in range(chips) for c in range(2)]
        return [lax.ppermute(part, "rows", pairs) for part in parts]

    def moved(origin, targets):
        return {targets[k]: origin[k] for k in range(chips)}

    def tie(*places):
        fixed = lax.optimization_barrier(tuple(where[i] for where, i in places))
        for (where, i), value in zip(places, fixed):
            where[i] = value

    here = {k: k for k in range(chips)}
    early, late = [([block], here)], []
    own_again = [block]
    crossed = last = None
    if depth == 2:
        crossed = send([block], across)
    steps = length - 2
    parts, origin = list(halves), here
    for step in range(1, steps + 1):
        parts, origin = send(parts, onward), moved(origin, onward)
        for h in range(2):
            places = [(parts, h)]
            if last:
                places.append((last, h))
            if step == 1 and h == 1:
                places.append((own_again, 0))
                if depth == 2:
                    places.append((crossed, 0))
            tie(*places)
        early.append((parts, origin))
        if depth == 2:
            last = send(parts, across)
            (late if step == steps else early).append((last, moved(origin, across)))
    if length > 1:
        late.append((send(own_again, backward), moved(here, backward)))
    if depth == 2:
        (early if length > 1 else late).append((crossed, moved(here, across)))
        if length > 1:
            if steps > 0:
                crossed = list(crossed)
                tie((crossed, 0), (parts, 0))
            late.append((send(crossed, backward), moved(moved(here, across), backward)))
    return early, late


def shards(
    latents,
    conv_cache,
    norm_gain,
    conv_weight,
    attn_gain,
    query_weight,
    key_weight,
    value_weight,
    out_weight,
    up_weight,
):
    frames, rows_here, width, channels = latents.shape
    outputs = up_weight.shape[3]
    count = lax.axis_size("rows")
    span = 2 * rows_here * width
    own = rows_here * width
    edge = jax.ShapeDtypeStruct((width, channels), BF16)
    anywhere = pl.BlockSpec(memory_space=pl.ANY)
    hbm = pl.BlockSpec(memory_space=pltpu.HBM)

    chips = count // 2
    swap = [(2 * k + c, 2 * k + 1 - c) for k in range(chips) for c in range(2)]
    neighbour = [(2 * k + 1, 2 * k + 2) for k in range(chips - 1)]
    neighbour = neighbour + [(target, source) for source, target in neighbour]

    latents_in = pltpu.with_memory_space_constraint(latents, pltpu.HBM)
    cache_in = pltpu.with_memory_space_constraint(conv_cache, pltpu.HBM)
    edge_rows, both = pl.pallas_call(
        edges_kernel,
        out_shape=(
            jax.ShapeDtypeStruct((2 * frames, width, channels), BF16),
            jax.ShapeDtypeStruct((3, rows_here, width, channels), BF16),
        ),
        in_specs=[hbm] * 2,
        out_specs=(anywhere,) * 2,
        scratch_shapes=[pltpu.SemaphoreType.DMA((5,))],
        cost_estimate=cost(0, 20 * width * channels),
        compiler_params=params(4),
    )(latents_in, cache_in)
    edge_rows = lax.ppermute(edge_rows, "rows", neighbour)
    both = lax.ppermute(both, "rows", swap)
    act, own_rows, staged = pl.pallas_call(
        prepare_kernel,
        out_shape=(
            jax.ShapeDtypeStruct((frames, own, channels), BF16),
            jax.ShapeDtypeStruct((3, own, channels), BF16),
            jax.ShapeDtypeStruct((3, 3, channels, 3 * channels), BF16),
        ),
        in_specs=[hbm] * 4,
        out_specs=(anywhere, vmem(), anywhere),
        scratch_shapes=[
            pltpu.VMEM((frames, own, channels), BF16),
            pltpu.VMEM((frames, own, channels), BF16),
            pltpu.VMEM((channels,), F32),
            pltpu.VMEM((frames, own, channels), BF16),
            pltpu.SemaphoreType.DMA((13,)),
        ],
        cost_estimate=cost(10 * frames * own * channels, 2 * 27 * channels * channels),
        compiler_params=params(8),
    )(
        pltpu.with_memory_space_constraint(latents.reshape(frames, own, channels), pltpu.HBM),
        pltpu.with_memory_space_constraint(conv_cache.reshape(frames, own, channels), pltpu.HBM),
        pltpu.with_memory_space_constraint(conv_weight, pltpu.HBM),
        pltpu.with_memory_space_constraint(norm_gain, pltpu.HBM),
    )

    edge_rows, own_rows = lax.optimization_barrier((edge_rows, own_rows))
    far_rows = lax.ppermute(edge_rows, "rows", swap)
    block = jax.ShapeDtypeStruct((span + EXTRA, channels), BF16)
    half = jax.ShapeDtypeStruct((span // 2 + EXTRA, channels), BF16)
    sent, front, back, resid = pl.pallas_call(
        functools.partial(conv_kernel, width),
        out_shape=(block, half, half, jax.ShapeDtypeStruct((span, channels), F32)),
        in_specs=[vmem()] * 7,
        out_specs=(vmem(),) * 4,
        scratch_shapes=[
            pltpu.VMEM((3, 6 * width, channels), BF16),
            pltpu.VMEM((6 * width, channels), BF16),
            pltpu.VMEM((6 * width, channels), BF16),
            pltpu.VMEM((span, 3 * channels), F32),
        ],
        cost_estimate=cost(2 * 27 * span * channels * channels, 2 * 27 * channels * channels),
        compiler_params=params(20),
    )(
        own_rows,
        both.reshape(3, own, channels),
        edge_rows,
        far_rows,
        norm_gain,
        attn_gain,
        staged,
    )

    early, late = gather_blocks(sent, (front, back), count)
    blocks = early + late
    sources = [[origin[k] for k in range(chips)] for _, origin in blocks]
    counts = [len(parts) for parts, _ in blocks]
    early_parts = [part for parts, _ in early for part in parts]
    all_parts = [part for parts, _ in blocks for part in parts]

    scale = channels ** (-0.5) * 1.4426950408889634
    square = jax.ShapeDtypeStruct((channels, channels), BF16)
    score_weight, mix_weight = pl.pallas_call(
        functools.partial(fuse_kernel, scale),
        out_shape=(square, square),
        in_specs=[vmem()] * 4,
        out_specs=(vmem(),) * 2,
        cost_estimate=cost(4 * channels**3, 12 * channels * channels),
        compiler_params=params(8),
    )(query_weight, key_weight, value_weight, out_weight)

    wide = span + 2 * width
    lanes = jax.ShapeDtypeStruct((span, 128), F32)
    own_query, peak, sums, added = pl.pallas_call(
        functools.partial(early_kernel, counts[: len(early)]),
        out_shape=(
            jax.ShapeDtypeStruct((span, channels), BF16),
            lanes,
            lanes,
            jax.ShapeDtypeStruct((span, channels), F32),
        ),
        in_specs=[vmem()] * (1 + len(early_parts)),
        out_specs=(vmem(),) * 4,
        scratch_shapes=[pltpu.VMEM((len(early), span, span), F32)],
        cost_estimate=cost(
            4 * span * span * len(early) * channels,
            2 * span * channels * len(early),
            span * span * len(early),
        ),
        compiler_params=params(24),
    )(score_weight, *early_parts)

    mid, swap_rows = pl.pallas_call(
        functools.partial(late_kernel, width, sources, counts, len(early)),
        out_shape=(jax.ShapeDtypeStruct((4 * width, channels), BF16),) * 2,
        in_specs=[vmem()] * (8 + len(all_parts)),
        out_specs=(vmem(),) * 2,
        scratch_shapes=[
            pltpu.VMEM((len(blocks), wide, span), F32),
            pltpu.VMEM((wide, channels), BF16),
            pltpu.VMEM((2 * width, channels), BF16),
            pltpu.VMEM((2, EXTRA, 2 * width), BF16),
        ],
        cost_estimate=cost(
            2 * wide * span * len(blocks) * channels,
            2 * span * channels * len(blocks),
            wide * span * len(blocks) // 2,
        ),
        compiler_params=params(28),
    )(
        own_query,
        peak,
        sums,
        added,
        resid,
        attn_gain,
        score_weight,
        mix_weight,
        *all_parts,
    )

    swap_rows = lax.ppermute(swap_rows, "rows", swap)

    fine_shape = (2 * rows_here, outputs, 2 * width)
    decoded = pl.pallas_call(
        functools.partial(up_kernel, width),
        out_shape=jax.ShapeDtypeStruct((frames, *fine_shape), BF16),
        in_specs=[vmem()] * 3,
        out_specs=anywhere,
        scratch_shapes=[
            pltpu.VMEM((2, channels // 128, 8 * width, 128), F32),
            pltpu.VMEM((2, 9 * outputs, 8 * width), F32),
            pltpu.VMEM((2, *fine_shape), BF16),
            pltpu.SemaphoreType.DMA((2,)),
        ],
        cost_estimate=cost(
            2 * 9 * outputs * channels * 16 * width, 2 * 9 * outputs * channels
        ),
        compiler_params=params(24),
    )(mid, swap_rows, jnp.transpose(up_weight, (0, 1, 3, 2)))
    decoded = jnp.transpose(decoded, (0, 1, 3, 2))
    return (decoded, act.reshape(frames, rows_here, width, channels))


def solution(mesh):
    return jax.shard_map(
        shards,
        mesh=mesh,
        in_specs=(
            P("videos", "rows", None, None),
            P("videos", "rows", None, None),
            P(),
            P(),
            P(),
            P(),
            P(),
            P(),
            P(),
            P(),
        ),
        out_specs=(P("videos", "rows", None, None), P("videos", "rows", None, None)),
        check_vma=False,
    )
```

```python
import functools

import jax
import jax.numpy as jnp
from jax import lax
from jax.experimental import pallas as pl
from jax.experimental.pallas import tpu as pltpu
from jax.sharding import PartitionSpec as P

BF16 = jnp.bfloat16
F32 = jnp.float32
EPS = 1e-06
MIB = 1024 * 1024
EXTRA = 16


def normalize(values, gain):
    return values * lax.rsqrt(jnp.mean(values * values, axis=-1, keepdims=True) + EPS) * gain


def activate(values, gain):
    normed = normalize(values.astype(F32), gain)
    return (normed / (1.0 + jnp.exp(-normed))).astype(BF16)


def vmem():
    return pl.BlockSpec(memory_space=pltpu.VMEM)


def params(mib):
    return pltpu.CompilerParams(vmem_limit_bytes=mib * MIB)


def cost(flops, size, exps=0):
    return pl.CostEstimate(flops=flops, bytes_accessed=size, transcendentals=exps)


def edges_kernel(latents_ref, cache_ref, edge_ref, both_ref, sems):
    core = lax.axis_index("rows") % 2
    row = core * (latents_ref.shape[1] - 1)
    copies = [
        pltpu.make_async_copy(cache_ref.at[:, row], edge_ref.at[pl.ds(0, 2)], sems.at[0]),
        pltpu.make_async_copy(latents_ref.at[:, row], edge_ref.at[pl.ds(2, 2)], sems.at[1]),
        pltpu.make_async_copy(cache_ref.at[1], both_ref.at[core], sems.at[2]),
        pltpu.make_async_copy(latents_ref.at[0], both_ref.at[1 + core], sems.at[3]),
    ]
    for copy in copies:
        copy.start()

    @pl.when(core == 0)
    def _():
        last = pltpu.make_async_copy(latents_ref.at[1], both_ref.at[2], sems.at[4])
        last.start()
        last.wait()

    @pl.when(core == 1)
    def _():
        last = pltpu.make_async_copy(cache_ref.at[0], both_ref.at[0], sems.at[4])
        last.start()
        last.wait()

    for copy in copies:
        copy.wait()


def start_all(pairs, sems, first=0):
    copies = [
        pltpu.make_async_copy(source, target, sems.at[first + i])
        for i, (source, target) in enumerate(pairs)
    ]
    for copy in copies:
        copy.start()
    return copies


def wait_all(copies):
    for copy in copies:
        copy.wait()


def prepare_kernel(
    latents_ref,
    cache_ref,
    weight_ref,
    gain_ref,
    act_ref,
    own_ref,
    staged_ref,
    latents,
    cache,
    gain,
    act,
    sems,
):
    channels = latents_ref.shape[-1]
    core = lax.axis_index("rows") % 2
    loads = start_all([(latents_ref, latents), (cache_ref, cache), (gain_ref, gain)], sems)
    stages = start_all(
        [
            (
                weight_ref.at[time, :, col],
                staged_ref.at[time, :, :, pl.ds(col * channels, channels)],
            )
            for time in range(3)
            for col in range(3)
        ],
        sems,
        4,
    )
    wait_all(loads)
    act[...] = activate(latents[...], gain[...].reshape(1, channels))
    store = start_all([(act, act_ref)], sems, 3)
    own_ref[0] = cache[core]
    own_ref[1] = jnp.where(core == 0, cache[1], latents[0])
    own_ref[2] = latents[core]
    wait_all(store + stages)


def conv_kernel(
    width,
    own_ref,
    swap_ref,
    edge_ref,
    far_ref,
    norm_gain_ref,
    attn_gain_ref,
    weights,
    sent_ref,
    front_ref,
    back_ref,
    resid_ref,
    raw,
    second,
    third,
    total,
):
    channels = own_ref.shape[-1]
    core = lax.axis_index("rows") % 2
    own = 2 * width
    span = 4 * width
    gain = norm_gain_ref[...].reshape(1, channels)

    def put(index, values):
        rows = pl.ds(pl.multiple_of(index * width, width), values.shape[1])
        raw[:, rows, :] = values

    put(1 + 2 * core, own_ref[...])
    put(3 - 2 * core, swap_ref[...])
    put(5 * core, edge_ref[pl.ds(core, 3)])
    put(5 * (1 - core), far_ref[pl.ds(core, 3)])

    def taps(ref, time):
        lhs = jnp.concatenate([ref[row * width : row * width + span] for row in range(3)], axis=1)
        rhs = weights[time].reshape(3 * channels, 3 * channels)
        return jnp.dot(lhs, rhs, preferred_element_type=F32)

    total[...] = taps(raw.at[0], 0)
    second[...] = jnp.where(core == 1, activate(raw[1], gain), raw[1])
    third[...] = activate(raw[2], gain)
    total[...] += taps(second, 1)
    total[...] += taps(third, 2)

    column = lax.broadcasted_iota(jnp.int32, (span, 1), 0) % width
    left = pltpu.roll(total[:, :channels], 1, axis=0)
    right = pltpu.roll(total[:, 2 * channels :], span - 1, axis=0)
    conv_out = total[:, channels : 2 * channels]
    conv_out = conv_out + jnp.where(column == 0, 0.0, left)
    conv_out = conv_out + jnp.where(column == width - 1, 0.0, right)
    resid = raw[2, width : width + span].astype(F32) + conv_out
    resid_ref[...] = resid
    size = jnp.mean(resid * resid, axis=-1, keepdims=True) + EPS
    normed = resid * lax.rsqrt(size) * attn_gain_ref[...].reshape(1, channels)
    edges = jnp.sqrt(jnp.concatenate([size[:width], size[span - width :]], axis=0))
    across = jnp.transpose(jnp.broadcast_to(edges, (2 * width, 128)))[:EXTRA]
    high = across.astype(BF16).astype(F32)
    line = lax.broadcasted_iota(jnp.int32, (EXTRA, 1), 0)
    extra = jnp.where(line == 0, high, jnp.where(line == 1, across - high, 0.0)).astype(BF16)
    half = span // 2
    for ref, low, count in ((sent_ref, 0, span), (front_ref, 0, half), (back_ref, half, half)):
        ref[:count] = normed[low : low + count].astype(BF16)
        ref[count:] = jnp.zeros((EXTRA, channels), BF16)
        ref[count:, : 2 * width] = extra


def nt_dot(a, b):
    return lax.dot_general(a, b, (((1,), (1,)), ((), ())), preferred_element_type=F32)


def whole(parts):
    rows = [part[: part.shape[0] - EXTRA] for part in parts]
    return rows[0] if len(rows) == 1 else jnp.concatenate(rows, axis=0)


def grouped(refs, counts):
    blocks, first = [], 0
    for count in counts:
        blocks.append(refs[first : first + count])
        first += count
    return blocks


def fold(values, combine, total):
    for lane in range(0, values.shape[1], 128):
        piece = values[:, lane : lane + 128]
        total = piece if total is None else combine(total, piece)
    return total


def attend(queries, keys, scores, start, peak, sums, added):
    height = queries.shape[0]
    top = None
    for i, key in enumerate(keys):
        part = nt_dot(queries, key)
        scores[i, start : start + height] = part
        top = fold(part, jnp.maximum, top)
    top = jnp.max(top, axis=-1, keepdims=True)
    if peak is not None:
        top = jnp.maximum(top, peak)
        shrink = jnp.exp2(peak - top)
        sums = sums * shrink
        added = added * shrink
    for i, key in enumerate(keys):
        weights = jnp.exp2(scores[i, start : start + height] - top)
        sums = fold(weights, jnp.add, sums)
        part = jnp.dot(weights.astype(BF16), key, preferred_element_type=F32)
        added = part if added is None else added + part
    return top, sums, added


def fuse_kernel(scale, query_ref, key_ref, value_ref, out_ref, score_ref, mix_ref):
    score_ref[...] = (nt_dot(query_ref[...], key_ref[...]) * scale).astype(BF16)
    mix_ref[...] = jnp.dot(
        value_ref[...], out_ref[...], preferred_element_type=F32
    ).astype(BF16)


def lead(rows, score_weight):
    return jnp.dot(rows, score_weight[...], preferred_element_type=F32).astype(BF16)


def early_kernel(counts, score_ref, *refs):
    blocks = grouped(refs, counts)
    own_query_ref, peak_ref, sums_ref, added_ref, scores = refs[-5:]
    keys = [whole(parts) for parts in blocks]
    queries = lead(keys[0], score_ref)
    own_query_ref[...] = queries
    peak, sums, added = attend(queries, keys, scores, 0, None, None, None)
    peak_ref[...] = jnp.broadcast_to(peak, peak_ref.shape)
    sums_ref[...] = sums
    added_ref[...] = added


def late_kernel(
    width,
    sources,
    counts,
    early,
    own_query_ref,
    peak_ref,
    sums_ref,
    added_ref,
    resid_ref,
    gain_ref,
    score_ref,
    mix_weight_ref,
    *refs,
):
    blocks = grouped(refs, counts)
    mid_ref, swap_ref, scores, mid, halo, sizes = refs[sum(counts) :]
    place = lax.axis_index("rows")
    core = place % 2
    chip = place // 2
    own, channels = own_query_ref.shape
    chips = len(sources[0])

    for block, origin in zip(blocks, sources):
        for step, part, low in ((-1, block[-1], 0), (1, block[0], width)):
            rows = part.shape[0] - EXTRA
            first = rows - width if step < 0 else 0
            takers = [k for k in range(chips) if origin[k] == k + step]
            if not takers:
                continue
            wanted = chip == takers[0]
            for k in takers[1:]:
                wanted = jnp.logical_or(wanted, chip == k)

            @pl.when(wanted)
            def _(part=part, rows=rows, first=first, low=low):
                halo[low : low + width] = part[first : first + width, :]
                sizes[low // width] = part[rows : rows + EXTRA, : 2 * width]

    no_above = chip == 0
    no_below = chip == chips - 1

    @pl.when(no_above)
    def _():
        halo[:width] = jnp.zeros((width, channels), BF16)
        sizes[0] = jnp.zeros((EXTRA, 2 * width), BF16)

    @pl.when(no_below)
    def _():
        halo[width:] = jnp.zeros((width, channels), BF16)
        sizes[1] = jnp.zeros((EXTRA, 2 * width), BF16)

    def column(index):
        parts = sizes[index].astype(F32)
        line = parts[0:1] + parts[1:2]
        return jnp.transpose(jnp.broadcast_to(line, (128, 2 * width)))[:, :1]

    edge_rows = halo[...]
    edge_size = jnp.concatenate([column(0)[width:], column(1)[:width]], axis=0)
    edge_resid = edge_rows.astype(F32) * edge_size / gain_ref[...].reshape(1, channels)
    edge_query = lead(edge_rows, score_ref)
    keys = [whole(parts) for parts in blocks]
    _, edge_sums, edge_added = attend(edge_query, keys, scores, own, None, None, None)
    _, own_sums, own_added = attend(
        own_query_ref[...],
        keys[early:],
        scores,
        0,
        peak_ref[:, :1],
        sums_ref[...],
        added_ref[...],
    )

    def finish(added, sums):
        return (added / jnp.sum(sums, axis=-1, keepdims=True)).astype(BF16)

    mixed = jnp.concatenate([finish(own_added, own_sums), finish(edge_added, edge_sums)], axis=0)
    projected = jnp.dot(mixed, mix_weight_ref[...], preferred_element_type=F32)
    inner = own + width
    mid[width:inner] = (resid_ref[...] + projected[:own]).astype(BF16)
    edges = edge_resid + projected[own:]
    mid[:width] = jnp.where(no_above, 0.0, edges[:width]).astype(BF16)
    mid[inner:] = jnp.where(no_below, 0.0, edges[width:]).astype(BF16)
    mid_ref[...] = mid[pl.ds(pl.multiple_of(2 * core * width, width), 4 * width), :]
    swap_ref[...] = mid[pl.ds(pl.multiple_of(2 * (1 - core) * width, width), 4 * width), :]


def up_kernel(width, mid_ref, swap_ref, weight_ref, out_ref, fine, total, results, sems):
    core = lax.axis_index("rows") % 2
    channels = mid_ref.shape[1]
    outputs = weight_ref.shape[2]
    wide = 2 * width
    lane = lax.broadcasted_iota(jnp.int32, (1, wide), 1)
    lhs = weight_ref[...].reshape(9 * outputs, channels)
    stores = []
    for slot, ref, frame in ((0, mid_ref, core), (1, swap_ref, 1 - core)):
        values = ref[...].astype(F32)
        pieces = []
        for i in range(channels // 128):
            piece = values[:, 128 * i : 128 * (i + 1)]
            fine[slot, i, pl.ds(0, 4 * width, stride=2), :] = piece
            fine[slot, i, pl.ds(1, 4 * width, stride=2), :] = piece
            pieces.append(fine[slot, i].astype(BF16))
        total[slot] = nt_dot(lhs, jnp.concatenate(pieces, axis=1))
        for row in range(4):
            low = row // 2 + 1
            picks = (low - 1, low, low) if row % 2 == 0 else (low, low, low + 1)
            taps = []
            for col in range(3):
                tap = None
                for j, pick in enumerate(picks):
                    piece = total[
                        slot,
                        (3 * j + col) * outputs : (3 * j + col + 1) * outputs,
                        pick * wide : (pick + 1) * wide,
                    ]
                    tap = piece if tap is None else tap + piece
                taps.append(tap)
            result = taps[1]
            result = result + jnp.where(lane == 0, 0.0, pltpu.roll(taps[0], 1, axis=1))
            result = result + jnp.where(
                lane == wide - 1, 0.0, pltpu.roll(taps[2], wide - 1, axis=1)
            )
            results[slot, row] = result.astype(BF16)
        stores = stores + start_all([(results.at[slot], out_ref.at[frame])], sems, slot)
    wait_all(stores)


def gather_blocks(block, halves, count):
    chips = count // 2
    depth = 2 if chips % 2 == 0 else 1
    length = chips // depth

    ring = [0] + list(range(1, length, 2)) + list(range(2, length, 2))[::-1]
    follow = {a: ring[(i + 1) % length] for i, a in enumerate(ring)}
    onward = {a * depth + b: follow[a] * depth + b for a in range(length) for b in range(depth)}
    backward = {target: source for source, target in onward.items()}
    across = {k: k ^ 1 for k in range(chips)}

    def send(parts, targets):
        pairs = [(2 * k + c, 2 * targets[k] + c) for k in range(chips) for c in range(2)]
        return [lax.ppermute(part, "rows", pairs) for part in parts]

    def moved(origin, targets):
        return {targets[k]: origin[k] for k in range(chips)}

    def tie(*places):
        fixed = lax.optimization_barrier(tuple(where[i] for where, i in places))
        for (where, i), value in zip(places, fixed):
            where[i] = value

    here = {k: k for k in range(chips)}
    early, late = [([block], here)], []
    own_again = [block]
    crossed = last = None
    if depth == 2:
        crossed = send([block], across)
    steps = length - 2
    parts, origin = list(halves), here
    for step in range(1, steps + 1):
        parts, origin = send(parts, onward), moved(origin, onward)
        for h in range(2):
            places = [(parts, h)]
            if last:
                places.append((last, h))
            if step == 1 and h == 1:
                places.append((own_again, 0))
                if depth == 2:
                    places.append((crossed, 0))
            tie(*places)
        early.append((parts, origin))
        if depth == 2:
            last = send(parts, across)
            (late if step == steps else early).append((last, moved(origin, across)))
    if length > 1:
        late.append((send(own_again, backward), moved(here, backward)))
    if depth == 2:
        (early if length > 1 else late).append((crossed, moved(here, across)))
        if length > 1:
            if steps > 0:
                crossed = list(crossed)
                tie((crossed, 0), (parts, 1))
            late.append((send(crossed, backward), moved(moved(here, across), backward)))
    return early, late


def shards(
    latents,
    conv_cache,
    norm_gain,
    conv_weight,
    attn_gain,
    query_weight,
    key_weight,
    value_weight,
    out_weight,
    up_weight,
):
    frames, rows_here, width, channels = latents.shape
    outputs = up_weight.shape[3]
    count = lax.axis_size("rows")
    span = 2 * rows_here * width
    own = rows_here * width
    edge = jax.ShapeDtypeStruct((width, channels), BF16)
    anywhere = pl.BlockSpec(memory_space=pl.ANY)
    hbm = pl.BlockSpec(memory_space=pltpu.HBM)

    chips = count // 2
    swap = [(2 * k + c, 2 * k + 1 - c) for k in range(chips) for c in range(2)]
    neighbour = [(2 * k + 1, 2 * k + 2) for k in range(chips - 1)]
    neighbour = neighbour + [(target, source) for source, target in neighbour]

    latents_in = pltpu.with_memory_space_constraint(latents, pltpu.HBM)
    cache_in = pltpu.with_memory_space_constraint(conv_cache, pltpu.HBM)
    edge_rows, both = pl.pallas_call(
        edges_kernel,
        out_shape=(
            jax.ShapeDtypeStruct((2 * frames, width, channels), BF16),
            jax.ShapeDtypeStruct((3, rows_here, width, channels), BF16),
        ),
        in_specs=[hbm] * 2,
        out_specs=(anywhere,) * 2,
        scratch_shapes=[pltpu.SemaphoreType.DMA((5,))],
        cost_estimate=cost(0, 20 * width * channels),
        compiler_params=params(4),
    )(latents_in, cache_in)
    edge_rows = lax.ppermute(edge_rows, "rows", neighbour)
    both = lax.ppermute(both, "rows", swap)
    act, own_rows, staged = pl.pallas_call(
        prepare_kernel,
        out_shape=(
            jax.ShapeDtypeStruct((frames, own, channels), BF16),
            jax.ShapeDtypeStruct((3, own, channels), BF16),
            jax.ShapeDtypeStruct((3, 3, channels, 3 * channels), BF16),
        ),
        in_specs=[hbm] * 4,
        out_specs=(anywhere, vmem(), anywhere),
        scratch_shapes=[
            pltpu.VMEM((frames, own, channels), BF16),
            pltpu.VMEM((frames, own, channels), BF16),
            pltpu.VMEM((channels,), F32),
            pltpu.VMEM((frames, own, channels), BF16),
            pltpu.SemaphoreType.DMA((13,)),
        ],
        cost_estimate=cost(10 * frames * own * channels, 2 * 27 * channels * channels),
        compiler_params=params(8),
    )(
        pltpu.with_memory_space_constraint(latents.reshape(frames, own, channels), pltpu.HBM),
        pltpu.with_memory_space_constraint(conv_cache.reshape(frames, own, channels), pltpu.HBM),
        pltpu.with_memory_space_constraint(conv_weight, pltpu.HBM),
        pltpu.with_memory_space_constraint(norm_gain, pltpu.HBM),
    )

    edge_rows, own_rows = lax.optimization_barrier((edge_rows, own_rows))
    far_rows = lax.ppermute(edge_rows, "rows", swap)
    block = jax.ShapeDtypeStruct((span + EXTRA, channels), BF16)
    half = jax.ShapeDtypeStruct((span // 2 + EXTRA, channels), BF16)
    sent, front, back, resid = pl.pallas_call(
        functools.partial(conv_kernel, width),
        out_shape=(block, half, half, jax.ShapeDtypeStruct((span, channels), F32)),
        in_specs=[vmem()] * 7,
        out_specs=(vmem(),) * 4,
        scratch_shapes=[
            pltpu.VMEM((3, 6 * width, channels), BF16),
            pltpu.VMEM((6 * width, channels), BF16),
            pltpu.VMEM((6 * width, channels), BF16),
            pltpu.VMEM((span, 3 * channels), F32),
        ],
        cost_estimate=cost(2 * 27 * span * channels * channels, 2 * 27 * channels * channels),
        compiler_params=params(20),
    )(
        own_rows,
        both.reshape(3, own, channels),
        edge_rows,
        far_rows,
        norm_gain,
        attn_gain,
        staged,
    )

    early, late = gather_blocks(sent, (front, back), count)
    blocks = early + late
    sources = [[origin[k] for k in range(chips)] for _, origin in blocks]
    counts = [len(parts) for parts, _ in blocks]
    early_parts = [part for parts, _ in early for part in parts]
    all_parts = [part for parts, _ in blocks for part in parts]

    scale = channels ** (-0.5) * 1.4426950408889634
    square = jax.ShapeDtypeStruct((channels, channels), BF16)
    score_weight, mix_weight = pl.pallas_call(
        functools.partial(fuse_kernel, scale),
        out_shape=(square, square),
        in_specs=[vmem()] * 4,
        out_specs=(vmem(),) * 2,
        cost_estimate=cost(4 * channels**3, 12 * channels * channels),
        compiler_params=params(8),
    )(query_weight, key_weight, value_weight, out_weight)

    wide = span + 2 * width
    lanes = jax.ShapeDtypeStruct((span, 128), F32)
    own_query, peak, sums, added = pl.pallas_call(
        functools.partial(early_kernel, counts[: len(early)]),
        out_shape=(
            jax.ShapeDtypeStruct((span, channels), BF16),
            lanes,
            lanes,
            jax.ShapeDtypeStruct((span, channels), F32),
        ),
        in_specs=[vmem()] * (1 + len(early_parts)),
        out_specs=(vmem(),) * 4,
        scratch_shapes=[pltpu.VMEM((len(early), span, span), F32)],
        cost_estimate=cost(
            4 * span * span * len(early) * channels,
            2 * span * channels * len(early),
            span * span * len(early),
        ),
        compiler_params=params(24),
    )(score_weight, *early_parts)

    mid, swap_rows = pl.pallas_call(
        functools.partial(late_kernel, width, sources, counts, len(early)),
        out_shape=(jax.ShapeDtypeStruct((4 * width, channels), BF16),) * 2,
        in_specs=[vmem()] * (8 + len(all_parts)),
        out_specs=(vmem(),) * 2,
        scratch_shapes=[
            pltpu.VMEM((len(blocks), wide, span), F32),
            pltpu.VMEM((wide, channels), BF16),
            pltpu.VMEM((2 * width, channels), BF16),
            pltpu.VMEM((2, EXTRA, 2 * width), BF16),
        ],
        cost_estimate=cost(
            2 * wide * span * len(blocks) * channels,
            2 * span * channels * len(blocks),
            wide * span * len(blocks) // 2,
        ),
        compiler_params=params(28),
    )(
        own_query,
        peak,
        sums,
        added,
        resid,
        attn_gain,
        score_weight,
        mix_weight,
        *all_parts,
    )

    swap_rows = lax.ppermute(swap_rows, "rows", swap)

    fine_shape = (2 * rows_here, outputs, 2 * width)
    decoded = pl.pallas_call(
        functools.partial(up_kernel, width),
        out_shape=jax.ShapeDtypeStruct((frames, *fine_shape), BF16),
        in_specs=[vmem()] * 3,
        out_specs=anywhere,
        scratch_shapes=[
            pltpu.VMEM((2, channels // 128, 8 * width, 128), F32),
            pltpu.VMEM((2, 9 * outputs, 8 * width), F32),
            pltpu.VMEM((2, *fine_shape), BF16),
            pltpu.SemaphoreType.DMA((2,)),
        ],
        cost_estimate=cost(
            2 * 9 * outputs * channels * 16 * width, 2 * 9 * outputs * channels
        ),
        compiler_params=params(24),
    )(mid, swap_rows, jnp.transpose(up_weight, (0, 1, 3, 2)))
    decoded = jnp.transpose(decoded, (0, 1, 3, 2))
    return (decoded, act.reshape(frames, rows_here, width, channels))


def solution(mesh):
    return jax.shard_map(
        shards,
        mesh=mesh,
        in_specs=(
            P("videos", "rows", None, None),
            P("videos", "rows", None, None),
            P(),
            P(),
            P(),
            P(),
            P(),
            P(),
            P(),
            P(),
        ),
        out_specs=(P("videos", "rows", None, None), P("videos", "rows", None, None)),
        check_vma=False,
    )
```

```python
import functools

import jax
import jax.numpy as jnp
from jax import lax
from jax.experimental import pallas as pl
from jax.experimental.pallas import tpu as pltpu
from jax.sharding import PartitionSpec as P

BF16 = jnp.bfloat16
F32 = jnp.float32
EPS = 1e-06
MIB = 1024 * 1024
EXTRA = 16


def normalize(values, gain):
    return values * lax.rsqrt(jnp.mean(values * values, axis=-1, keepdims=True) + EPS) * gain


def activate(values, gain):
    normed = normalize(values.astype(F32), gain)
    return (normed / (1.0 + jnp.exp(-normed))).astype(BF16)


def vmem():
    return pl.BlockSpec(memory_space=pltpu.VMEM)


def params(mib):
    return pltpu.CompilerParams(vmem_limit_bytes=mib * MIB)


def cost(flops, size, exps=0):
    return pl.CostEstimate(flops=flops, bytes_accessed=size, transcendentals=exps)


def edges_kernel(latents_ref, cache_ref, edge_ref, both_ref, sems):
    core = lax.axis_index("rows") % 2
    row = core * (latents_ref.shape[1] - 1)
    copies = [
        pltpu.make_async_copy(cache_ref.at[:, row], edge_ref.at[pl.ds(0, 2)], sems.at[0]),
        pltpu.make_async_copy(latents_ref.at[:, row], edge_ref.at[pl.ds(2, 2)], sems.at[1]),
        pltpu.make_async_copy(cache_ref.at[1], both_ref.at[core], sems.at[2]),
        pltpu.make_async_copy(latents_ref.at[0], both_ref.at[1 + core], sems.at[3]),
    ]
    for copy in copies:
        copy.start()

    @pl.when(core == 0)
    def _():
        last = pltpu.make_async_copy(latents_ref.at[1], both_ref.at[2], sems.at[4])
        last.start()
        last.wait()

    @pl.when(core == 1)
    def _():
        last = pltpu.make_async_copy(cache_ref.at[0], both_ref.at[0], sems.at[4])
        last.start()
        last.wait()

    for copy in copies:
        copy.wait()


def start_all(pairs, sems, first=0):
    copies = [
        pltpu.make_async_copy(source, target, sems.at[first + i])
        for i, (source, target) in enumerate(pairs)
    ]
    for copy in copies:
        copy.start()
    return copies


def wait_all(copies):
    for copy in copies:
        copy.wait()


def prepare_kernel(
    latents_ref,
    cache_ref,
    weight_ref,
    gain_ref,
    act_ref,
    own_ref,
    staged_ref,
    latents,
    cache,
    gain,
    act,
    sems,
):
    channels = latents_ref.shape[-1]
    core = lax.axis_index("rows") % 2
    loads = start_all([(latents_ref, latents), (cache_ref, cache), (gain_ref, gain)], sems)
    stages = start_all(
        [
            (
                weight_ref.at[time, :, col],
                staged_ref.at[time, :, :, pl.ds(col * channels, channels)],
            )
            for time in range(3)
            for col in range(3)
        ],
        sems,
        4,
    )
    wait_all(loads)
    act[...] = activate(latents[...], gain[...].reshape(1, channels))
    store = start_all([(act, act_ref)], sems, 3)
    own_ref[0] = cache[core]
    own_ref[1] = jnp.where(core == 0, cache[1], latents[0])
    own_ref[2] = latents[core]
    wait_all(store + stages)


def conv_kernel(
    width,
    own_ref,
    swap_ref,
    edge_ref,
    far_ref,
    norm_gain_ref,
    attn_gain_ref,
    weights,
    sent_ref,
    front_ref,
    back_ref,
    resid_ref,
    raw,
    second,
    third,
    total,
):
    channels = own_ref.shape[-1]
    core = lax.axis_index("rows") % 2
    own = 2 * width
    span = 4 * width
    gain = norm_gain_ref[...].reshape(1, channels)

    def put(index, values):
        rows = pl.ds(pl.multiple_of(index * width, width), values.shape[1])
        raw[:, rows, :] = values

    put(1 + 2 * core, own_ref[...])
    put(3 - 2 * core, swap_ref[...])
    put(5 * core, edge_ref[pl.ds(core, 3)])
    put(5 * (1 - core), far_ref[pl.ds(core, 3)])

    def taps(ref, time):
        lhs = jnp.concatenate([ref[row * width : row * width + span] for row in range(3)], axis=1)
        rhs = weights[time].reshape(3 * channels, 3 * channels)
        return jnp.dot(lhs, rhs, preferred_element_type=F32)

    total[...] = taps(raw.at[0], 0)
    second[...] = jnp.where(core == 1, activate(raw[1], gain), raw[1])
    third[...] = activate(raw[2], gain)
    total[...] += taps(second, 1)
    total[...] += taps(third, 2)

    column = lax.broadcasted_iota(jnp.int32, (span, 1), 0) % width
    left = pltpu.roll(total[:, :channels], 1, axis=0)
    right = pltpu.roll(total[:, 2 * channels :], span - 1, axis=0)
    conv_out = total[:, channels : 2 * channels]
    conv_out = conv_out + jnp.where(column == 0, 0.0, left)
    conv_out = conv_out + jnp.where(column == width - 1, 0.0, right)
    resid = raw[2, width : width + span].astype(F32) + conv_out
    resid_ref[...] = resid
    size = jnp.mean(resid * resid, axis=-1, keepdims=True) + EPS
    normed = resid * lax.rsqrt(size) * attn_gain_ref[...].reshape(1, channels)
    edges = jnp.sqrt(jnp.concatenate([size[:width], size[span - width :]], axis=0))
    across = jnp.transpose(jnp.broadcast_to(edges, (2 * width, 128)))[:EXTRA]
    high = across.astype(BF16).astype(F32)
    line = lax.broadcasted_iota(jnp.int32, (EXTRA, 1), 0)
    extra = jnp.where(line == 0, high, jnp.where(line == 1, across - high, 0.0)).astype(BF16)
    half = span // 2
    for ref, low, count in ((sent_ref, 0, span), (front_ref, 0, half), (back_ref, half, half)):
        ref[:count] = normed[low : low + count].astype(BF16)
        ref[count:] = jnp.zeros((EXTRA, channels), BF16)
        ref[count:, : 2 * width] = extra


def nt_dot(a, b):
    return lax.dot_general(a, b, (((1,), (1,)), ((), ())), preferred_element_type=F32)


def whole(parts):
    rows = [part[: part.shape[0] - EXTRA] for part in parts]
    return rows[0] if len(rows) == 1 else jnp.concatenate(rows, axis=0)


def grouped(refs, counts):
    blocks, first = [], 0
    for count in counts:
        blocks.append(refs[first : first + count])
        first += count
    return blocks


def fold(values, combine, total):
    for lane in range(0, values.shape[1], 128):
        piece = values[:, lane : lane + 128]
        total = piece if total is None else combine(total, piece)
    return total


def attend(queries, keys, scores, start, peak, sums, added):
    height = queries.shape[0]
    top = None
    for i, key in enumerate(keys):
        part = nt_dot(queries, key)
        scores[i, start : start + height] = part
        top = fold(part, jnp.maximum, top)
    top = jnp.max(top, axis=-1, keepdims=True)
    if peak is not None:
        top = jnp.maximum(top, peak)
        shrink = jnp.exp2(peak - top)
        sums = sums * shrink
        added = added * shrink
    for i, key in enumerate(keys):
        weights = jnp.exp2(scores[i, start : start + height] - top)
        sums = fold(weights, jnp.add, sums)
        part = jnp.dot(weights.astype(BF16), key, preferred_element_type=F32)
        added = part if added is None else added + part
    return top, sums, added


def fuse_kernel(scale, query_ref, key_ref, value_ref, out_ref, score_ref, mix_ref):
    score_ref[...] = (nt_dot(query_ref[...], key_ref[...]) * scale).astype(BF16)
    mix_ref[...] = jnp.dot(
        value_ref[...], out_ref[...], preferred_element_type=F32
    ).astype(BF16)


def lead(rows, score_weight):
    return jnp.dot(rows, score_weight[...], preferred_element_type=F32).astype(BF16)


def early_kernel(counts, score_ref, *refs):
    blocks = grouped(refs, counts)
    own_query_ref, peak_ref, sums_ref, added_ref, scores = refs[-5:]
    keys = [whole(parts) for parts in blocks]
    queries = lead(keys[0], score_ref)
    own_query_ref[...] = queries
    peak, sums, added = attend(queries, keys, scores, 0, None, None, None)
    peak_ref[...] = jnp.broadcast_to(peak, peak_ref.shape)
    sums_ref[...] = sums
    added_ref[...] = added


def late_kernel(
    width,
    sources,
    counts,
    early,
    own_query_ref,
    peak_ref,
    sums_ref,
    added_ref,
    resid_ref,
    gain_ref,
    score_ref,
    mix_weight_ref,
    *refs,
):
    blocks = grouped(refs, counts)
    mid_ref, swap_ref, scores, mid, halo, sizes = refs[sum(counts) :]
    place = lax.axis_index("rows")
    core = place % 2
    chip = place // 2
    own, channels = own_query_ref.shape
    chips = len(sources[0])

    for block, origin in zip(blocks, sources):
        for step, part, low in ((-1, block[-1], 0), (1, block[0], width)):
            rows = part.shape[0] - EXTRA
            first = rows - width if step < 0 else 0
            takers = [k for k in range(chips) if origin[k] == k + step]
            if not takers:
                continue
            wanted = chip == takers[0]
            for k in takers[1:]:
                wanted = jnp.logical_or(wanted, chip == k)

            @pl.when(wanted)
            def _(part=part, rows=rows, first=first, low=low):
                halo[low : low + width] = part[first : first + width, :]
                sizes[low // width] = part[rows : rows + EXTRA, : 2 * width]

    no_above = chip == 0
    no_below = chip == chips - 1

    @pl.when(no_above)
    def _():
        halo[:width] = jnp.zeros((width, channels), BF16)
        sizes[0] = jnp.zeros((EXTRA, 2 * width), BF16)

    @pl.when(no_below)
    def _():
        halo[width:] = jnp.zeros((width, channels), BF16)
        sizes[1] = jnp.zeros((EXTRA, 2 * width), BF16)

    def column(index):
        parts = sizes[index].astype(F32)
        line = parts[0:1] + parts[1:2]
        return jnp.transpose(jnp.broadcast_to(line, (128, 2 * width)))[:, :1]

    edge_rows = halo[...]
    edge_size = jnp.concatenate([column(0)[width:], column(1)[:width]], axis=0)
    edge_resid = edge_rows.astype(F32) * edge_size / gain_ref[...].reshape(1, channels)
    edge_query = lead(edge_rows, score_ref)
    keys = [whole(parts) for parts in blocks]
    _, edge_sums, edge_added = attend(edge_query, keys, scores, own, None, None, None)
    _, own_sums, own_added = attend(
        own_query_ref[...],
        keys[early:],
        scores,
        0,
        peak_ref[:, :1],
        sums_ref[...],
        added_ref[...],
    )

    def finish(added, sums):
        return (added / jnp.sum(sums, axis=-1, keepdims=True)).astype(BF16)

    mixed = jnp.concatenate([finish(own_added, own_sums), finish(edge_added, edge_sums)], axis=0)
    projected = jnp.dot(mixed, mix_weight_ref[...], preferred_element_type=F32)
    inner = own + width
    mid[width:inner] = (resid_ref[...] + projected[:own]).astype(BF16)
    edges = edge_resid + projected[own:]
    mid[:width] = jnp.where(no_above, 0.0, edges[:width]).astype(BF16)
    mid[inner:] = jnp.where(no_below, 0.0, edges[width:]).astype(BF16)
    mid_ref[...] = mid[pl.ds(pl.multiple_of(2 * core * width, width), 4 * width), :]
    swap_ref[...] = mid[pl.ds(pl.multiple_of(2 * (1 - core) * width, width), 4 * width), :]


def up_kernel(width, mid_ref, swap_ref, weight_ref, out_ref, fine, total, results, sems):
    core = lax.axis_index("rows") % 2
    channels = mid_ref.shape[1]
    outputs = weight_ref.shape[2]
    wide = 2 * width
    lane = lax.broadcasted_iota(jnp.int32, (1, wide), 1)
    lhs = weight_ref[...].reshape(9 * outputs, channels)
    stores = []
    for slot, ref, frame in ((0, mid_ref, core), (1, swap_ref, 1 - core)):
        values = ref[...].astype(F32)
        pieces = []
        for i in range(channels // 128):
            piece = values[:, 128 * i : 128 * (i + 1)]
            fine[slot, i, pl.ds(0, 4 * width, stride=2), :] = piece
            fine[slot, i, pl.ds(1, 4 * width, stride=2), :] = piece
            pieces.append(fine[slot, i].astype(BF16))
        total[slot] = nt_dot(lhs, jnp.concatenate(pieces, axis=1))
        for row in range(4):
            low = row // 2 + 1
            picks = (low - 1, low, low) if row % 2 == 0 else (low, low, low + 1)
            taps = []
            for col in range(3):
                tap = None
                for j, pick in enumerate(picks):
                    piece = total[
                        slot,
                        (3 * j + col) * outputs : (3 * j + col + 1) * outputs,
                        pick * wide : (pick + 1) * wide,
                    ]
                    tap = piece if tap is None else tap + piece
                taps.append(tap)
            result = taps[1]
            result = result + jnp.where(lane == 0, 0.0, pltpu.roll(taps[0], 1, axis=1))
            result = result + jnp.where(
                lane == wide - 1, 0.0, pltpu.roll(taps[2], wide - 1, axis=1)
            )
            results[slot, row] = result.astype(BF16)
        stores = stores + start_all([(results.at[slot], out_ref.at[frame])], sems, slot)
    wait_all(stores)


def gather_blocks(block, halves, count):
    chips = count // 2
    depth = 2 if chips % 2 == 0 else 1
    length = chips // depth

    ring = [0] + list(range(1, length, 2)) + list(range(2, length, 2))[::-1]
    follow = {a: ring[(i + 1) % length] for i, a in enumerate(ring)}
    onward = {a * depth + b: follow[a] * depth + b for a in range(length) for b in range(depth)}
    backward = {target: source for source, target in onward.items()}
    across = {k: k ^ 1 for k in range(chips)}

    def send(parts, targets):
        pairs = [(2 * k + c, 2 * targets[k] + c) for k in range(chips) for c in range(2)]
        return [lax.ppermute(part, "rows", pairs) for part in parts]

    def moved(origin, targets):
        return {targets[k]: origin[k] for k in range(chips)}

    def tie(*places):
        fixed = lax.optimization_barrier(tuple(where[i] for where, i in places))
        for (where, i), value in zip(places, fixed):
            where[i] = value

    here = {k: k for k in range(chips)}
    early, late = [([block], here)], []
    back = crossed = last = None
    if length > 1:
        back = send([block], backward)
    if depth == 2:
        crossed = send([block], across)
    ties = {(2, 0): back}
    steps = length - 2
    parts, origin = list(halves), here
    for step in range(1, steps + 1):
        parts, origin = send(parts, onward), moved(origin, onward)
        for h in range(2):
            places = [(parts, h)]
            if last:
                places.append((last, h))
            if ties.get((step, h)):
                places.append((ties[(step, h)], 0))
            tie(*places)
        early.append((parts, origin))
        if depth == 2:
            last = send(parts, across)
            (late if step == steps else early).append((last, moved(origin, across)))
    if depth == 2:
        (early if length > 1 else late).append((crossed, moved(here, across)))
    if last:
        tie((early[0][0], 0), (last, 0))
    if back:
        origin = moved(here, backward)
        early.append((back, origin))
        if depth == 2:
            late.append((send(back, across), moved(origin, across)))
    return early, late


def shards(
    latents,
    conv_cache,
    norm_gain,
    conv_weight,
    attn_gain,
    query_weight,
    key_weight,
    value_weight,
    out_weight,
    up_weight,
):
    frames, rows_here, width, channels = latents.shape
    outputs = up_weight.shape[3]
    count = lax.axis_size("rows")
    span = 2 * rows_here * width
    own = rows_here * width
    edge = jax.ShapeDtypeStruct((width, channels), BF16)
    anywhere = pl.BlockSpec(memory_space=pl.ANY)
    hbm = pl.BlockSpec(memory_space=pltpu.HBM)

    chips = count // 2
    swap = [(2 * k + c, 2 * k + 1 - c) for k in range(chips) for c in range(2)]
    neighbour = [(2 * k + 1, 2 * k + 2) for k in range(chips - 1)]
    neighbour = neighbour + [(target, source) for source, target in neighbour]

    latents_in = pltpu.with_memory_space_constraint(latents, pltpu.HBM)
    cache_in = pltpu.with_memory_space_constraint(conv_cache, pltpu.HBM)
    edge_rows, both = pl.pallas_call(
        edges_kernel,
        out_shape=(
            jax.ShapeDtypeStruct((2 * frames, width, channels), BF16),
            jax.ShapeDtypeStruct((3, rows_here, width, channels), BF16),
        ),
        in_specs=[hbm] * 2,
        out_specs=(anywhere,) * 2,
        scratch_shapes=[pltpu.SemaphoreType.DMA((5,))],
        cost_estimate=cost(0, 20 * width * channels),
        compiler_params=params(4),
    )(latents_in, cache_in)
    edge_rows = lax.ppermute(edge_rows, "rows", neighbour)
    both = lax.ppermute(both, "rows", swap)
    act, own_rows, staged = pl.pallas_call(
        prepare_kernel,
        out_shape=(
            jax.ShapeDtypeStruct((frames, own, channels), BF16),
            jax.ShapeDtypeStruct((3, own, channels), BF16),
            jax.ShapeDtypeStruct((3, 3, channels, 3 * channels), BF16),
        ),
        in_specs=[hbm] * 4,
        out_specs=(anywhere, vmem(), anywhere),
        scratch_shapes=[
            pltpu.VMEM((frames, own, channels), BF16),
            pltpu.VMEM((frames, own, channels), BF16),
            pltpu.VMEM((channels,), F32),
            pltpu.VMEM((frames, own, channels), BF16),
            pltpu.SemaphoreType.DMA((13,)),
        ],
        cost_estimate=cost(10 * frames * own * channels, 2 * 27 * channels * channels),
        compiler_params=params(8),
    )(
        pltpu.with_memory_space_constraint(latents.reshape(frames, own, channels), pltpu.HBM),
        pltpu.with_memory_space_constraint(conv_cache.reshape(frames, own, channels), pltpu.HBM),
        pltpu.with_memory_space_constraint(conv_weight, pltpu.HBM),
        pltpu.with_memory_space_constraint(norm_gain, pltpu.HBM),
    )

    edge_rows, own_rows = lax.optimization_barrier((edge_rows, own_rows))
    far_rows = lax.ppermute(edge_rows, "rows", swap)
    block = jax.ShapeDtypeStruct((span + EXTRA, channels), BF16)
    half = jax.ShapeDtypeStruct((span // 2 + EXTRA, channels), BF16)
    sent, front, back, resid = pl.pallas_call(
        functools.partial(conv_kernel, width),
        out_shape=(block, half, half, jax.ShapeDtypeStruct((span, channels), F32)),
        in_specs=[vmem()] * 7,
        out_specs=(vmem(),) * 4,
        scratch_shapes=[
            pltpu.VMEM((3, 6 * width, channels), BF16),
            pltpu.VMEM((6 * width, channels), BF16),
            pltpu.VMEM((6 * width, channels), BF16),
            pltpu.VMEM((span, 3 * channels), F32),
        ],
        cost_estimate=cost(2 * 27 * span * channels * channels, 2 * 27 * channels * channels),
        compiler_params=params(20),
    )(
        own_rows,
        both.reshape(3, own, channels),
        edge_rows,
        far_rows,
        norm_gain,
        attn_gain,
        staged,
    )

    early, late = gather_blocks(sent, (front, back), count)
    blocks = early + late
    sources = [[origin[k] for k in range(chips)] for _, origin in blocks]
    counts = [len(parts) for parts, _ in blocks]
    early_parts = [part for parts, _ in early for part in parts]
    all_parts = [part for parts, _ in blocks for part in parts]

    scale = channels ** (-0.5) * 1.4426950408889634
    square = jax.ShapeDtypeStruct((channels, channels), BF16)
    score_weight, mix_weight = pl.pallas_call(
        functools.partial(fuse_kernel, scale),
        out_shape=(square, square),
        in_specs=[vmem()] * 4,
        out_specs=(vmem(),) * 2,
        cost_estimate=cost(4 * channels**3, 12 * channels * channels),
        compiler_params=params(8),
    )(query_weight, key_weight, value_weight, out_weight)

    wide = span + 2 * width
    lanes = jax.ShapeDtypeStruct((span, 128), F32)
    own_query, peak, sums, added = pl.pallas_call(
        functools.partial(early_kernel, counts[: len(early)]),
        out_shape=(
            jax.ShapeDtypeStruct((span, channels), BF16),
            lanes,
            lanes,
            jax.ShapeDtypeStruct((span, channels), F32),
        ),
        in_specs=[vmem()] * (1 + len(early_parts)),
        out_specs=(vmem(),) * 4,
        scratch_shapes=[pltpu.VMEM((len(early), span, span), F32)],
        cost_estimate=cost(
            4 * span * span * len(early) * channels,
            2 * span * channels * len(early),
            span * span * len(early),
        ),
        compiler_params=params(24),
    )(score_weight, *early_parts)

    mid, swap_rows = pl.pallas_call(
        functools.partial(late_kernel, width, sources, counts, len(early)),
        out_shape=(jax.ShapeDtypeStruct((4 * width, channels), BF16),) * 2,
        in_specs=[vmem()] * (8 + len(all_parts)),
        out_specs=(vmem(),) * 2,
        scratch_shapes=[
            pltpu.VMEM((len(blocks), wide, span), F32),
            pltpu.VMEM((wide, channels), BF16),
            pltpu.VMEM((2 * width, channels), BF16),
            pltpu.VMEM((2, EXTRA, 2 * width), BF16),
        ],
        cost_estimate=cost(
            2 * wide * span * len(blocks) * channels,
            2 * span * channels * len(blocks),
            wide * span * len(blocks) // 2,
        ),
        compiler_params=params(28),
    )(
        own_query,
        peak,
        sums,
        added,
        resid,
        attn_gain,
        score_weight,
        mix_weight,
        *all_parts,
    )

    swap_rows = lax.ppermute(swap_rows, "rows", swap)

    fine_shape = (2 * rows_here, outputs, 2 * width)
    decoded = pl.pallas_call(
        functools.partial(up_kernel, width),
        out_shape=jax.ShapeDtypeStruct((frames, *fine_shape), BF16),
        in_specs=[vmem()] * 3,
        out_specs=anywhere,
        scratch_shapes=[
            pltpu.VMEM((2, channels // 128, 8 * width, 128), F32),
            pltpu.VMEM((2, 9 * outputs, 8 * width), F32),
            pltpu.VMEM((2, *fine_shape), BF16),
            pltpu.SemaphoreType.DMA((2,)),
        ],
        cost_estimate=cost(
            2 * 9 * outputs * channels * 16 * width, 2 * 9 * outputs * channels
        ),
        compiler_params=params(24),
    )(mid, swap_rows, jnp.transpose(up_weight, (0, 1, 3, 2)))
    decoded = jnp.transpose(decoded, (0, 1, 3, 2))
    return (decoded, act.reshape(frames, rows_here, width, channels))


def solution(mesh):
    return jax.shard_map(
        shards,
        mesh=mesh,
        in_specs=(
            P("videos", "rows", None, None),
            P("videos", "rows", None, None),
            P(),
            P(),
            P(),
            P(),
            P(),
            P(),
            P(),
            P(),
        ),
        out_specs=(P("videos", "rows", None, None), P("videos", "rows", None, None)),
        check_vma=False,
    )
```

```python
import functools

import jax
import jax.numpy as jnp
from jax import lax
from jax.experimental import pallas as pl
from jax.experimental.pallas import tpu as pltpu
from jax.sharding import PartitionSpec as P

BF16 = jnp.bfloat16
F32 = jnp.float32
EPS = 1e-06
MIB = 1024 * 1024
EXTRA = 16


def normalize(values, gain):
    return values * lax.rsqrt(jnp.mean(values * values, axis=-1, keepdims=True) + EPS) * gain


def activate(values, gain):
    normed = normalize(values.astype(F32), gain)
    return (normed / (1.0 + jnp.exp(-normed))).astype(BF16)


def vmem():
    return pl.BlockSpec(memory_space=pltpu.VMEM)


def params(mib):
    return pltpu.CompilerParams(vmem_limit_bytes=mib * MIB)


def cost(flops, size, exps=0):
    return pl.CostEstimate(flops=flops, bytes_accessed=size, transcendentals=exps)


def edges_kernel(latents_ref, cache_ref, edge_ref, both_ref, sems):
    core = lax.axis_index("rows") % 2
    row = core * (latents_ref.shape[1] - 1)
    copies = [
        pltpu.make_async_copy(cache_ref.at[:, row], edge_ref.at[pl.ds(0, 2)], sems.at[0]),
        pltpu.make_async_copy(latents_ref.at[:, row], edge_ref.at[pl.ds(2, 2)], sems.at[1]),
        pltpu.make_async_copy(cache_ref.at[1], both_ref.at[core], sems.at[2]),
        pltpu.make_async_copy(latents_ref.at[0], both_ref.at[1 + core], sems.at[3]),
    ]
    for copy in copies:
        copy.start()

    @pl.when(core == 0)
    def _():
        last = pltpu.make_async_copy(latents_ref.at[1], both_ref.at[2], sems.at[4])
        last.start()
        last.wait()

    @pl.when(core == 1)
    def _():
        last = pltpu.make_async_copy(cache_ref.at[0], both_ref.at[0], sems.at[4])
        last.start()
        last.wait()

    for copy in copies:
        copy.wait()


def start_all(pairs, sems, first=0):
    copies = [
        pltpu.make_async_copy(source, target, sems.at[first + i])
        for i, (source, target) in enumerate(pairs)
    ]
    for copy in copies:
        copy.start()
    return copies


def wait_all(copies):
    for copy in copies:
        copy.wait()


def prepare_kernel(
    latents_ref,
    cache_ref,
    weight_ref,
    gain_ref,
    act_ref,
    own_ref,
    staged_ref,
    latents,
    cache,
    gain,
    act,
    sems,
):
    channels = latents_ref.shape[-1]
    core = lax.axis_index("rows") % 2
    loads = start_all([(latents_ref, latents), (cache_ref, cache), (gain_ref, gain)], sems)
    stages = start_all(
        [
            (
                weight_ref.at[time, :, col],
                staged_ref.at[time, :, :, pl.ds(col * channels, channels)],
            )
            for time in range(3)
            for col in range(3)
        ],
        sems,
        4,
    )
    wait_all(loads)
    act[...] = activate(latents[...], gain[...].reshape(1, channels))
    store = start_all([(act, act_ref)], sems, 3)
    own_ref[0] = cache[core]
    own_ref[1] = jnp.where(core == 0, cache[1], latents[0])
    own_ref[2] = latents[core]
    wait_all(store + stages)


def conv_kernel(
    width,
    own_ref,
    swap_ref,
    edge_ref,
    far_ref,
    norm_gain_ref,
    attn_gain_ref,
    weights,
    sent_ref,
    front_ref,
    back_ref,
    resid_ref,
    raw,
    second,
    third,
    total,
):
    channels = own_ref.shape[-1]
    core = lax.axis_index("rows") % 2
    own = 2 * width
    span = 4 * width
    gain = norm_gain_ref[...].reshape(1, channels)

    def put(index, values):
        rows = pl.ds(pl.multiple_of(index * width, width), values.shape[1])
        raw[:, rows, :] = values

    put(1 + 2 * core, own_ref[...])
    put(3 - 2 * core, swap_ref[...])
    put(5 * core, edge_ref[pl.ds(core, 3)])
    put(5 * (1 - core), far_ref[pl.ds(core, 3)])

    def taps(ref, time):
        lhs = jnp.concatenate([ref[row * width : row * width + span] for row in range(3)], axis=1)
        rhs = weights[time].reshape(3 * channels, 3 * channels)
        return jnp.dot(lhs, rhs, preferred_element_type=F32)

    total[...] = taps(raw.at[0], 0)
    second[...] = jnp.where(core == 1, activate(raw[1], gain), raw[1])
    third[...] = activate(raw[2], gain)
    total[...] += taps(second, 1)
    total[...] += taps(third, 2)

    column = lax.broadcasted_iota(jnp.int32, (span, 1), 0) % width
    left = pltpu.roll(total[:, :channels], 1, axis=0)
    right = pltpu.roll(total[:, 2 * channels :], span - 1, axis=0)
    conv_out = total[:, channels : 2 * channels]
    conv_out = conv_out + jnp.where(column == 0, 0.0, left)
    conv_out = conv_out + jnp.where(column == width - 1, 0.0, right)
    resid = raw[2, width : width + span].astype(F32) + conv_out
    resid_ref[...] = resid
    size = jnp.mean(resid * resid, axis=-1, keepdims=True) + EPS
    normed = resid * lax.rsqrt(size) * attn_gain_ref[...].reshape(1, channels)
    edges = jnp.sqrt(jnp.concatenate([size[:width], size[span - width :]], axis=0))
    across = jnp.transpose(jnp.broadcast_to(edges, (2 * width, 128)))[:EXTRA]
    high = across.astype(BF16).astype(F32)
    line = lax.broadcasted_iota(jnp.int32, (EXTRA, 1), 0)
    extra = jnp.where(line == 0, high, jnp.where(line == 1, across - high, 0.0)).astype(BF16)
    half = span // 2
    for ref, low, count in ((sent_ref, 0, span), (front_ref, 0, half), (back_ref, half, half)):
        ref[:count] = normed[low : low + count].astype(BF16)
        ref[count:] = jnp.zeros((EXTRA, channels), BF16)
        ref[count:, : 2 * width] = extra


def nt_dot(a, b):
    return lax.dot_general(a, b, (((1,), (1,)), ((), ())), preferred_element_type=F32)


def whole(parts):
    rows = [part[: part.shape[0] - EXTRA] for part in parts]
    return rows[0] if len(rows) == 1 else jnp.concatenate(rows, axis=0)


def grouped(refs, counts):
    blocks, first = [], 0
    for count in counts:
        blocks.append(refs[first : first + count])
        first += count
    return blocks


def fold(values, combine, total):
    for lane in range(0, values.shape[1], 128):
        piece = values[:, lane : lane + 128]
        total = piece if total is None else combine(total, piece)
    return total


def attend(queries, keys, scores, start, peak, sums, added):
    height = queries.shape[0]
    top = None
    for i, key in enumerate(keys):
        part = nt_dot(queries, key)
        scores[i, start : start + height] = part
        top = fold(part, jnp.maximum, top)
    top = jnp.max(top, axis=-1, keepdims=True)
    if peak is not None:
        top = jnp.maximum(top, peak)
        shrink = jnp.exp2(peak - top)
        sums = sums * shrink
        added = added * shrink
    for i, key in enumerate(keys):
        weights = jnp.exp2(scores[i, start : start + height] - top)
        sums = fold(weights, jnp.add, sums)
        part = jnp.dot(weights.astype(BF16), key, preferred_element_type=F32)
        added = part if added is None else added + part
    return top, sums, added


def fuse_kernel(scale, query_ref, key_ref, value_ref, out_ref, score_ref, mix_ref):
    score_ref[...] = (nt_dot(query_ref[...], key_ref[...]) * scale).astype(BF16)
    mix_ref[...] = jnp.dot(
        value_ref[...], out_ref[...], preferred_element_type=F32
    ).astype(BF16)


def lead(rows, score_weight):
    return jnp.dot(rows, score_weight[...], preferred_element_type=F32).astype(BF16)


def early_kernel(counts, score_ref, *refs):
    blocks = grouped(refs, counts)
    own_query_ref, peak_ref, sums_ref, added_ref, scores = refs[-5:]
    keys = [whole(parts) for parts in blocks]
    queries = lead(keys[0], score_ref)
    own_query_ref[...] = queries
    peak, sums, added = attend(queries, keys, scores, 0, None, None, None)
    peak_ref[...] = jnp.broadcast_to(peak, peak_ref.shape)
    sums_ref[...] = sums
    added_ref[...] = added


def late_kernel(
    width,
    sources,
    counts,
    early,
    own_query_ref,
    peak_ref,
    sums_ref,
    added_ref,
    resid_ref,
    gain_ref,
    score_ref,
    mix_weight_ref,
    *refs,
):
    blocks = grouped(refs, counts)
    mid_ref, swap_ref, scores, mid, halo, sizes = refs[sum(counts) :]
    place = lax.axis_index("rows")
    core = place % 2
    chip = place // 2
    own, channels = own_query_ref.shape
    chips = len(sources[0])

    for block, origin in zip(blocks, sources):
        for step, part, low in ((-1, block[-1], 0), (1, block[0], width)):
            rows = part.shape[0] - EXTRA
            first = rows - width if step < 0 else 0
            takers = [k for k in range(chips) if origin[k] == k + step]
            if not takers:
                continue
            wanted = chip == takers[0]
            for k in takers[1:]:
                wanted = jnp.logical_or(wanted, chip == k)

            @pl.when(wanted)
            def _(part=part, rows=rows, first=first, low=low):
                halo[low : low + width] = part[first : first + width, :]
                sizes[low // width] = part[rows : rows + EXTRA, : 2 * width]

    no_above = chip == 0
    no_below = chip == chips - 1

    @pl.when(no_above)
    def _():
        halo[:width] = jnp.zeros((width, channels), BF16)
        sizes[0] = jnp.zeros((EXTRA, 2 * width), BF16)

    @pl.when(no_below)
    def _():
        halo[width:] = jnp.zeros((width, channels), BF16)
        sizes[1] = jnp.zeros((EXTRA, 2 * width), BF16)

    def column(index):
        parts = sizes[index].astype(F32)
        line = parts[0:1] + parts[1:2]
        return jnp.transpose(jnp.broadcast_to(line, (128, 2 * width)))[:, :1]

    edge_rows = halo[...]
    edge_size = jnp.concatenate([column(0)[width:], column(1)[:width]], axis=0)
    edge_resid = edge_rows.astype(F32) * edge_size / gain_ref[...].reshape(1, channels)
    edge_query = lead(edge_rows, score_ref)
    keys = [whole(parts) for parts in blocks]
    _, edge_sums, edge_added = attend(edge_query, keys, scores, own, None, None, None)
    _, own_sums, own_added = attend(
        own_query_ref[...],
        keys[early:],
        scores,
        0,
        peak_ref[:, :1],
        sums_ref[...],
        added_ref[...],
    )

    def finish(added, sums):
        return (added / jnp.sum(sums, axis=-1, keepdims=True)).astype(BF16)

    mixed = jnp.concatenate([finish(own_added, own_sums), finish(edge_added, edge_sums)], axis=0)
    projected = jnp.dot(mixed, mix_weight_ref[...], preferred_element_type=F32)
    inner = own + width
    mid[width:inner] = (resid_ref[...] + projected[:own]).astype(BF16)
    edges = edge_resid + projected[own:]
    mid[:width] = jnp.where(no_above, 0.0, edges[:width]).astype(BF16)
    mid[inner:] = jnp.where(no_below, 0.0, edges[width:]).astype(BF16)
    mid_ref[...] = mid[pl.ds(pl.multiple_of(2 * core * width, width), 4 * width), :]
    swap_ref[...] = mid[pl.ds(pl.multiple_of(2 * (1 - core) * width, width), 4 * width), :]


def up_kernel(width, mid_ref, swap_ref, weight_ref, out_ref, fine, total, results, sems):
    core = lax.axis_index("rows") % 2
    channels = mid_ref.shape[1]
    outputs = weight_ref.shape[2]
    wide = 2 * width
    lane = lax.broadcasted_iota(jnp.int32, (1, wide), 1)
    lhs = weight_ref[...].reshape(9 * outputs, channels)
    stores = []
    for slot, ref, frame in ((0, mid_ref, core), (1, swap_ref, 1 - core)):
        values = ref[...].astype(F32)
        pieces = []
        for i in range(channels // 128):
            piece = values[:, 128 * i : 128 * (i + 1)]
            fine[slot, i, pl.ds(0, 4 * width, stride=2), :] = piece
            fine[slot, i, pl.ds(1, 4 * width, stride=2), :] = piece
            pieces.append(fine[slot, i].astype(BF16))
        total[slot] = nt_dot(lhs, jnp.concatenate(pieces, axis=1))
        for row in range(4):
            low = row // 2 + 1
            picks = (low - 1, low, low) if row % 2 == 0 else (low, low, low + 1)
            taps = []
            for col in range(3):
                tap = None
                for j, pick in enumerate(picks):
                    piece = total[
                        slot,
                        (3 * j + col) * outputs : (3 * j + col + 1) * outputs,
                        pick * wide : (pick + 1) * wide,
                    ]
                    tap = piece if tap is None else tap + piece
                taps.append(tap)
            result = taps[1]
            result = result + jnp.where(lane == 0, 0.0, pltpu.roll(taps[0], 1, axis=1))
            result = result + jnp.where(
                lane == wide - 1, 0.0, pltpu.roll(taps[2], wide - 1, axis=1)
            )
            results[slot, row] = result.astype(BF16)
        stores = stores + start_all([(results.at[slot], out_ref.at[frame])], sems, slot)
    wait_all(stores)


def gather_blocks(block, halves, count):
    chips = count // 2
    depth = 2 if chips % 2 == 0 else 1
    length = chips // depth

    ring = [0] + list(range(1, length, 2)) + list(range(2, length, 2))[::-1]
    follow = {a: ring[(i + 1) % length] for i, a in enumerate(ring)}
    onward = {a * depth + b: follow[a] * depth + b for a in range(length) for b in range(depth)}
    backward = {target: source for source, target in onward.items()}
    across = {k: k ^ 1 for k in range(chips)}

    def send(parts, targets):
        pairs = [(2 * k + c, 2 * targets[k] + c) for k in range(chips) for c in range(2)]
        return [lax.ppermute(part, "rows", pairs) for part in parts]

    def moved(origin, targets):
        return {targets[k]: origin[k] for k in range(chips)}

    def tie(*places):
        fixed = lax.optimization_barrier(tuple(where[i] for where, i in places))
        for (where, i), value in zip(places, fixed):
            where[i] = value

    here = {k: k for k in range(chips)}
    early, late = [([block], here)], []
    own_again = [block]
    crossed = last = None
    if depth == 2:
        crossed = send([block], across)
    steps = length - 2
    parts, origin = list(halves), here
    for step in range(1, steps + 1):
        parts, origin = send(parts, onward), moved(origin, onward)
        for h in range(2):
            places = [(parts, h)]
            if last:
                places.append((last, h))
            if (step, h) == (1, 1) and depth == 2:
                places.append((crossed, 0))
            tie(*places)
        early.append((parts, origin))
        if depth == 2:
            last = send(parts, across)
            (late if step == steps else early).append((last, moved(origin, across)))
    if length > 1:
        if steps > 0:
            tie((own_again, 0), (parts, 0))
        late.append((send(own_again, backward), moved(here, backward)))
    if depth == 2:
        (early if length > 1 else late).append((crossed, moved(here, across)))
        if length > 1:
            again = list(crossed)
            if steps > 0:
                tie((again, 0), (parts, 0))
            late.append((send(again, backward), moved(moved(here, across), backward)))
    return early, late


def shards(
    latents,
    conv_cache,
    norm_gain,
    conv_weight,
    attn_gain,
    query_weight,
    key_weight,
    value_weight,
    out_weight,
    up_weight,
):
    frames, rows_here, width, channels = latents.shape
    outputs = up_weight.shape[3]
    count = lax.axis_size("rows")
    span = 2 * rows_here * width
    own = rows_here * width
    edge = jax.ShapeDtypeStruct((width, channels), BF16)
    anywhere = pl.BlockSpec(memory_space=pl.ANY)
    hbm = pl.BlockSpec(memory_space=pltpu.HBM)

    chips = count // 2
    swap = [(2 * k + c, 2 * k + 1 - c) for k in range(chips) for c in range(2)]
    neighbour = [(2 * k + 1, 2 * k + 2) for k in range(chips - 1)]
    neighbour = neighbour + [(target, source) for source, target in neighbour]

    latents_in = pltpu.with_memory_space_constraint(latents, pltpu.HBM)
    cache_in = pltpu.with_memory_space_constraint(conv_cache, pltpu.HBM)
    edge_rows, both = pl.pallas_call(
        edges_kernel,
        out_shape=(
            jax.ShapeDtypeStruct((2 * frames, width, channels), BF16),
            jax.ShapeDtypeStruct((3, rows_here, width, channels), BF16),
        ),
        in_specs=[hbm] * 2,
        out_specs=(anywhere,) * 2,
        scratch_shapes=[pltpu.SemaphoreType.DMA((5,))],
        cost_estimate=cost(0, 20 * width * channels),
        compiler_params=params(4),
    )(latents_in, cache_in)
    edge_rows = lax.ppermute(edge_rows, "rows", neighbour)
    both = lax.ppermute(both, "rows", swap)
    act, own_rows, staged = pl.pallas_call(
        prepare_kernel,
        out_shape=(
            jax.ShapeDtypeStruct((frames, own, channels), BF16),
            jax.ShapeDtypeStruct((3, own, channels), BF16),
            jax.ShapeDtypeStruct((3, 3, channels, 3 * channels), BF16),
        ),
        in_specs=[hbm] * 4,
        out_specs=(anywhere, vmem(), anywhere),
        scratch_shapes=[
            pltpu.VMEM((frames, own, channels), BF16),
            pltpu.VMEM((frames, own, channels), BF16),
            pltpu.VMEM((channels,), F32),
            pltpu.VMEM((frames, own, channels), BF16),
            pltpu.SemaphoreType.DMA((13,)),
        ],
        cost_estimate=cost(10 * frames * own * channels, 2 * 27 * channels * channels),
        compiler_params=params(8),
    )(
        pltpu.with_memory_space_constraint(latents.reshape(frames, own, channels), pltpu.HBM),
        pltpu.with_memory_space_constraint(conv_cache.reshape(frames, own, channels), pltpu.HBM),
        pltpu.with_memory_space_constraint(conv_weight, pltpu.HBM),
        pltpu.with_memory_space_constraint(norm_gain, pltpu.HBM),
    )

    edge_rows, own_rows = lax.optimization_barrier((edge_rows, own_rows))
    far_rows = lax.ppermute(edge_rows, "rows", swap)
    block = jax.ShapeDtypeStruct((span + EXTRA, channels), BF16)
    half = jax.ShapeDtypeStruct((span // 2 + EXTRA, channels), BF16)
    sent, front, back, resid = pl.pallas_call(
        functools.partial(conv_kernel, width),
        out_shape=(block, half, half, jax.ShapeDtypeStruct((span, channels), F32)),
        in_specs=[vmem()] * 7,
        out_specs=(vmem(),) * 4,
        scratch_shapes=[
            pltpu.VMEM((3, 6 * width, channels), BF16),
            pltpu.VMEM((6 * width, channels), BF16),
            pltpu.VMEM((6 * width, channels), BF16),
            pltpu.VMEM((span, 3 * channels), F32),
        ],
        cost_estimate=cost(2 * 27 * span * channels * channels, 2 * 27 * channels * channels),
        compiler_params=params(20),
    )(
        own_rows,
        both.reshape(3, own, channels),
        edge_rows,
        far_rows,
        norm_gain,
        attn_gain,
        staged,
    )

    early, late = gather_blocks(sent, (front, back), count)
    blocks = early + late
    sources = [[origin[k] for k in range(chips)] for _, origin in blocks]
    counts = [len(parts) for parts, _ in blocks]
    early_parts = [part for parts, _ in early for part in parts]
    all_parts = [part for parts, _ in blocks for part in parts]

    scale = channels ** (-0.5) * 1.4426950408889634
    square = jax.ShapeDtypeStruct((channels, channels), BF16)
    score_weight, mix_weight = pl.pallas_call(
        functools.partial(fuse_kernel, scale),
        out_shape=(square, square),
        in_specs=[vmem()] * 4,
        out_specs=(vmem(),) * 2,
        cost_estimate=cost(4 * channels**3, 12 * channels * channels),
        compiler_params=params(8),
    )(query_weight, key_weight, value_weight, out_weight)

    wide = span + 2 * width
    lanes = jax.ShapeDtypeStruct((span, 128), F32)
    own_query, peak, sums, added = pl.pallas_call(
        functools.partial(early_kernel, counts[: len(early)]),
        out_shape=(
            jax.ShapeDtypeStruct((span, channels), BF16),
            lanes,
            lanes,
            jax.ShapeDtypeStruct((span, channels), F32),
        ),
        in_specs=[vmem()] * (1 + len(early_parts)),
        out_specs=(vmem(),) * 4,
        scratch_shapes=[pltpu.VMEM((len(early), span, span), F32)],
        cost_estimate=cost(
            4 * span * span * len(early) * channels,
            2 * span * channels * len(early),
            span * span * len(early),
        ),
        compiler_params=params(24),
    )(score_weight, *early_parts)

    mid, swap_rows = pl.pallas_call(
        functools.partial(late_kernel, width, sources, counts, len(early)),
        out_shape=(jax.ShapeDtypeStruct((4 * width, channels), BF16),) * 2,
        in_specs=[vmem()] * (8 + len(all_parts)),
        out_specs=(vmem(),) * 2,
        scratch_shapes=[
            pltpu.VMEM((len(blocks), wide, span), F32),
            pltpu.VMEM((wide, channels), BF16),
            pltpu.VMEM((2 * width, channels), BF16),
            pltpu.VMEM((2, EXTRA, 2 * width), BF16),
        ],
        cost_estimate=cost(
            2 * wide * span * len(blocks) * channels,
            2 * span * channels * len(blocks),
            wide * span * len(blocks) // 2,
        ),
        compiler_params=params(28),
    )(
        own_query,
        peak,
        sums,
        added,
        resid,
        attn_gain,
        score_weight,
        mix_weight,
        *all_parts,
    )

    swap_rows = lax.ppermute(swap_rows, "rows", swap)

    fine_shape = (2 * rows_here, outputs, 2 * width)
    decoded = pl.pallas_call(
        functools.partial(up_kernel, width),
        out_shape=jax.ShapeDtypeStruct((frames, *fine_shape), BF16),
        in_specs=[vmem()] * 3,
        out_specs=anywhere,
        scratch_shapes=[
            pltpu.VMEM((2, channels // 128, 8 * width, 128), F32),
            pltpu.VMEM((2, 9 * outputs, 8 * width), F32),
            pltpu.VMEM((2, *fine_shape), BF16),
            pltpu.SemaphoreType.DMA((2,)),
        ],
        cost_estimate=cost(
            2 * 9 * outputs * channels * 16 * width, 2 * 9 * outputs * channels
        ),
        compiler_params=params(24),
    )(mid, swap_rows, jnp.transpose(up_weight, (0, 1, 3, 2)))
    decoded = jnp.transpose(decoded, (0, 1, 3, 2))
    return (decoded, act.reshape(frames, rows_here, width, channels))


def solution(mesh):
    return jax.shard_map(
        shards,
        mesh=mesh,
        in_specs=(
            P("videos", "rows", None, None),
            P("videos", "rows", None, None),
            P(),
            P(),
            P(),
            P(),
            P(),
            P(),
            P(),
            P(),
        ),
        out_specs=(P("videos", "rows", None, None), P("videos", "rows", None, None)),
        check_vma=False,
    )
```

```python
import functools

import jax
import jax.numpy as jnp
from jax import lax
from jax.experimental import pallas as pl
from jax.experimental.pallas import tpu as pltpu
from jax.sharding import PartitionSpec as P

BF16 = jnp.bfloat16
F32 = jnp.float32
EPS = 1e-06
MIB = 1024 * 1024
EXTRA = 16


def normalize(values, gain):
    return values * lax.rsqrt(jnp.mean(values * values, axis=-1, keepdims=True) + EPS) * gain


def activate(values, gain):
    normed = normalize(values.astype(F32), gain)
    return (normed / (1.0 + jnp.exp(-normed))).astype(BF16)


def vmem():
    return pl.BlockSpec(memory_space=pltpu.VMEM)


def params(mib):
    return pltpu.CompilerParams(vmem_limit_bytes=mib * MIB)


def cost(flops, size, exps=0):
    return pl.CostEstimate(flops=flops, bytes_accessed=size, transcendentals=exps)


def edges_kernel(latents_ref, cache_ref, edge_ref, both_ref, sems):
    core = lax.axis_index("rows") % 2
    row = core * (latents_ref.shape[1] - 1)
    copies = [
        pltpu.make_async_copy(cache_ref.at[:, row], edge_ref.at[pl.ds(0, 2)], sems.at[0]),
        pltpu.make_async_copy(latents_ref.at[:, row], edge_ref.at[pl.ds(2, 2)], sems.at[1]),
        pltpu.make_async_copy(cache_ref.at[1], both_ref.at[core], sems.at[2]),
        pltpu.make_async_copy(latents_ref.at[0], both_ref.at[1 + core], sems.at[3]),
    ]
    for copy in copies:
        copy.start()

    @pl.when(core == 0)
    def _():
        last = pltpu.make_async_copy(latents_ref.at[1], both_ref.at[2], sems.at[4])
        last.start()
        last.wait()

    @pl.when(core == 1)
    def _():
        last = pltpu.make_async_copy(cache_ref.at[0], both_ref.at[0], sems.at[4])
        last.start()
        last.wait()

    for copy in copies:
        copy.wait()


def start_all(pairs, sems, first=0):
    copies = [
        pltpu.make_async_copy(source, target, sems.at[first + i])
        for i, (source, target) in enumerate(pairs)
    ]
    for copy in copies:
        copy.start()
    return copies


def wait_all(copies):
    for copy in copies:
        copy.wait()


def prepare_kernel(
    latents_ref,
    cache_ref,
    weight_ref,
    gain_ref,
    act_ref,
    own_ref,
    staged_ref,
    latents,
    cache,
    gain,
    act,
    sems,
):
    channels = latents_ref.shape[-1]
    core = lax.axis_index("rows") % 2
    loads = start_all([(latents_ref, latents), (cache_ref, cache), (gain_ref, gain)], sems)
    stages = start_all(
        [
            (
                weight_ref.at[time, :, col],
                staged_ref.at[time, :, :, pl.ds(col * channels, channels)],
            )
            for time in range(3)
            for col in range(3)
        ],
        sems,
        4,
    )
    wait_all(loads)
    act[...] = activate(latents[...], gain[...].reshape(1, channels))
    store = start_all([(act, act_ref)], sems, 3)
    own_ref[0] = cache[core]
    own_ref[1] = jnp.where(core == 0, cache[1], latents[0])
    own_ref[2] = latents[core]
    wait_all(store + stages)


def conv_kernel(
    width,
    own_ref,
    swap_ref,
    edge_ref,
    far_ref,
    norm_gain_ref,
    attn_gain_ref,
    weights,
    sent_ref,
    front_ref,
    back_ref,
    resid_ref,
    raw,
    second,
    third,
    total,
):
    channels = own_ref.shape[-1]
    core = lax.axis_index("rows") % 2
    own = 2 * width
    span = 4 * width
    gain = norm_gain_ref[...].reshape(1, channels)

    def put(index, values):
        rows = pl.ds(pl.multiple_of(index * width, width), values.shape[1])
        raw[:, rows, :] = values

    put(1 + 2 * core, own_ref[...])
    put(3 - 2 * core, swap_ref[...])
    put(5 * core, edge_ref[pl.ds(core, 3)])
    put(5 * (1 - core), far_ref[pl.ds(core, 3)])

    def taps(ref, time):
        lhs = jnp.concatenate([ref[row * width : row * width + span] for row in range(3)], axis=1)
        rhs = weights[time].reshape(3 * channels, 3 * channels)
        return jnp.dot(lhs, rhs, preferred_element_type=F32)

    total[...] = taps(raw.at[0], 0)
    second[...] = jnp.where(core == 1, activate(raw[1], gain), raw[1])
    third[...] = activate(raw[2], gain)
    total[...] += taps(second, 1)
    total[...] += taps(third, 2)

    column = lax.broadcasted_iota(jnp.int32, (span, 1), 0) % width
    left = pltpu.roll(total[:, :channels], 1, axis=0)
    right = pltpu.roll(total[:, 2 * channels :], span - 1, axis=0)
    conv_out = total[:, channels : 2 * channels]
    conv_out = conv_out + jnp.where(column == 0, 0.0, left)
    conv_out = conv_out + jnp.where(column == width - 1, 0.0, right)
    resid = raw[2, width : width + span].astype(F32) + conv_out
    resid_ref[...] = resid
    size = jnp.mean(resid * resid, axis=-1, keepdims=True) + EPS
    normed = resid * lax.rsqrt(size) * attn_gain_ref[...].reshape(1, channels)
    edges = jnp.sqrt(jnp.concatenate([size[:width], size[span - width :]], axis=0))
    across = jnp.transpose(jnp.broadcast_to(edges, (2 * width, 128)))[:EXTRA]
    high = across.astype(BF16).astype(F32)
    line = lax.broadcasted_iota(jnp.int32, (EXTRA, 1), 0)
    extra = jnp.where(line == 0, high, jnp.where(line == 1, across - high, 0.0)).astype(BF16)
    half = span // 2
    for ref, low, count in ((sent_ref, 0, span), (front_ref, 0, half), (back_ref, half, half)):
        ref[:count] = normed[low : low + count].astype(BF16)
        ref[count:] = jnp.zeros((EXTRA, channels), BF16)
        ref[count:, : 2 * width] = extra


def nt_dot(a, b):
    return lax.dot_general(a, b, (((1,), (1,)), ((), ())), preferred_element_type=F32)


def whole(parts):
    rows = [part[: part.shape[0] - EXTRA] for part in parts]
    return rows[0] if len(rows) == 1 else jnp.concatenate(rows, axis=0)


def grouped(refs, counts):
    blocks, first = [], 0
    for count in counts:
        blocks.append(refs[first : first + count])
        first += count
    return blocks


def fold(values, combine, total):
    for lane in range(0, values.shape[1], 128):
        piece = values[:, lane : lane + 128]
        total = piece if total is None else combine(total, piece)
    return total


def attend(queries, keys, scores, start, peak, sums, added):
    height = queries.shape[0]
    top = None
    for i, key in enumerate(keys):
        part = nt_dot(queries, key)
        scores[i, start : start + height] = part
        top = fold(part, jnp.maximum, top)
    top = jnp.max(top, axis=-1, keepdims=True)
    if peak is not None:
        top = jnp.maximum(top, peak)
        shrink = jnp.exp2(peak - top)
        sums = sums * shrink
        added = added * shrink
    for i, key in enumerate(keys):
        weights = jnp.exp2(scores[i, start : start + height] - top)
        sums = fold(weights, jnp.add, sums)
        part = jnp.dot(weights.astype(BF16), key, preferred_element_type=F32)
        added = part if added is None else added + part
    return top, sums, added


def fuse_kernel(scale, query_ref, key_ref, value_ref, out_ref, score_ref, mix_ref):
    score_ref[...] = (nt_dot(query_ref[...], key_ref[...]) * scale).astype(BF16)
    mix_ref[...] = jnp.dot(
        value_ref[...], out_ref[...], preferred_element_type=F32
    ).astype(BF16)


def lead(rows, score_weight):
    return jnp.dot(rows, score_weight[...], preferred_element_type=F32).astype(BF16)


def early_kernel(counts, score_ref, *refs):
    blocks = grouped(refs, counts)
    own_query_ref, peak_ref, sums_ref, added_ref, scores = refs[-5:]
    keys = [whole(parts) for parts in blocks]
    queries = lead(keys[0], score_ref)
    own_query_ref[...] = queries
    peak, sums, added = attend(queries, keys, scores, 0, None, None, None)
    peak_ref[...] = jnp.broadcast_to(peak, peak_ref.shape)
    sums_ref[...] = sums
    added_ref[...] = added


def late_kernel(
    width,
    sources,
    counts,
    early,
    own_query_ref,
    peak_ref,
    sums_ref,
    added_ref,
    resid_ref,
    gain_ref,
    score_ref,
    mix_weight_ref,
    *refs,
):
    blocks = grouped(refs, counts)
    mid_ref, swap_ref, scores, mid, halo, sizes = refs[sum(counts) :]
    place = lax.axis_index("rows")
    core = place % 2
    chip = place // 2
    own, channels = own_query_ref.shape
    devices = len(sources[0])

    for block, origin in zip(blocks, sources):
        for step, part, low in ((-1, block[-1], 0), (1, block[0], width)):
            rows = part.shape[0] - EXTRA
            first = rows - width if step < 0 else 0
            takers = [d for d in range(devices) if origin[d] == d // 2 + step]
            if not takers:
                continue
            wanted = place == takers[0]
            for d in takers[1:]:
                wanted = jnp.logical_or(wanted, place == d)

            @pl.when(wanted)
            def _(part=part, rows=rows, first=first, low=low):
                halo[low : low + width] = part[first : first + width, :]
                sizes[low // width] = part[rows : rows + EXTRA, : 2 * width]

    no_above = chip == 0
    no_below = chip == devices // 2 - 1

    @pl.when(no_above)
    def _():
        halo[:width] = jnp.zeros((width, channels), BF16)
        sizes[0] = jnp.zeros((EXTRA, 2 * width), BF16)

    @pl.when(no_below)
    def _():
        halo[width:] = jnp.zeros((width, channels), BF16)
        sizes[1] = jnp.zeros((EXTRA, 2 * width), BF16)

    def column(index):
        parts = sizes[index].astype(F32)
        line = parts[0:1] + parts[1:2]
        return jnp.transpose(jnp.broadcast_to(line, (128, 2 * width)))[:, :1]

    edge_rows = halo[...]
    edge_size = jnp.concatenate([column(0)[width:], column(1)[:width]], axis=0)
    edge_resid = edge_rows.astype(F32) * edge_size / gain_ref[...].reshape(1, channels)
    edge_query = lead(edge_rows, score_ref)
    keys = [whole(parts) for parts in blocks]
    _, edge_sums, edge_added = attend(edge_query, keys, scores, own, None, None, None)
    _, own_sums, own_added = attend(
        own_query_ref[...],
        keys[early:],
        scores,
        0,
        peak_ref[:, :1],
        sums_ref[...],
        added_ref[...],
    )

    def finish(added, sums):
        return (added / jnp.sum(sums, axis=-1, keepdims=True)).astype(BF16)

    mixed = jnp.concatenate([finish(own_added, own_sums), finish(edge_added, edge_sums)], axis=0)
    projected = jnp.dot(mixed, mix_weight_ref[...], preferred_element_type=F32)
    inner = own + width
    mid[width:inner] = (resid_ref[...] + projected[:own]).astype(BF16)
    edges = edge_resid + projected[own:]
    mid[:width] = jnp.where(no_above, 0.0, edges[:width]).astype(BF16)
    mid[inner:] = jnp.where(no_below, 0.0, edges[width:]).astype(BF16)
    mid_ref[...] = mid[pl.ds(pl.multiple_of(2 * core * width, width), 4 * width), :]
    swap_ref[...] = mid[pl.ds(pl.multiple_of(2 * (1 - core) * width, width), 4 * width), :]


def up_kernel(width, mid_ref, swap_ref, weight_ref, out_ref, fine, total, results, sems):
    core = lax.axis_index("rows") % 2
    channels = mid_ref.shape[1]
    outputs = weight_ref.shape[2]
    wide = 2 * width
    lane = lax.broadcasted_iota(jnp.int32, (1, wide), 1)
    lhs = weight_ref[...].reshape(9 * outputs, channels)
    stores = []
    for slot, ref, frame in ((0, mid_ref, core), (1, swap_ref, 1 - core)):
        values = ref[...].astype(F32)
        pieces = []
        for i in range(channels // 128):
            piece = values[:, 128 * i : 128 * (i + 1)]
            fine[slot, i, pl.ds(0, 4 * width, stride=2), :] = piece
            fine[slot, i, pl.ds(1, 4 * width, stride=2), :] = piece
            pieces.append(fine[slot, i].astype(BF16))
        total[slot] = nt_dot(lhs, jnp.concatenate(pieces, axis=1))
        for row in range(4):
            low = row // 2 + 1
            picks = (low - 1, low, low) if row % 2 == 0 else (low, low, low + 1)
            taps = []
            for col in range(3):
                tap = None
                for j, pick in enumerate(picks):
                    piece = total[
                        slot,
                        (3 * j + col) * outputs : (3 * j + col + 1) * outputs,
                        pick * wide : (pick + 1) * wide,
                    ]
                    tap = piece if tap is None else tap + piece
                taps.append(tap)
            result = taps[1]
            result = result + jnp.where(lane == 0, 0.0, pltpu.roll(taps[0], 1, axis=1))
            result = result + jnp.where(
                lane == wide - 1, 0.0, pltpu.roll(taps[2], wide - 1, axis=1)
            )
            results[slot, row] = result.astype(BF16)
        stores = stores + start_all([(results.at[slot], out_ref.at[frame])], sems, slot)
    wait_all(stores)


def gather_blocks(block, halves, count):
    chips = count // 2
    depth = 2 if chips % 2 == 0 else 1
    length = chips // depth

    ring = [0] + list(range(1, length, 2)) + list(range(2, length, 2))[::-1]
    follow = {a: ring[(i + 1) % length] for i, a in enumerate(ring)}
    forth = {a * depth + b: follow[a] * depth + b for a in range(length) for b in range(depth)}
    return_ = {target: source for source, target in forth.items()}
    onward = (forth, return_)
    backward = (return_, forth)
    across = ({k: k ^ 1 for k in range(chips)},) * 2

    def send(parts, targets):
        pairs = [(2 * k + c, 2 * targets[c][k] + c) for k in range(chips) for c in range(2)]
        return [lax.ppermute(part, "rows", pairs) for part in parts]

    def moved(origin, targets):
        return tuple({targets[c][k]: origin[c][k] for k in range(chips)} for c in range(2))

    def tie(*places):
        fixed = lax.optimization_barrier(tuple(where[i] for where, i in places))
        for (where, i), value in zip(places, fixed):
            where[i] = value

    here = ({k: k for k in range(chips)},) * 2
    early, late = [([block], here)], []
    own_again = [block]
    crossed = last = None
    if depth == 2:
        crossed = send([block], across)
    steps = length - 2
    parts, origin = list(halves), here
    for step in range(1, steps + 1):
        parts, origin = send(parts, onward), moved(origin, onward)
        for h in range(2):
            places = [(parts, h)]
            if last:
                places.append((last, h))
            if (step, h) == (1, 1) and depth == 2:
                places.append((crossed, 0))
            tie(*places)
        early.append((parts, origin))
        if depth == 2:
            last = send(parts, across)
            (late if step == steps else early).append((last, moved(origin, across)))
    if length > 1:
        if steps > 0:
            tie((own_again, 0), (parts, 0))
        late.append((send(own_again, backward), moved(here, backward)))
    if depth == 2:
        (early if length > 1 else late).append((crossed, moved(here, across)))
        if length > 1:
            again = list(crossed)
            if steps > 0:
                tie((again, 0), (parts, 0))
            late.append((send(again, backward), moved(moved(here, across), backward)))
    return early, late


def shards(
    latents,
    conv_cache,
    norm_gain,
    conv_weight,
    attn_gain,
    query_weight,
    key_weight,
    value_weight,
    out_weight,
    up_weight,
):
    frames, rows_here, width, channels = latents.shape
    outputs = up_weight.shape[3]
    count = lax.axis_size("rows")
    span = 2 * rows_here * width
    own = rows_here * width
    edge = jax.ShapeDtypeStruct((width, channels), BF16)
    anywhere = pl.BlockSpec(memory_space=pl.ANY)
    hbm = pl.BlockSpec(memory_space=pltpu.HBM)

    chips = count // 2
    swap = [(2 * k + c, 2 * k + 1 - c) for k in range(chips) for c in range(2)]
    neighbour = [(2 * k + 1, 2 * k + 2) for k in range(chips - 1)]
    neighbour = neighbour + [(target, source) for source, target in neighbour]

    latents_in = pltpu.with_memory_space_constraint(latents, pltpu.HBM)
    cache_in = pltpu.with_memory_space_constraint(conv_cache, pltpu.HBM)
    edge_rows, both = pl.pallas_call(
        edges_kernel,
        out_shape=(
            jax.ShapeDtypeStruct((2 * frames, width, channels), BF16),
            jax.ShapeDtypeStruct((3, rows_here, width, channels), BF16),
        ),
        in_specs=[hbm] * 2,
        out_specs=(anywhere,) * 2,
        scratch_shapes=[pltpu.SemaphoreType.DMA((5,))],
        cost_estimate=cost(0, 20 * width * channels),
        compiler_params=params(4),
    )(latents_in, cache_in)
    edge_rows = lax.ppermute(edge_rows, "rows", neighbour)
    both = lax.ppermute(both, "rows", swap)
    act, own_rows, staged = pl.pallas_call(
        prepare_kernel,
        out_shape=(
            jax.ShapeDtypeStruct((frames, own, channels), BF16),
            jax.ShapeDtypeStruct((3, own, channels), BF16),
            jax.ShapeDtypeStruct((3, 3, channels, 3 * channels), BF16),
        ),
        in_specs=[hbm] * 4,
        out_specs=(anywhere, vmem(), anywhere),
        scratch_shapes=[
            pltpu.VMEM((frames, own, channels), BF16),
            pltpu.VMEM((frames, own, channels), BF16),
            pltpu.VMEM((channels,), F32),
            pltpu.VMEM((frames, own, channels), BF16),
            pltpu.SemaphoreType.DMA((13,)),
        ],
        cost_estimate=cost(10 * frames * own * channels, 2 * 27 * channels * channels),
        compiler_params=params(8),
    )(
        pltpu.with_memory_space_constraint(latents.reshape(frames, own, channels), pltpu.HBM),
        pltpu.with_memory_space_constraint(conv_cache.reshape(frames, own, channels), pltpu.HBM),
        pltpu.with_memory_space_constraint(conv_weight, pltpu.HBM),
        pltpu.with_memory_space_constraint(norm_gain, pltpu.HBM),
    )

    edge_rows, own_rows = lax.optimization_barrier((edge_rows, own_rows))
    far_rows = lax.ppermute(edge_rows, "rows", swap)
    block = jax.ShapeDtypeStruct((span + EXTRA, channels), BF16)
    half = jax.ShapeDtypeStruct((span // 2 + EXTRA, channels), BF16)
    sent, front, back, resid = pl.pallas_call(
        functools.partial(conv_kernel, width),
        out_shape=(block, half, half, jax.ShapeDtypeStruct((span, channels), F32)),
        in_specs=[vmem()] * 7,
        out_specs=(vmem(),) * 4,
        scratch_shapes=[
            pltpu.VMEM((3, 6 * width, channels), BF16),
            pltpu.VMEM((6 * width, channels), BF16),
            pltpu.VMEM((6 * width, channels), BF16),
            pltpu.VMEM((span, 3 * channels), F32),
        ],
        cost_estimate=cost(2 * 27 * span * channels * channels, 2 * 27 * channels * channels),
        compiler_params=params(20),
    )(
        own_rows,
        both.reshape(3, own, channels),
        edge_rows,
        far_rows,
        norm_gain,
        attn_gain,
        staged,
    )

    early, late = gather_blocks(sent, (front, back), count)
    blocks = early + late
    sources = [[origin[d % 2][d // 2] for d in range(count)] for _, origin in blocks]
    counts = [len(parts) for parts, _ in blocks]
    early_parts = [part for parts, _ in early for part in parts]
    all_parts = [part for parts, _ in blocks for part in parts]

    scale = channels ** (-0.5) * 1.4426950408889634
    square = jax.ShapeDtypeStruct((channels, channels), BF16)
    score_weight, mix_weight = pl.pallas_call(
        functools.partial(fuse_kernel, scale),
        out_shape=(square, square),
        in_specs=[vmem()] * 4,
        out_specs=(vmem(),) * 2,
        cost_estimate=cost(4 * channels**3, 12 * channels * channels),
        compiler_params=params(8),
    )(query_weight, key_weight, value_weight, out_weight)

    wide = span + 2 * width
    lanes = jax.ShapeDtypeStruct((span, 128), F32)
    own_query, peak, sums, added = pl.pallas_call(
        functools.partial(early_kernel, counts[: len(early)]),
        out_shape=(
            jax.ShapeDtypeStruct((span, channels), BF16),
            lanes,
            lanes,
            jax.ShapeDtypeStruct((span, channels), F32),
        ),
        in_specs=[vmem()] * (1 + len(early_parts)),
        out_specs=(vmem(),) * 4,
        scratch_shapes=[pltpu.VMEM((len(early), span, span), F32)],
        cost_estimate=cost(
            4 * span * span * len(early) * channels,
            2 * span * channels * len(early),
            span * span * len(early),
        ),
        compiler_params=params(24),
    )(score_weight, *early_parts)

    mid, swap_rows = pl.pallas_call(
        functools.partial(late_kernel, width, sources, counts, len(early)),
        out_shape=(jax.ShapeDtypeStruct((4 * width, channels), BF16),) * 2,
        in_specs=[vmem()] * (8 + len(all_parts)),
        out_specs=(vmem(),) * 2,
        scratch_shapes=[
            pltpu.VMEM((len(blocks), wide, span), F32),
            pltpu.VMEM((wide, channels), BF16),
            pltpu.VMEM((2 * width, channels), BF16),
            pltpu.VMEM((2, EXTRA, 2 * width), BF16),
        ],
        cost_estimate=cost(
            2 * wide * span * len(blocks) * channels,
            2 * span * channels * len(blocks),
            wide * span * len(blocks) // 2,
        ),
        compiler_params=params(28),
    )(
        own_query,
        peak,
        sums,
        added,
        resid,
        attn_gain,
        score_weight,
        mix_weight,
        *all_parts,
    )

    swap_rows = lax.ppermute(swap_rows, "rows", swap)

    fine_shape = (2 * rows_here, outputs, 2 * width)
    decoded = pl.pallas_call(
        functools.partial(up_kernel, width),
        out_shape=jax.ShapeDtypeStruct((frames, *fine_shape), BF16),
        in_specs=[vmem()] * 3,
        out_specs=anywhere,
        scratch_shapes=[
            pltpu.VMEM((2, channels // 128, 8 * width, 128), F32),
            pltpu.VMEM((2, 9 * outputs, 8 * width), F32),
            pltpu.VMEM((2, *fine_shape), BF16),
            pltpu.SemaphoreType.DMA((2,)),
        ],
        cost_estimate=cost(
            2 * 9 * outputs * channels * 16 * width, 2 * 9 * outputs * channels
        ),
        compiler_params=params(24),
    )(mid, swap_rows, jnp.transpose(up_weight, (0, 1, 3, 2)))
    decoded = jnp.transpose(decoded, (0, 1, 3, 2))
    return (decoded, act.reshape(frames, rows_here, width, channels))


def solution(mesh):
    return jax.shard_map(
        shards,
        mesh=mesh,
        in_specs=(
            P("videos", "rows", None, None),
            P("videos", "rows", None, None),
            P(),
            P(),
            P(),
            P(),
            P(),
            P(),
            P(),
            P(),
        ),
        out_specs=(P("videos", "rows", None, None), P("videos", "rows", None, None)),
        check_vma=False,
    )
```

```python
import functools

import jax
import jax.numpy as jnp
from jax import lax
from jax.experimental import pallas as pl
from jax.experimental.pallas import tpu as pltpu
from jax.sharding import PartitionSpec as P

BF16 = jnp.bfloat16
F32 = jnp.float32
EPS = 1e-06
MIB = 1024 * 1024
EXTRA = 16


def normalize(values, gain):
    return values * lax.rsqrt(jnp.mean(values * values, axis=-1, keepdims=True) + EPS) * gain


def activate(values, gain):
    normed = normalize(values.astype(F32), gain)
    return (normed / (1.0 + jnp.exp(-normed))).astype(BF16)


def vmem():
    return pl.BlockSpec(memory_space=pltpu.VMEM)


def params(mib):
    return pltpu.CompilerParams(vmem_limit_bytes=mib * MIB)


def cost(flops, size, exps=0):
    return pl.CostEstimate(flops=flops, bytes_accessed=size, transcendentals=exps)


def edges_kernel(latents_ref, cache_ref, edge_ref, both_ref, sems):
    core = lax.axis_index("rows") % 2
    row = core * (latents_ref.shape[1] - 1)
    copies = [
        pltpu.make_async_copy(cache_ref.at[:, row], edge_ref.at[pl.ds(0, 2)], sems.at[0]),
        pltpu.make_async_copy(latents_ref.at[:, row], edge_ref.at[pl.ds(2, 2)], sems.at[1]),
        pltpu.make_async_copy(cache_ref.at[1], both_ref.at[core], sems.at[2]),
        pltpu.make_async_copy(latents_ref.at[0], both_ref.at[1 + core], sems.at[3]),
    ]
    for copy in copies:
        copy.start()

    @pl.when(core == 0)
    def _():
        last = pltpu.make_async_copy(latents_ref.at[1], both_ref.at[2], sems.at[4])
        last.start()
        last.wait()

    @pl.when(core == 1)
    def _():
        last = pltpu.make_async_copy(cache_ref.at[0], both_ref.at[0], sems.at[4])
        last.start()
        last.wait()

    for copy in copies:
        copy.wait()


def start_all(pairs, sems, first=0):
    copies = [
        pltpu.make_async_copy(source, target, sems.at[first + i])
        for i, (source, target) in enumerate(pairs)
    ]
    for copy in copies:
        copy.start()
    return copies


def wait_all(copies):
    for copy in copies:
        copy.wait()


def prepare_kernel(
    latents_ref,
    cache_ref,
    weight_ref,
    gain_ref,
    act_ref,
    own_ref,
    staged_ref,
    latents,
    cache,
    gain,
    act,
    sems,
):
    channels = latents_ref.shape[-1]
    core = lax.axis_index("rows") % 2
    loads = start_all([(latents_ref, latents), (cache_ref, cache), (gain_ref, gain)], sems)
    stages = start_all(
        [
            (
                weight_ref.at[time, :, col],
                staged_ref.at[time, :, :, pl.ds(col * channels, channels)],
            )
            for time in range(3)
            for col in range(3)
        ],
        sems,
        4,
    )
    wait_all(loads)
    act[...] = activate(latents[...], gain[...].reshape(1, channels))
    store = start_all([(act, act_ref)], sems, 3)
    own_ref[0] = cache[core]
    own_ref[1] = jnp.where(core == 0, cache[1], latents[0])
    own_ref[2] = latents[core]
    wait_all(store + stages)


def conv_kernel(
    width,
    own_ref,
    swap_ref,
    edge_ref,
    far_ref,
    norm_gain_ref,
    attn_gain_ref,
    weights,
    sent_ref,
    front_ref,
    back_ref,
    resid_ref,
    raw,
    second,
    third,
    total,
):
    channels = own_ref.shape[-1]
    core = lax.axis_index("rows") % 2
    own = 2 * width
    span = 4 * width
    gain = norm_gain_ref[...].reshape(1, channels)

    def put(index, values):
        rows = pl.ds(pl.multiple_of(index * width, width), values.shape[1])
        raw[:, rows, :] = values

    put(1 + 2 * core, own_ref[...])
    put(3 - 2 * core, swap_ref[...])
    put(5 * core, edge_ref[pl.ds(core, 3)])
    put(5 * (1 - core), far_ref[pl.ds(core, 3)])

    def taps(ref, time):
        lhs = jnp.concatenate([ref[row * width : row * width + span] for row in range(3)], axis=1)
        rhs = weights[time].reshape(3 * channels, 3 * channels)
        return jnp.dot(lhs, rhs, preferred_element_type=F32)

    total[...] = taps(raw.at[0], 0)
    second[...] = jnp.where(core == 1, activate(raw[1], gain), raw[1])
    third[...] = activate(raw[2], gain)
    total[...] += taps(second, 1)
    total[...] += taps(third, 2)

    column = lax.broadcasted_iota(jnp.int32, (span, 1), 0) % width
    left = pltpu.roll(total[:, :channels], 1, axis=0)
    right = pltpu.roll(total[:, 2 * channels :], span - 1, axis=0)
    conv_out = total[:, channels : 2 * channels]
    conv_out = conv_out + jnp.where(column == 0, 0.0, left)
    conv_out = conv_out + jnp.where(column == width - 1, 0.0, right)
    resid = raw[2, width : width + span].astype(F32) + conv_out
    resid_ref[...] = resid
    size = jnp.mean(resid * resid, axis=-1, keepdims=True) + EPS
    normed = resid * lax.rsqrt(size) * attn_gain_ref[...].reshape(1, channels)
    edges = jnp.sqrt(jnp.concatenate([size[:width], size[span - width :]], axis=0))
    across = jnp.transpose(jnp.broadcast_to(edges, (2 * width, 128)))[:EXTRA]
    high = across.astype(BF16).astype(F32)
    line = lax.broadcasted_iota(jnp.int32, (EXTRA, 1), 0)
    extra = jnp.where(line == 0, high, jnp.where(line == 1, across - high, 0.0)).astype(BF16)
    half = span // 2
    for ref, low, count in ((sent_ref, 0, span), (front_ref, 0, half), (back_ref, half, half)):
        ref[:count] = normed[low : low + count].astype(BF16)
        ref[count:] = jnp.zeros((EXTRA, channels), BF16)
        ref[count:, : 2 * width] = extra


def nt_dot(a, b):
    return lax.dot_general(a, b, (((1,), (1,)), ((), ())), preferred_element_type=F32)


def whole(parts):
    rows = [part[: part.shape[0] - EXTRA] for part in parts]
    return rows[0] if len(rows) == 1 else jnp.concatenate(rows, axis=0)


def grouped(refs, counts):
    blocks, first = [], 0
    for count in counts:
        blocks.append(refs[first : first + count])
        first += count
    return blocks


def fold(values, combine, total):
    for lane in range(0, values.shape[1], 128):
        piece = values[:, lane : lane + 128]
        total = piece if total is None else combine(total, piece)
    return total


def attend(queries, keys, scores, start, peak, sums, added):
    height = queries.shape[0]
    top = None
    for i, key in enumerate(keys):
        part = nt_dot(queries, key)
        scores[i, start : start + height] = part
        top = fold(part, jnp.maximum, top)
    top = jnp.max(top, axis=-1, keepdims=True)
    if peak is not None:
        top = jnp.maximum(top, peak)
        shrink = jnp.exp2(peak - top)
        sums = sums * shrink
        added = added * shrink
    for i, key in enumerate(keys):
        weights = jnp.exp2(scores[i, start : start + height] - top)
        sums = fold(weights, jnp.add, sums)
        part = jnp.dot(weights.astype(BF16), key, preferred_element_type=F32)
        added = part if added is None else added + part
    return top, sums, added


def fuse_kernel(scale, query_ref, key_ref, value_ref, out_ref, score_ref, mix_ref):
    score_ref[...] = (nt_dot(query_ref[...], key_ref[...]) * scale).astype(BF16)
    mix_ref[...] = jnp.dot(
        value_ref[...], out_ref[...], preferred_element_type=F32
    ).astype(BF16)


def lead(rows, score_weight):
    return jnp.dot(rows, score_weight[...], preferred_element_type=F32).astype(BF16)


def early_kernel(counts, score_ref, *refs):
    blocks = grouped(refs, counts)
    own_query_ref, peak_ref, sums_ref, added_ref, scores = refs[-5:]
    keys = [whole(parts) for parts in blocks]
    queries = lead(keys[0], score_ref)
    own_query_ref[...] = queries
    peak, sums, added = attend(queries, keys, scores, 0, None, None, None)
    peak_ref[...] = jnp.broadcast_to(peak, peak_ref.shape)
    sums_ref[...] = sums
    added_ref[...] = added


def late_kernel(
    width,
    sources,
    counts,
    early,
    own_query_ref,
    peak_ref,
    sums_ref,
    added_ref,
    resid_ref,
    gain_ref,
    score_ref,
    mix_weight_ref,
    *refs,
):
    blocks = grouped(refs, counts)
    mid_ref, swap_ref, scores, mid, halo, sizes = refs[sum(counts) :]
    place = lax.axis_index("rows")
    core = place % 2
    chip = place // 2
    own, channels = own_query_ref.shape
    devices = len(sources[0])

    for block, origin in zip(blocks, sources):
        for step, part, low in ((-1, block[-1], 0), (1, block[0], width)):
            rows = part.shape[0] - EXTRA
            first = rows - width if step < 0 else 0
            takers = [d for d in range(devices) if origin[d] == d // 2 + step]
            if not takers:
                continue
            wanted = place == takers[0]
            for d in takers[1:]:
                wanted = jnp.logical_or(wanted, place == d)

            @pl.when(wanted)
            def _(part=part, rows=rows, first=first, low=low):
                halo[low : low + width] = part[first : first + width, :]
                sizes[low // width] = part[rows : rows + EXTRA, : 2 * width]

    no_above = chip == 0
    no_below = chip == devices // 2 - 1

    @pl.when(no_above)
    def _():
        halo[:width] = jnp.zeros((width, channels), BF16)
        sizes[0] = jnp.zeros((EXTRA, 2 * width), BF16)

    @pl.when(no_below)
    def _():
        halo[width:] = jnp.zeros((width, channels), BF16)
        sizes[1] = jnp.zeros((EXTRA, 2 * width), BF16)

    def column(index):
        parts = sizes[index].astype(F32)
        line = parts[0:1] + parts[1:2]
        return jnp.transpose(jnp.broadcast_to(line, (128, 2 * width)))[:, :1]

    edge_rows = halo[...]
    edge_size = jnp.concatenate([column(0)[width:], column(1)[:width]], axis=0)
    edge_resid = edge_rows.astype(F32) * edge_size / gain_ref[...].reshape(1, channels)
    edge_query = lead(edge_rows, score_ref)
    keys = [whole(parts) for parts in blocks]
    _, edge_sums, edge_added = attend(edge_query, keys, scores, own, None, None, None)
    _, own_sums, own_added = attend(
        own_query_ref[...],
        keys[early:],
        scores,
        0,
        peak_ref[:, :1],
        sums_ref[...],
        added_ref[...],
    )

    def finish(added, sums):
        return (added / jnp.sum(sums, axis=-1, keepdims=True)).astype(BF16)

    mixed = jnp.concatenate([finish(own_added, own_sums), finish(edge_added, edge_sums)], axis=0)
    projected = jnp.dot(mixed, mix_weight_ref[...], preferred_element_type=F32)
    inner = own + width
    mid[width:inner] = (resid_ref[...] + projected[:own]).astype(BF16)
    edges = edge_resid + projected[own:]
    mid[:width] = jnp.where(no_above, 0.0, edges[:width]).astype(BF16)
    mid[inner:] = jnp.where(no_below, 0.0, edges[width:]).astype(BF16)
    mid_ref[...] = mid[pl.ds(pl.multiple_of(2 * core * width, width), 4 * width), :]
    swap_ref[...] = mid[pl.ds(pl.multiple_of(2 * (1 - core) * width, width), 4 * width), :]


def up_kernel(width, mid_ref, swap_ref, weight_ref, out_ref, results, sems):
    core = lax.axis_index("rows") % 2
    channels = mid_ref.shape[1]
    outputs = weight_ref.shape[2]
    wide = 2 * width
    lane = lax.broadcasted_iota(jnp.int32, (1, wide), 1)
    low = lax.broadcasted_iota(jnp.int32, (width, wide), 0)
    spread = (lax.broadcasted_iota(jnp.int32, (width, wide), 1) // 2 == low).astype(BF16)
    lhs = jnp.concatenate(
        [weight_ref[j].reshape(3 * outputs, channels) for j in range(3)], axis=1
    )
    stores = []
    for slot, ref, frame in ((0, mid_ref, core), (1, swap_ref, 1 - core)):
        rows = [
            lax.dot_general(
                ref[row * width : (row + 1) * width],
                spread,
                (((0,), (0,)), ((), ())),
                preferred_element_type=F32,
            ).astype(BF16)
            for row in range(4)
        ]
        for phase in range(2):
            pairs = [(0, 1, 1), (1, 2, 2)] if phase == 0 else [(1, 1, 2), (2, 2, 3)]
            rhs = jnp.concatenate(
                [jnp.concatenate([rows[p] for p in picks], axis=0) for picks in pairs], axis=1
            )
            taps = jnp.dot(lhs, rhs, preferred_element_type=F32)
            for i in range(2):
                left, middle, right = (
                    taps[col * outputs : (col + 1) * outputs, i * wide : (i + 1) * wide]
                    for col in range(3)
                )
                result = middle + jnp.where(lane == 0, 0.0, pltpu.roll(left, 1, axis=1))
                result = result + jnp.where(
                    lane == wide - 1, 0.0, pltpu.roll(right, wide - 1, axis=1)
                )
                results[slot, 2 * i + phase] = result.astype(BF16)
        stores = stores + start_all([(results.at[slot], out_ref.at[frame])], sems, slot)
    wait_all(stores)


def gather_blocks(block, halves, count):
    chips = count // 2
    depth = 2 if chips % 2 == 0 else 1
    length = chips // depth

    ring = [0] + list(range(1, length, 2)) + list(range(2, length, 2))[::-1]
    follow = {a: ring[(i + 1) % length] for i, a in enumerate(ring)}
    forth = {a * depth + b: follow[a] * depth + b for a in range(length) for b in range(depth)}
    return_ = {target: source for source, target in forth.items()}
    onward = (forth, return_)
    backward = (return_, forth)
    across = ({k: k ^ 1 for k in range(chips)},) * 2

    def send(parts, targets):
        pairs = [(2 * k + c, 2 * targets[c][k] + c) for k in range(chips) for c in range(2)]
        return [lax.ppermute(part, "rows", pairs) for part in parts]

    def moved(origin, targets):
        return tuple({targets[c][k]: origin[c][k] for k in range(chips)} for c in range(2))

    def tie(*places):
        fixed = lax.optimization_barrier(tuple(where[i] for where, i in places))
        for (where, i), value in zip(places, fixed):
            where[i] = value

    here = ({k: k for k in range(chips)},) * 2
    early, late = [([block], here)], []
    own_again = [block]
    crossed = last = None
    if depth == 2:
        crossed = send([block], across)
    steps = length - 2
    parts, origin = list(halves), here
    for step in range(1, steps + 1):
        parts, origin = send(parts, onward), moved(origin, onward)
        for h in range(2):
            places = [(parts, h)]
            if last:
                places.append((last, h))
            if step == 1 and h == 1:
                places.append((own_again, 0))
                if depth == 2:
                    places.append((crossed, 0))
            tie(*places)
        early.append((parts, origin))
        if depth == 2:
            last = send(parts, across)
            (late if step == steps else early).append((last, moved(origin, across)))
    if length > 1:
        late.append((send(own_again, backward), moved(here, backward)))
    if depth == 2:
        (early if length > 1 else late).append((crossed, moved(here, across)))
        if length > 1:
            if steps > 0:
                crossed = list(crossed)
                tie((crossed, 0), (parts, 0))
            late.append((send(crossed, backward), moved(moved(here, across), backward)))
    return early, late


def shards(
    latents,
    conv_cache,
    norm_gain,
    conv_weight,
    attn_gain,
    query_weight,
    key_weight,
    value_weight,
    out_weight,
    up_weight,
):
    frames, rows_here, width, channels = latents.shape
    outputs = up_weight.shape[3]
    count = lax.axis_size("rows")
    span = 2 * rows_here * width
    own = rows_here * width
    edge = jax.ShapeDtypeStruct((width, channels), BF16)
    anywhere = pl.BlockSpec(memory_space=pl.ANY)
    hbm = pl.BlockSpec(memory_space=pltpu.HBM)

    chips = count // 2
    swap = [(2 * k + c, 2 * k + 1 - c) for k in range(chips) for c in range(2)]
    neighbour = [(2 * k + 1, 2 * k + 2) for k in range(chips - 1)]
    neighbour = neighbour + [(target, source) for source, target in neighbour]

    latents_in = pltpu.with_memory_space_constraint(latents, pltpu.HBM)
    cache_in = pltpu.with_memory_space_constraint(conv_cache, pltpu.HBM)
    edge_rows, both = pl.pallas_call(
        edges_kernel,
        out_shape=(
            jax.ShapeDtypeStruct((2 * frames, width, channels), BF16),
            jax.ShapeDtypeStruct((3, rows_here, width, channels), BF16),
        ),
        in_specs=[hbm] * 2,
        out_specs=(anywhere,) * 2,
        scratch_shapes=[pltpu.SemaphoreType.DMA((5,))],
        cost_estimate=cost(0, 20 * width * channels),
        compiler_params=params(4),
    )(latents_in, cache_in)
    edge_rows = lax.ppermute(edge_rows, "rows", neighbour)
    both = lax.ppermute(both, "rows", swap)
    act, own_rows, staged = pl.pallas_call(
        prepare_kernel,
        out_shape=(
            jax.ShapeDtypeStruct((frames, own, channels), BF16),
            jax.ShapeDtypeStruct((3, own, channels), BF16),
            jax.ShapeDtypeStruct((3, 3, channels, 3 * channels), BF16),
        ),
        in_specs=[hbm] * 4,
        out_specs=(anywhere, vmem(), anywhere),
        scratch_shapes=[
            pltpu.VMEM((frames, own, channels), BF16),
            pltpu.VMEM((frames, own, channels), BF16),
            pltpu.VMEM((channels,), F32),
            pltpu.VMEM((frames, own, channels), BF16),
            pltpu.SemaphoreType.DMA((13,)),
        ],
        cost_estimate=cost(10 * frames * own * channels, 2 * 27 * channels * channels),
        compiler_params=params(8),
    )(
        pltpu.with_memory_space_constraint(latents.reshape(frames, own, channels), pltpu.HBM),
        pltpu.with_memory_space_constraint(conv_cache.reshape(frames, own, channels), pltpu.HBM),
        pltpu.with_memory_space_constraint(conv_weight, pltpu.HBM),
        pltpu.with_memory_space_constraint(norm_gain, pltpu.HBM),
    )

    edge_rows, own_rows = lax.optimization_barrier((edge_rows, own_rows))
    far_rows = lax.ppermute(edge_rows, "rows", swap)
    block = jax.ShapeDtypeStruct((span + EXTRA, channels), BF16)
    half = jax.ShapeDtypeStruct((span // 2 + EXTRA, channels), BF16)
    sent, front, back, resid = pl.pallas_call(
        functools.partial(conv_kernel, width),
        out_shape=(block, half, half, jax.ShapeDtypeStruct((span, channels), F32)),
        in_specs=[vmem()] * 7,
        out_specs=(vmem(),) * 4,
        scratch_shapes=[
            pltpu.VMEM((3, 6 * width, channels), BF16),
            pltpu.VMEM((6 * width, channels), BF16),
            pltpu.VMEM((6 * width, channels), BF16),
            pltpu.VMEM((span, 3 * channels), F32),
        ],
        cost_estimate=cost(2 * 27 * span * channels * channels, 2 * 27 * channels * channels),
        compiler_params=params(20),
    )(
        own_rows,
        both.reshape(3, own, channels),
        edge_rows,
        far_rows,
        norm_gain,
        attn_gain,
        staged,
    )

    early, late = gather_blocks(sent, (front, back), count)
    blocks = early + late
    sources = [[origin[d % 2][d // 2] for d in range(count)] for _, origin in blocks]
    counts = [len(parts) for parts, _ in blocks]
    early_parts = [part for parts, _ in early for part in parts]
    all_parts = [part for parts, _ in blocks for part in parts]

    scale = channels ** (-0.5) * 1.4426950408889634
    square = jax.ShapeDtypeStruct((channels, channels), BF16)
    score_weight, mix_weight = pl.pallas_call(
        functools.partial(fuse_kernel, scale),
        out_shape=(square, square),
        in_specs=[vmem()] * 4,
        out_specs=(vmem(),) * 2,
        cost_estimate=cost(4 * channels**3, 12 * channels * channels),
        compiler_params=params(8),
    )(query_weight, key_weight, value_weight, out_weight)

    wide = span + 2 * width
    lanes = jax.ShapeDtypeStruct((span, 128), F32)
    own_query, peak, sums, added = pl.pallas_call(
        functools.partial(early_kernel, counts[: len(early)]),
        out_shape=(
            jax.ShapeDtypeStruct((span, channels), BF16),
            lanes,
            lanes,
            jax.ShapeDtypeStruct((span, channels), F32),
        ),
        in_specs=[vmem()] * (1 + len(early_parts)),
        out_specs=(vmem(),) * 4,
        scratch_shapes=[pltpu.VMEM((len(early), span, span), F32)],
        cost_estimate=cost(
            4 * span * span * len(early) * channels,
            2 * span * channels * len(early),
            span * span * len(early),
        ),
        compiler_params=params(24),
    )(score_weight, *early_parts)

    mid, swap_rows = pl.pallas_call(
        functools.partial(late_kernel, width, sources, counts, len(early)),
        out_shape=(jax.ShapeDtypeStruct((4 * width, channels), BF16),) * 2,
        in_specs=[vmem()] * (8 + len(all_parts)),
        out_specs=(vmem(),) * 2,
        scratch_shapes=[
            pltpu.VMEM((len(blocks), wide, span), F32),
            pltpu.VMEM((wide, channels), BF16),
            pltpu.VMEM((2 * width, channels), BF16),
            pltpu.VMEM((2, EXTRA, 2 * width), BF16),
        ],
        cost_estimate=cost(
            2 * wide * span * len(blocks) * channels,
            2 * span * channels * len(blocks),
            wide * span * len(blocks) // 2,
        ),
        compiler_params=params(28),
    )(
        own_query,
        peak,
        sums,
        added,
        resid,
        attn_gain,
        score_weight,
        mix_weight,
        *all_parts,
    )

    swap_rows = lax.ppermute(swap_rows, "rows", swap)

    fine_shape = (2 * rows_here, outputs, 2 * width)
    decoded = pl.pallas_call(
        functools.partial(up_kernel, width),
        out_shape=jax.ShapeDtypeStruct((frames, *fine_shape), BF16),
        in_specs=[vmem()] * 3,
        out_specs=anywhere,
        scratch_shapes=[
            pltpu.VMEM((2, *fine_shape), BF16),
            pltpu.SemaphoreType.DMA((2,)),
        ],
        cost_estimate=cost(
            2 * 9 * outputs * channels * 16 * width, 2 * 9 * outputs * channels
        ),
        compiler_params=params(24),
    )(mid, swap_rows, jnp.transpose(up_weight, (0, 1, 3, 2)))
    decoded = jnp.transpose(decoded, (0, 1, 3, 2))
    return (decoded, act.reshape(frames, rows_here, width, channels))


def solution(mesh):
    return jax.shard_map(
        shards,
        mesh=mesh,
        in_specs=(
            P("videos", "rows", None, None),
            P("videos", "rows", None, None),
            P(),
            P(),
            P(),
            P(),
            P(),
            P(),
            P(),
            P(),
        ),
        out_specs=(P("videos", "rows", None, None), P("videos", "rows", None, None)),
        check_vma=False,
    )
```

```python
import functools

import jax
import jax.numpy as jnp
from jax import lax
from jax.experimental import pallas as pl
from jax.experimental.pallas import tpu as pltpu
from jax.sharding import PartitionSpec as P

BF16 = jnp.bfloat16
F32 = jnp.float32
EPS = 1e-06
MIB = 1024 * 1024
EXTRA = 16


def normalize(values, gain):
    return values * lax.rsqrt(jnp.mean(values * values, axis=-1, keepdims=True) + EPS) * gain


def activate(values, gain):
    normed = normalize(values.astype(F32), gain)
    return (normed / (1.0 + jnp.exp(-normed))).astype(BF16)


def vmem():
    return pl.BlockSpec(memory_space=pltpu.VMEM)


def params(mib):
    return pltpu.CompilerParams(vmem_limit_bytes=mib * MIB)


def cost(flops, size, exps=0):
    return pl.CostEstimate(flops=flops, bytes_accessed=size, transcendentals=exps)


def edges_kernel(latents_ref, cache_ref, edge_ref, both_ref, sems):
    core = lax.axis_index("rows") % 2
    row = core * (latents_ref.shape[1] - 1)
    copies = [
        pltpu.make_async_copy(cache_ref.at[:, row], edge_ref.at[pl.ds(0, 2)], sems.at[0]),
        pltpu.make_async_copy(latents_ref.at[:, row], edge_ref.at[pl.ds(2, 2)], sems.at[1]),
        pltpu.make_async_copy(cache_ref.at[1], both_ref.at[core], sems.at[2]),
        pltpu.make_async_copy(latents_ref.at[0], both_ref.at[1 + core], sems.at[3]),
    ]
    for copy in copies:
        copy.start()

    @pl.when(core == 0)
    def _():
        last = pltpu.make_async_copy(latents_ref.at[1], both_ref.at[2], sems.at[4])
        last.start()
        last.wait()

    @pl.when(core == 1)
    def _():
        last = pltpu.make_async_copy(cache_ref.at[0], both_ref.at[0], sems.at[4])
        last.start()
        last.wait()

    for copy in copies:
        copy.wait()


def start_all(pairs, sems, first=0):
    copies = [
        pltpu.make_async_copy(source, target, sems.at[first + i])
        for i, (source, target) in enumerate(pairs)
    ]
    for copy in copies:
        copy.start()
    return copies


def wait_all(copies):
    for copy in copies:
        copy.wait()


def prepare_kernel(
    latents_ref,
    cache_ref,
    weight_ref,
    gain_ref,
    act_ref,
    own_ref,
    staged_ref,
    latents,
    cache,
    gain,
    act,
    sems,
):
    channels = latents_ref.shape[-1]
    core = lax.axis_index("rows") % 2
    loads = start_all([(latents_ref, latents), (cache_ref, cache), (gain_ref, gain)], sems)
    stages = start_all(
        [
            (
                weight_ref.at[time, :, col],
                staged_ref.at[time, :, :, pl.ds(col * channels, channels)],
            )
            for time in range(3)
            for col in range(3)
        ],
        sems,
        4,
    )
    wait_all(loads)
    act[...] = activate(latents[...], gain[...].reshape(1, channels))
    store = start_all([(act, act_ref)], sems, 3)
    own_ref[0] = cache[core]
    own_ref[1] = jnp.where(core == 0, cache[1], latents[0])
    own_ref[2] = latents[core]
    wait_all(store + stages)


def conv_kernel(
    width,
    own_ref,
    swap_ref,
    edge_ref,
    far_ref,
    norm_gain_ref,
    attn_gain_ref,
    weights,
    sent_ref,
    front_ref,
    back_ref,
    resid_ref,
    raw,
    second,
    third,
    total,
):
    channels = own_ref.shape[-1]
    core = lax.axis_index("rows") % 2
    own = 2 * width
    span = 4 * width
    gain = norm_gain_ref[...].reshape(1, channels)

    def put(index, values):
        rows = pl.ds(pl.multiple_of(index * width, width), values.shape[1])
        raw[:, rows, :] = values

    put(1 + 2 * core, own_ref[...])
    put(3 - 2 * core, swap_ref[...])
    put(5 * core, edge_ref[pl.ds(core, 3)])
    put(5 * (1 - core), far_ref[pl.ds(core, 3)])

    def taps(ref, time):
        lhs = jnp.concatenate([ref[row * width : row * width + span] for row in range(3)], axis=1)
        rhs = weights[time].reshape(3 * channels, 3 * channels)
        return jnp.dot(lhs, rhs, preferred_element_type=F32)

    total[...] = taps(raw.at[0], 0)
    second[...] = jnp.where(core == 1, activate(raw[1], gain), raw[1])
    third[...] = activate(raw[2], gain)
    total[...] += taps(second, 1)
    total[...] += taps(third, 2)

    column = lax.broadcasted_iota(jnp.int32, (span, 1), 0) % width
    left = pltpu.roll(total[:, :channels], 1, axis=0)
    right = pltpu.roll(total[:, 2 * channels :], span - 1, axis=0)
    conv_out = total[:, channels : 2 * channels]
    conv_out = conv_out + jnp.where(column == 0, 0.0, left)
    conv_out = conv_out + jnp.where(column == width - 1, 0.0, right)
    resid = raw[2, width : width + span].astype(F32) + conv_out
    resid_ref[...] = resid
    size = jnp.mean(resid * resid, axis=-1, keepdims=True) + EPS
    normed = resid * lax.rsqrt(size) * attn_gain_ref[...].reshape(1, channels)
    edges = jnp.sqrt(jnp.concatenate([size[:width], size[span - width :]], axis=0))
    across = jnp.transpose(jnp.broadcast_to(edges, (2 * width, 128)))[:EXTRA]
    high = across.astype(BF16).astype(F32)
    line = lax.broadcasted_iota(jnp.int32, (EXTRA, 1), 0)
    extra = jnp.where(line == 0, high, jnp.where(line == 1, across - high, 0.0)).astype(BF16)
    half = span // 2
    for ref, low, count in ((sent_ref, 0, span), (front_ref, 0, half), (back_ref, half, half)):
        ref[:count] = normed[low : low + count].astype(BF16)
        ref[count:] = jnp.zeros((EXTRA, channels), BF16)
        ref[count:, : 2 * width] = extra


def nt_dot(a, b):
    return lax.dot_general(a, b, (((1,), (1,)), ((), ())), preferred_element_type=F32)


def whole(parts):
    rows = [part[: part.shape[0] - EXTRA] for part in parts]
    return rows[0] if len(rows) == 1 else jnp.concatenate(rows, axis=0)


def grouped(refs, counts):
    blocks, first = [], 0
    for count in counts:
        blocks.append(refs[first : first + count])
        first += count
    return blocks


def fold(values, combine, total):
    for lane in range(0, values.shape[1], 128):
        piece = values[:, lane : lane + 128]
        total = piece if total is None else combine(total, piece)
    return total


def attend(queries, keys, scores, start, peak, sums, added):
    height = queries.shape[0]
    top = None
    for i, key in enumerate(keys):
        part = nt_dot(queries, key)
        scores[i, start : start + height] = part
        top = fold(part, jnp.maximum, top)
    top = jnp.max(top, axis=-1, keepdims=True)
    if peak is not None:
        top = jnp.maximum(top, peak)
        shrink = jnp.exp2(peak - top)
        sums = sums * shrink
        added = added * shrink
    for i, key in enumerate(keys):
        weights = jnp.exp2(scores[i, start : start + height] - top)
        sums = fold(weights, jnp.add, sums)
        part = jnp.dot(weights.astype(BF16), key, preferred_element_type=F32)
        added = part if added is None else added + part
    return top, sums, added


def fuse_kernel(scale, query_ref, key_ref, value_ref, out_ref, score_ref, mix_ref):
    score_ref[...] = (nt_dot(query_ref[...], key_ref[...]) * scale).astype(BF16)
    mix_ref[...] = jnp.dot(
        value_ref[...], out_ref[...], preferred_element_type=F32
    ).astype(BF16)


def lead(rows, score_weight):
    return jnp.dot(rows, score_weight[...], preferred_element_type=F32).astype(BF16)


def early_kernel(counts, score_ref, *refs):
    blocks = grouped(refs, counts)
    own_query_ref, peak_ref, sums_ref, added_ref, scores = refs[-5:]
    keys = [whole(parts) for parts in blocks]
    queries = lead(keys[0], score_ref)
    own_query_ref[...] = queries
    peak, sums, added = attend(queries, keys, scores, 0, None, None, None)
    peak_ref[...] = jnp.broadcast_to(peak, peak_ref.shape)
    sums_ref[...] = sums
    added_ref[...] = added


def middle_kernel(
    width,
    sources,
    counts,
    early,
    own_query_ref,
    peak_ref,
    sums_ref,
    added_ref,
    gain_ref,
    score_ref,
    *refs,
):
    blocks = grouped(refs, counts)
    query_out, peak_out, sums_out, added_out, resid_out, scores, halo, sizes = refs[sum(counts) :]
    place = lax.axis_index("rows")
    chip = place // 2
    own, channels = own_query_ref.shape
    devices = len(sources[0])

    for block, origin in zip(blocks, sources):
        for step, part, low in ((-1, block[-1], 0), (1, block[0], width)):
            rows = part.shape[0] - EXTRA
            first = rows - width if step < 0 else 0
            takers = [d for d in range(devices) if origin[d] == d // 2 + step]
            if not takers:
                continue
            wanted = place == takers[0]
            for d in takers[1:]:
                wanted = jnp.logical_or(wanted, place == d)

            @pl.when(wanted)
            def _(part=part, rows=rows, first=first, low=low):
                halo[low : low + width] = part[first : first + width, :]
                sizes[low // width] = part[rows : rows + EXTRA, : 2 * width]

    @pl.when(chip == 0)
    def _():
        halo[:width] = jnp.zeros((width, channels), BF16)
        sizes[0] = jnp.zeros((EXTRA, 2 * width), BF16)

    @pl.when(chip == devices // 2 - 1)
    def _():
        halo[width:] = jnp.zeros((width, channels), BF16)
        sizes[1] = jnp.zeros((EXTRA, 2 * width), BF16)

    def column(index):
        parts = sizes[index].astype(F32)
        line = parts[0:1] + parts[1:2]
        return jnp.transpose(jnp.broadcast_to(line, (128, 2 * width)))[:, :1]

    edge_rows = halo[...]
    edge_size = jnp.concatenate([column(0)[width:], column(1)[:width]], axis=0)
    resid_out[...] = edge_rows.astype(F32) * edge_size / gain_ref[...].reshape(1, channels)
    edge_query = lead(edge_rows, score_ref)
    keys = [whole(parts) for parts in blocks]
    edge = attend(edge_query, keys, scores, own, None, None, None)
    mine = attend(
        own_query_ref[...],
        keys[early:],
        scores,
        0,
        peak_ref[:, :1],
        sums_ref[...],
        added_ref[...],
    )
    query_out[:own] = own_query_ref[...]
    query_out[own:] = edge_query
    for rows, state in ((slice(0, own), mine), (slice(own, None), edge)):
        peak_out[rows] = jnp.broadcast_to(state[0], state[1].shape)
        sums_out[rows] = state[1]
        added_out[rows] = state[2]


def late_kernel(
    width,
    counts,
    query_ref,
    peak_ref,
    sums_ref,
    added_ref,
    resid_ref,
    edge_resid_ref,
    mix_weight_ref,
    *refs,
):
    blocks = grouped(refs, counts)
    mid_ref, swap_ref, scores, mid = refs[sum(counts) :]
    place = lax.axis_index("rows")
    core = place % 2
    own, channels = resid_ref.shape
    sums, added = sums_ref[...], added_ref[...]
    if blocks:
        keys = [whole(parts) for parts in blocks]
        _, sums, added = attend(query_ref[...], keys, scores, 0, peak_ref[:, :1], sums, added)
    mixed = (added / jnp.sum(sums, axis=-1, keepdims=True)).astype(BF16)
    projected = jnp.dot(mixed, mix_weight_ref[...], preferred_element_type=F32)
    inner = own + width
    mid[width:inner] = (resid_ref[...] + projected[:own]).astype(BF16)
    edges = edge_resid_ref[...] + projected[own:]
    no_above = place < 2
    no_below = place >= lax.axis_size("rows") - 2
    mid[:width] = jnp.where(no_above, 0.0, edges[:width]).astype(BF16)
    mid[inner:] = jnp.where(no_below, 0.0, edges[width:]).astype(BF16)
    mid_ref[...] = mid[pl.ds(pl.multiple_of(2 * core * width, width), 4 * width), :]
    swap_ref[...] = mid[pl.ds(pl.multiple_of(2 * (1 - core) * width, width), 4 * width), :]


def up_kernel(width, mid_ref, swap_ref, weight_ref, out_ref, results, sems):
    core = lax.axis_index("rows") % 2
    channels = mid_ref.shape[1]
    outputs = weight_ref.shape[2]
    span = 4 * width
    wide = 2 * width
    column = lax.broadcasted_iota(jnp.int32, (1, span), 1) % width
    line = lax.broadcasted_iota(jnp.int32, (2 * wide, 2 * wide), 0)
    lane = lax.broadcasted_iota(jnp.int32, (2 * wide, 2 * wide), 1)
    target = 2 * (line % wide) + line // wide
    weave = (target == lane).astype(BF16)
    lhs = jnp.concatenate(
        [weight_ref[j].reshape(3 * outputs, channels) for j in range(3)], axis=1
    )
    picks = ((0, 1, 1), (1, 1, 2), (1, 2, 2), (2, 2, 3))
    stores = []
    for slot, ref, frame in ((0, mid_ref, core), (1, swap_ref, 1 - core)):
        turned = jnp.transpose(ref[...].astype(F32)).astype(BF16)
        rows = [turned[:, row * width : (row + 1) * width] for row in range(4)]
        rhs = jnp.concatenate(
            [jnp.concatenate([rows[pick[j]] for pick in picks], axis=1) for j in range(3)], axis=0
        )
        taps = jnp.dot(lhs, rhs, preferred_element_type=F32)
        left, middle, right = (taps[col * outputs : (col + 1) * outputs] for col in range(3))
        even = middle + right + jnp.where(column == 0, 0.0, pltpu.roll(left, 1, axis=1))
        odd = left + middle
        odd = odd + jnp.where(column == width - 1, 0.0, pltpu.roll(right, span - 1, axis=1))
        even, odd = even.astype(BF16), odd.astype(BF16)
        for pair in range(2):
            both = slice(pair * wide, (pair + 1) * wide)
            mixed = jnp.concatenate([even[:, both], odd[:, both]], axis=1)
            woven = jnp.dot(mixed, weave, preferred_element_type=F32).astype(BF16)
            for i in range(2):
                results[slot, 2 * pair + i] = woven[:, i * wide : (i + 1) * wide]
        stores = stores + start_all([(results.at[slot], out_ref.at[frame])], sems, slot)
    wait_all(stores)


def gather_blocks(block, halves, count):
    chips = count // 2
    depth = 2 if chips % 2 == 0 else 1
    length = chips // depth

    ring = [0] + list(range(1, length, 2)) + list(range(2, length, 2))[::-1]
    follow = {a: ring[(i + 1) % length] for i, a in enumerate(ring)}
    forth = {a * depth + b: follow[a] * depth + b for a in range(length) for b in range(depth)}
    return_ = {target: source for source, target in forth.items()}
    onward = (forth, return_)
    backward = (return_, forth)
    across = ({k: k ^ 1 for k in range(chips)},) * 2

    def send(parts, targets):
        pairs = [(2 * k + c, 2 * targets[c][k] + c) for k in range(chips) for c in range(2)]
        return [lax.ppermute(part, "rows", pairs) for part in parts]

    def moved(origin, targets):
        return tuple({targets[c][k]: origin[c][k] for k in range(chips)} for c in range(2))

    def tie(*places):
        fixed = lax.optimization_barrier(tuple(where[i] for where, i in places))
        for (where, i), value in zip(places, fixed):
            where[i] = value

    here = ({k: k for k in range(chips)},) * 2
    early, late = [([block], here)], []
    own_again = [block]
    crossed = last = None
    if depth == 2:
        crossed = send([block], across)
    steps = length - 2
    parts, origin = list(halves), here
    for step in range(1, steps + 1):
        parts, origin = send(parts, onward), moved(origin, onward)
        for h in range(2):
            places = [(parts, h)]
            if last:
                places.append((last, h))
            if step == 1 and h == 1 and depth == 2:
                places.append((crossed, 0))
            tie(*places)
        early.append((parts, origin))
        if depth == 2:
            last = send(parts, across)
            (late if step == steps else early).append((last, moved(origin, across)))
    if depth == 2:
        (early if length > 1 else late).append((crossed, moved(here, across)))
        if length > 1:
            far = send(crossed, backward)
            late.append((far, moved(moved(here, across), backward)))
    final = []
    if length > 1:
        if steps > 0:
            tie((own_again, 0), (parts, 0))
        final.append((send(own_again, backward), moved(here, backward)))
    return early, late, final


def shards(
    latents,
    conv_cache,
    norm_gain,
    conv_weight,
    attn_gain,
    query_weight,
    key_weight,
    value_weight,
    out_weight,
    up_weight,
):
    frames, rows_here, width, channels = latents.shape
    outputs = up_weight.shape[3]
    count = lax.axis_size("rows")
    span = 2 * rows_here * width
    own = rows_here * width
    edge = jax.ShapeDtypeStruct((width, channels), BF16)
    anywhere = pl.BlockSpec(memory_space=pl.ANY)
    hbm = pl.BlockSpec(memory_space=pltpu.HBM)

    chips = count // 2
    swap = [(2 * k + c, 2 * k + 1 - c) for k in range(chips) for c in range(2)]
    neighbour = [(2 * k + 1, 2 * k + 2) for k in range(chips - 1)]
    neighbour = neighbour + [(target, source) for source, target in neighbour]

    latents_in = pltpu.with_memory_space_constraint(latents, pltpu.HBM)
    cache_in = pltpu.with_memory_space_constraint(conv_cache, pltpu.HBM)
    edge_rows, both = pl.pallas_call(
        edges_kernel,
        out_shape=(
            jax.ShapeDtypeStruct((2 * frames, width, channels), BF16),
            jax.ShapeDtypeStruct((3, rows_here, width, channels), BF16),
        ),
        in_specs=[hbm] * 2,
        out_specs=(anywhere,) * 2,
        scratch_shapes=[pltpu.SemaphoreType.DMA((5,))],
        cost_estimate=cost(0, 20 * width * channels),
        compiler_params=params(4),
    )(latents_in, cache_in)
    edge_rows = lax.ppermute(edge_rows, "rows", neighbour)
    both = lax.ppermute(both, "rows", swap)
    act, own_rows, staged = pl.pallas_call(
        prepare_kernel,
        out_shape=(
            jax.ShapeDtypeStruct((frames, own, channels), BF16),
            jax.ShapeDtypeStruct((3, own, channels), BF16),
            jax.ShapeDtypeStruct((3, 3, channels, 3 * channels), BF16),
        ),
        in_specs=[hbm] * 4,
        out_specs=(anywhere, vmem(), anywhere),
        scratch_shapes=[
            pltpu.VMEM((frames, own, channels), BF16),
            pltpu.VMEM((frames, own, channels), BF16),
            pltpu.VMEM((channels,), F32),
            pltpu.VMEM((frames, own, channels), BF16),
            pltpu.SemaphoreType.DMA((13,)),
        ],
        cost_estimate=cost(10 * frames * own * channels, 2 * 27 * channels * channels),
        compiler_params=params(8),
    )(
        pltpu.with_memory_space_constraint(latents.reshape(frames, own, channels), pltpu.HBM),
        pltpu.with_memory_space_constraint(conv_cache.reshape(frames, own, channels), pltpu.HBM),
        pltpu.with_memory_space_constraint(conv_weight, pltpu.HBM),
        pltpu.with_memory_space_constraint(norm_gain, pltpu.HBM),
    )

    edge_rows, own_rows = lax.optimization_barrier((edge_rows, own_rows))
    far_rows = lax.ppermute(edge_rows, "rows", swap)
    block = jax.ShapeDtypeStruct((span + EXTRA, channels), BF16)
    half = jax.ShapeDtypeStruct((span // 2 + EXTRA, channels), BF16)
    sent, front, back, resid = pl.pallas_call(
        functools.partial(conv_kernel, width),
        out_shape=(block, half, half, jax.ShapeDtypeStruct((span, channels), F32)),
        in_specs=[vmem()] * 7,
        out_specs=(vmem(),) * 4,
        scratch_shapes=[
            pltpu.VMEM((3, 6 * width, channels), BF16),
            pltpu.VMEM((6 * width, channels), BF16),
            pltpu.VMEM((6 * width, channels), BF16),
            pltpu.VMEM((span, 3 * channels), F32),
        ],
        cost_estimate=cost(2 * 27 * span * channels * channels, 2 * 27 * channels * channels),
        compiler_params=params(20),
    )(
        own_rows,
        both.reshape(3, own, channels),
        edge_rows,
        far_rows,
        norm_gain,
        attn_gain,
        staged,
    )

    early, late, final = gather_blocks(sent, (front, back), count)
    blocks = early + late
    sources = [[origin[d % 2][d // 2] for d in range(count)] for _, origin in blocks]
    counts = [len(parts) for parts, _ in blocks]
    early_parts = [part for parts, _ in early for part in parts]
    all_parts = [part for parts, _ in blocks for part in parts]
    final_parts = [part for parts, _ in final for part in parts]

    scale = channels ** (-0.5) * 1.4426950408889634
    square = jax.ShapeDtypeStruct((channels, channels), BF16)
    score_weight, mix_weight = pl.pallas_call(
        functools.partial(fuse_kernel, scale),
        out_shape=(square, square),
        in_specs=[vmem()] * 4,
        out_specs=(vmem(),) * 2,
        cost_estimate=cost(4 * channels**3, 12 * channels * channels),
        compiler_params=params(8),
    )(query_weight, key_weight, value_weight, out_weight)

    wide = span + 2 * width
    lanes = jax.ShapeDtypeStruct((span, 128), F32)
    own_query, peak, sums, added = pl.pallas_call(
        functools.partial(early_kernel, counts[: len(early)]),
        out_shape=(
            jax.ShapeDtypeStruct((span, channels), BF16),
            lanes,
            lanes,
            jax.ShapeDtypeStruct((span, channels), F32),
        ),
        in_specs=[vmem()] * (1 + len(early_parts)),
        out_specs=(vmem(),) * 4,
        scratch_shapes=[pltpu.VMEM((len(early), span, span), F32)],
        cost_estimate=cost(
            4 * span * span * len(early) * channels,
            2 * span * channels * len(early),
            span * span * len(early),
        ),
        compiler_params=params(24),
    )(score_weight, *early_parts)

    wide_lanes = jax.ShapeDtypeStruct((wide, 128), F32)
    query, peak, sums, added, edge_resid = pl.pallas_call(
        functools.partial(middle_kernel, width, sources, counts, len(early)),
        out_shape=(
            jax.ShapeDtypeStruct((wide, channels), BF16),
            wide_lanes,
            wide_lanes,
            jax.ShapeDtypeStruct((wide, channels), F32),
            jax.ShapeDtypeStruct((2 * width, channels), F32),
        ),
        in_specs=[vmem()] * (6 + len(all_parts)),
        out_specs=(vmem(),) * 5,
        scratch_shapes=[
            pltpu.VMEM((len(blocks), wide, span), F32),
            pltpu.VMEM((2 * width, channels), BF16),
            pltpu.VMEM((2, EXTRA, 2 * width), BF16),
        ],
        cost_estimate=cost(
            2 * wide * span * len(blocks) * channels,
            2 * span * channels * len(blocks),
            wide * span * len(blocks) // 2,
        ),
        compiler_params=params(24),
    )(own_query, peak, sums, added, attn_gain, score_weight, *all_parts)

    mid, swap_rows = pl.pallas_call(
        functools.partial(late_kernel, width, [len(parts) for parts, _ in final]),
        out_shape=(jax.ShapeDtypeStruct((4 * width, channels), BF16),) * 2,
        in_specs=[vmem()] * (7 + len(final_parts)),
        out_specs=(vmem(),) * 2,
        scratch_shapes=[
            pltpu.VMEM((max(1, len(final)), wide, span), F32),
            pltpu.VMEM((wide, channels), BF16),
        ],
        cost_estimate=cost(
            4 * wide * span * channels, 8 * wide * channels, wide * span
        ),
        compiler_params=params(16),
    )(query, peak, sums, added, resid, edge_resid, mix_weight, *final_parts)

    swap_rows = lax.ppermute(swap_rows, "rows", swap)

    fine_shape = (2 * rows_here, outputs, 2 * width)
    decoded = pl.pallas_call(
        functools.partial(up_kernel, width),
        out_shape=jax.ShapeDtypeStruct((frames, *fine_shape), BF16),
        in_specs=[vmem()] * 3,
        out_specs=anywhere,
        scratch_shapes=[
            pltpu.VMEM((2, *fine_shape), BF16),
            pltpu.SemaphoreType.DMA((2,)),
        ],
        cost_estimate=cost(
            2 * 9 * outputs * channels * 16 * width, 2 * 9 * outputs * channels
        ),
        compiler_params=params(24),
    )(mid, swap_rows, jnp.transpose(up_weight, (0, 1, 3, 2)))
    decoded = jnp.transpose(decoded, (0, 1, 3, 2))
    return (decoded, act.reshape(frames, rows_here, width, channels))


def solution(mesh):
    return jax.shard_map(
        shards,
        mesh=mesh,
        in_specs=(
            P("videos", "rows", None, None),
            P("videos", "rows", None, None),
            P(),
            P(),
            P(),
            P(),
            P(),
            P(),
            P(),
            P(),
        ),
        out_specs=(P("videos", "rows", None, None), P("videos", "rows", None, None)),
        check_vma=False,
    )
```

```python
import functools

import jax
import jax.numpy as jnp
from jax import lax
from jax.experimental import pallas as pl
from jax.experimental.pallas import tpu as pltpu
from jax.sharding import PartitionSpec as P

BF16 = jnp.bfloat16
F32 = jnp.float32
EPS = 1e-06
MIB = 1024 * 1024
EXTRA = 16


def normalize(values, gain):
    return values * lax.rsqrt(jnp.mean(values * values, axis=-1, keepdims=True) + EPS) * gain


def activate(values, gain):
    normed = normalize(values.astype(F32), gain)
    return (normed / (1.0 + jnp.exp(-normed))).astype(BF16)


def vmem():
    return pl.BlockSpec(memory_space=pltpu.VMEM)


def params(mib):
    return pltpu.CompilerParams(vmem_limit_bytes=mib * MIB)


def cost(flops, size, exps=0):
    return pl.CostEstimate(flops=flops, bytes_accessed=size, transcendentals=exps)


def edges_kernel(latents_ref, cache_ref, edge_ref, both_ref, sems):
    core = lax.axis_index("rows") % 2
    row = core * (latents_ref.shape[1] - 1)
    copies = [
        pltpu.make_async_copy(cache_ref.at[:, row], edge_ref.at[pl.ds(0, 2)], sems.at[0]),
        pltpu.make_async_copy(latents_ref.at[:, row], edge_ref.at[pl.ds(2, 2)], sems.at[1]),
        pltpu.make_async_copy(cache_ref.at[1], both_ref.at[core], sems.at[2]),
        pltpu.make_async_copy(latents_ref.at[0], both_ref.at[1 + core], sems.at[3]),
    ]
    for copy in copies:
        copy.start()

    @pl.when(core == 0)
    def _():
        last = pltpu.make_async_copy(latents_ref.at[1], both_ref.at[2], sems.at[4])
        last.start()
        last.wait()

    @pl.when(core == 1)
    def _():
        last = pltpu.make_async_copy(cache_ref.at[0], both_ref.at[0], sems.at[4])
        last.start()
        last.wait()

    for copy in copies:
        copy.wait()


def start_all(pairs, sems, first=0):
    copies = [
        pltpu.make_async_copy(source, target, sems.at[first + i])
        for i, (source, target) in enumerate(pairs)
    ]
    for copy in copies:
        copy.start()
    return copies


def wait_all(copies):
    for copy in copies:
        copy.wait()


def prepare_kernel(
    latents_ref,
    cache_ref,
    weight_ref,
    gain_ref,
    act_ref,
    own_ref,
    staged_ref,
    latents,
    cache,
    gain,
    act,
    sems,
):
    channels = latents_ref.shape[-1]
    core = lax.axis_index("rows") % 2
    loads = start_all([(latents_ref, latents), (cache_ref, cache), (gain_ref, gain)], sems)
    stages = start_all(
        [
            (
                weight_ref.at[time, :, col],
                staged_ref.at[time, :, :, pl.ds(col * channels, channels)],
            )
            for time in range(3)
            for col in range(3)
        ],
        sems,
        4,
    )
    wait_all(loads)
    act[...] = activate(latents[...], gain[...].reshape(1, channels))
    store = start_all([(act, act_ref)], sems, 3)
    own_ref[0] = cache[core]
    own_ref[1] = jnp.where(core == 0, cache[1], latents[0])
    own_ref[2] = latents[core]
    wait_all(store + stages)


def conv_kernel(
    width,
    own_ref,
    swap_ref,
    edge_ref,
    far_ref,
    norm_gain_ref,
    attn_gain_ref,
    weights,
    sent_ref,
    plain_ref,
    front_ref,
    back_ref,
    resid_ref,
    raw,
    second,
    third,
    total,
):
    channels = own_ref.shape[-1]
    core = lax.axis_index("rows") % 2
    own = 2 * width
    span = 4 * width
    gain = norm_gain_ref[...].reshape(1, channels)

    def put(index, values):
        rows = pl.ds(pl.multiple_of(index * width, width), values.shape[1])
        raw[:, rows, :] = values

    put(1 + 2 * core, own_ref[...])
    put(3 - 2 * core, swap_ref[...])
    put(5 * core, edge_ref[pl.ds(core, 3)])
    put(5 * (1 - core), far_ref[pl.ds(core, 3)])

    def taps(ref, time):
        lhs = jnp.concatenate([ref[row * width : row * width + span] for row in range(3)], axis=1)
        rhs = weights[time].reshape(3 * channels, 3 * channels)
        return jnp.dot(lhs, rhs, preferred_element_type=F32)

    total[...] = taps(raw.at[0], 0)
    second[...] = jnp.where(core == 1, activate(raw[1], gain), raw[1])
    third[...] = activate(raw[2], gain)
    total[...] += taps(second, 1)
    total[...] += taps(third, 2)

    column = lax.broadcasted_iota(jnp.int32, (span, 1), 0) % width
    left = pltpu.roll(total[:, :channels], 1, axis=0)
    right = pltpu.roll(total[:, 2 * channels :], span - 1, axis=0)
    conv_out = total[:, channels : 2 * channels]
    conv_out = conv_out + jnp.where(column == 0, 0.0, left)
    conv_out = conv_out + jnp.where(column == width - 1, 0.0, right)
    resid = raw[2, width : width + span].astype(F32) + conv_out
    resid_ref[...] = resid
    size = jnp.mean(resid * resid, axis=-1, keepdims=True) + EPS
    normed = resid * lax.rsqrt(size) * attn_gain_ref[...].reshape(1, channels)
    edges = jnp.sqrt(jnp.concatenate([size[:width], size[span - width :]], axis=0))
    across = jnp.transpose(jnp.broadcast_to(edges, (2 * width, 128)))[:EXTRA]
    high = across.astype(BF16).astype(F32)
    line = lax.broadcasted_iota(jnp.int32, (EXTRA, 1), 0)
    extra = jnp.where(line == 0, high, jnp.where(line == 1, across - high, 0.0)).astype(BF16)
    normed = normed.astype(BF16)
    half = span // 2
    plain_ref[...] = normed
    back_ref[...] = normed[half:]
    for ref, count in ((sent_ref, span), (front_ref, half)):
        ref[:count] = normed[:count]
        ref[count:] = jnp.zeros((EXTRA, channels), BF16)
        ref[count:, : 2 * width] = extra


def nt_dot(a, b):
    return lax.dot_general(a, b, (((1,), (1,)), ((), ())), preferred_element_type=F32)


def whole(parts, span):
    rows = [part[: span // len(parts)] for part in parts]
    return rows[0] if len(rows) == 1 else jnp.concatenate(rows, axis=0)


def grouped(refs, counts):
    blocks, first = [], 0
    for count in counts:
        blocks.append(refs[first : first + count])
        first += count
    return blocks


def fold(values, combine, total):
    for lane in range(0, values.shape[1], 128):
        piece = values[:, lane : lane + 128]
        total = piece if total is None else combine(total, piece)
    return total


def attend(queries, keys, scores, start, peak, sums, added):
    height = queries.shape[0]
    top = None
    for i, key in enumerate(keys):
        part = nt_dot(queries, key)
        scores[i, start : start + height] = part
        top = fold(part, jnp.maximum, top)
    top = jnp.max(top, axis=-1, keepdims=True)
    if peak is not None:
        top = jnp.maximum(top, peak)
        shrink = jnp.exp2(peak - top)
        sums = sums * shrink
        added = added * shrink
    for i, key in enumerate(keys):
        weights = jnp.exp2(scores[i, start : start + height] - top)
        sums = fold(weights, jnp.add, sums)
        part = jnp.dot(weights.astype(BF16), key, preferred_element_type=F32)
        added = part if added is None else added + part
    return top, sums, added


def fuse_kernel(scale, query_ref, key_ref, value_ref, out_ref, score_ref, mix_ref):
    score_ref[...] = (nt_dot(query_ref[...], key_ref[...]) * scale).astype(BF16)
    mix_ref[...] = jnp.dot(
        value_ref[...], out_ref[...], preferred_element_type=F32
    ).astype(BF16)


def lead(rows, score_weight):
    return jnp.dot(rows, score_weight[...], preferred_element_type=F32).astype(BF16)


def early_kernel(counts, score_ref, *refs):
    blocks = grouped(refs, counts)
    own_query_ref, peak_ref, sums_ref, added_ref, scores = refs[-5:]
    keys = [whole(parts, own_query_ref.shape[0]) for parts in blocks]
    queries = lead(keys[0], score_ref)
    own_query_ref[...] = queries
    peak, sums, added = attend(queries, keys, scores, 0, None, None, None)
    peak_ref[...] = jnp.broadcast_to(peak, peak_ref.shape)
    sums_ref[...] = sums
    added_ref[...] = added


def middle_kernel(
    width,
    sources,
    counts,
    early,
    own_query_ref,
    peak_ref,
    sums_ref,
    added_ref,
    gain_ref,
    score_ref,
    *refs,
):
    blocks = grouped(refs, counts)
    query_out, peak_out, sums_out, added_out, resid_out, scores, halo, sizes = refs[sum(counts) :]
    place = lax.axis_index("rows")
    chip = place // 2
    own, channels = own_query_ref.shape
    devices = len(sources[0])

    for block, origin in zip(blocks, sources):
        rows = own // len(block)
        for step, part, first, low in (
            (-1, block[-1], rows - width, 0),
            (1, block[0], 0, width),
        ):
            takers = [d for d in range(devices) if origin[d] == d // 2 + step]
            if not takers:
                continue
            wanted = place == takers[0]
            for d in takers[1:]:
                wanted = jnp.logical_or(wanted, place == d)

            @pl.when(wanted)
            def _(part=part, notes=block[0], rows=rows, first=first, low=low):
                halo[low : low + width] = part[first : first + width, :]
                sizes[low // width] = notes[rows : rows + EXTRA, : 2 * width]

    @pl.when(chip == 0)
    def _():
        halo[:width] = jnp.zeros((width, channels), BF16)
        sizes[0] = jnp.zeros((EXTRA, 2 * width), BF16)

    @pl.when(chip == devices // 2 - 1)
    def _():
        halo[width:] = jnp.zeros((width, channels), BF16)
        sizes[1] = jnp.zeros((EXTRA, 2 * width), BF16)

    def column(index):
        parts = sizes[index].astype(F32)
        line = parts[0:1] + parts[1:2]
        return jnp.transpose(jnp.broadcast_to(line, (128, 2 * width)))[:, :1]

    edge_rows = halo[...]
    edge_size = jnp.concatenate([column(0)[width:], column(1)[:width]], axis=0)
    resid_out[...] = edge_rows.astype(F32) * edge_size / gain_ref[...].reshape(1, channels)
    edge_query = lead(edge_rows, score_ref)
    keys = [whole(parts, own) for parts in blocks]
    edge = attend(edge_query, keys, scores, own, None, None, None)
    mine = attend(
        own_query_ref[...],
        keys[early:],
        scores,
        0,
        peak_ref[:, :1],
        sums_ref[...],
        added_ref[...],
    )
    query_out[:own] = own_query_ref[...]
    query_out[own:] = edge_query
    for rows, state in ((slice(0, own), mine), (slice(own, None), edge)):
        peak_out[rows] = jnp.broadcast_to(state[0], state[1].shape)
        sums_out[rows] = state[1]
        added_out[rows] = state[2]


def late_kernel(
    width,
    counts,
    query_ref,
    peak_ref,
    sums_ref,
    added_ref,
    resid_ref,
    edge_resid_ref,
    mix_weight_ref,
    *refs,
):
    blocks = grouped(refs, counts)
    mid_ref, swap_ref, scores, mid = refs[sum(counts) :]
    place = lax.axis_index("rows")
    core = place % 2
    own, channels = resid_ref.shape
    sums, added = sums_ref[...], added_ref[...]
    if blocks:
        keys = [whole(parts, own) for parts in blocks]
        _, sums, added = attend(query_ref[...], keys, scores, 0, peak_ref[:, :1], sums, added)
    mixed = (added / jnp.sum(sums, axis=-1, keepdims=True)).astype(BF16)
    projected = jnp.dot(mixed, mix_weight_ref[...], preferred_element_type=F32)
    inner = own + width
    mid[width:inner] = (resid_ref[...] + projected[:own]).astype(BF16)
    edges = edge_resid_ref[...] + projected[own:]
    no_above = place < 2
    no_below = place >= lax.axis_size("rows") - 2
    mid[:width] = jnp.where(no_above, 0.0, edges[:width]).astype(BF16)
    mid[inner:] = jnp.where(no_below, 0.0, edges[width:]).astype(BF16)
    mid_ref[...] = mid[pl.ds(pl.multiple_of(2 * core * width, width), 4 * width), :]
    swap_ref[...] = mid[pl.ds(pl.multiple_of(2 * (1 - core) * width, width), 4 * width), :]


def up_rows(width, ref, weight_ref, out):
    channels = ref.shape[1]
    outputs = weight_ref.shape[2]
    span = 4 * width
    wide = 2 * width
    column = lax.broadcasted_iota(jnp.int32, (1, span), 1) % width
    line = lax.broadcasted_iota(jnp.int32, (2 * wide, 2 * wide), 0)
    lane = lax.broadcasted_iota(jnp.int32, (2 * wide, 2 * wide), 1)
    target = 2 * (line % wide) + line // wide
    weave = (target == lane).astype(BF16)
    lhs = jnp.concatenate(
        [weight_ref[j].reshape(3 * outputs, channels) for j in range(3)], axis=1
    )
    turned = jnp.transpose(ref[...].astype(F32)).astype(BF16)
    rows = [turned[:, row * width : (row + 1) * width] for row in range(4)]
    picks = ((0, 1, 1), (1, 1, 2), (1, 2, 2), (2, 2, 3))
    rhs = jnp.concatenate(
        [jnp.concatenate([rows[pick[j]] for pick in picks], axis=1) for j in range(3)], axis=0
    )
    taps = jnp.dot(lhs, rhs, preferred_element_type=F32)
    left, middle, right = (taps[col * outputs : (col + 1) * outputs] for col in range(3))
    even = middle + right + jnp.where(column == 0, 0.0, pltpu.roll(left, 1, axis=1))
    odd = left + middle
    odd = odd + jnp.where(column == width - 1, 0.0, pltpu.roll(right, span - 1, axis=1))
    even, odd = even.astype(BF16), odd.astype(BF16)
    for pair in range(2):
        both = slice(pair * wide, (pair + 1) * wide)
        mixed = jnp.concatenate([even[:, both], odd[:, both]], axis=1)
        woven = jnp.dot(mixed, weave, preferred_element_type=F32).astype(BF16)
        for i in range(2):
            out[2 * pair + i] = woven[:, i * wide : (i + 1) * wide]


def up_own_kernel(width, rows_ref, weight_ref, out_ref):
    up_rows(width, rows_ref, weight_ref, out_ref)


def up_kernel(width, rows_ref, weight_ref, own_ref, out_ref, result, sems):
    core = lax.axis_index("rows") % 2
    stores = start_all([(own_ref, out_ref.at[core])], sems)
    up_rows(width, rows_ref, weight_ref, result)
    stores = stores + start_all([(result, out_ref.at[1 - core])], sems, 1)
    wait_all(stores)


def gather_blocks(block, plain, halves, count):
    chips = count // 2
    depth = 2 if chips % 2 == 0 else 1
    length = chips // depth

    ring = [0] + list(range(1, length, 2)) + list(range(2, length, 2))[::-1]
    follow = {a: ring[(i + 1) % length] for i, a in enumerate(ring)}
    forth = {a * depth + b: follow[a] * depth + b for a in range(length) for b in range(depth)}
    return_ = {target: source for source, target in forth.items()}
    onward = (forth, return_)
    backward = (return_, forth)
    across = ({k: k ^ 1 for k in range(chips)},) * 2

    def send(parts, targets):
        pairs = [(2 * k + c, 2 * targets[c][k] + c) for k in range(chips) for c in range(2)]
        return [lax.ppermute(part, "rows", pairs) for part in parts]

    def moved(origin, targets):
        return tuple({targets[c][k]: origin[c][k] for k in range(chips)} for c in range(2))

    def tie(*places):
        fixed = lax.optimization_barrier(tuple(where[i] for where, i in places))
        for (where, i), value in zip(places, fixed):
            where[i] = value

    here = ({k: k for k in range(chips)},) * 2
    early, late = [([block], here)], []
    own_again = [plain]
    crossed = last = None
    if depth == 2:
        crossed = send([block], across)
    steps = length - 2
    parts, origin = list(halves), here
    for step in range(1, steps + 1):
        parts, origin = send(parts, onward), moved(origin, onward)
        for h in range(2):
            places = [(parts, h)]
            if last:
                places.append((last, h))
            if step == 1 and h == 1 and depth == 2:
                places.append((crossed, 0))
            tie(*places)
        early.append((parts, origin))
        if depth == 2:
            last = send(parts, across)
            (late if step == steps else early).append((last, moved(origin, across)))
    if depth == 2:
        (early if length > 1 else late).append((crossed, moved(here, across)))
        if length > 1:
            again = list(crossed)
            if steps > 0:
                tie((again, 0), (parts, 0))
            late.append((send(again, backward), moved(moved(here, across), backward)))
    final = []
    if length > 1:
        if steps > 0:
            tie((own_again, 0), (parts, 0))
        final.append((send(own_again, backward), moved(here, backward)))
    return early, late, final


def shards(
    latents,
    conv_cache,
    norm_gain,
    conv_weight,
    attn_gain,
    query_weight,
    key_weight,
    value_weight,
    out_weight,
    up_weight,
):
    frames, rows_here, width, channels = latents.shape
    outputs = up_weight.shape[3]
    count = lax.axis_size("rows")
    span = 2 * rows_here * width
    own = rows_here * width
    edge = jax.ShapeDtypeStruct((width, channels), BF16)
    anywhere = pl.BlockSpec(memory_space=pl.ANY)
    hbm = pl.BlockSpec(memory_space=pltpu.HBM)

    chips = count // 2
    swap = [(2 * k + c, 2 * k + 1 - c) for k in range(chips) for c in range(2)]
    neighbour = [(2 * k + 1, 2 * k + 2) for k in range(chips - 1)]
    neighbour = neighbour + [(target, source) for source, target in neighbour]

    latents_in = pltpu.with_memory_space_constraint(latents, pltpu.HBM)
    cache_in = pltpu.with_memory_space_constraint(conv_cache, pltpu.HBM)
    edge_rows, both = pl.pallas_call(
        edges_kernel,
        out_shape=(
            jax.ShapeDtypeStruct((2 * frames, width, channels), BF16),
            jax.ShapeDtypeStruct((3, rows_here, width, channels), BF16),
        ),
        in_specs=[hbm] * 2,
        out_specs=(anywhere,) * 2,
        scratch_shapes=[pltpu.SemaphoreType.DMA((5,))],
        cost_estimate=cost(0, 20 * width * channels),
        compiler_params=params(4),
    )(latents_in, cache_in)
    edge_rows = lax.ppermute(edge_rows, "rows", neighbour)
    both = lax.ppermute(both, "rows", swap)
    act, own_rows, staged = pl.pallas_call(
        prepare_kernel,
        out_shape=(
            jax.ShapeDtypeStruct((frames, own, channels), BF16),
            jax.ShapeDtypeStruct((3, own, channels), BF16),
            jax.ShapeDtypeStruct((3, 3, channels, 3 * channels), BF16),
        ),
        in_specs=[hbm] * 4,
        out_specs=(anywhere, vmem(), anywhere),
        scratch_shapes=[
            pltpu.VMEM((frames, own, channels), BF16),
            pltpu.VMEM((frames, own, channels), BF16),
            pltpu.VMEM((channels,), F32),
            pltpu.VMEM((frames, own, channels), BF16),
            pltpu.SemaphoreType.DMA((13,)),
        ],
        cost_estimate=cost(10 * frames * own * channels, 2 * 27 * channels * channels),
        compiler_params=params(8),
    )(
        pltpu.with_memory_space_constraint(latents.reshape(frames, own, channels), pltpu.HBM),
        pltpu.with_memory_space_constraint(conv_cache.reshape(frames, own, channels), pltpu.HBM),
        pltpu.with_memory_space_constraint(conv_weight, pltpu.HBM),
        pltpu.with_memory_space_constraint(norm_gain, pltpu.HBM),
    )

    edge_rows, own_rows = lax.optimization_barrier((edge_rows, own_rows))
    far_rows = lax.ppermute(edge_rows, "rows", swap)
    block = jax.ShapeDtypeStruct((span + EXTRA, channels), BF16)
    sent, plain, front, back, resid = pl.pallas_call(
        functools.partial(conv_kernel, width),
        out_shape=(
            block,
            jax.ShapeDtypeStruct((span, channels), BF16),
            jax.ShapeDtypeStruct((span // 2 + EXTRA, channels), BF16),
            jax.ShapeDtypeStruct((span // 2, channels), BF16),
            jax.ShapeDtypeStruct((span, channels), F32),
        ),
        in_specs=[vmem()] * 7,
        out_specs=(vmem(),) * 5,
        scratch_shapes=[
            pltpu.VMEM((3, 6 * width, channels), BF16),
            pltpu.VMEM((6 * width, channels), BF16),
            pltpu.VMEM((6 * width, channels), BF16),
            pltpu.VMEM((span, 3 * channels), F32),
        ],
        cost_estimate=cost(2 * 27 * span * channels * channels, 2 * 27 * channels * channels),
        compiler_params=params(20),
    )(
        own_rows,
        both.reshape(3, own, channels),
        edge_rows,
        far_rows,
        norm_gain,
        attn_gain,
        staged,
    )

    early, late, final = gather_blocks(sent, plain, (front, back), count)
    blocks = early + late
    sources = [[origin[d % 2][d // 2] for d in range(count)] for _, origin in blocks]
    counts = [len(parts) for parts, _ in blocks]
    early_parts = [part for parts, _ in early for part in parts]
    all_parts = [part for parts, _ in blocks for part in parts]
    final_parts = [part for parts, _ in final for part in parts]

    scale = channels ** (-0.5) * 1.4426950408889634
    square = jax.ShapeDtypeStruct((channels, channels), BF16)
    score_weight, mix_weight = pl.pallas_call(
        functools.partial(fuse_kernel, scale),
        out_shape=(square, square),
        in_specs=[vmem()] * 4,
        out_specs=(vmem(),) * 2,
        cost_estimate=cost(4 * channels**3, 12 * channels * channels),
        compiler_params=params(8),
    )(query_weight, key_weight, value_weight, out_weight)

    wide = span + 2 * width
    lanes = jax.ShapeDtypeStruct((span, 128), F32)
    own_query, peak, sums, added = pl.pallas_call(
        functools.partial(early_kernel, counts[: len(early)]),
        out_shape=(
            jax.ShapeDtypeStruct((span, channels), BF16),
            lanes,
            lanes,
            jax.ShapeDtypeStruct((span, channels), F32),
        ),
        in_specs=[vmem()] * (1 + len(early_parts)),
        out_specs=(vmem(),) * 4,
        scratch_shapes=[pltpu.VMEM((len(early), span, span), F32)],
        cost_estimate=cost(
            4 * span * span * len(early) * channels,
            2 * span * channels * len(early),
            span * span * len(early),
        ),
        compiler_params=params(24),
    )(score_weight, *early_parts)

    wide_lanes = jax.ShapeDtypeStruct((wide, 128), F32)
    query, peak, sums, added, edge_resid = pl.pallas_call(
        functools.partial(middle_kernel, width, sources, counts, len(early)),
        out_shape=(
            jax.ShapeDtypeStruct((wide, channels), BF16),
            wide_lanes,
            wide_lanes,
            jax.ShapeDtypeStruct((wide, channels), F32),
            jax.ShapeDtypeStruct((2 * width, channels), F32),
        ),
        in_specs=[vmem()] * (6 + len(all_parts)),
        out_specs=(vmem(),) * 5,
        scratch_shapes=[
            pltpu.VMEM((len(blocks), wide, span), F32),
            pltpu.VMEM((2 * width, channels), BF16),
            pltpu.VMEM((2, EXTRA, 2 * width), BF16),
        ],
        cost_estimate=cost(
            2 * wide * span * len(blocks) * channels,
            2 * span * channels * len(blocks),
            wide * span * len(blocks) // 2,
        ),
        compiler_params=params(24),
    )(own_query, peak, sums, added, attn_gain, score_weight, *all_parts)

    mid, swap_rows = pl.pallas_call(
        functools.partial(late_kernel, width, [len(parts) for parts, _ in final]),
        out_shape=(jax.ShapeDtypeStruct((4 * width, channels), BF16),) * 2,
        in_specs=[vmem()] * (7 + len(final_parts)),
        out_specs=(vmem(),) * 2,
        scratch_shapes=[
            pltpu.VMEM((max(1, len(final)), wide, span), F32),
            pltpu.VMEM((wide, channels), BF16),
        ],
        cost_estimate=cost(
            4 * wide * span * channels, 8 * wide * channels, wide * span
        ),
        compiler_params=params(16),
    )(query, peak, sums, added, resid, edge_resid, mix_weight, *final_parts)

    swap_rows = lax.ppermute(swap_rows, "rows", swap)

    fine_shape = (2 * rows_here, outputs, 2 * width)
    taps = jnp.transpose(up_weight, (0, 1, 3, 2))
    up_cost = cost(2 * 9 * outputs * channels * 4 * width, 2 * 9 * outputs * channels)
    own_fine = pl.pallas_call(
        functools.partial(up_own_kernel, width),
        out_shape=jax.ShapeDtypeStruct(fine_shape, BF16),
        in_specs=[vmem()] * 2,
        out_specs=vmem(),
        cost_estimate=up_cost,
        compiler_params=params(16),
    )(mid, taps)
    decoded = pl.pallas_call(
        functools.partial(up_kernel, width),
        out_shape=jax.ShapeDtypeStruct((frames, *fine_shape), BF16),
        in_specs=[vmem()] * 3,
        out_specs=anywhere,
        scratch_shapes=[
            pltpu.VMEM(fine_shape, BF16),
            pltpu.SemaphoreType.DMA((2,)),
        ],
        cost_estimate=up_cost,
        compiler_params=params(16),
    )(swap_rows, taps, own_fine)
    decoded = jnp.transpose(decoded, (0, 1, 3, 2))
    return (decoded, act.reshape(frames, rows_here, width, channels))


def solution(mesh):
    return jax.shard_map(
        shards,
        mesh=mesh,
        in_specs=(
            P("videos", "rows", None, None),
            P("videos", "rows", None, None),
            P(),
            P(),
            P(),
            P(),
            P(),
            P(),
            P(),
            P(),
        ),
        out_specs=(P("videos", "rows", None, None), P("videos", "rows", None, None)),
        check_vma=False,
    )
```

```python
import functools

import jax
import jax.numpy as jnp
from jax import lax
from jax.experimental import pallas as pl
from jax.experimental.pallas import tpu as pltpu
from jax.sharding import PartitionSpec as P

BF16 = jnp.bfloat16
F32 = jnp.float32
EPS = 1e-06
MIB = 1024 * 1024
EXTRA = 16


def normalize(values, gain):
    return values * lax.rsqrt(jnp.mean(values * values, axis=-1, keepdims=True) + EPS) * gain


def activate(values, gain):
    normed = normalize(values.astype(F32), gain)
    return (normed / (1.0 + jnp.exp(-normed))).astype(BF16)


def vmem():
    return pl.BlockSpec(memory_space=pltpu.VMEM)


def params(mib):
    return pltpu.CompilerParams(vmem_limit_bytes=mib * MIB)


def cost(flops, size, exps=0):
    return pl.CostEstimate(flops=flops, bytes_accessed=size, transcendentals=exps)


def edges_kernel(latents_ref, cache_ref, edge_ref, both_ref, sems):
    core = lax.axis_index("rows") % 2
    row = core * (latents_ref.shape[1] - 1)
    copies = [
        pltpu.make_async_copy(cache_ref.at[:, row], edge_ref.at[pl.ds(0, 2)], sems.at[0]),
        pltpu.make_async_copy(latents_ref.at[:, row], edge_ref.at[pl.ds(2, 2)], sems.at[1]),
        pltpu.make_async_copy(cache_ref.at[1], both_ref.at[core], sems.at[2]),
        pltpu.make_async_copy(latents_ref.at[0], both_ref.at[1 + core], sems.at[3]),
    ]
    for copy in copies:
        copy.start()

    @pl.when(core == 0)
    def _():
        last = pltpu.make_async_copy(latents_ref.at[1], both_ref.at[2], sems.at[4])
        last.start()
        last.wait()

    @pl.when(core == 1)
    def _():
        last = pltpu.make_async_copy(cache_ref.at[0], both_ref.at[0], sems.at[4])
        last.start()
        last.wait()

    for copy in copies:
        copy.wait()


def start_all(pairs, sems, first=0):
    copies = [
        pltpu.make_async_copy(source, target, sems.at[first + i])
        for i, (source, target) in enumerate(pairs)
    ]
    for copy in copies:
        copy.start()
    return copies


def wait_all(copies):
    for copy in copies:
        copy.wait()


def prepare_kernel(
    latents_ref,
    cache_ref,
    weight_ref,
    gain_ref,
    act_ref,
    own_ref,
    staged_ref,
    latents,
    cache,
    gain,
    act,
    sems,
):
    channels = latents_ref.shape[-1]
    core = lax.axis_index("rows") % 2
    loads = start_all([(latents_ref, latents), (cache_ref, cache), (gain_ref, gain)], sems)
    stages = start_all(
        [
            (
                weight_ref.at[time, :, col],
                staged_ref.at[time, :, :, pl.ds(col * channels, channels)],
            )
            for time in range(3)
            for col in range(3)
        ],
        sems,
        4,
    )
    wait_all(loads)
    act[...] = activate(latents[...], gain[...].reshape(1, channels))
    store = start_all([(act, act_ref)], sems, 3)
    own_ref[0] = cache[core]
    own_ref[1] = jnp.where(core == 0, cache[1], latents[0])
    own_ref[2] = latents[core]
    wait_all(store + stages)


def conv_kernel(
    width,
    own_ref,
    swap_ref,
    edge_ref,
    far_ref,
    norm_gain_ref,
    attn_gain_ref,
    weights,
    sent_ref,
    front_ref,
    back_ref,
    resid_ref,
    raw,
    second,
    third,
    total,
):
    channels = own_ref.shape[-1]
    core = lax.axis_index("rows") % 2
    own = 2 * width
    span = 4 * width
    gain = norm_gain_ref[...].reshape(1, channels)

    def put(index, values):
        rows = pl.ds(pl.multiple_of(index * width, width), values.shape[1])
        raw[:, rows, :] = values

    put(1 + 2 * core, own_ref[...])
    put(3 - 2 * core, swap_ref[...])
    put(5 * core, edge_ref[pl.ds(core, 3)])
    put(5 * (1 - core), far_ref[pl.ds(core, 3)])

    def taps(ref, time):
        lhs = jnp.concatenate([ref[row * width : row * width + span] for row in range(3)], axis=1)
        rhs = weights[time].reshape(3 * channels, 3 * channels)
        return jnp.dot(lhs, rhs, preferred_element_type=F32)

    total[...] = taps(raw.at[0], 0)
    second[...] = jnp.where(core == 1, activate(raw[1], gain), raw[1])
    third[...] = activate(raw[2], gain)
    total[...] += taps(second, 1)
    total[...] += taps(third, 2)

    column = lax.broadcasted_iota(jnp.int32, (span, 1), 0) % width
    left = pltpu.roll(total[:, :channels], 1, axis=0)
    right = pltpu.roll(total[:, 2 * channels :], span - 1, axis=0)
    conv_out = total[:, channels : 2 * channels]
    conv_out = conv_out + jnp.where(column == 0, 0.0, left)
    conv_out = conv_out + jnp.where(column == width - 1, 0.0, right)
    resid = raw[2, width : width + span].astype(F32) + conv_out
    resid_ref[...] = resid
    size = jnp.mean(resid * resid, axis=-1, keepdims=True) + EPS
    normed = resid * lax.rsqrt(size) * attn_gain_ref[...].reshape(1, channels)
    edges = jnp.sqrt(jnp.concatenate([size[:width], size[span - width :]], axis=0))
    across = jnp.transpose(jnp.broadcast_to(edges, (2 * width, 128)))[:EXTRA]
    high = across.astype(BF16).astype(F32)
    line = lax.broadcasted_iota(jnp.int32, (EXTRA, 1), 0)
    extra = jnp.where(line == 0, high, jnp.where(line == 1, across - high, 0.0)).astype(BF16)
    normed = normed.astype(BF16)
    half = span // 2
    for ref, low, count in ((sent_ref, 0, span), (front_ref, 0, half), (back_ref, half, half)):
        ref[:count] = normed[low : low + count]
        ref[count:] = jnp.zeros((EXTRA, channels), BF16)
        ref[count:, : 2 * width] = extra


def nt_dot(a, b):
    return lax.dot_general(a, b, (((1,), (1,)), ((), ())), preferred_element_type=F32)


def whole(parts, span):
    rows = [part[: span // len(parts)] for part in parts]
    return rows[0] if len(rows) == 1 else jnp.concatenate(rows, axis=0)


def grouped(refs, counts):
    blocks, first = [], 0
    for count in counts:
        blocks.append(refs[first : first + count])
        first += count
    return blocks


def fold(values, combine, total):
    for lane in range(0, values.shape[1], 128):
        piece = values[:, lane : lane + 128]
        total = piece if total is None else combine(total, piece)
    return total


def attend(queries, keys, scores, start, peak, sums, added):
    height = queries.shape[0]
    top = None
    for i, key in enumerate(keys):
        part = nt_dot(queries, key)
        scores[i, start : start + height] = part
        top = fold(part, jnp.maximum, top)
    top = jnp.max(top, axis=-1, keepdims=True)
    if peak is not None:
        top = jnp.maximum(top, peak)
        shrink = jnp.exp2(peak - top)
        sums = sums * shrink
        added = added * shrink
    for i, key in enumerate(keys):
        weights = jnp.exp2(scores[i, start : start + height] - top)
        sums = fold(weights, jnp.add, sums)
        part = jnp.dot(weights.astype(BF16), key, preferred_element_type=F32)
        added = part if added is None else added + part
    return top, sums, added


def fuse_kernel(scale, query_ref, key_ref, value_ref, out_ref, score_ref, mix_ref):
    score_ref[...] = (nt_dot(query_ref[...], key_ref[...]) * scale).astype(BF16)
    mix_ref[...] = jnp.dot(
        value_ref[...], out_ref[...], preferred_element_type=F32
    ).astype(BF16)


def lead(rows, score_weight):
    return jnp.dot(rows, score_weight[...], preferred_element_type=F32).astype(BF16)


def early_kernel(counts, score_ref, *refs):
    blocks = grouped(refs, counts)
    own_query_ref, peak_ref, sums_ref, added_ref, scores = refs[-5:]
    keys = [whole(parts, own_query_ref.shape[0]) for parts in blocks]
    queries = lead(keys[0], score_ref)
    own_query_ref[...] = queries
    peak, sums, added = attend(queries, keys, scores, 0, None, None, None)
    peak_ref[...] = jnp.broadcast_to(peak, peak_ref.shape)
    sums_ref[...] = sums
    added_ref[...] = added


def middle_kernel(
    width,
    sources,
    counts,
    early,
    own_query_ref,
    peak_ref,
    sums_ref,
    added_ref,
    gain_ref,
    score_ref,
    *refs,
):
    blocks = grouped(refs, counts)
    query_out, peak_out, sums_out, added_out, resid_out, scores, halo, sizes = refs[sum(counts) :]
    place = lax.axis_index("rows")
    chip = place // 2
    own, channels = own_query_ref.shape
    devices = len(sources[0])

    for block, origin in zip(blocks, sources):
        rows = own // len(block)
        for step, part, first, low in (
            (-1, block[-1], rows - width, 0),
            (1, block[0], 0, width),
        ):
            takers = [d for d in range(devices) if origin[d] == d // 2 + step]
            if not takers:
                continue
            wanted = place == takers[0]
            for d in takers[1:]:
                wanted = jnp.logical_or(wanted, place == d)

            @pl.when(wanted)
            def _(part=part, notes=block[0], rows=rows, first=first, low=low):
                halo[low : low + width] = part[first : first + width, :]
                sizes[low // width] = notes[rows : rows + EXTRA, : 2 * width]

    @pl.when(chip == 0)
    def _():
        halo[:width] = jnp.zeros((width, channels), BF16)
        sizes[0] = jnp.zeros((EXTRA, 2 * width), BF16)

    @pl.when(chip == devices // 2 - 1)
    def _():
        halo[width:] = jnp.zeros((width, channels), BF16)
        sizes[1] = jnp.zeros((EXTRA, 2 * width), BF16)

    def column(index):
        parts = sizes[index].astype(F32)
        line = parts[0:1] + parts[1:2]
        return jnp.transpose(jnp.broadcast_to(line, (128, 2 * width)))[:, :1]

    edge_rows = halo[...]
    edge_size = jnp.concatenate([column(0)[width:], column(1)[:width]], axis=0)
    resid_out[...] = edge_rows.astype(F32) * edge_size / gain_ref[...].reshape(1, channels)
    edge_query = lead(edge_rows, score_ref)
    keys = [whole(parts, own) for parts in blocks]
    edge = attend(edge_query, keys, scores, own, None, None, None)
    mine = attend(
        own_query_ref[...],
        keys[early:],
        scores,
        0,
        peak_ref[:, :1],
        sums_ref[...],
        added_ref[...],
    )
    query_out[:own] = own_query_ref[...]
    query_out[own:] = edge_query
    for rows, state in ((slice(0, own), mine), (slice(own, None), edge)):
        peak_out[rows] = jnp.broadcast_to(state[0], state[1].shape)
        sums_out[rows] = state[1]
        added_out[rows] = state[2]


def late_kernel(
    width,
    counts,
    query_ref,
    peak_ref,
    sums_ref,
    added_ref,
    resid_ref,
    edge_resid_ref,
    mix_weight_ref,
    *refs,
):
    blocks = grouped(refs, counts)
    mid_ref, swap_ref, scores, mid = refs[sum(counts) :]
    place = lax.axis_index("rows")
    core = place % 2
    own, channels = resid_ref.shape
    sums, added = sums_ref[...], added_ref[...]
    if blocks:
        keys = [whole(parts, own) for parts in blocks]
        _, sums, added = attend(query_ref[...], keys, scores, 0, peak_ref[:, :1], sums, added)
    mixed = (added / jnp.sum(sums, axis=-1, keepdims=True)).astype(BF16)
    projected = jnp.dot(mixed, mix_weight_ref[...], preferred_element_type=F32)
    inner = own + width
    mid[width:inner] = (resid_ref[...] + projected[:own]).astype(BF16)
    edges = edge_resid_ref[...] + projected[own:]
    no_above = place < 2
    no_below = place >= lax.axis_size("rows") - 2
    mid[:width] = jnp.where(no_above, 0.0, edges[:width]).astype(BF16)
    mid[inner:] = jnp.where(no_below, 0.0, edges[width:]).astype(BF16)
    mid_ref[...] = mid[pl.ds(pl.multiple_of(2 * core * width, width), 4 * width), :]
    swap_ref[...] = mid[pl.ds(pl.multiple_of(2 * (1 - core) * width, width), 4 * width), :]


def up_rows(width, ref, weight_ref, out):
    channels = ref.shape[1]
    outputs = weight_ref.shape[2]
    span = 4 * width
    wide = 2 * width
    column = lax.broadcasted_iota(jnp.int32, (1, span), 1) % width
    line = lax.broadcasted_iota(jnp.int32, (2 * wide, 2 * wide), 0)
    lane = lax.broadcasted_iota(jnp.int32, (2 * wide, 2 * wide), 1)
    target = 2 * (line % wide) + line // wide
    weave = (target == lane).astype(BF16)
    lhs = jnp.concatenate(
        [weight_ref[j].reshape(3 * outputs, channels) for j in range(3)], axis=1
    )
    turned = jnp.transpose(ref[...].astype(F32)).astype(BF16)
    rows = [turned[:, row * width : (row + 1) * width] for row in range(4)]
    picks = ((0, 1, 1), (1, 1, 2), (1, 2, 2), (2, 2, 3))
    rhs = jnp.concatenate(
        [jnp.concatenate([rows[pick[j]] for pick in picks], axis=1) for j in range(3)], axis=0
    )
    taps = jnp.dot(lhs, rhs, preferred_element_type=F32)
    left, middle, right = (taps[col * outputs : (col + 1) * outputs] for col in range(3))
    even = middle + right + jnp.where(column == 0, 0.0, pltpu.roll(left, 1, axis=1))
    odd = left + middle
    odd = odd + jnp.where(column == width - 1, 0.0, pltpu.roll(right, span - 1, axis=1))
    even, odd = even.astype(BF16), odd.astype(BF16)
    for pair in range(2):
        both = slice(pair * wide, (pair + 1) * wide)
        mixed = jnp.concatenate([even[:, both], odd[:, both]], axis=1)
        woven = jnp.dot(mixed, weave, preferred_element_type=F32).astype(BF16)
        for i in range(2):
            out[2 * pair + i] = woven[:, i * wide : (i + 1) * wide]


def up_own_kernel(width, rows_ref, weight_ref, out_ref):
    up_rows(width, rows_ref, weight_ref, out_ref)


def up_kernel(width, rows_ref, weight_ref, own_ref, out_ref, result, sems):
    core = lax.axis_index("rows") % 2
    stores = start_all([(own_ref, out_ref.at[core])], sems)
    up_rows(width, rows_ref, weight_ref, result)
    stores = stores + start_all([(result, out_ref.at[1 - core])], sems, 1)
    wait_all(stores)


def gather_blocks(block, halves, count):
    chips = count // 2
    depth = 2 if chips % 2 == 0 else 1
    length = chips // depth

    ring = [0] + list(range(1, length, 2)) + list(range(2, length, 2))[::-1]
    follow = {a: ring[(i + 1) % length] for i, a in enumerate(ring)}
    forth = {a * depth + b: follow[a] * depth + b for a in range(length) for b in range(depth)}
    return_ = {target: source for source, target in forth.items()}
    onward = (forth, return_)
    backward = (return_, forth)
    across = ({k: k ^ 1 for k in range(chips)},) * 2

    def send(parts, targets):
        pairs = [(2 * k + c, 2 * targets[c][k] + c) for k in range(chips) for c in range(2)]
        return [lax.ppermute(part, "rows", pairs) for part in parts]

    def moved(origin, targets):
        return tuple({targets[c][k]: origin[c][k] for k in range(chips)} for c in range(2))

    def tie(*places):
        fixed = lax.optimization_barrier(tuple(where[i] for where, i in places))
        for (where, i), value in zip(places, fixed):
            where[i] = value

    here = ({k: k for k in range(chips)},) * 2
    early, late = [([block], here)], []
    own_again = [block]
    crossed = last = None
    if depth == 2:
        crossed = send([block], across)
    steps = length - 2
    parts, origin = list(halves), here
    for step in range(1, steps + 1):
        parts, origin = send(parts, onward), moved(origin, onward)
        for h in range(2):
            places = [(parts, h)]
            if last:
                places.append((last, h))
            if step == 1 and h == 1 and depth == 2:
                places.append((crossed, 0))
            tie(*places)
        early.append((parts, origin))
        if depth == 2:
            last = send(parts, across)
            (late if step == steps else early).append((last, moved(origin, across)))
    if depth == 2:
        (early if length > 1 else late).append((crossed, moved(here, across)))
        if length > 1:
            again = list(crossed)
            if steps > 0:
                tie((again, 0), (parts, 0))
            late.append((send(again, backward), moved(moved(here, across), backward)))
    final = []
    if length > 1:
        if steps > 0:
            tie((own_again, 0), (parts, 0))
        final.append((send(own_again, backward), moved(here, backward)))
    return early, late, final


def shards(
    latents,
    conv_cache,
    norm_gain,
    conv_weight,
    attn_gain,
    query_weight,
    key_weight,
    value_weight,
    out_weight,
    up_weight,
):
    frames, rows_here, width, channels = latents.shape
    outputs = up_weight.shape[3]
    count = lax.axis_size("rows")
    span = 2 * rows_here * width
    own = rows_here * width
    edge = jax.ShapeDtypeStruct((width, channels), BF16)
    anywhere = pl.BlockSpec(memory_space=pl.ANY)
    hbm = pl.BlockSpec(memory_space=pltpu.HBM)

    chips = count // 2
    swap = [(2 * k + c, 2 * k + 1 - c) for k in range(chips) for c in range(2)]
    neighbour = [(2 * k + 1, 2 * k + 2) for k in range(chips - 1)]
    neighbour = neighbour + [(target, source) for source, target in neighbour]

    latents_in = pltpu.with_memory_space_constraint(latents, pltpu.HBM)
    cache_in = pltpu.with_memory_space_constraint(conv_cache, pltpu.HBM)
    edge_rows, both = pl.pallas_call(
        edges_kernel,
        out_shape=(
            jax.ShapeDtypeStruct((2 * frames, width, channels), BF16),
            jax.ShapeDtypeStruct((3, rows_here, width, channels), BF16),
        ),
        in_specs=[hbm] * 2,
        out_specs=(anywhere,) * 2,
        scratch_shapes=[pltpu.SemaphoreType.DMA((5,))],
        cost_estimate=cost(0, 20 * width * channels),
        compiler_params=params(4),
    )(latents_in, cache_in)
    edge_rows = lax.ppermute(edge_rows, "rows", neighbour)
    both = lax.ppermute(both, "rows", swap)
    act, own_rows, staged = pl.pallas_call(
        prepare_kernel,
        out_shape=(
            jax.ShapeDtypeStruct((frames, own, channels), BF16),
            jax.ShapeDtypeStruct((3, own, channels), BF16),
            jax.ShapeDtypeStruct((3, 3, channels, 3 * channels), BF16),
        ),
        in_specs=[hbm] * 4,
        out_specs=(anywhere, vmem(), anywhere),
        scratch_shapes=[
            pltpu.VMEM((frames, own, channels), BF16),
            pltpu.VMEM((frames, own, channels), BF16),
            pltpu.VMEM((channels,), F32),
            pltpu.VMEM((frames, own, channels), BF16),
            pltpu.SemaphoreType.DMA((13,)),
        ],
        cost_estimate=cost(10 * frames * own * channels, 2 * 27 * channels * channels),
        compiler_params=params(8),
    )(
        pltpu.with_memory_space_constraint(latents.reshape(frames, own, channels), pltpu.HBM),
        pltpu.with_memory_space_constraint(conv_cache.reshape(frames, own, channels), pltpu.HBM),
        pltpu.with_memory_space_constraint(conv_weight, pltpu.HBM),
        pltpu.with_memory_space_constraint(norm_gain, pltpu.HBM),
    )

    edge_rows, own_rows = lax.optimization_barrier((edge_rows, own_rows))
    far_rows = lax.ppermute(edge_rows, "rows", swap)
    block = jax.ShapeDtypeStruct((span + EXTRA, channels), BF16)
    half = jax.ShapeDtypeStruct((span // 2 + EXTRA, channels), BF16)
    sent, front, back, resid = pl.pallas_call(
        functools.partial(conv_kernel, width),
        out_shape=(
            block,
            half,
            half,
            jax.ShapeDtypeStruct((span, channels), F32),
        ),
        in_specs=[vmem()] * 7,
        out_specs=(vmem(),) * 4,
        scratch_shapes=[
            pltpu.VMEM((3, 6 * width, channels), BF16),
            pltpu.VMEM((6 * width, channels), BF16),
            pltpu.VMEM((6 * width, channels), BF16),
            pltpu.VMEM((span, 3 * channels), F32),
        ],
        cost_estimate=cost(2 * 27 * span * channels * channels, 2 * 27 * channels * channels),
        compiler_params=params(20),
    )(
        own_rows,
        both.reshape(3, own, channels),
        edge_rows,
        far_rows,
        norm_gain,
        attn_gain,
        staged,
    )

    early, late, final = gather_blocks(sent, (front, back), count)
    blocks = early + late
    sources = [[origin[d % 2][d // 2] for d in range(count)] for _, origin in blocks]
    counts = [len(parts) for parts, _ in blocks]
    early_parts = [part for parts, _ in early for part in parts]
    all_parts = [part for parts, _ in blocks for part in parts]
    final_parts = [part for parts, _ in final for part in parts]

    scale = channels ** (-0.5) * 1.4426950408889634
    square = jax.ShapeDtypeStruct((channels, channels), BF16)
    score_weight, mix_weight = pl.pallas_call(
        functools.partial(fuse_kernel, scale),
        out_shape=(square, square),
        in_specs=[vmem()] * 4,
        out_specs=(vmem(),) * 2,
        cost_estimate=cost(4 * channels**3, 12 * channels * channels),
        compiler_params=params(8),
    )(query_weight, key_weight, value_weight, out_weight)

    wide = span + 2 * width
    lanes = jax.ShapeDtypeStruct((span, 128), F32)
    own_query, peak, sums, added = pl.pallas_call(
        functools.partial(early_kernel, counts[: len(early)]),
        out_shape=(
            jax.ShapeDtypeStruct((span, channels), BF16),
            lanes,
            lanes,
            jax.ShapeDtypeStruct((span, channels), F32),
        ),
        in_specs=[vmem()] * (1 + len(early_parts)),
        out_specs=(vmem(),) * 4,
        scratch_shapes=[pltpu.VMEM((len(early), span, span), F32)],
        cost_estimate=cost(
            4 * span * span * len(early) * channels,
            2 * span * channels * len(early),
            span * span * len(early),
        ),
        compiler_params=params(24),
    )(score_weight, *early_parts)

    wide_lanes = jax.ShapeDtypeStruct((wide, 128), F32)
    query, peak, sums, added, edge_resid = pl.pallas_call(
        functools.partial(middle_kernel, width, sources, counts, len(early)),
        out_shape=(
            jax.ShapeDtypeStruct((wide, channels), BF16),
            wide_lanes,
            wide_lanes,
            jax.ShapeDtypeStruct((wide, channels), F32),
            jax.ShapeDtypeStruct((2 * width, channels), F32),
        ),
        in_specs=[vmem()] * (6 + len(all_parts)),
        out_specs=(vmem(),) * 5,
        scratch_shapes=[
            pltpu.VMEM((len(blocks), wide, span), F32),
            pltpu.VMEM((2 * width, channels), BF16),
            pltpu.VMEM((2, EXTRA, 2 * width), BF16),
        ],
        cost_estimate=cost(
            2 * wide * span * len(blocks) * channels,
            2 * span * channels * len(blocks),
            wide * span * len(blocks) // 2,
        ),
        compiler_params=params(24),
    )(own_query, peak, sums, added, attn_gain, score_weight, *all_parts)

    mid, swap_rows = pl.pallas_call(
        functools.partial(late_kernel, width, [len(parts) for parts, _ in final]),
        out_shape=(jax.ShapeDtypeStruct((4 * width, channels), BF16),) * 2,
        in_specs=[vmem()] * (7 + len(final_parts)),
        out_specs=(vmem(),) * 2,
        scratch_shapes=[
            pltpu.VMEM((max(1, len(final)), wide, span), F32),
            pltpu.VMEM((wide, channels), BF16),
        ],
        cost_estimate=cost(
            4 * wide * span * channels, 8 * wide * channels, wide * span
        ),
        compiler_params=params(16),
    )(query, peak, sums, added, resid, edge_resid, mix_weight, *final_parts)

    swap_rows = lax.ppermute(swap_rows, "rows", swap)

    fine_shape = (2 * rows_here, outputs, 2 * width)
    taps = jnp.transpose(up_weight, (0, 1, 3, 2))
    up_cost = cost(2 * 9 * outputs * channels * 4 * width, 2 * 9 * outputs * channels)
    own_fine = pl.pallas_call(
        functools.partial(up_own_kernel, width),
        out_shape=jax.ShapeDtypeStruct(fine_shape, BF16),
        in_specs=[vmem()] * 2,
        out_specs=vmem(),
        cost_estimate=up_cost,
        compiler_params=params(16),
    )(mid, taps)
    decoded = pl.pallas_call(
        functools.partial(up_kernel, width),
        out_shape=jax.ShapeDtypeStruct((frames, *fine_shape), BF16),
        in_specs=[vmem()] * 3,
        out_specs=anywhere,
        scratch_shapes=[
            pltpu.VMEM(fine_shape, BF16),
            pltpu.SemaphoreType.DMA((2,)),
        ],
        cost_estimate=up_cost,
        compiler_params=params(16),
    )(swap_rows, taps, own_fine)
    decoded = jnp.transpose(decoded, (0, 1, 3, 2))
    return (decoded, act.reshape(frames, rows_here, width, channels))


def solution(mesh):
    return jax.shard_map(
        shards,
        mesh=mesh,
        in_specs=(
            P("videos", "rows", None, None),
            P("videos", "rows", None, None),
            P(),
            P(),
            P(),
            P(),
            P(),
            P(),
            P(),
            P(),
        ),
        out_specs=(P("videos", "rows", None, None), P("videos", "rows", None, None)),
        check_vma=False,
    )
```

```python
import functools

import jax
import jax.numpy as jnp
from jax import lax
from jax.experimental import pallas as pl
from jax.experimental.pallas import tpu as pltpu
from jax.sharding import PartitionSpec as P

BF16 = jnp.bfloat16
F32 = jnp.float32
EPS = 1e-06
MIB = 1024 * 1024
EXTRA = 16


def normalize(values, gain):
    return values * lax.rsqrt(jnp.mean(values * values, axis=-1, keepdims=True) + EPS) * gain


def activate(values, gain):
    normed = normalize(values.astype(F32), gain)
    return (normed / (1.0 + jnp.exp(-normed))).astype(BF16)


def vmem():
    return pl.BlockSpec(memory_space=pltpu.VMEM)


def params(mib):
    return pltpu.CompilerParams(vmem_limit_bytes=mib * MIB)


def cost(flops, size, exps=0):
    return pl.CostEstimate(flops=flops, bytes_accessed=size, transcendentals=exps)


def edges_kernel(latents_ref, cache_ref, edge_ref, both_ref, sems):
    core = lax.axis_index("rows") % 2
    row = core * (latents_ref.shape[1] - 1)
    copies = [
        pltpu.make_async_copy(cache_ref.at[:, row], edge_ref.at[pl.ds(0, 2)], sems.at[0]),
        pltpu.make_async_copy(latents_ref.at[:, row], edge_ref.at[pl.ds(2, 2)], sems.at[1]),
        pltpu.make_async_copy(cache_ref.at[1], both_ref.at[core], sems.at[2]),
        pltpu.make_async_copy(latents_ref.at[0], both_ref.at[1 + core], sems.at[3]),
    ]
    for copy in copies:
        copy.start()

    @pl.when(core == 0)
    def _():
        last = pltpu.make_async_copy(latents_ref.at[1], both_ref.at[2], sems.at[4])
        last.start()
        last.wait()

    @pl.when(core == 1)
    def _():
        last = pltpu.make_async_copy(cache_ref.at[0], both_ref.at[0], sems.at[4])
        last.start()
        last.wait()

    for copy in copies:
        copy.wait()


def start_all(pairs, sems, first=0):
    copies = [
        pltpu.make_async_copy(source, target, sems.at[first + i])
        for i, (source, target) in enumerate(pairs)
    ]
    for copy in copies:
        copy.start()
    return copies


def wait_all(copies):
    for copy in copies:
        copy.wait()


def prepare_kernel(
    latents_ref,
    cache_ref,
    weight_ref,
    gain_ref,
    act_ref,
    own_ref,
    staged_ref,
    latents,
    cache,
    gain,
    act,
    sems,
):
    channels = latents_ref.shape[-1]
    core = lax.axis_index("rows") % 2
    loads = start_all([(latents_ref, latents), (cache_ref, cache), (gain_ref, gain)], sems)
    stages = start_all(
        [
            (
                weight_ref.at[time, :, col],
                staged_ref.at[time, :, :, pl.ds(col * channels, channels)],
            )
            for time in range(3)
            for col in range(3)
        ],
        sems,
        4,
    )
    wait_all(loads)
    act[...] = activate(latents[...], gain[...].reshape(1, channels))
    store = start_all([(act, act_ref)], sems, 3)
    own_ref[0] = cache[core]
    own_ref[1] = jnp.where(core == 0, cache[1], latents[0])
    own_ref[2] = latents[core]
    wait_all(store + stages)


def conv_kernel(
    width,
    own_ref,
    swap_ref,
    edge_ref,
    far_ref,
    norm_gain_ref,
    attn_gain_ref,
    weights,
    sent_ref,
    front_ref,
    back_ref,
    resid_ref,
    raw,
    second,
    third,
    total,
):
    channels = own_ref.shape[-1]
    core = lax.axis_index("rows") % 2
    own = 2 * width
    span = 4 * width
    gain = norm_gain_ref[...].reshape(1, channels)

    def put(index, values):
        rows = pl.ds(pl.multiple_of(index * width, width), values.shape[1])
        raw[:, rows, :] = values

    put(1 + 2 * core, own_ref[...])
    put(3 - 2 * core, swap_ref[...])
    put(5 * core, edge_ref[pl.ds(core, 3)])
    put(5 * (1 - core), far_ref[pl.ds(core, 3)])

    def taps(ref, time):
        lhs = jnp.concatenate([ref[row * width : row * width + span] for row in range(3)], axis=1)
        rhs = weights[time].reshape(3 * channels, 3 * channels)
        return jnp.dot(lhs, rhs, preferred_element_type=F32)

    total[...] = taps(raw.at[0], 0)
    second[...] = jnp.where(core == 1, activate(raw[1], gain), raw[1])
    third[...] = activate(raw[2], gain)
    total[...] += taps(second, 1)
    total[...] += taps(third, 2)

    column = lax.broadcasted_iota(jnp.int32, (span, 1), 0) % width
    left = pltpu.roll(total[:, :channels], 1, axis=0)
    right = pltpu.roll(total[:, 2 * channels :], span - 1, axis=0)
    conv_out = total[:, channels : 2 * channels]
    conv_out = conv_out + jnp.where(column == 0, 0.0, left)
    conv_out = conv_out + jnp.where(column == width - 1, 0.0, right)
    resid = raw[2, width : width + span].astype(F32) + conv_out
    resid_ref[...] = resid
    size = jnp.mean(resid * resid, axis=-1, keepdims=True) + EPS
    normed = resid * lax.rsqrt(size) * attn_gain_ref[...].reshape(1, channels)
    edges = jnp.sqrt(jnp.concatenate([size[:width], size[span - width :]], axis=0))
    across = jnp.transpose(jnp.broadcast_to(edges, (2 * width, 128)))[:EXTRA]
    high = across.astype(BF16).astype(F32)
    line = lax.broadcasted_iota(jnp.int32, (EXTRA, 1), 0)
    extra = jnp.where(line == 0, high, jnp.where(line == 1, across - high, 0.0)).astype(BF16)
    half = span // 2
    for ref, low, count in ((sent_ref, 0, span), (front_ref, 0, half), (back_ref, half, half)):
        ref[:count] = normed[low : low + count].astype(BF16)
        ref[count:] = jnp.zeros((EXTRA, channels), BF16)
        ref[count:, : 2 * width] = extra


def nt_dot(a, b):
    return lax.dot_general(a, b, (((1,), (1,)), ((), ())), preferred_element_type=F32)


def whole(parts):
    rows = [part[: part.shape[0] - EXTRA] for part in parts]
    return rows[0] if len(rows) == 1 else jnp.concatenate(rows, axis=0)


def grouped(refs, counts):
    blocks, first = [], 0
    for count in counts:
        blocks.append(refs[first : first + count])
        first += count
    return blocks


def fold(values, combine, total):
    for lane in range(0, values.shape[1], 128):
        piece = values[:, lane : lane + 128]
        total = piece if total is None else combine(total, piece)
    return total


def attend(queries, keys, scores, start, peak, sums, added):
    height = queries.shape[0]
    top = None
    for i, key in enumerate(keys):
        part = nt_dot(queries, key)
        scores[i, start : start + height] = part
        top = fold(part, jnp.maximum, top)
    top = jnp.max(top, axis=-1, keepdims=True)
    if peak is not None:
        top = jnp.maximum(top, peak)
        shrink = jnp.exp2(peak - top)
        sums = sums * shrink
        added = added * shrink
    for i, key in enumerate(keys):
        weights = jnp.exp2(scores[i, start : start + height] - top)
        sums = fold(weights, jnp.add, sums)
        part = jnp.dot(weights.astype(BF16), key, preferred_element_type=F32)
        added = part if added is None else added + part
    return top, sums, added


def fuse_kernel(scale, query_ref, key_ref, value_ref, out_ref, score_ref, mix_ref):
    score_ref[...] = (nt_dot(query_ref[...], key_ref[...]) * scale).astype(BF16)
    mix_ref[...] = jnp.dot(
        value_ref[...], out_ref[...], preferred_element_type=F32
    ).astype(BF16)


def lead(rows, score_weight):
    return jnp.dot(rows, score_weight[...], preferred_element_type=F32).astype(BF16)


def early_kernel(counts, score_ref, *refs):
    blocks = grouped(refs, counts)
    own_query_ref, peak_ref, sums_ref, added_ref, scores = refs[-5:]
    keys = [whole(parts) for parts in blocks]
    queries = lead(keys[0], score_ref)
    own_query_ref[...] = queries
    peak, sums, added = attend(queries, keys, scores, 0, None, None, None)
    peak_ref[...] = jnp.broadcast_to(peak, peak_ref.shape)
    sums_ref[...] = sums
    added_ref[...] = added


def late_kernel(
    width,
    sources,
    counts,
    early,
    own_query_ref,
    peak_ref,
    sums_ref,
    added_ref,
    resid_ref,
    gain_ref,
    score_ref,
    mix_weight_ref,
    *refs,
):
    blocks = grouped(refs, counts)
    mid_ref, swap_ref, scores, mid, halo, sizes = refs[sum(counts) :]
    place = lax.axis_index("rows")
    core = place % 2
    chip = place // 2
    own, channels = own_query_ref.shape
    devices = len(sources[0])

    for block, origin in zip(blocks, sources):
        for step, part, low in ((-1, block[-1], 0), (1, block[0], width)):
            rows = part.shape[0] - EXTRA
            first = rows - width if step < 0 else 0
            takers = [d for d in range(devices) if origin[d] == d // 2 + step]
            if not takers:
                continue
            wanted = place == takers[0]
            for d in takers[1:]:
                wanted = jnp.logical_or(wanted, place == d)

            @pl.when(wanted)
            def _(part=part, rows=rows, first=first, low=low):
                halo[low : low + width] = part[first : first + width, :]
                sizes[low // width] = part[rows : rows + EXTRA, : 2 * width]

    no_above = chip == 0
    no_below = chip == devices // 2 - 1

    @pl.when(no_above)
    def _():
        halo[:width] = jnp.zeros((width, channels), BF16)
        sizes[0] = jnp.zeros((EXTRA, 2 * width), BF16)

    @pl.when(no_below)
    def _():
        halo[width:] = jnp.zeros((width, channels), BF16)
        sizes[1] = jnp.zeros((EXTRA, 2 * width), BF16)

    def column(index):
        parts = sizes[index].astype(F32)
        line = parts[0:1] + parts[1:2]
        return jnp.transpose(jnp.broadcast_to(line, (128, 2 * width)))[:, :1]

    edge_rows = halo[...]
    edge_size = jnp.concatenate([column(0)[width:], column(1)[:width]], axis=0)
    edge_resid = edge_rows.astype(F32) * edge_size / gain_ref[...].reshape(1, channels)
    edge_query = lead(edge_rows, score_ref)
    keys = [whole(parts) for parts in blocks]
    _, edge_sums, edge_added = attend(edge_query, keys, scores, own, None, None, None)
    _, own_sums, own_added = attend(
        own_query_ref[...],
        keys[early:],
        scores,
        0,
        peak_ref[:, :1],
        sums_ref[...],
        added_ref[...],
    )

    def finish(added, sums):
        return (added / jnp.sum(sums, axis=-1, keepdims=True)).astype(BF16)

    mixed = jnp.concatenate([finish(own_added, own_sums), finish(edge_added, edge_sums)], axis=0)
    projected = jnp.dot(mixed, mix_weight_ref[...], preferred_element_type=F32)
    inner = own + width
    mid[width:inner] = (resid_ref[...] + projected[:own]).astype(BF16)
    edges = edge_resid + projected[own:]
    mid[:width] = jnp.where(no_above, 0.0, edges[:width]).astype(BF16)
    mid[inner:] = jnp.where(no_below, 0.0, edges[width:]).astype(BF16)
    mid_ref[...] = mid[pl.ds(pl.multiple_of(2 * core * width, width), 4 * width), :]
    swap_ref[...] = mid[pl.ds(pl.multiple_of(2 * (1 - core) * width, width), 4 * width), :]


def up_rows(width, ref, weight_ref, out):
    channels = ref.shape[1]
    outputs = weight_ref.shape[2]
    span = 4 * width
    wide = 2 * width
    column = lax.broadcasted_iota(jnp.int32, (1, span), 1) % width
    line = lax.broadcasted_iota(jnp.int32, (2 * wide, 2 * wide), 0)
    lane = lax.broadcasted_iota(jnp.int32, (2 * wide, 2 * wide), 1)
    target = 2 * (line % wide) + line // wide
    weave = (target == lane).astype(BF16)
    lhs = jnp.concatenate(
        [weight_ref[j].reshape(3 * outputs, channels) for j in range(3)], axis=1
    )
    turned = jnp.transpose(ref[...].astype(F32)).astype(BF16)
    rows = [turned[:, row * width : (row + 1) * width] for row in range(4)]
    picks = ((0, 1, 1), (1, 1, 2), (1, 2, 2), (2, 2, 3))
    rhs = jnp.concatenate(
        [jnp.concatenate([rows[pick[j]] for pick in picks], axis=1) for j in range(3)], axis=0
    )
    taps = jnp.dot(lhs, rhs, preferred_element_type=F32)
    left, middle, right = (taps[col * outputs : (col + 1) * outputs] for col in range(3))
    even = middle + right + jnp.where(column == 0, 0.0, pltpu.roll(left, 1, axis=1))
    odd = left + middle
    odd = odd + jnp.where(column == width - 1, 0.0, pltpu.roll(right, span - 1, axis=1))
    even, odd = even.astype(BF16), odd.astype(BF16)
    for pair in range(2):
        both = slice(pair * wide, (pair + 1) * wide)
        mixed = jnp.concatenate([even[:, both], odd[:, both]], axis=1)
        woven = jnp.dot(mixed, weave, preferred_element_type=F32).astype(BF16)
        for i in range(2):
            out[2 * pair + i] = woven[:, i * wide : (i + 1) * wide]


def up_own_kernel(width, rows_ref, weight_ref, out_ref):
    up_rows(width, rows_ref, weight_ref, out_ref)


def up_kernel(width, rows_ref, weight_ref, own_ref, out_ref, result, sems):
    core = lax.axis_index("rows") % 2
    stores = start_all([(own_ref, out_ref.at[core])], sems)
    up_rows(width, rows_ref, weight_ref, result)
    stores = stores + start_all([(result, out_ref.at[1 - core])], sems, 1)
    wait_all(stores)


def gather_blocks(block, halves, count):
    chips = count // 2
    depth = 2 if chips % 2 == 0 else 1
    length = chips // depth

    ring = [0] + list(range(1, length, 2)) + list(range(2, length, 2))[::-1]
    follow = {a: ring[(i + 1) % length] for i, a in enumerate(ring)}
    forth = {a * depth + b: follow[a] * depth + b for a in range(length) for b in range(depth)}
    return_ = {target: source for source, target in forth.items()}
    onward = (forth, return_)
    backward = (return_, forth)
    across = ({k: k ^ 1 for k in range(chips)},) * 2

    def send(parts, targets):
        pairs = [(2 * k + c, 2 * targets[c][k] + c) for k in range(chips) for c in range(2)]
        return [lax.ppermute(part, "rows", pairs) for part in parts]

    def moved(origin, targets):
        return tuple({targets[c][k]: origin[c][k] for k in range(chips)} for c in range(2))

    def tie(*places):
        fixed = lax.optimization_barrier(tuple(where[i] for where, i in places))
        for (where, i), value in zip(places, fixed):
            where[i] = value

    here = ({k: k for k in range(chips)},) * 2
    early, late = [([block], here)], []
    own_again = [block]
    crossed = last = None
    if depth == 2:
        crossed = send([block], across)
    steps = length - 2
    parts, origin = list(halves), here
    for step in range(1, steps + 1):
        parts, origin = send(parts, onward), moved(origin, onward)
        for h in range(2):
            places = [(parts, h)]
            if last:
                places.append((last, h))
            if step == 1 and h == 1:
                places.append((own_again, 0))
                if depth == 2:
                    places.append((crossed, 0))
            tie(*places)
        early.append((parts, origin))
        if depth == 2:
            last = send(parts, across)
            (late if step == steps else early).append((last, moved(origin, across)))
    if length > 1:
        late.append((send(own_again, backward), moved(here, backward)))
    if depth == 2:
        (early if length > 1 else late).append((crossed, moved(here, across)))
        if length > 1:
            if steps > 0:
                crossed = list(crossed)
                tie((crossed, 0), (parts, 0))
            late.append((send(crossed, backward), moved(moved(here, across), backward)))
    return early, late


def shards(
    latents,
    conv_cache,
    norm_gain,
    conv_weight,
    attn_gain,
    query_weight,
    key_weight,
    value_weight,
    out_weight,
    up_weight,
):
    frames, rows_here, width, channels = latents.shape
    outputs = up_weight.shape[3]
    count = lax.axis_size("rows")
    span = 2 * rows_here * width
    own = rows_here * width
    edge = jax.ShapeDtypeStruct((width, channels), BF16)
    anywhere = pl.BlockSpec(memory_space=pl.ANY)
    hbm = pl.BlockSpec(memory_space=pltpu.HBM)

    chips = count // 2
    swap = [(2 * k + c, 2 * k + 1 - c) for k in range(chips) for c in range(2)]
    neighbour = [(2 * k + 1, 2 * k + 2) for k in range(chips - 1)]
    neighbour = neighbour + [(target, source) for source, target in neighbour]

    latents_in = pltpu.with_memory_space_constraint(latents, pltpu.HBM)
    cache_in = pltpu.with_memory_space_constraint(conv_cache, pltpu.HBM)
    edge_rows, both = pl.pallas_call(
        edges_kernel,
        out_shape=(
            jax.ShapeDtypeStruct((2 * frames, width, channels), BF16),
            jax.ShapeDtypeStruct((3, rows_here, width, channels), BF16),
        ),
        in_specs=[hbm] * 2,
        out_specs=(anywhere,) * 2,
        scratch_shapes=[pltpu.SemaphoreType.DMA((5,))],
        cost_estimate=cost(0, 20 * width * channels),
        compiler_params=params(4),
    )(latents_in, cache_in)
    edge_rows = lax.ppermute(edge_rows, "rows", neighbour)
    both = lax.ppermute(both, "rows", swap)
    act, own_rows, staged = pl.pallas_call(
        prepare_kernel,
        out_shape=(
            jax.ShapeDtypeStruct((frames, own, channels), BF16),
            jax.ShapeDtypeStruct((3, own, channels), BF16),
            jax.ShapeDtypeStruct((3, 3, channels, 3 * channels), BF16),
        ),
        in_specs=[hbm] * 4,
        out_specs=(anywhere, vmem(), anywhere),
        scratch_shapes=[
            pltpu.VMEM((frames, own, channels), BF16),
            pltpu.VMEM((frames, own, channels), BF16),
            pltpu.VMEM((channels,), F32),
            pltpu.VMEM((frames, own, channels), BF16),
            pltpu.SemaphoreType.DMA((13,)),
        ],
        cost_estimate=cost(10 * frames * own * channels, 2 * 27 * channels * channels),
        compiler_params=params(8),
    )(
        pltpu.with_memory_space_constraint(latents.reshape(frames, own, channels), pltpu.HBM),
        pltpu.with_memory_space_constraint(conv_cache.reshape(frames, own, channels), pltpu.HBM),
        pltpu.with_memory_space_constraint(conv_weight, pltpu.HBM),
        pltpu.with_memory_space_constraint(norm_gain, pltpu.HBM),
    )

    edge_rows, own_rows = lax.optimization_barrier((edge_rows, own_rows))
    far_rows = lax.ppermute(edge_rows, "rows", swap)
    block = jax.ShapeDtypeStruct((span + EXTRA, channels), BF16)
    half = jax.ShapeDtypeStruct((span // 2 + EXTRA, channels), BF16)
    sent, front, back, resid = pl.pallas_call(
        functools.partial(conv_kernel, width),
        out_shape=(block, half, half, jax.ShapeDtypeStruct((span, channels), F32)),
        in_specs=[vmem()] * 7,
        out_specs=(vmem(),) * 4,
        scratch_shapes=[
            pltpu.VMEM((3, 6 * width, channels), BF16),
            pltpu.VMEM((6 * width, channels), BF16),
            pltpu.VMEM((6 * width, channels), BF16),
            pltpu.VMEM((span, 3 * channels), F32),
        ],
        cost_estimate=cost(2 * 27 * span * channels * channels, 2 * 27 * channels * channels),
        compiler_params=params(20),
    )(
        own_rows,
        both.reshape(3, own, channels),
        edge_rows,
        far_rows,
        norm_gain,
        attn_gain,
        staged,
    )

    early, late = gather_blocks(sent, (front, back), count)
    blocks = early + late
    sources = [[origin[d % 2][d // 2] for d in range(count)] for _, origin in blocks]
    counts = [len(parts) for parts, _ in blocks]
    early_parts = [part for parts, _ in early for part in parts]
    all_parts = [part for parts, _ in blocks for part in parts]

    scale = channels ** (-0.5) * 1.4426950408889634
    square = jax.ShapeDtypeStruct((channels, channels), BF16)
    score_weight, mix_weight = pl.pallas_call(
        functools.partial(fuse_kernel, scale),
        out_shape=(square, square),
        in_specs=[vmem()] * 4,
        out_specs=(vmem(),) * 2,
        cost_estimate=cost(4 * channels**3, 12 * channels * channels),
        compiler_params=params(8),
    )(query_weight, key_weight, value_weight, out_weight)

    wide = span + 2 * width
    lanes = jax.ShapeDtypeStruct((span, 128), F32)
    own_query, peak, sums, added = pl.pallas_call(
        functools.partial(early_kernel, counts[: len(early)]),
        out_shape=(
            jax.ShapeDtypeStruct((span, channels), BF16),
            lanes,
            lanes,
            jax.ShapeDtypeStruct((span, channels), F32),
        ),
        in_specs=[vmem()] * (1 + len(early_parts)),
        out_specs=(vmem(),) * 4,
        scratch_shapes=[pltpu.VMEM((len(early), span, span), F32)],
        cost_estimate=cost(
            4 * span * span * len(early) * channels,
            2 * span * channels * len(early),
            span * span * len(early),
        ),
        compiler_params=params(24),
    )(score_weight, *early_parts)

    mid, swap_rows = pl.pallas_call(
        functools.partial(late_kernel, width, sources, counts, len(early)),
        out_shape=(jax.ShapeDtypeStruct((4 * width, channels), BF16),) * 2,
        in_specs=[vmem()] * (8 + len(all_parts)),
        out_specs=(vmem(),) * 2,
        scratch_shapes=[
            pltpu.VMEM((len(blocks), wide, span), F32),
            pltpu.VMEM((wide, channels), BF16),
            pltpu.VMEM((2 * width, channels), BF16),
            pltpu.VMEM((2, EXTRA, 2 * width), BF16),
        ],
        cost_estimate=cost(
            2 * wide * span * len(blocks) * channels,
            2 * span * channels * len(blocks),
            wide * span * len(blocks) // 2,
        ),
        compiler_params=params(28),
    )(
        own_query,
        peak,
        sums,
        added,
        resid,
        attn_gain,
        score_weight,
        mix_weight,
        *all_parts,
    )

    swap_rows = lax.ppermute(swap_rows, "rows", swap)

    fine_shape = (2 * rows_here, outputs, 2 * width)
    taps = jnp.transpose(up_weight, (0, 1, 3, 2))
    up_cost = cost(2 * 9 * outputs * channels * 4 * width, 2 * 9 * outputs * channels)
    own_fine = pl.pallas_call(
        functools.partial(up_own_kernel, width),
        out_shape=jax.ShapeDtypeStruct(fine_shape, BF16),
        in_specs=[vmem()] * 2,
        out_specs=vmem(),
        cost_estimate=up_cost,
        compiler_params=params(16),
    )(mid, taps)
    decoded = pl.pallas_call(
        functools.partial(up_kernel, width),
        out_shape=jax.ShapeDtypeStruct((frames, *fine_shape), BF16),
        in_specs=[vmem()] * 3,
        out_specs=anywhere,
        scratch_shapes=[
            pltpu.VMEM(fine_shape, BF16),
            pltpu.SemaphoreType.DMA((2,)),
        ],
        cost_estimate=up_cost,
        compiler_params=params(16),
    )(swap_rows, taps, own_fine)
    decoded = jnp.transpose(decoded, (0, 1, 3, 2))
    return (decoded, act.reshape(frames, rows_here, width, channels))


def solution(mesh):
    return jax.shard_map(
        shards,
        mesh=mesh,
        in_specs=(
            P("videos", "rows", None, None),
            P("videos", "rows", None, None),
            P(),
            P(),
            P(),
            P(),
            P(),
            P(),
            P(),
            P(),
        ),
        out_specs=(P("videos", "rows", None, None), P("videos", "rows", None, None)),
        check_vma=False,
    )
```

```python
import functools

import jax
import jax.numpy as jnp
from jax import lax
from jax.experimental import pallas as pl
from jax.experimental.pallas import tpu as pltpu
from jax.sharding import PartitionSpec as P

BF16 = jnp.bfloat16
F32 = jnp.float32
EPS = 1e-06
MIB = 1024 * 1024


def normalize(values, gain):
    return values * lax.rsqrt(jnp.mean(values * values, axis=-1, keepdims=True) + EPS) * gain


def activate(values, gain):
    normed = normalize(values.astype(F32), gain)
    return (normed / (1.0 + jnp.exp(-normed))).astype(BF16)


def vmem():
    return pl.BlockSpec(memory_space=pltpu.VMEM)


def params(mib):
    return pltpu.CompilerParams(vmem_limit_bytes=mib * MIB)


def cost(flops, size, exps=0):
    return pl.CostEstimate(flops=flops, bytes_accessed=size, transcendentals=exps)


def edges_kernel(latents_ref, cache_ref, edge_ref, both_ref, sems):
    core = lax.axis_index("rows") % 2
    row = core * (latents_ref.shape[1] - 1)
    copies = [
        pltpu.make_async_copy(cache_ref.at[:, row], edge_ref.at[pl.ds(0, 2)], sems.at[0]),
        pltpu.make_async_copy(latents_ref.at[:, row], edge_ref.at[pl.ds(2, 2)], sems.at[1]),
        pltpu.make_async_copy(cache_ref.at[1], both_ref.at[core], sems.at[2]),
        pltpu.make_async_copy(latents_ref.at[0], both_ref.at[1 + core], sems.at[3]),
    ]
    for copy in copies:
        copy.start()

    @pl.when(core == 0)
    def _():
        last = pltpu.make_async_copy(latents_ref.at[1], both_ref.at[2], sems.at[4])
        last.start()
        last.wait()

    @pl.when(core == 1)
    def _():
        last = pltpu.make_async_copy(cache_ref.at[0], both_ref.at[0], sems.at[4])
        last.start()
        last.wait()

    for copy in copies:
        copy.wait()


def start_all(pairs, sems, first=0):
    copies = [
        pltpu.make_async_copy(source, target, sems.at[first + i])
        for i, (source, target) in enumerate(pairs)
    ]
    for copy in copies:
        copy.start()
    return copies


def wait_all(copies):
    for copy in copies:
        copy.wait()


def prepare_kernel(
    latents_ref,
    cache_ref,
    weight_ref,
    gain_ref,
    act_ref,
    own_ref,
    staged_ref,
    latents,
    cache,
    gain,
    act,
    sems,
):
    channels = latents_ref.shape[-1]
    core = lax.axis_index("rows") % 2
    loads = start_all([(latents_ref, latents), (cache_ref, cache), (gain_ref, gain)], sems)
    stages = start_all(
        [
            (
                weight_ref.at[time, :, col],
                staged_ref.at[time, :, :, pl.ds(col * channels, channels)],
            )
            for time in range(3)
            for col in range(3)
        ],
        sems,
        4,
    )
    wait_all(loads)
    act[...] = activate(latents[...], gain[...].reshape(1, channels))
    store = start_all([(act, act_ref)], sems, 3)
    own_ref[0] = cache[core]
    own_ref[1] = jnp.where(core == 0, cache[1], latents[0])
    own_ref[2] = latents[core]
    wait_all(store + stages)


def conv_kernel(
    width,
    own_ref,
    swap_ref,
    edge_ref,
    far_ref,
    norm_gain_ref,
    weights,
    sent_ref,
    front_ref,
    back_ref,
    resid_ref,
    raw,
    second,
    third,
    total,
):
    channels = own_ref.shape[-1]
    core = lax.axis_index("rows") % 2
    own = 2 * width
    span = 4 * width
    gain = norm_gain_ref[...].reshape(1, channels)

    def put(index, values):
        rows = pl.ds(pl.multiple_of(index * width, width), values.shape[1])
        raw[:, rows, :] = values

    put(1 + 2 * core, own_ref[...])
    put(3 - 2 * core, swap_ref[...])
    put(5 * core, edge_ref[pl.ds(core, 3)])
    put(5 * (1 - core), far_ref[pl.ds(core, 3)])

    def taps(ref, time):
        lhs = jnp.concatenate([ref[row * width : row * width + span] for row in range(3)], axis=1)
        rhs = weights[time].reshape(3 * channels, 3 * channels)
        return jnp.dot(lhs, rhs, preferred_element_type=F32)

    total[...] = taps(raw.at[0], 0)
    second[...] = jnp.where(core == 1, activate(raw[1], gain), raw[1])
    third[...] = activate(raw[2], gain)
    total[...] += taps(second, 1)
    total[...] += taps(third, 2)

    column = lax.broadcasted_iota(jnp.int32, (span, 1), 0) % width
    left = pltpu.roll(total[:, :channels], 1, axis=0)
    right = pltpu.roll(total[:, 2 * channels :], span - 1, axis=0)
    conv_out = total[:, channels : 2 * channels]
    conv_out = conv_out + jnp.where(column == 0, 0.0, left)
    conv_out = conv_out + jnp.where(column == width - 1, 0.0, right)
    resid = raw[2, width : width + span].astype(F32) + conv_out
    resid_ref[...] = resid
    rounded = resid.astype(BF16)
    sent_ref[...] = rounded
    front_ref[...] = rounded[: span // 2]
    back_ref[...] = rounded[span // 2 :]


def nt_dot(a, b):
    return lax.dot_general(a, b, (((1,), (1,)), ((), ())), preferred_element_type=F32)


def normed(rows, gain):
    return normalize(rows.astype(F32), gain).astype(BF16)


def whole(parts, gain):
    rows = [part[...] for part in parts]
    return normed(rows[0] if len(rows) == 1 else jnp.concatenate(rows, axis=0), gain)


def grouped(refs, counts):
    blocks, first = [], 0
    for count in counts:
        blocks.append(refs[first : first + count])
        first += count
    return blocks


def fold(values, combine, total):
    for lane in range(0, values.shape[1], 128):
        piece = values[:, lane : lane + 128]
        total = piece if total is None else combine(total, piece)
    return total


def attend(queries, keys, scores, start, peak, sums, added):
    height = queries.shape[0]
    top = None
    for i, key in enumerate(keys):
        part = nt_dot(queries, key)
        scores[i, start : start + height] = part
        top = fold(part, jnp.maximum, top)
    top = jnp.max(top, axis=-1, keepdims=True)
    if peak is not None:
        top = jnp.maximum(top, peak)
        shrink = jnp.exp2(peak - top)
        sums = sums * shrink
        added = added * shrink
    for i, key in enumerate(keys):
        weights = jnp.exp2(scores[i, start : start + height] - top)
        sums = fold(weights, jnp.add, sums)
        part = jnp.dot(weights.astype(BF16), key, preferred_element_type=F32)
        added = part if added is None else added + part
    return top, sums, added


def fuse_kernel(scale, query_ref, key_ref, value_ref, out_ref, score_ref, mix_ref):
    score_ref[...] = (nt_dot(query_ref[...], key_ref[...]) * scale).astype(BF16)
    mix_ref[...] = jnp.dot(
        value_ref[...], out_ref[...], preferred_element_type=F32
    ).astype(BF16)


def lead(rows, score_weight):
    return jnp.dot(rows, score_weight[...], preferred_element_type=F32).astype(BF16)


def early_kernel(counts, score_ref, gain_ref, *refs):
    blocks = grouped(refs, counts)
    own_query_ref, peak_ref, sums_ref, added_ref, keys_ref, scores = refs[-6:]
    gain = gain_ref[...].reshape(1, score_ref.shape[0])
    keys = [whole(parts, gain) for parts in blocks]
    for i, key in enumerate(keys):
        keys_ref[i] = key
    queries = lead(keys[0], score_ref)
    own_query_ref[...] = queries
    peak, sums, added = attend(queries, keys, scores, 0, None, None, None)
    peak_ref[...] = jnp.broadcast_to(peak, peak_ref.shape)
    sums_ref[...] = sums
    added_ref[...] = added


def late_kernel(
    width,
    sources,
    counts,
    early,
    own_query_ref,
    peak_ref,
    sums_ref,
    added_ref,
    keys_ref,
    resid_ref,
    gain_ref,
    score_ref,
    mix_weight_ref,
    *refs,
):
    blocks = grouped(refs, counts)
    mid_ref, swap_ref, scores, mid, halo = refs[sum(counts) :]
    place = lax.axis_index("rows")
    core = place % 2
    chip = place // 2
    own, channels = own_query_ref.shape
    devices = len(sources[0])

    for block, origin in zip(blocks, sources):
        for step, part, low in ((-1, block[-1], 0), (1, block[0], width)):
            first = part.shape[0] - width if step < 0 else 0
            takers = [d for d in range(devices) if origin[d] == d // 2 + step]
            if not takers:
                continue
            wanted = place == takers[0]
            for d in takers[1:]:
                wanted = jnp.logical_or(wanted, place == d)

            @pl.when(wanted)
            def _(part=part, first=first, low=low):
                halo[low : low + width] = part[first : first + width, :]

    no_above = chip == 0
    no_below = chip == devices // 2 - 1

    @pl.when(no_above)
    def _():
        halo[:width] = jnp.zeros((width, channels), BF16)

    @pl.when(no_below)
    def _():
        halo[width:] = jnp.zeros((width, channels), BF16)

    gain = gain_ref[...].reshape(1, channels)
    edge_resid = halo[...].astype(F32)
    edge_query = lead(normed(edge_resid, gain), score_ref)
    keys = [keys_ref[i] for i in range(early)]
    keys = keys + [whole(parts, gain) for parts in blocks[early:]]
    _, edge_sums, edge_added = attend(edge_query, keys, scores, own, None, None, None)
    _, own_sums, own_added = attend(
        own_query_ref[...],
        keys[early:],
        scores,
        0,
        peak_ref[:, :1],
        sums_ref[...],
        added_ref[...],
    )

    def finish(added, sums):
        return (added / jnp.sum(sums, axis=-1, keepdims=True)).astype(BF16)

    mixed = jnp.concatenate([finish(own_added, own_sums), finish(edge_added, edge_sums)], axis=0)
    projected = jnp.dot(mixed, mix_weight_ref[...], preferred_element_type=F32)
    inner = own + width
    mid[width:inner] = (resid_ref[...] + projected[:own]).astype(BF16)
    edges = edge_resid + projected[own:]
    mid[:width] = jnp.where(no_above, 0.0, edges[:width]).astype(BF16)
    mid[inner:] = jnp.where(no_below, 0.0, edges[width:]).astype(BF16)
    mid_ref[...] = mid[pl.ds(pl.multiple_of(2 * core * width, width), 4 * width), :]
    swap_ref[...] = mid[pl.ds(pl.multiple_of(2 * (1 - core) * width, width), 4 * width), :]


def up_rows(width, ref, weight_ref, out):
    channels = ref.shape[1]
    outputs = weight_ref.shape[2]
    span = 4 * width
    wide = 2 * width
    column = lax.broadcasted_iota(jnp.int32, (1, span), 1) % width
    line = lax.broadcasted_iota(jnp.int32, (2 * wide, 2 * wide), 0)
    lane = lax.broadcasted_iota(jnp.int32, (2 * wide, 2 * wide), 1)
    target = 2 * (line % wide) + line // wide
    weave = (target == lane).astype(BF16)
    lhs = jnp.concatenate(
        [weight_ref[j].reshape(3 * outputs, channels) for j in range(3)], axis=1
    )
    turned = jnp.transpose(ref[...].astype(F32)).astype(BF16)
    rows = [turned[:, row * width : (row + 1) * width] for row in range(4)]
    picks = ((0, 1, 1), (1, 1, 2), (1, 2, 2), (2, 2, 3))
    rhs = jnp.concatenate(
        [jnp.concatenate([rows[pick[j]] for pick in picks], axis=1) for j in range(3)], axis=0
    )
    taps = jnp.dot(lhs, rhs, preferred_element_type=F32)
    left, middle, right = (taps[col * outputs : (col + 1) * outputs] for col in range(3))
    even = middle + right + jnp.where(column == 0, 0.0, pltpu.roll(left, 1, axis=1))
    odd = left + middle
    odd = odd + jnp.where(column == width - 1, 0.0, pltpu.roll(right, span - 1, axis=1))
    even, odd = even.astype(BF16), odd.astype(BF16)
    for pair in range(2):
        both = slice(pair * wide, (pair + 1) * wide)
        mixed = jnp.concatenate([even[:, both], odd[:, both]], axis=1)
        woven = jnp.dot(mixed, weave, preferred_element_type=F32).astype(BF16)
        for i in range(2):
            out[2 * pair + i] = woven[:, i * wide : (i + 1) * wide]


def up_own_kernel(width, rows_ref, weight_ref, out_ref):
    up_rows(width, rows_ref, weight_ref, out_ref)


def up_kernel(width, rows_ref, weight_ref, own_ref, out_ref, result, sems):
    core = lax.axis_index("rows") % 2
    stores = start_all([(own_ref, out_ref.at[core])], sems)
    up_rows(width, rows_ref, weight_ref, result)
    stores = stores + start_all([(result, out_ref.at[1 - core])], sems, 1)
    wait_all(stores)


def gather_blocks(block, halves, count):
    chips = count // 2
    depth = 2 if chips % 2 == 0 else 1
    length = chips // depth

    ring = [0] + list(range(1, length, 2)) + list(range(2, length, 2))[::-1]
    follow = {a: ring[(i + 1) % length] for i, a in enumerate(ring)}
    forth = {a * depth + b: follow[a] * depth + b for a in range(length) for b in range(depth)}
    return_ = {target: source for source, target in forth.items()}
    onward = (forth, return_)
    backward = (return_, forth)
    across = ({k: k ^ 1 for k in range(chips)},) * 2

    def send(parts, targets):
        pairs = [(2 * k + c, 2 * targets[c][k] + c) for k in range(chips) for c in range(2)]
        return [lax.ppermute(part, "rows", pairs) for part in parts]

    def moved(origin, targets):
        return tuple({targets[c][k]: origin[c][k] for k in range(chips)} for c in range(2))

    def tie(*places):
        fixed = lax.optimization_barrier(tuple(where[i] for where, i in places))
        for (where, i), value in zip(places, fixed):
            where[i] = value

    here = ({k: k for k in range(chips)},) * 2
    early, late = [([block], here)], []
    own_again = [block]
    crossed = last = None
    if depth == 2:
        crossed = send(halves, across)
    steps = length - 2
    parts, origin = list(halves), here
    for step in range(1, steps + 1):
        parts, origin = send(parts, onward), moved(origin, onward)
        for h in range(2):
            places = [(parts, h)]
            if last:
                places.append((last, h))
            if step == 1 and h == 1:
                places.append((own_again, 0))
                if depth == 2:
                    places.append((crossed, 0))
            tie(*places)
        early.append((parts, origin))
        if depth == 2:
            last = send(parts, across)
            (late if step == steps else early).append((last, moved(origin, across)))
    if length > 1:
        late.append((send(own_again, backward), moved(here, backward)))
    if depth == 2:
        (early if length > 1 else late).append((crossed, moved(here, across)))
        if length > 1:
            if steps > 0:
                crossed = list(crossed)
                tie((crossed, 0), (parts, 0))
            late.append((send(crossed, backward), moved(moved(here, across), backward)))
    return early, late


def shards(
    latents,
    conv_cache,
    norm_gain,
    conv_weight,
    attn_gain,
    query_weight,
    key_weight,
    value_weight,
    out_weight,
    up_weight,
):
    frames, rows_here, width, channels = latents.shape
    outputs = up_weight.shape[3]
    count = lax.axis_size("rows")
    span = 2 * rows_here * width
    own = rows_here * width
    edge = jax.ShapeDtypeStruct((width, channels), BF16)
    anywhere = pl.BlockSpec(memory_space=pl.ANY)
    hbm = pl.BlockSpec(memory_space=pltpu.HBM)

    chips = count // 2
    swap = [(2 * k + c, 2 * k + 1 - c) for k in range(chips) for c in range(2)]
    neighbour = [(2 * k + 1, 2 * k + 2) for k in range(chips - 1)]
    neighbour = neighbour + [(target, source) for source, target in neighbour]

    latents_in = pltpu.with_memory_space_constraint(latents, pltpu.HBM)
    cache_in = pltpu.with_memory_space_constraint(conv_cache, pltpu.HBM)
    edge_rows, both = pl.pallas_call(
        edges_kernel,
        out_shape=(
            jax.ShapeDtypeStruct((2 * frames, width, channels), BF16),
            jax.ShapeDtypeStruct((3, rows_here, width, channels), BF16),
        ),
        in_specs=[hbm] * 2,
        out_specs=(anywhere,) * 2,
        scratch_shapes=[pltpu.SemaphoreType.DMA((5,))],
        cost_estimate=cost(0, 20 * width * channels),
        compiler_params=params(4),
    )(latents_in, cache_in)
    edge_rows = lax.ppermute(edge_rows, "rows", neighbour)
    both = lax.ppermute(both, "rows", swap)
    act, own_rows, staged = pl.pallas_call(
        prepare_kernel,
        out_shape=(
            jax.ShapeDtypeStruct((frames, own, channels), BF16),
            jax.ShapeDtypeStruct((3, own, channels), BF16),
            jax.ShapeDtypeStruct((3, 3, channels, 3 * channels), BF16),
        ),
        in_specs=[hbm] * 4,
        out_specs=(anywhere, vmem(), anywhere),
        scratch_shapes=[
            pltpu.VMEM((frames, own, channels), BF16),
            pltpu.VMEM((frames, own, channels), BF16),
            pltpu.VMEM((channels,), F32),
            pltpu.VMEM((frames, own, channels), BF16),
            pltpu.SemaphoreType.DMA((13,)),
        ],
        cost_estimate=cost(10 * frames * own * channels, 2 * 27 * channels * channels),
        compiler_params=params(8),
    )(
        pltpu.with_memory_space_constraint(latents.reshape(frames, own, channels), pltpu.HBM),
        pltpu.with_memory_space_constraint(conv_cache.reshape(frames, own, channels), pltpu.HBM),
        pltpu.with_memory_space_constraint(conv_weight, pltpu.HBM),
        pltpu.with_memory_space_constraint(norm_gain, pltpu.HBM),
    )

    edge_rows, own_rows = lax.optimization_barrier((edge_rows, own_rows))
    far_rows = lax.ppermute(edge_rows, "rows", swap)
    block = jax.ShapeDtypeStruct((span, channels), BF16)
    half = jax.ShapeDtypeStruct((span // 2, channels), BF16)
    sent, front, back, resid = pl.pallas_call(
        functools.partial(conv_kernel, width),
        out_shape=(block, half, half, jax.ShapeDtypeStruct((span, channels), F32)),
        in_specs=[vmem()] * 6,
        out_specs=(vmem(),) * 4,
        scratch_shapes=[
            pltpu.VMEM((3, 6 * width, channels), BF16),
            pltpu.VMEM((6 * width, channels), BF16),
            pltpu.VMEM((6 * width, channels), BF16),
            pltpu.VMEM((span, 3 * channels), F32),
        ],
        cost_estimate=cost(2 * 27 * span * channels * channels, 2 * 27 * channels * channels),
        compiler_params=params(20),
    )(
        own_rows,
        both.reshape(3, own, channels),
        edge_rows,
        far_rows,
        norm_gain,
        staged,
    )

    early, late = gather_blocks(sent, (front, back), count)
    blocks = early + late
    sources = [[origin[d % 2][d // 2] for d in range(count)] for _, origin in blocks]
    counts = [len(parts) for parts, _ in blocks]
    early_parts = [part for parts, _ in early for part in parts]
    all_parts = [part for parts, _ in blocks for part in parts]

    scale = channels ** (-0.5) * 1.4426950408889634
    square = jax.ShapeDtypeStruct((channels, channels), BF16)
    score_weight, mix_weight = pl.pallas_call(
        functools.partial(fuse_kernel, scale),
        out_shape=(square, square),
        in_specs=[vmem()] * 4,
        out_specs=(vmem(),) * 2,
        cost_estimate=cost(4 * channels**3, 12 * channels * channels),
        compiler_params=params(8),
    )(query_weight, key_weight, value_weight, out_weight)

    wide = span + 2 * width
    lanes = jax.ShapeDtypeStruct((span, 128), F32)
    own_query, peak, sums, added, early_keys = pl.pallas_call(
        functools.partial(early_kernel, counts[: len(early)]),
        out_shape=(
            jax.ShapeDtypeStruct((span, channels), BF16),
            lanes,
            lanes,
            jax.ShapeDtypeStruct((span, channels), F32),
            jax.ShapeDtypeStruct((len(early), span, channels), BF16),
        ),
        in_specs=[vmem()] * (2 + len(early_parts)),
        out_specs=(vmem(),) * 5,
        scratch_shapes=[pltpu.VMEM((len(early), span, span), F32)],
        cost_estimate=cost(
            4 * span * span * len(early) * channels,
            2 * span * channels * len(early),
            span * span * len(early),
        ),
        compiler_params=params(24),
    )(score_weight, attn_gain, *early_parts)

    mid, swap_rows = pl.pallas_call(
        functools.partial(late_kernel, width, sources, counts, len(early)),
        out_shape=(jax.ShapeDtypeStruct((4 * width, channels), BF16),) * 2,
        in_specs=[vmem()] * (9 + len(all_parts)),
        out_specs=(vmem(),) * 2,
        scratch_shapes=[
            pltpu.VMEM((len(blocks), wide, span), F32),
            pltpu.VMEM((wide, channels), BF16),
            pltpu.VMEM((2 * width, channels), BF16),
        ],
        cost_estimate=cost(
            2 * wide * span * len(blocks) * channels,
            2 * span * channels * len(blocks),
            wide * span * len(blocks) // 2,
        ),
        compiler_params=params(28),
    )(
        own_query,
        peak,
        sums,
        added,
        early_keys,
        resid,
        attn_gain,
        score_weight,
        mix_weight,
        *all_parts,
    )

    swap_rows = lax.ppermute(swap_rows, "rows", swap)

    fine_shape = (2 * rows_here, outputs, 2 * width)
    taps = jnp.transpose(up_weight, (0, 1, 3, 2))
    up_cost = cost(2 * 9 * outputs * channels * 4 * width, 2 * 9 * outputs * channels)
    own_fine = pl.pallas_call(
        functools.partial(up_own_kernel, width),
        out_shape=jax.ShapeDtypeStruct(fine_shape, BF16),
        in_specs=[vmem()] * 2,
        out_specs=vmem(),
        cost_estimate=up_cost,
        compiler_params=params(16),
    )(mid, taps)
    decoded = pl.pallas_call(
        functools.partial(up_kernel, width),
        out_shape=jax.ShapeDtypeStruct((frames, *fine_shape), BF16),
        in_specs=[vmem()] * 3,
        out_specs=anywhere,
        scratch_shapes=[
            pltpu.VMEM(fine_shape, BF16),
            pltpu.SemaphoreType.DMA((2,)),
        ],
        cost_estimate=up_cost,
        compiler_params=params(16),
    )(swap_rows, taps, own_fine)
    decoded = jnp.transpose(decoded, (0, 1, 3, 2))
    return (decoded, act.reshape(frames, rows_here, width, channels))


def solution(mesh):
    return jax.shard_map(
        shards,
        mesh=mesh,
        in_specs=(
            P("videos", "rows", None, None),
            P("videos", "rows", None, None),
            P(),
            P(),
            P(),
            P(),
            P(),
            P(),
            P(),
            P(),
        ),
        out_specs=(P("videos", "rows", None, None), P("videos", "rows", None, None)),
        check_vma=False,
    )
```

```python
import functools

import jax
import jax.numpy as jnp
from jax import lax
from jax.experimental import pallas as pl
from jax.experimental.pallas import tpu as pltpu
from jax.sharding import PartitionSpec as P

BF16 = jnp.bfloat16
F32 = jnp.float32
EPS = 1e-06
MIB = 1024 * 1024


def normalize(values, gain):
    return values * lax.rsqrt(jnp.mean(values * values, axis=-1, keepdims=True) + EPS) * gain


def activate(values, gain):
    normed = normalize(values.astype(F32), gain)
    return (normed / (1.0 + jnp.exp(-normed))).astype(BF16)


def vmem():
    return pl.BlockSpec(memory_space=pltpu.VMEM)


def params(mib):
    return pltpu.CompilerParams(vmem_limit_bytes=mib * MIB)


def cost(flops, size, exps=0):
    return pl.CostEstimate(flops=flops, bytes_accessed=size, transcendentals=exps)


def edges_kernel(latents_ref, cache_ref, edge_ref, both_ref, sems):
    core = lax.axis_index("rows") % 2
    row = core * (latents_ref.shape[1] - 1)
    copies = [
        pltpu.make_async_copy(cache_ref.at[:, row], edge_ref.at[pl.ds(0, 2)], sems.at[0]),
        pltpu.make_async_copy(latents_ref.at[:, row], edge_ref.at[pl.ds(2, 2)], sems.at[1]),
        pltpu.make_async_copy(cache_ref.at[1], both_ref.at[core], sems.at[2]),
        pltpu.make_async_copy(latents_ref.at[0], both_ref.at[1 + core], sems.at[3]),
    ]
    for copy in copies:
        copy.start()

    @pl.when(core == 0)
    def _():
        last = pltpu.make_async_copy(latents_ref.at[1], both_ref.at[2], sems.at[4])
        last.start()
        last.wait()

    @pl.when(core == 1)
    def _():
        last = pltpu.make_async_copy(cache_ref.at[0], both_ref.at[0], sems.at[4])
        last.start()
        last.wait()

    for copy in copies:
        copy.wait()


def start_all(pairs, sems, first=0):
    copies = [
        pltpu.make_async_copy(source, target, sems.at[first + i])
        for i, (source, target) in enumerate(pairs)
    ]
    for copy in copies:
        copy.start()
    return copies


def wait_all(copies):
    for copy in copies:
        copy.wait()


def prepare_kernel(
    latents_ref,
    cache_ref,
    weight_ref,
    gain_ref,
    act_ref,
    own_ref,
    staged_ref,
    latents,
    cache,
    gain,
    act,
    sems,
):
    channels = latents_ref.shape[-1]
    core = lax.axis_index("rows") % 2
    loads = start_all([(latents_ref, latents), (cache_ref, cache), (gain_ref, gain)], sems)
    stages = start_all(
        [
            (
                weight_ref.at[time, :, col],
                staged_ref.at[time, :, :, pl.ds(col * channels, channels)],
            )
            for time in range(3)
            for col in range(3)
        ],
        sems,
        4,
    )
    wait_all(loads)
    act[...] = activate(latents[...], gain[...].reshape(1, channels))
    store = start_all([(act, act_ref)], sems, 3)
    own_ref[0] = cache[core]
    own_ref[1] = jnp.where(core == 0, cache[1], latents[0])
    own_ref[2] = latents[core]
    wait_all(store + stages)


def conv_kernel(
    width,
    own_ref,
    swap_ref,
    edge_ref,
    far_ref,
    norm_gain_ref,
    weights,
    sent_ref,
    front_ref,
    back_ref,
    resid_ref,
    raw,
    second,
    third,
    total,
):
    channels = own_ref.shape[-1]
    core = lax.axis_index("rows") % 2
    own = 2 * width
    span = 4 * width
    gain = norm_gain_ref[...].reshape(1, channels)

    def put(index, values):
        rows = pl.ds(pl.multiple_of(index * width, width), values.shape[1])
        raw[:, rows, :] = values

    put(1 + 2 * core, own_ref[...])
    put(3 - 2 * core, swap_ref[...])
    put(5 * core, edge_ref[pl.ds(core, 3)])
    put(5 * (1 - core), far_ref[pl.ds(core, 3)])

    def taps(ref, time):
        lhs = jnp.concatenate([ref[row * width : row * width + span] for row in range(3)], axis=1)
        rhs = weights[time].reshape(3 * channels, 3 * channels)
        return jnp.dot(lhs, rhs, preferred_element_type=F32)

    total[...] = taps(raw.at[0], 0)
    second[...] = jnp.where(core == 1, activate(raw[1], gain), raw[1])
    third[...] = activate(raw[2], gain)
    total[...] += taps(second, 1)
    total[...] += taps(third, 2)

    column = lax.broadcasted_iota(jnp.int32, (span, 1), 0) % width
    left = pltpu.roll(total[:, :channels], 1, axis=0)
    right = pltpu.roll(total[:, 2 * channels :], span - 1, axis=0)
    conv_out = total[:, channels : 2 * channels]
    conv_out = conv_out + jnp.where(column == 0, 0.0, left)
    conv_out = conv_out + jnp.where(column == width - 1, 0.0, right)
    resid = raw[2, width : width + span].astype(F32) + conv_out
    resid_ref[...] = resid
    rounded = resid.astype(BF16)
    sent_ref[...] = rounded
    front_ref[...] = rounded[: span // 2]
    back_ref[...] = rounded[span // 2 :]


def nt_dot(a, b):
    return lax.dot_general(a, b, (((1,), (1,)), ((), ())), preferred_element_type=F32)


def normed(rows, gain):
    return normalize(rows.astype(F32), gain).astype(BF16)


def whole(parts, gain):
    rows = [part[...] for part in parts]
    return normed(rows[0] if len(rows) == 1 else jnp.concatenate(rows, axis=0), gain)


def grouped(refs, counts):
    blocks, first = [], 0
    for count in counts:
        blocks.append(refs[first : first + count])
        first += count
    return blocks


def fold(values, combine, total):
    for lane in range(0, values.shape[1], 128):
        piece = values[:, lane : lane + 128]
        total = piece if total is None else combine(total, piece)
    return total


def attend(queries, keys, scores, start, peak, sums, added):
    height = queries.shape[0]
    top = None
    for i, key in enumerate(keys):
        part = nt_dot(queries, key)
        scores[i, start : start + height] = part
        top = fold(part, jnp.maximum, top)
    top = jnp.max(top, axis=-1, keepdims=True)
    if peak is not None:
        top = jnp.maximum(top, peak)
        shrink = jnp.exp2(peak - top)
        sums = sums * shrink
        added = added * shrink
    for i, key in enumerate(keys):
        weights = jnp.exp2(scores[i, start : start + height] - top)
        sums = fold(weights, jnp.add, sums)
        part = jnp.dot(weights.astype(BF16), key, preferred_element_type=F32)
        added = part if added is None else added + part
    return top, sums, added


def fuse_kernel(scale, query_ref, key_ref, value_ref, out_ref, score_ref, mix_ref):
    score_ref[...] = (nt_dot(query_ref[...], key_ref[...]) * scale).astype(BF16)
    mix_ref[...] = jnp.dot(
        value_ref[...], out_ref[...], preferred_element_type=F32
    ).astype(BF16)


def lead(rows, score_weight):
    return jnp.dot(rows, score_weight[...], preferred_element_type=F32).astype(BF16)


def early_kernel(counts, score_ref, gain_ref, *refs):
    blocks = grouped(refs, counts)
    own_query_ref, peak_ref, sums_ref, added_ref, keys_ref, scores = refs[-6:]
    gain = gain_ref[...].reshape(1, score_ref.shape[0])
    keys = [whole(parts, gain) for parts in blocks]
    for i, key in enumerate(keys):
        keys_ref[i] = key
    queries = lead(keys[0], score_ref)
    own_query_ref[...] = queries
    peak, sums, added = attend(queries, keys, scores, 0, None, None, None)
    peak_ref[...] = jnp.broadcast_to(peak, peak_ref.shape)
    sums_ref[...] = sums
    added_ref[...] = added


def late_kernel(
    width,
    sources,
    counts,
    early,
    own_query_ref,
    peak_ref,
    sums_ref,
    added_ref,
    keys_ref,
    resid_ref,
    gain_ref,
    score_ref,
    mix_weight_ref,
    *refs,
):
    blocks = grouped(refs, counts)
    mid_ref, swap_ref, scores, mid, halo = refs[sum(counts) :]
    place = lax.axis_index("rows")
    core = place % 2
    chip = place // 2
    own, channels = own_query_ref.shape
    devices = len(sources[0])

    for block, origin in zip(blocks, sources):
        for step, part, low in ((-1, block[-1], 0), (1, block[0], width)):
            first = part.shape[0] - width if step < 0 else 0
            takers = [d for d in range(devices) if origin[d] == d // 2 + step]
            if not takers:
                continue
            wanted = place == takers[0]
            for d in takers[1:]:
                wanted = jnp.logical_or(wanted, place == d)

            @pl.when(wanted)
            def _(part=part, first=first, low=low):
                halo[low : low + width] = part[first : first + width, :]

    no_above = chip == 0
    no_below = chip == devices // 2 - 1

    @pl.when(no_above)
    def _():
        halo[:width] = jnp.zeros((width, channels), BF16)

    @pl.when(no_below)
    def _():
        halo[width:] = jnp.zeros((width, channels), BF16)

    gain = gain_ref[...].reshape(1, channels)
    edge_resid = halo[...].astype(F32)
    edge_query = lead(normed(edge_resid, gain), score_ref)
    keys = [keys_ref[i] for i in range(early)]
    keys = keys + [whole(parts, gain) for parts in blocks[early:]]
    _, edge_sums, edge_added = attend(edge_query, keys, scores, own, None, None, None)
    _, own_sums, own_added = attend(
        own_query_ref[...],
        keys[early:],
        scores,
        0,
        peak_ref[:, :1],
        sums_ref[...],
        added_ref[...],
    )

    def finish(added, sums):
        return (added / jnp.sum(sums, axis=-1, keepdims=True)).astype(BF16)

    mixed = jnp.concatenate([finish(own_added, own_sums), finish(edge_added, edge_sums)], axis=0)
    projected = jnp.dot(mixed, mix_weight_ref[...], preferred_element_type=F32)
    inner = own + width
    mid[width:inner] = (resid_ref[...] + projected[:own]).astype(BF16)
    edges = edge_resid + projected[own:]
    mid[:width] = jnp.where(no_above, 0.0, edges[:width]).astype(BF16)
    mid[inner:] = jnp.where(no_below, 0.0, edges[width:]).astype(BF16)
    mid_ref[...] = mid[pl.ds(pl.multiple_of(2 * core * width, width), 4 * width), :]
    swap_ref[...] = mid[pl.ds(pl.multiple_of(2 * (1 - core) * width, width), 4 * width), :]


def up_rows(width, ref, weight_ref, out, done=lambda pair: None):
    channels = ref.shape[1]
    outputs = weight_ref.shape[2]
    span = 4 * width
    wide = 2 * width
    column = lax.broadcasted_iota(jnp.int32, (1, span), 1) % width
    line = lax.broadcasted_iota(jnp.int32, (2 * wide, 2 * wide), 0)
    lane = lax.broadcasted_iota(jnp.int32, (2 * wide, 2 * wide), 1)
    target = 2 * (line % wide) + line // wide
    weave = (target == lane).astype(BF16)
    lhs = jnp.concatenate(
        [weight_ref[j].reshape(3 * outputs, channels) for j in range(3)], axis=1
    )
    turned = jnp.transpose(ref[...].astype(F32)).astype(BF16)
    rows = [turned[:, row * width : (row + 1) * width] for row in range(4)]
    picks = ((0, 1, 1), (1, 1, 2), (1, 2, 2), (2, 2, 3))
    rhs = jnp.concatenate(
        [jnp.concatenate([rows[pick[j]] for pick in picks], axis=1) for j in range(3)], axis=0
    )
    taps = jnp.dot(lhs, rhs, preferred_element_type=F32)
    left, middle, right = (taps[col * outputs : (col + 1) * outputs] for col in range(3))
    even = middle + right + jnp.where(column == 0, 0.0, pltpu.roll(left, 1, axis=1))
    odd = left + middle
    odd = odd + jnp.where(column == width - 1, 0.0, pltpu.roll(right, span - 1, axis=1))
    even, odd = even.astype(BF16), odd.astype(BF16)
    for pair in range(2):
        both = slice(pair * wide, (pair + 1) * wide)
        mixed = jnp.concatenate([even[:, both], odd[:, both]], axis=1)
        woven = jnp.dot(mixed, weave, preferred_element_type=F32).astype(BF16)
        for i in range(2):
            out[2 * pair + i] = woven[:, i * wide : (i + 1) * wide]
        done(pair)


def up_own_kernel(width, rows_ref, weight_ref, out_ref):
    up_rows(width, rows_ref, weight_ref, out_ref)


def up_kernel(width, rows_ref, weight_ref, own_ref, out_ref, result, sems):
    core = lax.axis_index("rows") % 2
    stores = start_all([(own_ref, out_ref.at[core])], sems)

    def store(pair):
        rows = pl.ds(2 * pair, 2)
        stores.extend(start_all([(result.at[rows], out_ref.at[1 - core, rows])], sems, 1 + pair))

    up_rows(width, rows_ref, weight_ref, result, store)
    wait_all(stores)


def gather_blocks(block, halves, count):
    chips = count // 2
    depth = 2 if chips % 2 == 0 else 1
    length = chips // depth

    ring = [0] + list(range(1, length, 2)) + list(range(2, length, 2))[::-1]
    follow = {a: ring[(i + 1) % length] for i, a in enumerate(ring)}
    forth = {a * depth + b: follow[a] * depth + b for a in range(length) for b in range(depth)}
    return_ = {target: source for source, target in forth.items()}
    onward = (return_, forth)
    backward = (forth, return_)
    across = ({k: k ^ 1 for k in range(chips)},) * 2

    def send(parts, targets):
        pairs = [(2 * k + c, 2 * targets[c][k] + c) for k in range(chips) for c in range(2)]
        return [lax.ppermute(part, "rows", pairs) for part in parts]

    def moved(origin, targets):
        return tuple({targets[c][k]: origin[c][k] for k in range(chips)} for c in range(2))

    def tie(*places):
        fixed = lax.optimization_barrier(tuple(where[i] for where, i in places))
        for (where, i), value in zip(places, fixed):
            where[i] = value

    here = ({k: k for k in range(chips)},) * 2
    early, late = [([block], here)], []
    own_again = [block]
    crossed = last = None
    if depth == 2:
        crossed = send(halves, across)
    steps = length - 2
    parts, origin = list(halves), here
    for step in range(1, steps + 1):
        parts, origin = send(parts, onward), moved(origin, onward)
        for h in range(2):
            places = [(parts, h)]
            if last:
                places.append((last, h))
            if step == 1 and h == 1:
                places.append((own_again, 0))
                if depth == 2:
                    places.append((crossed, 0))
            tie(*places)
        early.append((parts, origin))
        if depth == 2:
            last = send(parts, across)
            (late if step == steps else early).append((last, moved(origin, across)))
    if length > 1:
        late.append((send(own_again, backward), moved(here, backward)))
    if depth == 2:
        (early if length > 1 else late).append((crossed, moved(here, across)))
        if length > 1:
            if steps > 0:
                crossed = list(crossed)
                tie((crossed, 0), (parts, 0))
            late.append((send(crossed, backward), moved(moved(here, across), backward)))
    return early, late


def shards(
    latents,
    conv_cache,
    norm_gain,
    conv_weight,
    attn_gain,
    query_weight,
    key_weight,
    value_weight,
    out_weight,
    up_weight,
):
    frames, rows_here, width, channels = latents.shape
    outputs = up_weight.shape[3]
    count = lax.axis_size("rows")
    span = 2 * rows_here * width
    own = rows_here * width
    edge = jax.ShapeDtypeStruct((width, channels), BF16)
    anywhere = pl.BlockSpec(memory_space=pl.ANY)
    hbm = pl.BlockSpec(memory_space=pltpu.HBM)

    chips = count // 2
    swap = [(2 * k + c, 2 * k + 1 - c) for k in range(chips) for c in range(2)]
    neighbour = [(2 * k + 1, 2 * k + 2) for k in range(chips - 1)]
    neighbour = neighbour + [(target, source) for source, target in neighbour]

    latents_in = pltpu.with_memory_space_constraint(latents, pltpu.HBM)
    cache_in = pltpu.with_memory_space_constraint(conv_cache, pltpu.HBM)
    edge_rows, both = pl.pallas_call(
        edges_kernel,
        out_shape=(
            jax.ShapeDtypeStruct((2 * frames, width, channels), BF16),
            jax.ShapeDtypeStruct((3, rows_here, width, channels), BF16),
        ),
        in_specs=[hbm] * 2,
        out_specs=(anywhere,) * 2,
        scratch_shapes=[pltpu.SemaphoreType.DMA((5,))],
        cost_estimate=cost(0, 20 * width * channels),
        compiler_params=params(4),
    )(latents_in, cache_in)
    edge_rows = lax.ppermute(edge_rows, "rows", neighbour)
    both = lax.ppermute(both, "rows", swap)
    act, own_rows, staged = pl.pallas_call(
        prepare_kernel,
        out_shape=(
            jax.ShapeDtypeStruct((frames, own, channels), BF16),
            jax.ShapeDtypeStruct((3, own, channels), BF16),
            jax.ShapeDtypeStruct((3, 3, channels, 3 * channels), BF16),
        ),
        in_specs=[hbm] * 4,
        out_specs=(anywhere, vmem(), anywhere),
        scratch_shapes=[
            pltpu.VMEM((frames, own, channels), BF16),
            pltpu.VMEM((frames, own, channels), BF16),
            pltpu.VMEM((channels,), F32),
            pltpu.VMEM((frames, own, channels), BF16),
            pltpu.SemaphoreType.DMA((13,)),
        ],
        cost_estimate=cost(10 * frames * own * channels, 2 * 27 * channels * channels),
        compiler_params=params(8),
    )(
        pltpu.with_memory_space_constraint(latents.reshape(frames, own, channels), pltpu.HBM),
        pltpu.with_memory_space_constraint(conv_cache.reshape(frames, own, channels), pltpu.HBM),
        pltpu.with_memory_space_constraint(conv_weight, pltpu.HBM),
        pltpu.with_memory_space_constraint(norm_gain, pltpu.HBM),
    )

    edge_rows, own_rows = lax.optimization_barrier((edge_rows, own_rows))
    far_rows = lax.ppermute(edge_rows, "rows", swap)
    block = jax.ShapeDtypeStruct((span, channels), BF16)
    half = jax.ShapeDtypeStruct((span // 2, channels), BF16)
    sent, front, back, resid = pl.pallas_call(
        functools.partial(conv_kernel, width),
        out_shape=(block, half, half, jax.ShapeDtypeStruct((span, channels), F32)),
        in_specs=[vmem()] * 6,
        out_specs=(vmem(),) * 4,
        scratch_shapes=[
            pltpu.VMEM((3, 6 * width, channels), BF16),
            pltpu.VMEM((6 * width, channels), BF16),
            pltpu.VMEM((6 * width, channels), BF16),
            pltpu.VMEM((span, 3 * channels), F32),
        ],
        cost_estimate=cost(2 * 27 * span * channels * channels, 2 * 27 * channels * channels),
        compiler_params=params(20),
    )(
        own_rows,
        both.reshape(3, own, channels),
        edge_rows,
        far_rows,
        norm_gain,
        staged,
    )

    early, late = gather_blocks(sent, (front, back), count)
    blocks = early + late
    sources = [[origin[d % 2][d // 2] for d in range(count)] for _, origin in blocks]
    counts = [len(parts) for parts, _ in blocks]
    early_parts = [part for parts, _ in early for part in parts]
    all_parts = [part for parts, _ in blocks for part in parts]

    scale = channels ** (-0.5) * 1.4426950408889634
    square = jax.ShapeDtypeStruct((channels, channels), BF16)
    score_weight, mix_weight = pl.pallas_call(
        functools.partial(fuse_kernel, scale),
        out_shape=(square, square),
        in_specs=[vmem()] * 4,
        out_specs=(vmem(),) * 2,
        cost_estimate=cost(4 * channels**3, 12 * channels * channels),
        compiler_params=params(8),
    )(query_weight, key_weight, value_weight, out_weight)

    wide = span + 2 * width
    lanes = jax.ShapeDtypeStruct((span, 128), F32)
    own_query, peak, sums, added, early_keys = pl.pallas_call(
        functools.partial(early_kernel, counts[: len(early)]),
        out_shape=(
            jax.ShapeDtypeStruct((span, channels), BF16),
            lanes,
            lanes,
            jax.ShapeDtypeStruct((span, channels), F32),
            jax.ShapeDtypeStruct((len(early), span, channels), BF16),
        ),
        in_specs=[vmem()] * (2 + len(early_parts)),
        out_specs=(vmem(),) * 5,
        scratch_shapes=[pltpu.VMEM((len(early), span, span), F32)],
        cost_estimate=cost(
            4 * span * span * len(early) * channels,
            2 * span * channels * len(early),
            span * span * len(early),
        ),
        compiler_params=params(24),
    )(score_weight, attn_gain, *early_parts)

    mid, swap_rows = pl.pallas_call(
        functools.partial(late_kernel, width, sources, counts, len(early)),
        out_shape=(jax.ShapeDtypeStruct((4 * width, channels), BF16),) * 2,
        in_specs=[vmem()] * (9 + len(all_parts)),
        out_specs=(vmem(),) * 2,
        scratch_shapes=[
            pltpu.VMEM((len(blocks), wide, span), F32),
            pltpu.VMEM((wide, channels), BF16),
            pltpu.VMEM((2 * width, channels), BF16),
        ],
        cost_estimate=cost(
            2 * wide * span * len(blocks) * channels,
            2 * span * channels * len(blocks),
            wide * span * len(blocks) // 2,
        ),
        compiler_params=params(28),
    )(
        own_query,
        peak,
        sums,
        added,
        early_keys,
        resid,
        attn_gain,
        score_weight,
        mix_weight,
        *all_parts,
    )

    swap_rows = lax.ppermute(swap_rows, "rows", swap)

    fine_shape = (2 * rows_here, outputs, 2 * width)
    taps = jnp.transpose(up_weight, (0, 1, 3, 2))
    up_cost = cost(2 * 9 * outputs * channels * 4 * width, 2 * 9 * outputs * channels)
    own_fine = pl.pallas_call(
        functools.partial(up_own_kernel, width),
        out_shape=jax.ShapeDtypeStruct(fine_shape, BF16),
        in_specs=[vmem()] * 2,
        out_specs=vmem(),
        cost_estimate=up_cost,
        compiler_params=params(16),
    )(mid, taps)
    decoded = pl.pallas_call(
        functools.partial(up_kernel, width),
        out_shape=jax.ShapeDtypeStruct((frames, *fine_shape), BF16),
        in_specs=[vmem()] * 3,
        out_specs=anywhere,
        scratch_shapes=[
            pltpu.VMEM(fine_shape, BF16),
            pltpu.SemaphoreType.DMA((3,)),
        ],
        cost_estimate=up_cost,
        compiler_params=params(16),
    )(swap_rows, taps, own_fine)
    decoded = jnp.transpose(decoded, (0, 1, 3, 2))
    return (decoded, act.reshape(frames, rows_here, width, channels))


def solution(mesh):
    return jax.shard_map(
        shards,
        mesh=mesh,
        in_specs=(
            P("videos", "rows", None, None),
            P("videos", "rows", None, None),
            P(),
            P(),
            P(),
            P(),
            P(),
            P(),
            P(),
            P(),
        ),
        out_specs=(P("videos", "rows", None, None), P("videos", "rows", None, None)),
        check_vma=False,
    )
```

```python
import functools

import jax
import jax.numpy as jnp
from jax import lax
from jax.experimental import pallas as pl
from jax.experimental.pallas import tpu as pltpu
from jax.sharding import PartitionSpec as P

BF16 = jnp.bfloat16
F32 = jnp.float32
EPS = 1e-06
MIB = 1024 * 1024


def normalize(values, gain):
    return values * lax.rsqrt(jnp.mean(values * values, axis=-1, keepdims=True) + EPS) * gain


def activate(values, gain):
    normed = normalize(values.astype(F32), gain)
    return (normed / (1.0 + jnp.exp(-normed))).astype(BF16)


def vmem():
    return pl.BlockSpec(memory_space=pltpu.VMEM)


def params(mib):
    return pltpu.CompilerParams(vmem_limit_bytes=mib * MIB)


def cost(flops, size, exps=0):
    return pl.CostEstimate(flops=flops, bytes_accessed=size, transcendentals=exps)


def edges_kernel(latents_ref, cache_ref, edge_ref, both_ref, sems):
    core = lax.axis_index("rows") % 2
    row = core * (latents_ref.shape[1] - 1)
    copies = [
        pltpu.make_async_copy(cache_ref.at[:, row], edge_ref.at[pl.ds(0, 2)], sems.at[0]),
        pltpu.make_async_copy(latents_ref.at[:, row], edge_ref.at[pl.ds(2, 2)], sems.at[1]),
        pltpu.make_async_copy(cache_ref.at[1], both_ref.at[core], sems.at[2]),
        pltpu.make_async_copy(latents_ref.at[0], both_ref.at[1 + core], sems.at[3]),
    ]
    for copy in copies:
        copy.start()

    @pl.when(core == 0)
    def _():
        last = pltpu.make_async_copy(latents_ref.at[1], both_ref.at[2], sems.at[4])
        last.start()
        last.wait()

    @pl.when(core == 1)
    def _():
        last = pltpu.make_async_copy(cache_ref.at[0], both_ref.at[0], sems.at[4])
        last.start()
        last.wait()

    for copy in copies:
        copy.wait()


def start_all(pairs, sems, first=0):
    copies = [
        pltpu.make_async_copy(source, target, sems.at[first + i])
        for i, (source, target) in enumerate(pairs)
    ]
    for copy in copies:
        copy.start()
    return copies


def wait_all(copies):
    for copy in copies:
        copy.wait()


def prepare_kernel(
    latents_ref,
    cache_ref,
    weight_ref,
    gain_ref,
    act_ref,
    own_ref,
    staged_ref,
    latents,
    cache,
    gain,
    act,
    sems,
):
    channels = latents_ref.shape[-1]
    core = lax.axis_index("rows") % 2
    loads = start_all([(latents_ref, latents), (cache_ref, cache), (gain_ref, gain)], sems)
    stages = start_all(
        [
            (
                weight_ref.at[time, :, col],
                staged_ref.at[time, :, :, pl.ds(col * channels, channels)],
            )
            for time in range(3)
            for col in range(3)
        ],
        sems,
        4,
    )
    wait_all(loads)
    act[...] = activate(latents[...], gain[...].reshape(1, channels))
    store = start_all([(act, act_ref)], sems, 3)
    own_ref[0] = cache[core]
    own_ref[1] = jnp.where(core == 0, cache[1], latents[0])
    own_ref[2] = latents[core]
    wait_all(store + stages)


def conv_kernel(
    width,
    own_ref,
    swap_ref,
    edge_ref,
    far_ref,
    norm_gain_ref,
    weights,
    sent_ref,
    front_ref,
    back_ref,
    resid_ref,
    raw,
    second,
    third,
    total,
):
    channels = own_ref.shape[-1]
    core = lax.axis_index("rows") % 2
    own = 2 * width
    span = 4 * width
    gain = norm_gain_ref[...].reshape(1, channels)

    def put(index, values):
        rows = pl.ds(pl.multiple_of(index * width, width), values.shape[1])
        raw[:, rows, :] = values

    put(1 + 2 * core, own_ref[...])
    put(3 - 2 * core, swap_ref[...])
    put(5 * core, edge_ref[pl.ds(core, 3)])
    put(5 * (1 - core), far_ref[pl.ds(core, 3)])

    def taps(ref, time):
        lhs = jnp.concatenate([ref[row * width : row * width + span] for row in range(3)], axis=1)
        rhs = weights[time].reshape(3 * channels, 3 * channels)
        return jnp.dot(lhs, rhs, preferred_element_type=F32)

    total[...] = taps(raw.at[0], 0)
    second[...] = jnp.where(core == 1, activate(raw[1], gain), raw[1])
    third[...] = activate(raw[2], gain)
    total[...] += taps(second, 1)
    total[...] += taps(third, 2)

    column = lax.broadcasted_iota(jnp.int32, (span, 1), 0) % width
    left = pltpu.roll(total[:, :channels], 1, axis=0)
    right = pltpu.roll(total[:, 2 * channels :], span - 1, axis=0)
    conv_out = total[:, channels : 2 * channels]
    conv_out = conv_out + jnp.where(column == 0, 0.0, left)
    conv_out = conv_out + jnp.where(column == width - 1, 0.0, right)
    resid = raw[2, width : width + span].astype(F32) + conv_out
    resid_ref[...] = resid
    rounded = resid.astype(BF16)
    sent_ref[...] = rounded
    front_ref[...] = rounded[: span // 2]
    back_ref[...] = rounded[span // 2 :]


def nt_dot(a, b):
    return lax.dot_general(a, b, (((1,), (1,)), ((), ())), preferred_element_type=F32)


def normed(rows, gain):
    return normalize(rows.astype(F32), gain).astype(BF16)


def whole(parts, gain):
    rows = [part[...] for part in parts]
    return normed(rows[0] if len(rows) == 1 else jnp.concatenate(rows, axis=0), gain)


def grouped(refs, counts):
    blocks, first = [], 0
    for count in counts:
        blocks.append(refs[first : first + count])
        first += count
    return blocks


def fold(values, combine, total):
    for lane in range(0, values.shape[1], 128):
        piece = values[:, lane : lane + 128]
        total = piece if total is None else combine(total, piece)
    return total


def attend(queries, keys, scores, start, peak, sums, added):
    height = queries.shape[0]
    top = None
    for i, key in enumerate(keys):
        part = nt_dot(queries, key)
        scores[i, start : start + height] = part
        top = fold(part, jnp.maximum, top)
    top = jnp.max(top, axis=-1, keepdims=True)
    if peak is not None:
        top = jnp.maximum(top, peak)
        shrink = jnp.exp2(peak - top)
        sums = sums * shrink
        added = added * shrink
    for i, key in enumerate(keys):
        weights = jnp.exp2(scores[i, start : start + height] - top)
        sums = fold(weights, jnp.add, sums)
        part = jnp.dot(weights.astype(BF16), key, preferred_element_type=F32)
        added = part if added is None else added + part
    return top, sums, added


def fuse_kernel(scale, query_ref, key_ref, value_ref, out_ref, score_ref, mix_ref):
    score_ref[...] = (nt_dot(query_ref[...], key_ref[...]) * scale).astype(BF16)
    mix_ref[...] = jnp.dot(
        value_ref[...], out_ref[...], preferred_element_type=F32
    ).astype(BF16)


def lead(rows, score_weight):
    return jnp.dot(rows, score_weight[...], preferred_element_type=F32).astype(BF16)


def early_kernel(counts, score_ref, gain_ref, *refs):
    blocks = grouped(refs, counts)
    own_query_ref, peak_ref, sums_ref, added_ref, keys_ref, scores = refs[-6:]
    gain = gain_ref[...].reshape(1, score_ref.shape[0])
    keys = [whole(parts, gain) for parts in blocks]
    for i, key in enumerate(keys):
        keys_ref[i] = key
    queries = lead(keys[0], score_ref)
    own_query_ref[...] = queries
    peak, sums, added = attend(queries, keys, scores, 0, None, None, None)
    peak_ref[...] = jnp.broadcast_to(peak, peak_ref.shape)
    sums_ref[...] = sums
    added_ref[...] = added


def late_kernel(
    width,
    sources,
    counts,
    early,
    own_query_ref,
    peak_ref,
    sums_ref,
    added_ref,
    keys_ref,
    resid_ref,
    gain_ref,
    score_ref,
    mix_weight_ref,
    *refs,
):
    blocks = grouped(refs, counts)
    mid_ref, swap_ref, scores, mid, halo = refs[sum(counts) :]
    place = lax.axis_index("rows")
    core = place % 2
    chip = place // 2
    own, channels = own_query_ref.shape
    devices = len(sources[0])

    for block, origin in zip(blocks, sources):
        for step, part, low in ((-1, block[-1], 0), (1, block[0], width)):
            first = part.shape[0] - width if step < 0 else 0
            takers = [d for d in range(devices) if origin[d] == d // 2 + step]
            if not takers:
                continue
            wanted = place == takers[0]
            for d in takers[1:]:
                wanted = jnp.logical_or(wanted, place == d)

            @pl.when(wanted)
            def _(part=part, first=first, low=low):
                halo[low : low + width] = part[first : first + width, :]

    no_above = chip == 0
    no_below = chip == devices // 2 - 1

    @pl.when(no_above)
    def _():
        halo[:width] = jnp.zeros((width, channels), BF16)

    @pl.when(no_below)
    def _():
        halo[width:] = jnp.zeros((width, channels), BF16)

    gain = gain_ref[...].reshape(1, channels)
    edge_resid = halo[...].astype(F32)
    edge_query = lead(normed(edge_resid, gain), score_ref)
    keys = [keys_ref[i] for i in range(early)]
    keys = keys + [whole(parts, gain) for parts in blocks[early:]]
    _, edge_sums, edge_added = attend(edge_query, keys, scores, own, None, None, None)
    _, own_sums, own_added = attend(
        own_query_ref[...],
        keys[early:],
        scores,
        0,
        peak_ref[:, :1],
        sums_ref[...],
        added_ref[...],
    )

    def finish(added, sums):
        return (added / jnp.sum(sums, axis=-1, keepdims=True)).astype(BF16)

    mixed = jnp.concatenate([finish(own_added, own_sums), finish(edge_added, edge_sums)], axis=0)
    projected = jnp.dot(mixed, mix_weight_ref[...], preferred_element_type=F32)
    inner = own + width
    mid[width:inner] = (resid_ref[...] + projected[:own]).astype(BF16)
    edges = edge_resid + projected[own:]
    mid[:width] = jnp.where(no_above, 0.0, edges[:width]).astype(BF16)
    mid[inner:] = jnp.where(no_below, 0.0, edges[width:]).astype(BF16)
    mid_ref[...] = mid[pl.ds(pl.multiple_of(2 * core * width, width), 4 * width), :]
    swap_ref[...] = mid[pl.ds(pl.multiple_of(2 * (1 - core) * width, width), 4 * width), :]


def up_rows(width, ref, weight_ref, out, done=lambda pair: None):
    channels = ref.shape[1]
    outputs = weight_ref.shape[2]
    span = 4 * width
    wide = 2 * width
    column = lax.broadcasted_iota(jnp.int32, (1, span), 1) % width
    line = lax.broadcasted_iota(jnp.int32, (2 * wide, 2 * wide), 0)
    lane = lax.broadcasted_iota(jnp.int32, (2 * wide, 2 * wide), 1)
    target = 2 * (line % wide) + line // wide
    weave = (target == lane).astype(BF16)
    lhs = jnp.concatenate(
        [weight_ref[j].reshape(3 * outputs, channels) for j in range(3)], axis=1
    )
    turned = jnp.transpose(ref[...].astype(F32)).astype(BF16)
    rows = [turned[:, row * width : (row + 1) * width] for row in range(4)]
    picks = ((0, 1, 1), (1, 1, 2), (1, 2, 2), (2, 2, 3))
    rhs = jnp.concatenate(
        [jnp.concatenate([rows[pick[j]] for pick in picks], axis=1) for j in range(3)], axis=0
    )
    taps = jnp.dot(lhs, rhs, preferred_element_type=F32)
    left, middle, right = (taps[col * outputs : (col + 1) * outputs] for col in range(3))
    even = middle + right + jnp.where(column == 0, 0.0, pltpu.roll(left, 1, axis=1))
    odd = left + middle
    odd = odd + jnp.where(column == width - 1, 0.0, pltpu.roll(right, span - 1, axis=1))
    even, odd = even.astype(BF16), odd.astype(BF16)
    for pair in range(2):
        both = slice(pair * wide, (pair + 1) * wide)
        mixed = jnp.concatenate([even[:, both], odd[:, both]], axis=1)
        woven = jnp.dot(mixed, weave, preferred_element_type=F32).astype(BF16)
        for i in range(2):
            out[2 * pair + i] = woven[:, i * wide : (i + 1) * wide]
        done(pair)


def up_own_kernel(width, rows_ref, weight_ref, out_ref):
    up_rows(width, rows_ref, weight_ref, out_ref)


def up_kernel(width, rows_ref, weight_ref, own_ref, out_ref, result, sems):
    core = lax.axis_index("rows") % 2
    stores = start_all([(own_ref, out_ref.at[core])], sems)

    def store(pair):
        rows = pl.ds(2 * pair, 2)
        stores.extend(start_all([(result.at[rows], out_ref.at[1 - core, rows])], sems, 1 + pair))

    up_rows(width, rows_ref, weight_ref, result, store)
    wait_all(stores)


def gather_blocks(block, halves, count):
    chips = count // 2
    depth = 2 if chips % 2 == 0 else 1
    length = chips // depth

    ring = [0] + list(range(1, length, 2)) + list(range(2, length, 2))[::-1]
    follow = {a: ring[(i + 1) % length] for i, a in enumerate(ring)}
    forth = {a * depth + b: follow[a] * depth + b for a in range(length) for b in range(depth)}
    return_ = {target: source for source, target in forth.items()}
    onward = (return_, forth)
    backward = (forth, return_)
    across = ({k: k ^ 1 for k in range(chips)},) * 2

    def send(parts, targets):
        pairs = [(2 * k + c, 2 * targets[c][k] + c) for k in range(chips) for c in range(2)]
        return [lax.ppermute(part, "rows", pairs) for part in parts]

    def moved(origin, targets):
        return tuple({targets[c][k]: origin[c][k] for k in range(chips)} for c in range(2))

    def tie(*places):
        fixed = lax.optimization_barrier(tuple(where[i] for where, i in places))
        for (where, i), value in zip(places, fixed):
            where[i] = value

    here = ({k: k for k in range(chips)},) * 2
    early, late = [([block], here)], []
    own_again = [block]
    crossed = last = None
    if depth == 2:
        crossed = send(halves, across)
    steps = length - 2
    parts, origin = list(halves), here
    for step in range(1, steps + 1):
        parts, origin = send(parts, onward), moved(origin, onward)
        for h in range(2):
            places = [(parts, h)]
            if last:
                places.append((last, h))
            if step == 1 and h == 1:
                places.append((own_again, 0))
                if depth == 2:
                    places.append((crossed, 0))
            tie(*places)
        early.append((parts, origin))
        if depth == 2:
            last = send(parts, across)
            (late if step == steps else early).append((last, moved(origin, across)))
    if length > 1:
        late.append((send(own_again, backward), moved(here, backward)))
    if depth == 2:
        (early if length > 1 else late).append((crossed, moved(here, across)))
        if length > 1:
            late.append((send(crossed, backward), moved(moved(here, across), backward)))
    return early, late


def shards(
    latents,
    conv_cache,
    norm_gain,
    conv_weight,
    attn_gain,
    query_weight,
    key_weight,
    value_weight,
    out_weight,
    up_weight,
):
    frames, rows_here, width, channels = latents.shape
    outputs = up_weight.shape[3]
    count = lax.axis_size("rows")
    span = 2 * rows_here * width
    own = rows_here * width
    edge = jax.ShapeDtypeStruct((width, channels), BF16)
    anywhere = pl.BlockSpec(memory_space=pl.ANY)
    hbm = pl.BlockSpec(memory_space=pltpu.HBM)

    chips = count // 2
    swap = [(2 * k + c, 2 * k + 1 - c) for k in range(chips) for c in range(2)]
    neighbour = [(2 * k + 1, 2 * k + 2) for k in range(chips - 1)]
    neighbour = neighbour + [(target, source) for source, target in neighbour]

    latents_in = pltpu.with_memory_space_constraint(latents, pltpu.HBM)
    cache_in = pltpu.with_memory_space_constraint(conv_cache, pltpu.HBM)
    edge_rows, both = pl.pallas_call(
        edges_kernel,
        out_shape=(
            jax.ShapeDtypeStruct((2 * frames, width, channels), BF16),
            jax.ShapeDtypeStruct((3, rows_here, width, channels), BF16),
        ),
        in_specs=[hbm] * 2,
        out_specs=(anywhere,) * 2,
        scratch_shapes=[pltpu.SemaphoreType.DMA((5,))],
        cost_estimate=cost(0, 20 * width * channels),
        compiler_params=params(4),
    )(latents_in, cache_in)
    edge_rows = lax.ppermute(edge_rows, "rows", neighbour)
    both = lax.ppermute(both, "rows", swap)
    act, own_rows, staged = pl.pallas_call(
        prepare_kernel,
        out_shape=(
            jax.ShapeDtypeStruct((frames, own, channels), BF16),
            jax.ShapeDtypeStruct((3, own, channels), BF16),
            jax.ShapeDtypeStruct((3, 3, channels, 3 * channels), BF16),
        ),
        in_specs=[hbm] * 4,
        out_specs=(anywhere, vmem(), anywhere),
        scratch_shapes=[
            pltpu.VMEM((frames, own, channels), BF16),
            pltpu.VMEM((frames, own, channels), BF16),
            pltpu.VMEM((channels,), F32),
            pltpu.VMEM((frames, own, channels), BF16),
            pltpu.SemaphoreType.DMA((13,)),
        ],
        cost_estimate=cost(10 * frames * own * channels, 2 * 27 * channels * channels),
        compiler_params=params(8),
    )(
        pltpu.with_memory_space_constraint(latents.reshape(frames, own, channels), pltpu.HBM),
        pltpu.with_memory_space_constraint(conv_cache.reshape(frames, own, channels), pltpu.HBM),
        pltpu.with_memory_space_constraint(conv_weight, pltpu.HBM),
        pltpu.with_memory_space_constraint(norm_gain, pltpu.HBM),
    )

    edge_rows, own_rows = lax.optimization_barrier((edge_rows, own_rows))
    far_rows = lax.ppermute(edge_rows, "rows", swap)
    block = jax.ShapeDtypeStruct((span, channels), BF16)
    half = jax.ShapeDtypeStruct((span // 2, channels), BF16)
    sent, front, back, resid = pl.pallas_call(
        functools.partial(conv_kernel, width),
        out_shape=(block, half, half, jax.ShapeDtypeStruct((span, channels), F32)),
        in_specs=[vmem()] * 6,
        out_specs=(vmem(),) * 4,
        scratch_shapes=[
            pltpu.VMEM((3, 6 * width, channels), BF16),
            pltpu.VMEM((6 * width, channels), BF16),
            pltpu.VMEM((6 * width, channels), BF16),
            pltpu.VMEM((span, 3 * channels), F32),
        ],
        cost_estimate=cost(2 * 27 * span * channels * channels, 2 * 27 * channels * channels),
        compiler_params=params(20),
    )(
        own_rows,
        both.reshape(3, own, channels),
        edge_rows,
        far_rows,
        norm_gain,
        staged,
    )

    early, late = gather_blocks(sent, (front, back), count)
    blocks = early + late
    sources = [[origin[d % 2][d // 2] for d in range(count)] for _, origin in blocks]
    counts = [len(parts) for parts, _ in blocks]
    early_parts = [part for parts, _ in early for part in parts]
    all_parts = [part for parts, _ in blocks for part in parts]

    scale = channels ** (-0.5) * 1.4426950408889634
    square = jax.ShapeDtypeStruct((channels, channels), BF16)
    score_weight, mix_weight = pl.pallas_call(
        functools.partial(fuse_kernel, scale),
        out_shape=(square, square),
        in_specs=[vmem()] * 4,
        out_specs=(vmem(),) * 2,
        cost_estimate=cost(4 * channels**3, 12 * channels * channels),
        compiler_params=params(8),
    )(query_weight, key_weight, value_weight, out_weight)

    wide = span + 2 * width
    lanes = jax.ShapeDtypeStruct((span, 128), F32)
    own_query, peak, sums, added, early_keys = pl.pallas_call(
        functools.partial(early_kernel, counts[: len(early)]),
        out_shape=(
            jax.ShapeDtypeStruct((span, channels), BF16),
            lanes,
            lanes,
            jax.ShapeDtypeStruct((span, channels), F32),
            jax.ShapeDtypeStruct((len(early), span, channels), BF16),
        ),
        in_specs=[vmem()] * (2 + len(early_parts)),
        out_specs=(vmem(),) * 5,
        scratch_shapes=[pltpu.VMEM((len(early), span, span), F32)],
        cost_estimate=cost(
            4 * span * span * len(early) * channels,
            2 * span * channels * len(early),
            span * span * len(early),
        ),
        compiler_params=params(24),
    )(score_weight, attn_gain, *early_parts)

    mid, swap_rows = pl.pallas_call(
        functools.partial(late_kernel, width, sources, counts, len(early)),
        out_shape=(jax.ShapeDtypeStruct((4 * width, channels), BF16),) * 2,
        in_specs=[vmem()] * (9 + len(all_parts)),
        out_specs=(vmem(),) * 2,
        scratch_shapes=[
            pltpu.VMEM((len(blocks), wide, span), F32),
            pltpu.VMEM((wide, channels), BF16),
            pltpu.VMEM((2 * width, channels), BF16),
        ],
        cost_estimate=cost(
            2 * wide * span * len(blocks) * channels,
            2 * span * channels * len(blocks),
            wide * span * len(blocks) // 2,
        ),
        compiler_params=params(28),
    )(
        own_query,
        peak,
        sums,
        added,
        early_keys,
        resid,
        attn_gain,
        score_weight,
        mix_weight,
        *all_parts,
    )

    swap_rows = lax.ppermute(swap_rows, "rows", swap)

    fine_shape = (2 * rows_here, outputs, 2 * width)
    taps = jnp.transpose(up_weight, (0, 1, 3, 2))
    up_cost = cost(2 * 9 * outputs * channels * 4 * width, 2 * 9 * outputs * channels)
    own_fine = pl.pallas_call(
        functools.partial(up_own_kernel, width),
        out_shape=jax.ShapeDtypeStruct(fine_shape, BF16),
        in_specs=[vmem()] * 2,
        out_specs=vmem(),
        cost_estimate=up_cost,
        compiler_params=params(16),
    )(mid, taps)
    decoded = pl.pallas_call(
        functools.partial(up_kernel, width),
        out_shape=jax.ShapeDtypeStruct((frames, *fine_shape), BF16),
        in_specs=[vmem()] * 3,
        out_specs=anywhere,
        scratch_shapes=[
            pltpu.VMEM(fine_shape, BF16),
            pltpu.SemaphoreType.DMA((3,)),
        ],
        cost_estimate=up_cost,
        compiler_params=params(16),
    )(swap_rows, taps, own_fine)
    decoded = jnp.transpose(decoded, (0, 1, 3, 2))
    return (decoded, act.reshape(frames, rows_here, width, channels))


def solution(mesh):
    return jax.shard_map(
        shards,
        mesh=mesh,
        in_specs=(
            P("videos", "rows", None, None),
            P("videos", "rows", None, None),
            P(),
            P(),
            P(),
            P(),
            P(),
            P(),
            P(),
            P(),
        ),
        out_specs=(P("videos", "rows", None, None), P("videos", "rows", None, None)),
        check_vma=False,
    )
```

```python
import functools

import jax
import jax.numpy as jnp
from jax import lax
from jax.experimental import pallas as pl
from jax.experimental.pallas import tpu as pltpu
from jax.sharding import PartitionSpec as P

BF16 = jnp.bfloat16
F32 = jnp.float32
EPS = 1e-06
MIB = 1024 * 1024


def normalize(values, gain):
    return values * lax.rsqrt(jnp.mean(values * values, axis=-1, keepdims=True) + EPS) * gain


def activate(values, gain):
    normed = normalize(values.astype(F32), gain)
    return (normed / (1.0 + jnp.exp(-normed))).astype(BF16)


def vmem():
    return pl.BlockSpec(memory_space=pltpu.VMEM)


def params(mib):
    return pltpu.CompilerParams(vmem_limit_bytes=mib * MIB)


def cost(flops, size, exps=0):
    return pl.CostEstimate(flops=flops, bytes_accessed=size, transcendentals=exps)


def edges_kernel(latents_ref, cache_ref, edge_ref, sems):
    row = lax.axis_index("rows") % 2 * (latents_ref.shape[1] - 1)
    copies = [
        pltpu.make_async_copy(cache_ref.at[:, row], edge_ref.at[pl.ds(0, 2)], sems.at[0]),
        pltpu.make_async_copy(latents_ref.at[:, row], edge_ref.at[pl.ds(2, 2)], sems.at[1]),
    ]
    for copy in copies:
        copy.start()
    for copy in copies:
        copy.wait()


def start_all(pairs, sems, first=0):
    copies = [
        pltpu.make_async_copy(source, target, sems.at[first + i])
        for i, (source, target) in enumerate(pairs)
    ]
    for copy in copies:
        copy.start()
    return copies


def wait_all(copies):
    for copy in copies:
        copy.wait()


def prepare_kernel(
    latents_ref,
    cache_ref,
    weight_ref,
    gain_ref,
    act_ref,
    own_ref,
    both_ref,
    staged_ref,
    latents,
    cache,
    gain,
    act,
    sems,
):
    channels = latents_ref.shape[-1]
    core = lax.axis_index("rows") % 2
    loads = start_all([(latents_ref, latents), (cache_ref, cache), (gain_ref, gain)], sems)
    stages = start_all(
        [
            (
                weight_ref.at[time, :, col],
                staged_ref.at[time, :, :, pl.ds(col * channels, channels)],
            )
            for time in range(3)
            for col in range(3)
        ],
        sems,
        4,
    )
    wait_all(loads)
    act[...] = activate(latents[...], gain[...].reshape(1, channels))
    store = start_all([(act, act_ref)], sems, 3)
    own_ref[0] = cache[core]
    own_ref[1] = jnp.where(core == 0, cache[1], latents[0])
    own_ref[2] = latents[core]
    both_ref[0] = cache[1 - core]
    both_ref[1] = jnp.where(core == 0, latents[0], cache[1])
    both_ref[2] = latents[1 - core]
    wait_all(store + stages)


def conv_kernel(
    width,
    own_ref,
    swap_ref,
    edge_ref,
    far_ref,
    norm_gain_ref,
    weights,
    sent_ref,
    front_ref,
    back_ref,
    resid_ref,
    raw,
    second,
    third,
    total,
):
    channels = own_ref.shape[-1]
    core = lax.axis_index("rows") % 2
    own = 2 * width
    span = 4 * width
    gain = norm_gain_ref[...].reshape(1, channels)

    def put(index, values):
        rows = pl.ds(pl.multiple_of(index * width, width), values.shape[1])
        raw[:, rows, :] = values

    put(1 + 2 * core, own_ref[...])
    put(3 - 2 * core, swap_ref[...])
    put(5 * core, edge_ref[pl.ds(core, 3)])
    put(5 * (1 - core), far_ref[pl.ds(core, 3)])

    def taps(ref, time):
        lhs = jnp.concatenate([ref[row * width : row * width + span] for row in range(3)], axis=1)
        rhs = weights[time].reshape(3 * channels, 3 * channels)
        return jnp.dot(lhs, rhs, preferred_element_type=F32)

    total[...] = taps(raw.at[0], 0)
    second[...] = jnp.where(core == 1, activate(raw[1], gain), raw[1])
    third[...] = activate(raw[2], gain)
    total[...] += taps(second, 1)
    total[...] += taps(third, 2)

    column = lax.broadcasted_iota(jnp.int32, (span, 1), 0) % width
    left = pltpu.roll(total[:, :channels], 1, axis=0)
    right = pltpu.roll(total[:, 2 * channels :], span - 1, axis=0)
    conv_out = total[:, channels : 2 * channels]
    conv_out = conv_out + jnp.where(column == 0, 0.0, left)
    conv_out = conv_out + jnp.where(column == width - 1, 0.0, right)
    resid = raw[2, width : width + span].astype(F32) + conv_out
    resid_ref[...] = resid
    rounded = resid.astype(BF16)
    sent_ref[...] = rounded
    front_ref[...] = rounded[: span // 2]
    back_ref[...] = rounded[span // 2 :]


def nt_dot(a, b):
    return lax.dot_general(a, b, (((1,), (1,)), ((), ())), preferred_element_type=F32)


def normed(rows, gain):
    return normalize(rows.astype(F32), gain).astype(BF16)


def whole(parts, gain):
    rows = [part[...] for part in parts]
    return normed(rows[0] if len(rows) == 1 else jnp.concatenate(rows, axis=0), gain)


def grouped(refs, counts):
    blocks, first = [], 0
    for count in counts:
        blocks.append(refs[first : first + count])
        first += count
    return blocks


def fold(values, combine, total):
    for lane in range(0, values.shape[1], 128):
        piece = values[:, lane : lane + 128]
        total = piece if total is None else combine(total, piece)
    return total


def attend(queries, keys, scores, start, peak, sums, added):
    height = queries.shape[0]
    top = None
    for i, key in enumerate(keys):
        part = nt_dot(queries, key)
        scores[i, start : start + height] = part
        top = fold(part, jnp.maximum, top)
    top = jnp.max(top, axis=-1, keepdims=True)
    if peak is not None:
        top = jnp.maximum(top, peak)
        shrink = jnp.exp2(peak - top)
        sums = sums * shrink
        added = added * shrink
    for i, key in enumerate(keys):
        weights = jnp.exp2(scores[i, start : start + height] - top)
        sums = fold(weights, jnp.add, sums)
        part = jnp.dot(weights.astype(BF16), key, preferred_element_type=F32)
        added = part if added is None else added + part
    return top, sums, added


def fuse_kernel(scale, query_ref, key_ref, value_ref, out_ref, score_ref, mix_ref):
    score_ref[...] = (nt_dot(query_ref[...], key_ref[...]) * scale).astype(BF16)
    mix_ref[...] = jnp.dot(
        value_ref[...], out_ref[...], preferred_element_type=F32
    ).astype(BF16)


def lead(rows, score_weight):
    return jnp.dot(rows, score_weight[...], preferred_element_type=F32).astype(BF16)


def early_kernel(counts, score_ref, gain_ref, *refs):
    blocks = grouped(refs, counts)
    own_query_ref, peak_ref, sums_ref, added_ref, keys_ref, scores = refs[-6:]
    gain = gain_ref[...].reshape(1, score_ref.shape[0])
    keys = [whole(parts, gain) for parts in blocks]
    for i, key in enumerate(keys):
        keys_ref[i] = key
    queries = lead(keys[0], score_ref)
    own_query_ref[...] = queries
    peak, sums, added = attend(queries, keys, scores, 0, None, None, None)
    peak_ref[...] = jnp.broadcast_to(peak, peak_ref.shape)
    sums_ref[...] = sums
    added_ref[...] = added


def late_kernel(
    width,
    sources,
    counts,
    early,
    own_query_ref,
    peak_ref,
    sums_ref,
    added_ref,
    keys_ref,
    resid_ref,
    gain_ref,
    score_ref,
    mix_weight_ref,
    *refs,
):
    blocks = grouped(refs, counts)
    mid_ref, swap_ref, scores, mid, halo = refs[sum(counts) :]
    place = lax.axis_index("rows")
    core = place % 2
    chip = place // 2
    own, channels = own_query_ref.shape
    devices = len(sources[0])

    for block, origin in zip(blocks, sources):
        for step, part, low in ((-1, block[-1], 0), (1, block[0], width)):
            first = part.shape[0] - width if step < 0 else 0
            takers = [d for d in range(devices) if origin[d] == d // 2 + step]
            if not takers:
                continue
            wanted = place == takers[0]
            for d in takers[1:]:
                wanted = jnp.logical_or(wanted, place == d)

            @pl.when(wanted)
            def _(part=part, first=first, low=low):
                halo[low : low + width] = part[first : first + width, :]

    no_above = chip == 0
    no_below = chip == devices // 2 - 1

    @pl.when(no_above)
    def _():
        halo[:width] = jnp.zeros((width, channels), BF16)

    @pl.when(no_below)
    def _():
        halo[width:] = jnp.zeros((width, channels), BF16)

    gain = gain_ref[...].reshape(1, channels)
    edge_resid = halo[...].astype(F32)
    edge_query = lead(normed(edge_resid, gain), score_ref)
    keys = [keys_ref[i] for i in range(early)]
    keys = keys + [whole(parts, gain) for parts in blocks[early:]]
    _, edge_sums, edge_added = attend(edge_query, keys, scores, own, None, None, None)
    _, own_sums, own_added = attend(
        own_query_ref[...],
        keys[early:],
        scores,
        0,
        peak_ref[:, :1],
        sums_ref[...],
        added_ref[...],
    )

    def finish(added, sums):
        return (added / jnp.sum(sums, axis=-1, keepdims=True)).astype(BF16)

    mixed = jnp.concatenate([finish(own_added, own_sums), finish(edge_added, edge_sums)], axis=0)
    projected = jnp.dot(mixed, mix_weight_ref[...], preferred_element_type=F32)
    inner = own + width
    mid[width:inner] = (resid_ref[...] + projected[:own]).astype(BF16)
    edges = edge_resid + projected[own:]
    mid[:width] = jnp.where(no_above, 0.0, edges[:width]).astype(BF16)
    mid[inner:] = jnp.where(no_below, 0.0, edges[width:]).astype(BF16)
    mid_ref[...] = mid[pl.ds(pl.multiple_of(2 * core * width, width), 4 * width), :]
    swap_ref[...] = mid[pl.ds(pl.multiple_of(2 * (1 - core) * width, width), 4 * width), :]


def up_rows(width, ref, weight_ref, out):
    channels = ref.shape[1]
    outputs = weight_ref.shape[2]
    span = 4 * width
    wide = 2 * width
    column = lax.broadcasted_iota(jnp.int32, (1, span), 1) % width
    line = lax.broadcasted_iota(jnp.int32, (2 * wide, 2 * wide), 0)
    lane = lax.broadcasted_iota(jnp.int32, (2 * wide, 2 * wide), 1)
    target = 2 * (line % wide) + line // wide
    weave = (target == lane).astype(BF16)
    lhs = jnp.concatenate(
        [weight_ref[j].reshape(3 * outputs, channels) for j in range(3)], axis=1
    )
    turned = jnp.transpose(ref[...].astype(F32)).astype(BF16)
    rows = [turned[:, row * width : (row + 1) * width] for row in range(4)]
    picks = ((0, 1, 1), (1, 1, 2), (1, 2, 2), (2, 2, 3))
    rhs = jnp.concatenate(
        [jnp.concatenate([rows[pick[j]] for pick in picks], axis=1) for j in range(3)], axis=0
    )
    taps = jnp.dot(lhs, rhs, preferred_element_type=F32)
    left, middle, right = (taps[col * outputs : (col + 1) * outputs] for col in range(3))
    even = middle + right + jnp.where(column == 0, 0.0, pltpu.roll(left, 1, axis=1))
    odd = left + middle
    odd = odd + jnp.where(column == width - 1, 0.0, pltpu.roll(right, span - 1, axis=1))
    even, odd = even.astype(BF16), odd.astype(BF16)
    for pair in range(2):
        both = slice(pair * wide, (pair + 1) * wide)
        mixed = jnp.concatenate([even[:, both], odd[:, both]], axis=1)
        woven = jnp.dot(mixed, weave, preferred_element_type=F32).astype(BF16)
        for i in range(2):
            out[2 * pair + i] = woven[:, i * wide : (i + 1) * wide]


def up_own_kernel(width, rows_ref, weight_ref, out_ref):
    up_rows(width, rows_ref, weight_ref, out_ref)


def up_kernel(width, rows_ref, weight_ref, own_ref, out_ref, result, sems):
    core = lax.axis_index("rows") % 2
    stores = start_all([(own_ref, out_ref.at[core])], sems)
    up_rows(width, rows_ref, weight_ref, result)
    stores = stores + start_all([(result, out_ref.at[1 - core])], sems, 1)
    wait_all(stores)


def gather_blocks(block, halves, count):
    chips = count // 2
    depth = 2 if chips % 2 == 0 else 1
    length = chips // depth

    ring = [0] + list(range(1, length, 2)) + list(range(2, length, 2))[::-1]
    follow = {a: ring[(i + 1) % length] for i, a in enumerate(ring)}
    forth = {a * depth + b: follow[a] * depth + b for a in range(length) for b in range(depth)}
    return_ = {target: source for source, target in forth.items()}
    onward = (forth, return_)
    backward = (return_, forth)
    across = ({k: k ^ 1 for k in range(chips)},) * 2

    def send(parts, targets):
        pairs = [(2 * k + c, 2 * targets[c][k] + c) for k in range(chips) for c in range(2)]
        return [lax.ppermute(part, "rows", pairs) for part in parts]

    def moved(origin, targets):
        return tuple({targets[c][k]: origin[c][k] for k in range(chips)} for c in range(2))

    def tie(*places):
        fixed = lax.optimization_barrier(tuple(where[i] for where, i in places))
        for (where, i), value in zip(places, fixed):
            where[i] = value

    here = ({k: k for k in range(chips)},) * 2
    early, late = [([block], here)], []
    own_again = [block]
    crossed = last = None
    if depth == 2:
        crossed = send(halves, across)
    steps = length - 2
    parts, origin = list(halves), here
    for step in range(1, steps + 1):
        parts, origin = send(parts, onward), moved(origin, onward)
        for h in range(2):
            places = [(parts, h)]
            if last:
                places.append((last, h))
            if step == 1 and h == 1:
                places.append((own_again, 0))
                if depth == 2:
                    places.append((crossed, 0))
            tie(*places)
        early.append((parts, origin))
        if depth == 2:
            last = send(parts, across)
            (late if step == steps else early).append((last, moved(origin, across)))
    if length > 1:
        late.append((send(own_again, backward), moved(here, backward)))
    if depth == 2:
        (early if length > 1 else late).append((crossed, moved(here, across)))
        if length > 1:
            if steps > 0:
                crossed = list(crossed)
                tie((crossed, 0), (parts, 0))
            late.append((send(crossed, backward), moved(moved(here, across), backward)))
    return early, late


def shards(
    latents,
    conv_cache,
    norm_gain,
    conv_weight,
    attn_gain,
    query_weight,
    key_weight,
    value_weight,
    out_weight,
    up_weight,
):
    frames, rows_here, width, channels = latents.shape
    outputs = up_weight.shape[3]
    count = lax.axis_size("rows")
    span = 2 * rows_here * width
    own = rows_here * width
    edge = jax.ShapeDtypeStruct((width, channels), BF16)
    anywhere = pl.BlockSpec(memory_space=pl.ANY)
    hbm = pl.BlockSpec(memory_space=pltpu.HBM)

    chips = count // 2
    swap = [(2 * k + c, 2 * k + 1 - c) for k in range(chips) for c in range(2)]
    neighbour = [(2 * k + 1, 2 * k + 2) for k in range(chips - 1)]
    neighbour = neighbour + [(target, source) for source, target in neighbour]

    latents_in = pltpu.with_memory_space_constraint(latents, pltpu.HBM)
    cache_in = pltpu.with_memory_space_constraint(conv_cache, pltpu.HBM)
    edge_rows = pl.pallas_call(
        edges_kernel,
        out_shape=jax.ShapeDtypeStruct((2 * frames, width, channels), BF16),
        in_specs=[hbm] * 2,
        out_specs=anywhere,
        scratch_shapes=[pltpu.SemaphoreType.DMA((2,))],
        cost_estimate=cost(0, 8 * width * channels),
        compiler_params=params(4),
    )(latents_in, cache_in)
    edge_rows = lax.ppermute(edge_rows, "rows", neighbour)
    act, own_rows, both, staged = pl.pallas_call(
        prepare_kernel,
        out_shape=(
            jax.ShapeDtypeStruct((frames, own, channels), BF16),
            jax.ShapeDtypeStruct((3, own, channels), BF16),
            jax.ShapeDtypeStruct((3, own, channels), BF16),
            jax.ShapeDtypeStruct((3, 3, channels, 3 * channels), BF16),
        ),
        in_specs=[hbm] * 4,
        out_specs=(anywhere, vmem(), vmem(), anywhere),
        scratch_shapes=[
            pltpu.VMEM((frames, own, channels), BF16),
            pltpu.VMEM((frames, own, channels), BF16),
            pltpu.VMEM((channels,), F32),
            pltpu.VMEM((frames, own, channels), BF16),
            pltpu.SemaphoreType.DMA((13,)),
        ],
        cost_estimate=cost(10 * frames * own * channels, 2 * 27 * channels * channels),
        compiler_params=params(8),
    )(
        pltpu.with_memory_space_constraint(latents.reshape(frames, own, channels), pltpu.HBM),
        pltpu.with_memory_space_constraint(conv_cache.reshape(frames, own, channels), pltpu.HBM),
        pltpu.with_memory_space_constraint(conv_weight, pltpu.HBM),
        pltpu.with_memory_space_constraint(norm_gain, pltpu.HBM),
    )

    both = lax.ppermute(both, "rows", swap)
    edge_rows, own_rows = lax.optimization_barrier((edge_rows, own_rows))
    far_rows = lax.ppermute(edge_rows, "rows", swap)
    block = jax.ShapeDtypeStruct((span, channels), BF16)
    half = jax.ShapeDtypeStruct((span // 2, channels), BF16)
    sent, front, back, resid = pl.pallas_call(
        functools.partial(conv_kernel, width),
        out_shape=(block, half, half, jax.ShapeDtypeStruct((span, channels), F32)),
        in_specs=[vmem()] * 6,
        out_specs=(vmem(),) * 4,
        scratch_shapes=[
            pltpu.VMEM((3, 6 * width, channels), BF16),
            pltpu.VMEM((6 * width, channels), BF16),
            pltpu.VMEM((6 * width, channels), BF16),
            pltpu.VMEM((span, 3 * channels), F32),
        ],
        cost_estimate=cost(2 * 27 * span * channels * channels, 2 * 27 * channels * channels),
        compiler_params=params(20),
    )(
        own_rows,
        both,
        edge_rows,
        far_rows,
        norm_gain,
        staged,
    )

    early, late = gather_blocks(sent, (front, back), count)
    blocks = early + late
    sources = [[origin[d % 2][d // 2] for d in range(count)] for _, origin in blocks]
    counts = [len(parts) for parts, _ in blocks]
    early_parts = [part for parts, _ in early for part in parts]
    all_parts = [part for parts, _ in blocks for part in parts]

    scale = channels ** (-0.5) * 1.4426950408889634
    square = jax.ShapeDtypeStruct((channels, channels), BF16)
    score_weight, mix_weight = pl.pallas_call(
        functools.partial(fuse_kernel, scale),
        out_shape=(square, square),
        in_specs=[vmem()] * 4,
        out_specs=(vmem(),) * 2,
        cost_estimate=cost(4 * channels**3, 12 * channels * channels),
        compiler_params=params(8),
    )(query_weight, key_weight, value_weight, out_weight)

    wide = span + 2 * width
    lanes = jax.ShapeDtypeStruct((span, 128), F32)
    own_query, peak, sums, added, early_keys = pl.pallas_call(
        functools.partial(early_kernel, counts[: len(early)]),
        out_shape=(
            jax.ShapeDtypeStruct((span, channels), BF16),
            lanes,
            lanes,
            jax.ShapeDtypeStruct((span, channels), F32),
            jax.ShapeDtypeStruct((len(early), span, channels), BF16),
        ),
        in_specs=[vmem()] * (2 + len(early_parts)),
        out_specs=(vmem(),) * 5,
        scratch_shapes=[pltpu.VMEM((len(early), span, span), F32)],
        cost_estimate=cost(
            4 * span * span * len(early) * channels,
            2 * span * channels * len(early),
            span * span * len(early),
        ),
        compiler_params=params(24),
    )(score_weight, attn_gain, *early_parts)

    mid, swap_rows = pl.pallas_call(
        functools.partial(late_kernel, width, sources, counts, len(early)),
        out_shape=(jax.ShapeDtypeStruct((4 * width, channels), BF16),) * 2,
        in_specs=[vmem()] * (9 + len(all_parts)),
        out_specs=(vmem(),) * 2,
        scratch_shapes=[
            pltpu.VMEM((len(blocks), wide, span), F32),
            pltpu.VMEM((wide, channels), BF16),
            pltpu.VMEM((2 * width, channels), BF16),
        ],
        cost_estimate=cost(
            2 * wide * span * len(blocks) * channels,
            2 * span * channels * len(blocks),
            wide * span * len(blocks) // 2,
        ),
        compiler_params=params(28),
    )(
        own_query,
        peak,
        sums,
        added,
        early_keys,
        resid,
        attn_gain,
        score_weight,
        mix_weight,
        *all_parts,
    )

    swap_rows = lax.ppermute(swap_rows, "rows", swap)

    fine_shape = (2 * rows_here, outputs, 2 * width)
    taps = jnp.transpose(up_weight, (0, 1, 3, 2))
    up_cost = cost(2 * 9 * outputs * channels * 4 * width, 2 * 9 * outputs * channels)
    own_fine = pl.pallas_call(
        functools.partial(up_own_kernel, width),
        out_shape=jax.ShapeDtypeStruct(fine_shape, BF16),
        in_specs=[vmem()] * 2,
        out_specs=vmem(),
        cost_estimate=up_cost,
        compiler_params=params(16),
    )(mid, taps)
    decoded = pl.pallas_call(
        functools.partial(up_kernel, width),
        out_shape=jax.ShapeDtypeStruct((frames, *fine_shape), BF16),
        in_specs=[vmem()] * 3,
        out_specs=anywhere,
        scratch_shapes=[
            pltpu.VMEM(fine_shape, BF16),
            pltpu.SemaphoreType.DMA((2,)),
        ],
        cost_estimate=up_cost,
        compiler_params=params(16),
    )(swap_rows, taps, own_fine)
    decoded = jnp.transpose(decoded, (0, 1, 3, 2))
    return (decoded, act.reshape(frames, rows_here, width, channels))


def solution(mesh):
    return jax.shard_map(
        shards,
        mesh=mesh,
        in_specs=(
            P("videos", "rows", None, None),
            P("videos", "rows", None, None),
            P(),
            P(),
            P(),
            P(),
            P(),
            P(),
            P(),
            P(),
        ),
        out_specs=(P("videos", "rows", None, None), P("videos", "rows", None, None)),
        check_vma=False,
    )
```

```python
import functools

import jax
import jax.numpy as jnp
from jax import lax
from jax.experimental import pallas as pl
from jax.experimental.pallas import tpu as pltpu
from jax.sharding import PartitionSpec as P

BF16 = jnp.bfloat16
F32 = jnp.float32
EPS = 1e-06
MIB = 1024 * 1024


def normalize(values, gain):
    return values * lax.rsqrt(jnp.mean(values * values, axis=-1, keepdims=True) + EPS) * gain


def activate(values, gain):
    normed = normalize(values.astype(F32), gain)
    return (normed / (1.0 + jnp.exp(-normed))).astype(BF16)


def vmem():
    return pl.BlockSpec(memory_space=pltpu.VMEM)


def params(mib):
    return pltpu.CompilerParams(vmem_limit_bytes=mib * MIB)


def cost(flops, size, exps=0):
    return pl.CostEstimate(flops=flops, bytes_accessed=size, transcendentals=exps)


def edges_kernel(latents_ref, cache_ref, edge_ref, sems):
    row = lax.axis_index("rows") % 2 * (latents_ref.shape[1] - 1)
    copies = [
        pltpu.make_async_copy(cache_ref.at[:, row], edge_ref.at[pl.ds(0, 2)], sems.at[0]),
        pltpu.make_async_copy(latents_ref.at[:, row], edge_ref.at[pl.ds(2, 2)], sems.at[1]),
    ]
    for copy in copies:
        copy.start()
    for copy in copies:
        copy.wait()


def start_all(pairs, sems, first=0):
    copies = [
        pltpu.make_async_copy(source, target, sems.at[first + i])
        for i, (source, target) in enumerate(pairs)
    ]
    for copy in copies:
        copy.start()
    return copies


def wait_all(copies):
    for copy in copies:
        copy.wait()


def prepare_kernel(
    latents_ref,
    cache_ref,
    weight_ref,
    gain_ref,
    act_ref,
    own_ref,
    both_ref,
    staged_ref,
    latents,
    cache,
    gain,
    act,
    sems,
):
    channels = latents_ref.shape[-1]
    core = lax.axis_index("rows") % 2
    loads = start_all([(latents_ref, latents), (cache_ref, cache), (gain_ref, gain)], sems)
    stages = start_all(
        [
            (
                weight_ref.at[time, :, col],
                staged_ref.at[time, :, :, pl.ds(col * channels, channels)],
            )
            for time in range(3)
            for col in range(3)
        ],
        sems,
        4,
    )
    wait_all(loads)
    act[...] = activate(latents[...], gain[...].reshape(1, channels))
    store = start_all([(act, act_ref)], sems, 3)
    own_ref[0] = cache[core]
    own_ref[1] = jnp.where(core == 0, cache[1], latents[0])
    own_ref[2] = latents[core]
    both_ref[0] = cache[1 - core]
    both_ref[1] = jnp.where(core == 0, latents[0], cache[1])
    both_ref[2] = latents[1 - core]
    wait_all(store + stages)


def conv_kernel(
    width,
    own_ref,
    swap_ref,
    edge_ref,
    far_ref,
    norm_gain_ref,
    weights,
    sent_ref,
    front_ref,
    back_ref,
    resid_ref,
    raw,
    second,
    third,
    total,
):
    channels = own_ref.shape[-1]
    core = lax.axis_index("rows") % 2
    own = 2 * width
    span = 4 * width
    gain = norm_gain_ref[...].reshape(1, channels)

    def put(index, values):
        rows = pl.ds(pl.multiple_of(index * width, width), values.shape[1])
        raw[:, rows, :] = values

    put(1 + 2 * core, own_ref[...])
    put(3 - 2 * core, swap_ref[...])
    put(5 * core, edge_ref[pl.ds(core, 3)])
    put(5 * (1 - core), far_ref[pl.ds(core, 3)])

    def taps(ref, time):
        lhs = jnp.concatenate([ref[row * width : row * width + span] for row in range(3)], axis=1)
        rhs = weights[time].reshape(3 * channels, 3 * channels)
        return jnp.dot(lhs, rhs, preferred_element_type=F32)

    total[...] = taps(raw.at[0], 0)
    second[...] = jnp.where(core == 1, activate(raw[1], gain), raw[1])
    third[...] = activate(raw[2], gain)
    total[...] += taps(second, 1)
    total[...] += taps(third, 2)

    column = lax.broadcasted_iota(jnp.int32, (span, 1), 0) % width
    left = pltpu.roll(total[:, :channels], 1, axis=0)
    right = pltpu.roll(total[:, 2 * channels :], span - 1, axis=0)
    conv_out = total[:, channels : 2 * channels]
    conv_out = conv_out + jnp.where(column == 0, 0.0, left)
    conv_out = conv_out + jnp.where(column == width - 1, 0.0, right)
    resid = raw[2, width : width + span].astype(F32) + conv_out
    resid_ref[...] = resid
    rounded = resid.astype(BF16)
    sent_ref[...] = rounded
    front_ref[...] = rounded[: span // 2]
    back_ref[...] = rounded[span // 2 :]


def nt_dot(a, b):
    return lax.dot_general(a, b, (((1,), (1,)), ((), ())), preferred_element_type=F32)


def normed(rows, gain):
    return normalize(rows.astype(F32), gain).astype(BF16)


def whole(parts, gain):
    rows = [part[...] for part in parts]
    return normed(rows[0] if len(rows) == 1 else jnp.concatenate(rows, axis=0), gain)


def grouped(refs, counts):
    blocks, first = [], 0
    for count in counts:
        blocks.append(refs[first : first + count])
        first += count
    return blocks


def fold(values, combine, total):
    for lane in range(0, values.shape[1], 128):
        piece = values[:, lane : lane + 128]
        total = piece if total is None else combine(total, piece)
    return total


def attend(queries, keys, scores, start, peak, sums, added):
    height = queries.shape[0]
    top = None
    for i, key in enumerate(keys):
        part = nt_dot(queries, key)
        scores[i, start : start + height] = part
        top = fold(part, jnp.maximum, top)
    top = jnp.max(top, axis=-1, keepdims=True)
    if peak is not None:
        top = jnp.maximum(top, peak)
        shrink = jnp.exp2(peak - top)
        sums = sums * shrink
        added = added * shrink
    for i, key in enumerate(keys):
        weights = jnp.exp2(scores[i, start : start + height] - top)
        sums = fold(weights, jnp.add, sums)
        part = jnp.dot(weights.astype(BF16), key, preferred_element_type=F32)
        added = part if added is None else added + part
    return top, sums, added


def fuse_kernel(scale, query_ref, key_ref, value_ref, out_ref, score_ref, mix_ref):
    score_ref[...] = (nt_dot(query_ref[...], key_ref[...]) * scale).astype(BF16)
    mix_ref[...] = jnp.dot(
        value_ref[...], out_ref[...], preferred_element_type=F32
    ).astype(BF16)


def lead(rows, score_weight):
    return jnp.dot(rows, score_weight[...], preferred_element_type=F32).astype(BF16)


def early_kernel(counts, score_ref, gain_ref, *refs):
    blocks = grouped(refs, counts)
    own_query_ref, peak_ref, sums_ref, added_ref, keys_ref, scores = refs[-6:]
    gain = gain_ref[...].reshape(1, score_ref.shape[0])
    keys = [whole(parts, gain) for parts in blocks]
    for i, key in enumerate(keys):
        keys_ref[i] = key
    queries = lead(keys[0], score_ref)
    own_query_ref[...] = queries
    peak, sums, added = attend(queries, keys, scores, 0, None, None, None)
    peak_ref[...] = jnp.broadcast_to(peak, peak_ref.shape)
    sums_ref[...] = sums
    added_ref[...] = added


def late_kernel(
    width,
    sources,
    counts,
    early,
    own_query_ref,
    peak_ref,
    sums_ref,
    added_ref,
    keys_ref,
    resid_ref,
    gain_ref,
    score_ref,
    mix_weight_ref,
    *refs,
):
    blocks = grouped(refs, counts)
    mid_ref, swap_ref, scores, mid, halo = refs[sum(counts) :]
    place = lax.axis_index("rows")
    core = place % 2
    chip = place // 2
    own, channels = own_query_ref.shape
    devices = len(sources[0])

    for block, origin in zip(blocks, sources):
        for step, part, low in ((-1, block[-1], 0), (1, block[0], width)):
            first = part.shape[0] - width if step < 0 else 0
            takers = [d for d in range(devices) if origin[d] == d // 2 + step]
            if not takers:
                continue
            wanted = place == takers[0]
            for d in takers[1:]:
                wanted = jnp.logical_or(wanted, place == d)

            @pl.when(wanted)
            def _(part=part, first=first, low=low):
                halo[low : low + width] = part[first : first + width, :]

    no_above = chip == 0
    no_below = chip == devices // 2 - 1

    @pl.when(no_above)
    def _():
        halo[:width] = jnp.zeros((width, channels), BF16)

    @pl.when(no_below)
    def _():
        halo[width:] = jnp.zeros((width, channels), BF16)

    gain = gain_ref[...].reshape(1, channels)
    edge_resid = halo[...].astype(F32)
    edge_query = lead(normed(edge_resid, gain), score_ref)
    keys = [keys_ref[i] for i in range(early)]
    keys = keys + [whole(parts, gain) for parts in blocks[early:]]
    _, edge_sums, edge_added = attend(edge_query, keys, scores, own, None, None, None)
    _, own_sums, own_added = attend(
        own_query_ref[...],
        keys[early:],
        scores,
        0,
        peak_ref[:, :1],
        sums_ref[...],
        added_ref[...],
    )

    def finish(added, sums):
        return (added / jnp.sum(sums, axis=-1, keepdims=True)).astype(BF16)

    mixed = jnp.concatenate([finish(own_added, own_sums), finish(edge_added, edge_sums)], axis=0)
    projected = jnp.dot(mixed, mix_weight_ref[...], preferred_element_type=F32)
    inner = own + width
    mid[width:inner] = (resid_ref[...] + projected[:own]).astype(BF16)
    edges = edge_resid + projected[own:]
    mid[:width] = jnp.where(no_above, 0.0, edges[:width]).astype(BF16)
    mid[inner:] = jnp.where(no_below, 0.0, edges[width:]).astype(BF16)
    mid_ref[...] = mid[pl.ds(pl.multiple_of(2 * core * width, width), 4 * width), :]
    swap_ref[...] = mid[pl.ds(pl.multiple_of(2 * (1 - core) * width, width), 4 * width), :]


def up_rows(width, ref, weight_ref, out, done=lambda pair: None):
    channels = ref.shape[1]
    outputs = weight_ref.shape[2]
    span = 4 * width
    wide = 2 * width
    column = lax.broadcasted_iota(jnp.int32, (1, span), 1) % width
    line = lax.broadcasted_iota(jnp.int32, (2 * wide, 2 * wide), 0)
    lane = lax.broadcasted_iota(jnp.int32, (2 * wide, 2 * wide), 1)
    target = 2 * (line % wide) + line // wide
    weave = (target == lane).astype(BF16)
    lhs = jnp.concatenate(
        [weight_ref[j].reshape(3 * outputs, channels) for j in range(3)], axis=1
    )
    turned = jnp.transpose(ref[...].astype(F32)).astype(BF16)
    rows = [turned[:, row * width : (row + 1) * width] for row in range(4)]
    picks = ((0, 1, 1), (1, 1, 2), (1, 2, 2), (2, 2, 3))
    rhs = jnp.concatenate(
        [jnp.concatenate([rows[pick[j]] for pick in picks], axis=1) for j in range(3)], axis=0
    )
    taps = jnp.dot(lhs, rhs, preferred_element_type=F32)
    left, middle, right = (taps[col * outputs : (col + 1) * outputs] for col in range(3))
    even = middle + right + jnp.where(column == 0, 0.0, pltpu.roll(left, 1, axis=1))
    odd = left + middle
    odd = odd + jnp.where(column == width - 1, 0.0, pltpu.roll(right, span - 1, axis=1))
    even, odd = even.astype(BF16), odd.astype(BF16)
    for pair in range(2):
        both = slice(pair * wide, (pair + 1) * wide)
        mixed = jnp.concatenate([even[:, both], odd[:, both]], axis=1)
        woven = jnp.dot(mixed, weave, preferred_element_type=F32).astype(BF16)
        for i in range(2):
            out[2 * pair + i] = woven[:, i * wide : (i + 1) * wide]
        done(pair)


def up_own_kernel(width, rows_ref, weight_ref, out_ref):
    up_rows(width, rows_ref, weight_ref, out_ref)


def up_kernel(width, rows_ref, weight_ref, own_ref, out_ref, result, sems):
    core = lax.axis_index("rows") % 2
    stores = start_all([(own_ref, out_ref.at[core])], sems)

    def store(pair):
        rows = pl.ds(2 * pair, 2)
        stores.extend(start_all([(result.at[rows], out_ref.at[1 - core, rows])], sems, 1 + pair))

    up_rows(width, rows_ref, weight_ref, result, store)
    wait_all(stores)


def gather_blocks(block, halves, count):
    chips = count // 2
    depth = 2 if chips % 2 == 0 else 1
    length = chips // depth

    ring = [0] + list(range(1, length, 2)) + list(range(2, length, 2))[::-1]
    follow = {a: ring[(i + 1) % length] for i, a in enumerate(ring)}
    forth = {a * depth + b: follow[a] * depth + b for a in range(length) for b in range(depth)}
    return_ = {target: source for source, target in forth.items()}
    onward = (forth, return_)
    backward = (return_, forth)
    across = ({k: k ^ 1 for k in range(chips)},) * 2

    def send(parts, targets):
        pairs = [(2 * k + c, 2 * targets[c][k] + c) for k in range(chips) for c in range(2)]
        return [lax.ppermute(part, "rows", pairs) for part in parts]

    def moved(origin, targets):
        return tuple({targets[c][k]: origin[c][k] for k in range(chips)} for c in range(2))

    def tie(*places):
        fixed = lax.optimization_barrier(tuple(where[i] for where, i in places))
        for (where, i), value in zip(places, fixed):
            where[i] = value

    here = ({k: k for k in range(chips)},) * 2
    early, late = [([block], here)], []
    own_again = [block]
    crossed = last = None
    if depth == 2:
        crossed = send(halves, across)
    steps = length - 2
    parts, origin = list(halves), here
    for step in range(1, steps + 1):
        parts, origin = send(parts, onward), moved(origin, onward)
        for h in range(2):
            places = [(parts, h)]
            if last:
                places.append((last, h))
            if step == 1 and h == 1:
                places.append((own_again, 0))
                if depth == 2:
                    places.append((crossed, 0))
            tie(*places)
        early.append((parts, origin))
        if depth == 2:
            last = send(parts, across)
            (late if step == steps else early).append((last, moved(origin, across)))
    if length > 1:
        late.append((send(own_again, backward), moved(here, backward)))
    if depth == 2:
        (early if length > 1 else late).append((crossed, moved(here, across)))
        if length > 1:
            if steps > 0:
                crossed = list(crossed)
                tie((crossed, 0), (parts, 0))
            late.append((send(crossed, backward), moved(moved(here, across), backward)))
    return early, late


def shards(
    latents,
    conv_cache,
    norm_gain,
    conv_weight,
    attn_gain,
    query_weight,
    key_weight,
    value_weight,
    out_weight,
    up_weight,
):
    frames, rows_here, width, channels = latents.shape
    outputs = up_weight.shape[3]
    count = lax.axis_size("rows")
    span = 2 * rows_here * width
    own = rows_here * width
    edge = jax.ShapeDtypeStruct((width, channels), BF16)
    anywhere = pl.BlockSpec(memory_space=pl.ANY)
    hbm = pl.BlockSpec(memory_space=pltpu.HBM)

    chips = count // 2
    swap = [(2 * k + c, 2 * k + 1 - c) for k in range(chips) for c in range(2)]
    neighbour = [(2 * k + 1, 2 * k + 2) for k in range(chips - 1)]
    neighbour = neighbour + [(target, source) for source, target in neighbour]

    latents_in = pltpu.with_memory_space_constraint(latents, pltpu.HBM)
    cache_in = pltpu.with_memory_space_constraint(conv_cache, pltpu.HBM)
    edge_rows = pl.pallas_call(
        edges_kernel,
        out_shape=jax.ShapeDtypeStruct((2 * frames, width, channels), BF16),
        in_specs=[hbm] * 2,
        out_specs=anywhere,
        scratch_shapes=[pltpu.SemaphoreType.DMA((2,))],
        cost_estimate=cost(0, 8 * width * channels),
        compiler_params=params(4),
    )(latents_in, cache_in)
    edge_rows = lax.ppermute(edge_rows, "rows", neighbour)
    act, own_rows, both, staged = pl.pallas_call(
        prepare_kernel,
        out_shape=(
            jax.ShapeDtypeStruct((frames, own, channels), BF16),
            jax.ShapeDtypeStruct((3, own, channels), BF16),
            jax.ShapeDtypeStruct((3, own, channels), BF16),
            jax.ShapeDtypeStruct((3, 3, channels, 3 * channels), BF16),
        ),
        in_specs=[hbm] * 4,
        out_specs=(anywhere, vmem(), vmem(), anywhere),
        scratch_shapes=[
            pltpu.VMEM((frames, own, channels), BF16),
            pltpu.VMEM((frames, own, channels), BF16),
            pltpu.VMEM((channels,), F32),
            pltpu.VMEM((frames, own, channels), BF16),
            pltpu.SemaphoreType.DMA((13,)),
        ],
        cost_estimate=cost(10 * frames * own * channels, 2 * 27 * channels * channels),
        compiler_params=params(8),
    )(
        pltpu.with_memory_space_constraint(latents.reshape(frames, own, channels), pltpu.HBM),
        pltpu.with_memory_space_constraint(conv_cache.reshape(frames, own, channels), pltpu.HBM),
        pltpu.with_memory_space_constraint(conv_weight, pltpu.HBM),
        pltpu.with_memory_space_constraint(norm_gain, pltpu.HBM),
    )

    both = lax.ppermute(both, "rows", swap)
    edge_rows, own_rows = lax.optimization_barrier((edge_rows, own_rows))
    far_rows = lax.ppermute(edge_rows, "rows", swap)
    block = jax.ShapeDtypeStruct((span, channels), BF16)
    half = jax.ShapeDtypeStruct((span // 2, channels), BF16)
    sent, front, back, resid = pl.pallas_call(
        functools.partial(conv_kernel, width),
        out_shape=(block, half, half, jax.ShapeDtypeStruct((span, channels), F32)),
        in_specs=[vmem()] * 6,
        out_specs=(vmem(),) * 4,
        scratch_shapes=[
            pltpu.VMEM((3, 6 * width, channels), BF16),
            pltpu.VMEM((6 * width, channels), BF16),
            pltpu.VMEM((6 * width, channels), BF16),
            pltpu.VMEM((span, 3 * channels), F32),
        ],
        cost_estimate=cost(2 * 27 * span * channels * channels, 2 * 27 * channels * channels),
        compiler_params=params(20),
    )(
        own_rows,
        both,
        edge_rows,
        far_rows,
        norm_gain,
        staged,
    )

    early, late = gather_blocks(sent, (front, back), count)
    blocks = early + late
    sources = [[origin[d % 2][d // 2] for d in range(count)] for _, origin in blocks]
    counts = [len(parts) for parts, _ in blocks]
    early_parts = [part for parts, _ in early for part in parts]
    all_parts = [part for parts, _ in blocks for part in parts]

    scale = channels ** (-0.5) * 1.4426950408889634
    square = jax.ShapeDtypeStruct((channels, channels), BF16)
    score_weight, mix_weight = pl.pallas_call(
        functools.partial(fuse_kernel, scale),
        out_shape=(square, square),
        in_specs=[vmem()] * 4,
        out_specs=(vmem(),) * 2,
        cost_estimate=cost(4 * channels**3, 12 * channels * channels),
        compiler_params=params(8),
    )(query_weight, key_weight, value_weight, out_weight)

    wide = span + 2 * width
    lanes = jax.ShapeDtypeStruct((span, 128), F32)
    own_query, peak, sums, added, early_keys = pl.pallas_call(
        functools.partial(early_kernel, counts[: len(early)]),
        out_shape=(
            jax.ShapeDtypeStruct((span, channels), BF16),
            lanes,
            lanes,
            jax.ShapeDtypeStruct((span, channels), F32),
            jax.ShapeDtypeStruct((len(early), span, channels), BF16),
        ),
        in_specs=[vmem()] * (2 + len(early_parts)),
        out_specs=(vmem(),) * 5,
        scratch_shapes=[pltpu.VMEM((len(early), span, span), F32)],
        cost_estimate=cost(
            4 * span * span * len(early) * channels,
            2 * span * channels * len(early),
            span * span * len(early),
        ),
        compiler_params=params(24),
    )(score_weight, attn_gain, *early_parts)

    mid, swap_rows = pl.pallas_call(
        functools.partial(late_kernel, width, sources, counts, len(early)),
        out_shape=(jax.ShapeDtypeStruct((4 * width, channels), BF16),) * 2,
        in_specs=[vmem()] * (9 + len(all_parts)),
        out_specs=(vmem(),) * 2,
        scratch_shapes=[
            pltpu.VMEM((len(blocks), wide, span), F32),
            pltpu.VMEM((wide, channels), BF16),
            pltpu.VMEM((2 * width, channels), BF16),
        ],
        cost_estimate=cost(
            2 * wide * span * len(blocks) * channels,
            2 * span * channels * len(blocks),
            wide * span * len(blocks) // 2,
        ),
        compiler_params=params(28),
    )(
        own_query,
        peak,
        sums,
        added,
        early_keys,
        resid,
        attn_gain,
        score_weight,
        mix_weight,
        *all_parts,
    )

    swap_rows = lax.ppermute(swap_rows, "rows", swap)

    fine_shape = (2 * rows_here, outputs, 2 * width)
    taps = jnp.transpose(up_weight, (0, 1, 3, 2))
    up_cost = cost(2 * 9 * outputs * channels * 4 * width, 2 * 9 * outputs * channels)
    own_fine = pl.pallas_call(
        functools.partial(up_own_kernel, width),
        out_shape=jax.ShapeDtypeStruct(fine_shape, BF16),
        in_specs=[vmem()] * 2,
        out_specs=vmem(),
        cost_estimate=up_cost,
        compiler_params=params(16),
    )(mid, taps)
    decoded = pl.pallas_call(
        functools.partial(up_kernel, width),
        out_shape=jax.ShapeDtypeStruct((frames, *fine_shape), BF16),
        in_specs=[vmem()] * 3,
        out_specs=anywhere,
        scratch_shapes=[
            pltpu.VMEM(fine_shape, BF16),
            pltpu.SemaphoreType.DMA((3,)),
        ],
        cost_estimate=up_cost,
        compiler_params=params(16),
    )(swap_rows, taps, own_fine)
    decoded = jnp.transpose(decoded, (0, 1, 3, 2))
    return (decoded, act.reshape(frames, rows_here, width, channels))


def solution(mesh):
    return jax.shard_map(
        shards,
        mesh=mesh,
        in_specs=(
            P("videos", "rows", None, None),
            P("videos", "rows", None, None),
            P(),
            P(),
            P(),
            P(),
            P(),
            P(),
            P(),
            P(),
        ),
        out_specs=(P("videos", "rows", None, None), P("videos", "rows", None, None)),
        check_vma=False,
    )
```
